32 devices in a mesh: dp: 8 (over z, x), fsdp: 4 (over y, core).
Axes of the slice: x: 2, y: 2, z: 4, core: 2. Of those that a mesh axis runs over, the one named last changes fastest.
Arguments:
- patches: bfloat16 [128, 153, 768], P(('dp', 'fsdp')), may hold values from -6 to 6
- counts: int32 [128], P(('dp', 'fsdp')), may hold values from 26 to 153, as said below
- positions: int32 [128, 153], P(('dp', 'fsdp')), may hold values from 0 to 255, as said below
- ln1_gain: bfloat16 [768], P(('dp', 'fsdp')), may hold values from 0.5 to 1.5
- ln1_bias: bfloat16 [768], P(('dp', 'fsdp')), may hold values from -1 to 1
- qkv_weight: bfloat16 [768, 2304], P(('dp', 'fsdp')), may hold values from -0.21875 to 0.21875
- qv_bias: bfloat16 [1536], P(('dp', 'fsdp')), may hold values from -1.5 to 1.5
- out_weight: bfloat16 [768, 768], P(('dp', 'fsdp')), may hold values from -0.625 to 0.625
- out_bias: bfloat16 [768], P(('dp', 'fsdp')), may hold values from -1 to 1
- ln2_gain: bfloat16 [768], P(('dp', 'fsdp')), may hold values from 0.5 to 1.5
- ln2_bias: bfloat16 [768], P(('dp', 'fsdp')), may hold values from -1 to 1
- fc1_weight: bfloat16 [768, 3072], P(('dp', 'fsdp')), may hold values from -0.21875 to 0.21875
- fc1_bias: bfloat16 [3072], P(('dp', 'fsdp')), may hold values from -1.5 to 1.5
- fc2_weight: bfloat16 [3072, 768], P(('dp', 'fsdp')), may hold values from -0.109375 to 0.109375
- fc2_bias: bfloat16 [768], P(('dp', 'fsdp')), may hold values from -1 to 1
- cotangent: bfloat16 [128, 153, 768], P(('dp', 'fsdp')), may hold values from -6 to 6
Outputs:
- output: bfloat16 [128, 153, 768], P(('dp', 'fsdp'))
- input_grad: bfloat16 [128, 153, 768], P(('dp', 'fsdp'))
- ln1_gain_grad: float32 [768], P(('dp', 'fsdp'))
- ln1_bias_grad: float32 [768], P(('dp', 'fsdp'))
- qkv_weight_grad: float32 [768, 2304], P(('dp', 'fsdp'))
- qv_bias_grad: float32 [1536], P(('dp', 'fsdp'))
- out_weight_grad: float32 [768, 768], P(('dp', 'fsdp'))
- out_bias_grad: float32 [768], P(('dp', 'fsdp'))
- ln2_gain_grad: float32 [768], P(('dp', 'fsdp'))
- ln2_bias_grad: float32 [768], P(('dp', 'fsdp'))
- fc1_weight_grad: float32 [768, 3072], P(('dp', 'fsdp'))
- fc1_bias_grad: float32 [3072], P(('dp', 'fsdp'))
- fc2_weight_grad: float32 [3072, 768], P(('dp', 'fsdp'))
- fc2_bias_grad: float32 [768], P(('dp', 'fsdp'))
The draws below stay inside these ranges and needn't reach their ends.
Inputs may be any that keep to these rules, and one draw needn't show every extreme that they name: `counts`: rows at and beyond an image's count are padding; some image has exactly 153. `positions`: row index times 16 plus column index of the patch on the image's grid, distinct within an image; padding rows hold some grid index too.
All inputs are finite; a program needn't handle non-finite values.
Results may differ from the reference program's by a relative error of at most 0.012.
Values may be sent and summed in bfloat16 or wider, within the bound.
No kernel may reach another device: no remote copies, remote signals or barrier semaphores. Data moves between devices by JAX's collectives and lax.ppermute only.
A program may use at most 192 MiB of HBM per device.

```python
import math
import jax
import jax.numpy as jnp
from jax import lax

D = 768
HEADS = 12
FF = 3072
SIDE = 16
IMG_DEV = 4
CAP = 153
LOWEST = 26
IMAGES = 128
N_FSDP = 4


def draw_counts(key, part):
    key = jax.random.fold_in(key, 11)
    first_key, second_key = jax.random.split(key)
    drawn = jax.random.randint(first_key, (IMAGES,), LOWEST, CAP + 1, dtype=jnp.int32)
    chosen = jax.random.randint(second_key, (), 0, IMAGES, dtype=jnp.int32)
    return jnp.where(jnp.arange(IMAGES, dtype=jnp.int32) == chosen, CAP, drawn).astype(jnp.int32)


def draw_positions(key, part):
    key = jax.random.fold_in(key, 23)
    image_keys = jax.random.split(key, IMAGES)

    def one_image(image_key):
        return jax.random.permutation(image_key, SIDE * SIDE)[:CAP]
    return jax.vmap(one_image)(image_keys).astype(jnp.int32)


def steps_of(own_key, dims, cuts, smallest, largest):
    level, own = 1.0, jax.random.fold_in(own_key, 6)
    for axis_at, shards_of in cuts:
        draws = jnp.exp(jax.random.uniform(jax.random.fold_in(own, axis_at), (shards_of,), jnp.float32, smallest / len(cuts), largest / len(cuts)))
        level = level * jnp.repeat(draws, dims[axis_at] // shards_of).reshape([-1 if axis == axis_at else 1 for axis in range(len(dims))])
    return level


def centred(key, shape, scale, most, cuts=(), kind=jnp.bfloat16):
    values = scale * jax.random.normal(key, shape, jnp.float32)
    if cuts:
        values = values * steps_of(key, shape, cuts, -0.22, 0.18)
    return jnp.clip(values, -most, most).astype(kind)


def setup_inputs(seed: int = 0) -> dict:
    splits = jax.random.split(jax.random.key(seed), 17)
    patches = centred(splits[0], (IMAGES, CAP, D), 1.0, 6.0, ((0, 32),))
    counts = draw_counts(jax.random.fold_in(splits[16], 71), 0)
    positions = draw_positions(jax.random.fold_in(splits[16], 71), 0)
    ln1_gain = jnp.clip(1.0 + 0.1 * jax.random.normal(splits[3], (D,), jnp.float32), 0.5, 1.5).astype(jnp.bfloat16)
    ln1_bias = centred(splits[4], (D,), 0.2, 1.0, ((0, 32),))
    qkv_weight = centred(splits[5], (D, 3 * D), D ** -0.5, 0.21875, ((0, 32),))
    qv_bias = centred(splits[6], (2 * D,), 0.3, 1.5, ((0, 32),))
    out_weight = centred(splits[7], (D, D), (D // 8) ** -0.5, 0.625, ((0, 32),))
    out_bias = centred(splits[8], (D,), 0.2, 1.0, ((0, 32),))
    ln2_gain = jnp.clip(1.0 + 0.1 * jax.random.normal(splits[9], (D,), jnp.float32), 0.5, 1.5).astype(jnp.bfloat16)
    ln2_bias = centred(splits[10], (D,), 0.2, 1.0, ((0, 32),))
    fc1_weight = centred(splits[11], (D, FF), D ** -0.5, 0.21875, ((0, 32),))
    fc1_bias = centred(splits[12], (FF,), 0.3, 1.5, ((0, 32),))
    fc2_weight = centred(splits[13], (FF, D), FF ** -0.5, 0.109375, ((0, 32),))
    fc2_bias = centred(splits[14], (D,), 0.2, 1.0, ((0, 32),))
    cotangent = centred(splits[15], (IMAGES, CAP, D), 1.0, 6.0, ((0, 32),))
    return dict(patches=patches, counts=counts, positions=positions, ln1_gain=ln1_gain, ln1_bias=ln1_bias, qkv_weight=qkv_weight, qv_bias=qv_bias, out_weight=out_weight, out_bias=out_bias, ln2_gain=ln2_gain, ln2_bias=ln2_bias, fc1_weight=fc1_weight, fc1_bias=fc1_bias, fc2_weight=fc2_weight, fc2_bias=fc2_bias, cotangent=cotangent)


EPSILON = 1e-06
HIGHEST_PRECISION = lax.Precision.HIGHEST

@jax.custom_vjp
def low(v):
    return lax.optimization_barrier(v.astype(jnp.bfloat16)).astype(jnp.float32)

@jax.custom_vjp
def low_back(v):
    return v

def low_keep(v):
    return (low(v), None)

def low_pass(kept, grad):
    return (grad,)

def back_keep(v):
    return (v, None)

def back_low(kept, grad):
    return (low(grad),)
low.defvjp(low_keep, low_pass)
low_back.defvjp(back_keep, back_low)

def power_slopes(number):
    first_slope = 2.0 ** (-8.0 / number)
    return [first_slope ** (index + 1) for index in range(number)]

def slope_list(heads_total):
    lower_power = 2 ** int(math.floor(math.log2(heads_total)))
    if lower_power == heads_total:
        return power_slopes(heads_total)
    return power_slopes(lower_power) + power_slopes(2 * lower_power)[0::2][:heads_total - lower_power]

def alibi_table(positions, heads_total, side_count):
    grid_rows = (positions // side_count).astype(jnp.float32)
    grid_cols = (positions % side_count).astype(jnp.float32)
    row_delta = grid_rows[:, :, None] - grid_rows[:, None, :]
    col_delta = grid_cols[:, :, None] - grid_cols[:, None, :]
    distance = jnp.sqrt(row_delta * row_delta + col_delta * col_delta)
    slopes = jnp.array(slope_list(heads_total), jnp.float32)
    return -slopes[None, :, None, None] * distance[:, None, :, :]

def layer_norm(values, gain, shift):
    center = lax.optimization_barrier(jnp.mean(values, axis=-1, keepdims=True))
    centered = values - center
    variance = lax.optimization_barrier(jnp.mean(centered * centered, axis=-1, keepdims=True))
    return centered * lax.rsqrt(variance + EPSILON) * gain + shift

def forward(inputs, ln1_gain, ln1_bias, qkv_weight, qv_bias, out_weight, out_bias, ln2_gain, ln2_bias, fc1_weight, fc1_bias, fc2_weight, fc2_bias, alibi_bias, key_mask, valid_rows):
    images, length, width = inputs.shape
    head_dim = width // HEADS
    first_norm = low(layer_norm(inputs, ln1_gain, ln1_bias))
    projected = jnp.einsum('ncd,de->nce', first_norm, qkv_weight, precision=HIGHEST_PRECISION)
    bias_row = jnp.concatenate([qv_bias[:width], jnp.zeros((width,), jnp.float32), qv_bias[width:]])
    projected = low(low_back(projected + bias_row))
    queries = projected[..., :width].reshape(images, length, HEADS, head_dim)
    key_rows = projected[..., width:2 * width].reshape(images, length, HEADS, head_dim)
    values = projected[..., 2 * width:].reshape(images, length, HEADS, head_dim)
    scores = jnp.einsum('nqhe,nkhe->nhqk', queries, key_rows, precision=HIGHEST_PRECISION) * head_dim ** (-0.5)
    scores = low_back(scores + alibi_bias + key_mask[:, None, None, :])
    probs = low(jax.nn.softmax(scores, axis=-1))
    attended = jnp.einsum('nhqk,nkhe->nqhe', probs, values, precision=HIGHEST_PRECISION)
    attended = low(low_back(attended.reshape(images, length, width)))
    attn_out = low_back(jnp.einsum('ncd,de->nce', attended, out_weight, precision=HIGHEST_PRECISION) + out_bias)
    residual = inputs + attn_out
    second_norm = low(layer_norm(residual, ln2_gain, ln2_bias))
    hidden = low_back(jnp.einsum('ncd,df->ncf', second_norm, fc1_weight, precision=HIGHEST_PRECISION) + fc1_bias)
    activated = low(jax.nn.gelu(hidden, approximate=False))
    branch = low_back(jnp.einsum('ncf,fd->ncd', activated, fc2_weight, precision=HIGHEST_PRECISION) + fc2_bias)
    return valid_rows[:, :, None] * (residual + branch)

def reference(patches, counts, positions, ln1_gain, ln1_bias, qkv_weight, qv_bias, out_weight, out_bias, ln2_gain, ln2_bias, fc1_weight, fc1_bias, fc2_weight, fc2_bias, cotangent):
    group_size = IMG_DEV * N_FSDP
    group_count = IMAGES // group_size
    params = tuple((param.astype(jnp.float32) for param in (ln1_gain, ln1_bias, qkv_weight, qv_bias, out_weight, out_bias, ln2_gain, ln2_bias, fc1_weight, fc1_bias, fc2_weight, fc2_bias)))

    def one_group(totals, batch_items):
        group_patches, group_counts, group_positions, group_cotangent = batch_items
        row_index = jnp.arange(CAP, dtype=jnp.int32)
        is_live = row_index[None, :] < group_counts[:, None]
        valid_rows = is_live.astype(jnp.float32)
        key_mask = jnp.where(is_live, 0.0, -1000000000.0).astype(jnp.float32)
        alibi_bias = alibi_table(group_positions, HEADS, SIDE)

        def apply_block(inputs, *weights):
            return forward(inputs, *weights, alibi_bias, key_mask, valid_rows)
        result, pullback = jax.vjp(apply_block, group_patches.astype(jnp.float32), *params)
        gradients = pullback(group_cotangent.astype(jnp.float32))
        totals = tuple((total + grad for total, grad in zip(totals, gradients[1:])))
        return (totals, (result.astype(jnp.bfloat16), gradients[0].astype(jnp.bfloat16)))
    stacked = (patches.reshape(group_count, group_size, CAP, D), counts.reshape(group_count, group_size), positions.reshape(group_count, group_size, CAP), cotangent.reshape(group_count, group_size, CAP, D))
    start_totals = tuple((jnp.zeros_like(param) for param in params))
    totals, (results, input_grads) = lax.scan(one_group, start_totals, stacked)
    return (results.reshape(IMAGES, CAP, D), input_grads.reshape(IMAGES, CAP, D), totals[0], totals[1], totals[2], totals[3], totals[4], totals[5], totals[6], totals[7], totals[8], totals[9], totals[10], totals[11])
```

```python
import math

import jax
import jax.numpy as jnp
import numpy as np
from jax import lax
from jax.experimental import pallas as pl
from jax.experimental.pallas import tpu as pltpu
from jax.sharding import PartitionSpec as P

HEADS = 12
SIDE = 16
EPSILON = 1e-06
AXES = ("dp", "fsdp")
FAR = 1e30
CHIPS = 16
BLOCK = 384
MIB = 1024 * 1024

BF = jnp.bfloat16
F32 = jnp.float32


def power_slopes(number):
    first_slope = 2.0 ** (-8.0 / number)
    return [first_slope ** (index + 1) for index in range(number)]


def slope_list(heads_total):
    lower_power = 2 ** int(math.floor(math.log2(heads_total)))
    return (
        power_slopes(lower_power) + power_slopes(2 * lower_power)[0::2][: heads_total - lower_power]
    )


SLOPES = [float(np.float32(slope)) for slope in slope_list(HEADS)]


def dot(left, right, left_dim=1, right_dim=0):
    return lax.dot_general(
        left, right, (((left_dim,), (right_dim,)), ((), ())), preferred_element_type=F32
    )


def normed_rows(values):
    centered = values - jnp.mean(values, axis=-1, keepdims=True)
    scale = lax.rsqrt(jnp.mean(centered * centered, axis=-1, keepdims=True) + EPSILON)
    return centered * scale, scale


def norm_back(grad_normed, normed, scale):
    centered_mean = jnp.mean(grad_normed, axis=-1, keepdims=True)
    projected_mean = jnp.mean(grad_normed * normed, axis=-1, keepdims=True)
    return scale * (grad_normed - centered_mean - normed * projected_mean)


def row_of(vectors_ref, index):
    return jnp.concatenate(
        [vectors_ref[0, index : index + 1, :], vectors_ref[1, index : index + 1, :]], axis=1
    )


def gelu_parts(hidden):
    bell = jnp.exp(-0.5 * hidden * hidden)
    inner = 1.0 / (1.0 + (0.3275911 * math.sqrt(0.5)) * jnp.abs(hidden))
    poly = inner * (
        0.5 * 0.254829592
        + inner
        * (
            0.5 * -0.284496736
            + inner * (0.5 * 1.421413741 + inner * (0.5 * -1.453152027 + inner * (0.5 * 1.061405429)))
        )
    )
    tail = poly * bell
    cumulative = jnp.where(hidden >= 0.0, 1.0 - tail, tail)
    return cumulative, cumulative + hidden * bell * (1.0 / math.sqrt(2.0 * math.pi))


def qkv_kernel(
    place, own0, own1, other0, other1, rows_ref,
    wq_ref, wo_ref, vec_ref, qvb_ref, fcb_ref, h1_ref, qkv_ref,
    small, sems,
):
    core = place[48]

    for number, source in enumerate((own0, own1, other0, other1)):
        half = core if number < 2 else 1 - core

        def bring(index, _, source=source, number=number, half=half):
            chip = place[number * 8 + index]
            spot = pl.ds(pl.multiple_of(chip * 48, 16), 48)
            for part in range(3):
                pltpu.make_async_copy(
                    source.at[index, pl.ds(48 * part, 48)], wq_ref.at[3 * half + part, spot], sems.at[0]
                ).start()
            pltpu.make_async_copy(
                source.at[index, pl.ds(144, 48)], wo_ref.at[half, spot], sems.at[1]
            ).start()
            pltpu.make_async_copy(
                source.at[index, pl.ds(192, 16)], small.at[2 * chip + half], sems.at[2]
            ).start()
            return 0

        lax.fori_loop(0, 8, bring, 0)

    normed, _ = normed_rows(rows_ref[...].astype(F32))
    pltpu.make_async_copy(small, small, sems.at[2]).wait()
    spread = small[...].astype(F32)
    vec_ref[...] = jnp.sum(spread.reshape(2, 16, 16, BLOCK), axis=1)
    qvb_ref[...] = jnp.sum(spread.reshape(4, 8, 16, BLOCK), axis=1)
    fcb_ref[...] = jnp.sum(spread.reshape(8, 4, 16, BLOCK), axis=1)
    h1_ref[...] = (normed * row_of(vec_ref, 0) + row_of(vec_ref, 1)).astype(BF)
    pltpu.make_async_copy(wq_ref, wq_ref, sems.at[0]).wait()
    for part in range(6):
        result = dot(h1_ref[...], wq_ref[part])
        if part < 2:
            result = result + qvb_ref[part, 6:7, :]
        elif part >= 4:
            result = result + qvb_ref[part - 2, 6:7, :]
        qkv_ref[:, BLOCK * part : BLOCK * (part + 1)] = result.astype(BF)
    pltpu.make_async_copy(wo_ref, wo_ref, sems.at[1]).wait()


def attention_kernel(qkv_ref, far_ref, rows_ref, wo_ref, vec_ref, att_ref, resid_ref):
    width = rows_ref.shape[1]
    low_half = lax.broadcasted_iota(jnp.int32, (qkv_ref.shape[0], 128), 1) < 64
    nothing = jnp.zeros((qkv_ref.shape[0], 128), BF)
    far = far_ref[0]
    for pair in range(HEADS // 2):
        lanes = slice(128 * pair, 128 * (pair + 1))
        queries = qkv_ref[:, lanes] * jnp.asarray(0.125, BF)
        key_rows = qkv_ref[:, width + 128 * pair : width + 128 * (pair + 1)]
        values = qkv_ref[:, 2 * width + 128 * pair : 2 * width + 128 * (pair + 1)]
        parts = []
        for side in range(2):
            mine = jnp.where(low_half, queries, nothing) if side == 0 else jnp.where(low_half, nothing, queries)
            scores = dot(mine, key_rows, 1, 1) - SLOPES[2 * pair + side] * far
            shifted = jnp.exp(scores - jnp.max(scores, axis=-1, keepdims=True))
            probs = shifted * (1.0 / jnp.sum(shifted, axis=-1, keepdims=True))
            parts.append(dot(probs.astype(BF), values))
        att_ref[:, lanes] = jnp.where(low_half, parts[0], parts[1]).astype(BF)
    att = att_ref[...]
    for part in range(2):
        lanes = slice(BLOCK * part, BLOCK * (part + 1))
        resid_ref[:, lanes] = (
            rows_ref[:, lanes].astype(F32) + dot(att, wo_ref[part]) + vec_ref[part, 2:3, :]
        )


def give_rows(place, core, total, keep_ref, send_ref, block):
    for chip in range(CHIPS):
        for which, target in enumerate((keep_ref, send_ref)):
            slot = place[32 + 64 * which + chip]
            owner = core if which == 0 else 1 - core
            share = total[pl.ds(pl.multiple_of(48 * chip + 24 * owner, 8), 24), :]
            target[slot, block] = share.astype(BF)


def give_small(place, core, vec, qvb, fcb, keep_ref, send_ref, block):
    for chip in range(CHIPS):
        group = vec[chip // 8]
        if qvb is not None:
            group = group + qvb[chip // 4]
        if fcb is not None:
            group = group + fcb[chip // 2]
        group = jnp.concatenate([group, jnp.zeros((16, BLOCK), F32)], axis=0).astype(BF)
        keep_ref[place[32 + chip], block] = group
        send_ref[place[96 + chip], block] = group


def stack_rows(rows, height):
    blank = jnp.zeros((1, BLOCK), F32)
    halves = []
    for part in range(2):
        lines = [blank if row is None else row[:, BLOCK * part : BLOCK * (part + 1)] for row in rows]
        halves.append(jnp.concatenate(lines + [blank] * (height - len(lines)), axis=0))
    return halves


def mlp_kernel(
    place, counts, a0, a1, a2, a3, b0, b1, b2, b3, resid_ref, gout_ref, vec_ref, fcb_ref,
    out_ref, gresid_ref, act_ref, ghid_ref, h2, sums_ref, fcg,
    w1, w2, normed, total, gh2, sems,
):
    block = pl.program_id(0)
    gain = row_of(vec_ref, 3)

    @pl.when(block == 0)
    def _():
        core = place[48]
        for number, (source1, source2) in enumerate(((a0, b0), (a1, b1), (a2, b2), (a3, b3))):
            half = core if number < 2 else 1 - core

            def bring(index, _, source1=source1, source2=source2, number=number, half=half):
                chip1 = place[64 + number * 8 + index]
                spot1 = pl.ds(pl.multiple_of(chip1 * 48, 16), 48)
                for part in range(4):
                    pltpu.make_async_copy(
                        source1.at[index, pl.ds(48 * part, 48)], w1.at[4 * half + part, spot1], sems.at[0]
                    ).start()
                chip2 = place[number * 8 + index]
                spot2 = pl.ds(pl.multiple_of(chip2 * 192 + half * 96, 16), 96)
                for part in range(2):
                    pltpu.make_async_copy(
                        source2.at[index, pl.ds(96 * part, 96)],
                        w2.at[spot2, pl.ds(BLOCK * part, BLOCK)],
                        sems.at[1],
                    ).start()
                return 0

            lax.fori_loop(0, 8, bring, 0)

        normal, _ = normed_rows(resid_ref[...])
        normed[...] = normal
        h2[...] = (normal * gain + row_of(vec_ref, 4)).astype(BF)
        total[...] = jnp.zeros_like(total)
        gh2[...] = jnp.zeros_like(gh2)
        pltpu.make_async_copy(w1, w1, sems.at[0]).wait()
        pltpu.make_async_copy(w2, w2, sems.at[1]).wait()

    first = w1[block]
    second = w2[pl.ds(pl.multiple_of(block * BLOCK, BLOCK), BLOCK), :]
    hidden = dot(h2[...], first) + fcb_ref[block, 7:8, :]
    gactivated = dot(gout_ref[...], second, 1, 1)
    cumulative, slope = gelu_parts(hidden)
    activated = (hidden * cumulative).astype(BF)
    ghidden = (gactivated * slope).astype(BF)
    act_ref[...] = activated
    ghid_ref[...] = ghidden
    total[...] += dot(activated, second)
    gh2[...] += dot(ghidden, first, 1, 1)
    fcg[block] = jnp.concatenate(
        [
            jnp.zeros((3, BLOCK), F32),
            jnp.sum(ghidden.astype(F32), axis=0, keepdims=True),
            jnp.zeros((4, BLOCK), F32),
        ],
        axis=0,
    )

    @pl.when(block == pl.num_programs(0) - 1)
    def _():
        length = out_ref.shape[0] // 4
        fc2_bias = row_of(vec_ref, 5)
        row_index = lax.broadcasted_iota(jnp.int32, (length, 1), 0)
        for image in range(4):
            rows = slice(length * image, length * (image + 1))
            value = resid_ref[rows, :] + total[rows, :] + fc2_bias
            out_ref[rows, :] = jnp.where(row_index < counts[image], value, 0.0).astype(BF)
        _, scale = normed_rows(resid_ref[...])
        gradient = gh2[...]
        gout = gout_ref[...].astype(F32)
        gresid = gout + norm_back(gradient * gain, normed[...], scale)
        gresid_ref[...] = gresid
        rows = [
            jnp.sum(gradient * normed[...], axis=0, keepdims=True),
            jnp.sum(gradient, axis=0, keepdims=True),
            jnp.sum(gout, axis=0, keepdims=True),
            None,
            jnp.sum(gresid.astype(BF).astype(F32), axis=0, keepdims=True),
        ]
        halves = stack_rows(rows, 8)
        sums_ref[0] = halves[0]
        sums_ref[1] = halves[1]


def second_grad_kernel(
    place, act_ref, gout_ref, att_ref, gresid_ref, sums_ref, fcg_ref, keep_ref, send_ref, product
):
    core = place[48]
    block = pl.program_id(0)
    for part in range(2):
        lanes = slice(BLOCK * part, BLOCK * (part + 1))
        product[0:BLOCK, :] = dot(act_ref[...], gout_ref[:, lanes], 0, 0)
        for pair in range(2):
            for which, target in enumerate((keep_ref, send_ref)):
                slot = place[32 + 64 * which + 2 * block + pair]
                owner = core if which == 0 else 1 - core
                for piece in range(4):
                    start = pl.multiple_of(192 * pair + 96 * owner + 24 * piece, 8)
                    target[slot, 2 * piece + part] = product[pl.ds(start, 24), :].astype(BF)

    @pl.when(block == pl.num_programs(0) - 1)
    def _():
        for part in range(2):
            low = gresid_ref[:, BLOCK * part : BLOCK * (part + 1)].astype(BF)
            product[...] = dot(att_ref[...], low, 0, 0)
            give_rows(place, core, product, keep_ref, send_ref, 8 + part)
        give_small(place, core, sums_ref, None, fcg_ref, keep_ref, send_ref, 10)


def first_grad_kernel(place, h2_ref, ghid_ref, keep_ref, send_ref, product):
    product[...] = dot(h2_ref[...], ghid_ref[...], 0, 0)
    give_rows(place, place[48], product, keep_ref, send_ref, 0)


def attention_back_kernel(first_head, qkv_ref, far_ref, gresid_ref, wo_ref, gqkv_ref, gatt):
    width = gresid_ref.shape[1]
    start = first_head * 64
    low = gresid_ref[...].astype(BF)
    mine = slice(start, start + BLOCK)
    gatt[...] = (
        dot(low[:, :BLOCK], wo_ref[0, mine, :], 1, 1) + dot(low[:, BLOCK:], wo_ref[1, mine, :], 1, 1)
    ).astype(BF)
    low_half = lax.broadcasted_iota(jnp.int32, (qkv_ref.shape[0], 128), 1) < 64
    nothing = jnp.zeros((qkv_ref.shape[0], 128), BF)
    far = far_ref[0]
    for pair in range(BLOCK // 128):
        at = start + 128 * pair
        queries = qkv_ref[:, at : at + 128] * jnp.asarray(0.125, BF)
        key_rows = qkv_ref[:, width + at : width + at + 128]
        values = qkv_ref[:, 2 * width + at : 2 * width + at + 128]
        grads = gatt[:, 128 * pair : 128 * (pair + 1)]
        parts = []
        for side in range(2):
            if side == 0:
                my_keys = jnp.where(low_half, key_rows, nothing)
                my_values = jnp.where(low_half, values, nothing)
            else:
                my_keys = jnp.where(low_half, nothing, key_rows)
                my_values = jnp.where(low_half, nothing, values)
            scores = dot(my_keys, queries, 1, 1) - SLOPES[first_head + 2 * pair + side] * far
            shifted = jnp.exp(scores - jnp.max(scores, axis=0, keepdims=True))
            probs = shifted * (1.0 / jnp.sum(shifted, axis=0, keepdims=True))
            gprobs = dot(my_values, grads, 1, 1)
            inner = jnp.sum(probs * gprobs, axis=0, keepdims=True)
            gscores = (probs * (gprobs - inner)).astype(BF)
            parts.append(
                (
                    dot(gscores, key_rows, 0, 0) * 0.125,
                    dot(gscores, queries),
                    dot(probs.astype(BF), grads),
                )
            )
        for which in range(3):
            gqkv_ref[:, which * BLOCK + 128 * pair : which * BLOCK + 128 * (pair + 1)] = jnp.where(
                low_half, parts[0][which], parts[1][which]
            ).astype(BF)


def qkv_grad_kernel(side, place, gqkv_ref, h1_ref, wq_ref, gh1_ref, keep_ref, send_ref, product):
    gradient = jnp.zeros(gh1_ref.shape, F32)
    for part in range(3):
        gqkv = gqkv_ref[:, BLOCK * part : BLOCK * (part + 1)]
        product[...] = dot(h1_ref[...], gqkv, 0, 0)
        give_rows(place, place[48], product, keep_ref, send_ref, part)
        gradient = gradient + dot(gqkv, wq_ref[2 * part + side], 1, 1)
    gh1_ref[...] = gradient


def input_kernel(
    place, gqkv_ref, before_ref, h1_ref, rows_ref, gresid_ref, gh1_ref, wq_ref, vec_ref,
    ginput_ref, keep_ref, send_ref, product,
):
    core = place[48]
    sums = []
    gradient = gh1_ref[...]
    for part in range(3):
        lanes = slice(BLOCK * part, BLOCK * (part + 1))
        gqkv = gqkv_ref[:, lanes]
        product[...] = dot(h1_ref[...], gqkv, 0, 0)
        give_rows(place, core, product, keep_ref, send_ref, part)
        gradient = gradient + dot(gqkv, wq_ref[2 * part + 1], 1, 1)
        if part != 1:
            for columns in (before_ref[:, lanes], gqkv):
                sums.append(
                    jnp.concatenate(
                        [
                            jnp.zeros((2, BLOCK), F32),
                            jnp.sum(columns.astype(F32), axis=0, keepdims=True),
                            jnp.zeros((5, BLOCK), F32),
                        ],
                        axis=0,
                    )
                )
    normed, scale = normed_rows(rows_ref[...].astype(F32))
    ginput_ref[...] = (
        gresid_ref[...] + norm_back(gradient * row_of(vec_ref, 0), normed, scale)
    ).astype(BF)
    rows = [
        jnp.sum(gradient * normed, axis=0, keepdims=True),
        jnp.sum(gradient, axis=0, keepdims=True),
    ]
    give_small(place, core, stack_rows(rows, 8), sums, None, keep_ref, send_ref, 3)


def after(value, *others):
    return lax.optimization_barrier((value,) + others)[0]


class Links:
    def __init__(self, depth):
        self.depth = depth

        def table(move):
            pairs = []
            for z in range(depth):
                for x in range(2):
                    for y in range(2):
                        for c in range(2):
                            nz, nx, ny, nc = move(z, x, y, c)
                            source = (z * 2 + x) * 4 + y * 2 + c
                            pairs.append((source, ((nz % depth) * 2 + nx) * 4 + ny * 2 + nc))
            return pairs

        self.ups = {step: table(lambda z, x, y, c: (z + step, x, y, c)) for step in (1, 2, 3)}
        self.first = table(lambda z, x, y, c: (z, x, 1 - y, c) if c else (z, 1 - x, y, c))
        self.second = table(lambda z, x, y, c: (z, 1 - x, y, c) if c else (z, x, 1 - y, c))
        self.cores = table(lambda z, x, y, c: (z, x, y, 1 - c))

    def move(self, value, pairs):
        return lax.ppermute(value, AXES, pairs)

    def spots(self):
        dp, fsdp = lax.axis_index("dp"), lax.axis_index("fsdp")
        z, x, y, core = dp // 2, dp % 2, fsdp // 2, fsdp % 2

        def chip(c, flip1, flip2, step):
            flip_x = jnp.where(c == 0, flip1, flip2)
            flip_y = jnp.where(c == 0, flip2, flip1)
            return (((z - step) % self.depth) * 2 + (x ^ flip_x)) * 2 + (y ^ flip_y)

        index = jnp.arange(32, dtype=jnp.int32)
        whose = jnp.where(index < 16, core, 1 - core)
        flip2 = (index // 8) % 2
        z_first = chip(whose, (index // 4) % 2, flip2, index % 4)
        x_first = chip(whose, index % 2, (index // 2) % 2, (index // 4) % 4)
        chips = jnp.arange(16, dtype=jnp.int32)
        turn_x, turn_y = ((chips // 2) % 2) ^ x, (chips % 2) ^ y
        step = (chips // 4 - z) % self.depth
        slots0 = turn_y * 8 + turn_x * 4 + step
        slots1 = turn_x * 8 + turn_y * 4 + step
        own_slots = jnp.where(core == 0, slots0, slots1)
        other_slots = jnp.where(core == 0, slots1, slots0)
        rest = jnp.full((16,), core, jnp.int32)
        return jnp.concatenate([z_first, own_slots, rest, x_first, other_slots]).astype(jnp.int32)

    def gather(self, piece_a, piece_b1, piece_b2, early):
        a_one, a_three = self.move(piece_a, self.ups[1]), self.move(piece_a, self.ups[3])
        b1_both = jnp.stack([piece_b1, self.move(piece_b1, self.first)])
        a_two = self.move(a_one, self.ups[1])
        b1_four = jnp.concatenate([b1_both, self.move(after(b1_both, a_one), self.second)])
        a_four = jnp.stack([piece_a, a_one, a_two, a_three])
        a_rest = self.move(a_four, self.first)
        held = after(piece_b2, a_two)
        b2_one, b2_three = self.move(held, self.ups[1]), self.move(held, self.ups[3])
        b2_two = self.move(b2_one, self.ups[1])
        a_eight = jnp.concatenate([a_four, a_rest])
        early, a_eight = lax.optimization_barrier((early, a_eight))
        a_other = self.move(a_eight, self.second)
        a = self.finish(a_eight, a_other)
        held = after(b1_four, b2_one, b2_three)
        b1_one, b1_three = self.move(held, self.ups[1]), self.move(held, self.ups[3])
        b2_four = jnp.stack([piece_b2, b2_one, b2_two, b2_three])
        b2_rest = self.move(after(b2_four, a_other), self.first)
        return a, early, (b1_four, b1_one, b1_three), (b2_four, b2_rest)

    def gather_on(self, b1, b2):
        b1_four, b1_one, b1_three = b1
        b1_two = self.move(b1_one, self.ups[1])
        b2_eight = jnp.concatenate(b2)
        b2_other = self.move(b2_eight, self.second)
        b1_mine = jnp.concatenate([b1_four, b1_one])
        b1_rest = jnp.concatenate([b1_two, b1_three])
        return (b1_mine, b1_rest, self.move(b1_mine, self.cores)), (b2_eight, b2_other)

    def gather_end(self, b1, b2):
        mine, rest, other = b1
        return (mine, rest, other, self.move(rest, self.cores)), self.finish(*b2)

    def finish(self, eight, rest):
        return (eight, rest, self.move(eight, self.cores), self.move(rest, self.cores))

    def reduce(self, stage, state):
        keep = state[0]
        wide = lambda *terms: sum(term.astype(F32) for term in terms)
        if stage == 0:
            return keep, self.move(state[1], self.cores)
        got = state[1]
        if stage == 1:
            return keep, got, self.move(wide(keep[8:], got[8:]).astype(BF), self.second)
        got1 = state[2]
        if stage == 2:
            part = wide(keep[4:8], got[4:8], got1[4:]).astype(BF)
            return keep, got, got1, self.move(part, self.first)
        got2 = state[3]
        if stage == 3:
            parts = [
                wide(keep[step], got[step], got1[step], got2[step]).astype(BF) for step in (1, 2, 3)
            ]
            return state + tuple(
                self.move(part, self.ups[step]) for part, step in zip(parts, (1, 2, 3))
            )
        return wide(keep[0], got[0], got1[0], got2[0], *state[4:])


def halves_of(weight, blocks):
    rows = weight.shape[0]
    return weight.reshape(rows, 2, blocks, BLOCK).transpose(1, 2, 0, 3)


def full_pieces(full, blocks):
    split = full.reshape(CHIPS, 48, 2, blocks, BLOCK).transpose(2, 0, 3, 1, 4)
    return split.reshape(2 * CHIPS, blocks * 48, BLOCK)


def eights(pieces):
    return tuple(pieces[8 * index : 8 * (index + 1)] for index in range(4))


def placed(vector, device, per_row):
    start = (device % per_row) * vector.shape[0]
    return lax.dynamic_update_slice(jnp.zeros((BLOCK,), vector.dtype), vector, (start,))


def shards(
    mesh_shape,
    patches,
    counts,
    positions,
    ln1_gain,
    ln1_bias,
    qkv_weight,
    qv_bias,
    out_weight,
    out_bias,
    ln2_gain,
    ln2_bias,
    fc1_weight,
    fc1_bias,
    fc2_weight,
    fc2_bias,
    cotangent,
):
    images, length, width = patches.shape
    padded = (length + 31) // 32 * 32
    rows = images * padded
    hidden_width = fc1_weight.shape[1]
    devices = mesh_shape["dp"] * mesh_shape["fsdp"]
    by_hand = devices == 2 * CHIPS and mesh_shape["fsdp"] == 4
    small_parts = (ln1_gain, ln1_bias, out_bias, ln2_gain, ln2_bias, fc2_bias, qv_bias, fc1_bias)

    row_index = jnp.arange(padded, dtype=jnp.int32)
    is_live = row_index[None, :] < counts[:, None]
    pad_rows = ((0, 0), (0, padded - length), (0, 0))
    rows_in = jnp.pad(patches, pad_rows).reshape(rows, width)
    gout = jnp.where(is_live[:, :, None], jnp.pad(cotangent, pad_rows), 0).reshape(rows, width)
    spots = jnp.pad(positions, pad_rows[:2])
    grid_rows = (spots // SIDE).astype(F32)
    grid_cols = (spots % SIDE).astype(F32)
    row_delta = grid_rows[:, :, None] - grid_rows[:, None, :]
    col_delta = grid_cols[:, :, None] - grid_cols[:, None, :]
    distance = jnp.sqrt(row_delta * row_delta + col_delta * col_delta)
    far = jnp.where(is_live[:, None, :], distance, FAR)
    far_turned = jnp.where(is_live[:, :, None], distance, FAR)

    if by_hand:
        links = Links(mesh_shape["dp"] // 2)
        place = links.spots()
        core = place[48]
        device = lax.axis_index("dp") * 4 + lax.axis_index("fsdp")
        lines = [placed(part, device, BLOCK // part.shape[0]) for part in small_parts]
        lines = jnp.concatenate([jnp.stack(lines), jnp.zeros((8, BLOCK), BF)])
        halves = jnp.concatenate(
            [halves_of(qkv_weight, 3), halves_of(out_weight, 1), halves_of(fc1_weight, 4)], axis=1
        )
        mine = lax.dynamic_index_in_dim(halves, core, 0, keepdims=False)
        theirs = lax.dynamic_index_in_dim(halves, 1 - core, 0, keepdims=False)
        got = links.move(theirs, links.cores)
        paired = jnp.concatenate(
            [jnp.where(core == 0, mine, got), jnp.where(core == 0, got, mine)], axis=1
        )
        piece_a = jnp.concatenate([paired[:4].reshape(192, BLOCK), lines])
        piece_b1 = paired[4:].reshape(192, BLOCK)
        piece_b2 = jnp.concatenate([fc2_weight[:, :BLOCK], fc2_weight[:, BLOCK:]])
    else:
        links = None
        place = jnp.concatenate(
            [
                jnp.arange(32, dtype=jnp.int32) % 16,
                jnp.arange(16, dtype=jnp.int32),
                jnp.zeros((16,), jnp.int32),
                jnp.arange(32, dtype=jnp.int32) % 16,
                jnp.arange(16, dtype=jnp.int32),
            ]
        )
        whole = [lax.all_gather(part, AXES, axis=0, tiled=True) for part in small_parts]
        lines = []
        for part in whole:
            share = part.shape[0] // 32
            chunks = part.reshape(32, share)
            lines.append(
                jnp.stack([placed(chunks[index], index, BLOCK // share) for index in range(32)])
            )
        lines = jnp.concatenate([jnp.stack(lines, axis=1), jnp.zeros((32, 8, BLOCK), BF)], axis=1)
        lines = lines.reshape(CHIPS, 2, 16, BLOCK).transpose(1, 0, 2, 3).reshape(32, 16, BLOCK)
        whole_qkv = lax.all_gather(qkv_weight, AXES, axis=0, tiled=True)
        whole_out = lax.all_gather(out_weight, AXES, axis=0, tiled=True)
        whole_fc1 = lax.all_gather(fc1_weight, AXES, axis=0, tiled=True)
        whole_fc2 = lax.all_gather(fc2_weight, AXES, axis=0, tiled=True)
        gathered_a = eights(
            jnp.concatenate([full_pieces(whole_qkv, 3), full_pieces(whole_out, 1), lines], axis=1)
        )
        gathered_b1 = eights(full_pieces(whole_fc1, 4))
        split = whole_fc2.reshape(CHIPS, 2, 96, 2, BLOCK).transpose(1, 0, 3, 2, 4)
        gathered_b2 = eights(split.reshape(32, 192, BLOCK))

    if by_hand:
        early = (rows_in, gout, far, far_turned)
        gathered_a, early, on_b1, on_b2 = links.gather(piece_a, piece_b1, piece_b2, early)
        rows_in, gout, far, far_turned = early

    smem = pl.BlockSpec(memory_space=pltpu.SMEM)
    vmem = pl.BlockSpec(memory_space=pltpu.VMEM)
    anywhere = pl.BlockSpec(memory_space=pltpu.HBM)
    struct = jax.ShapeDtypeStruct

    wq, wo, vec, qvb, fcb, h1, qkv = pl.pallas_call(
        qkv_kernel,
        out_shape=(
            struct((6, width, BLOCK), BF),
            struct((2, width, BLOCK), BF),
            struct((2, 16, BLOCK), F32),
            struct((4, 16, BLOCK), F32),
            struct((8, 16, BLOCK), F32),
            struct((rows, width), BF),
            struct((rows, 3 * width), BF),
        ),
        in_specs=[smem] + [anywhere] * 4 + [vmem],
        out_specs=(vmem,) * 7,
        scratch_shapes=[pltpu.VMEM((32, 16, BLOCK), BF), pltpu.SemaphoreType.DMA((3,))],
        compiler_params=pltpu.CompilerParams(vmem_limit_bytes=40 * MIB),
        cost_estimate=pl.CostEstimate(
            flops=2 * rows * width * 3 * width, bytes_accessed=14 * MIB, transcendentals=0
        ),
        name="qkv",
    )(place, *gathered_a, rows_in)

    if by_hand:
        qkv, on_b1, on_b2 = lax.optimization_barrier((qkv, on_b1, on_b2))
        on_b1, on_b2 = links.gather_on(on_b1, on_b2)

    image_rows = lambda columns: pl.BlockSpec((padded, columns), lambda image: (image, 0))
    image_far = pl.BlockSpec((1, padded, padded), lambda image: (image, 0, 0))
    fixed = lambda shape: pl.BlockSpec(shape, lambda image: (0,) * len(shape))
    att, resid = pl.pallas_call(
        attention_kernel,
        grid=(images,),
        out_shape=(struct((rows, width), BF), struct((rows, width), F32)),
        in_specs=[
            image_rows(3 * width), image_far, image_rows(width),
            fixed((2, width, BLOCK)), fixed((2, 16, BLOCK)),
        ],
        out_specs=(image_rows(width), image_rows(width)),
        compiler_params=pltpu.CompilerParams(vmem_limit_bytes=40 * MIB),
        cost_estimate=pl.CostEstimate(
            flops=8 * rows * 256 * width, bytes_accessed=10 * MIB, transcendentals=HEADS * rows * 256
        ),
        name="attention",
    )(qkv, far, rows_in, wo, vec)

    if by_hand:
        resid, on_b1, on_b2 = lax.optimization_barrier((resid, on_b1, on_b2))
        gathered_b1, gathered_b2 = links.gather_end(on_b1, on_b2)

    def join(value, *states):
        if not by_hand:
            return (value,) + states
        return lax.optimization_barrier((value,) + states)

    def reduce(stage, state):
        return links.reduce(stage, state) if by_hand else state

    step_rows = lambda columns: pl.BlockSpec((rows, columns), lambda block: (0, block))
    shares = lambda blocks: struct((CHIPS, blocks, 24, BLOCK), BF)
    steps = hidden_width // BLOCK
    out, gresid, act, ghid, h2, sums, fcg = pl.pallas_call(
        mlp_kernel,
        grid=(steps,),
        out_shape=(
            struct((rows, width), BF),
            struct((rows, width), F32),
            struct((rows, hidden_width), BF),
            struct((rows, hidden_width), BF),
            struct((rows, width), BF),
            struct((2, 8, BLOCK), F32),
            struct((steps, 8, BLOCK), F32),
        ),
        in_specs=[smem, smem] + [anywhere] * 8 + [
            fixed((rows, width)), fixed((rows, width)), fixed((2, 16, BLOCK)), fixed((8, 16, BLOCK)),
        ],
        out_specs=(
            fixed((rows, width)), fixed((rows, width)), step_rows(BLOCK), step_rows(BLOCK),
            fixed((rows, width)), fixed((2, 8, BLOCK)), fixed((steps, 8, BLOCK)),
        ),
        scratch_shapes=[
            pltpu.VMEM((steps, width, BLOCK), BF),
            pltpu.VMEM((hidden_width, width), BF),
            pltpu.VMEM((rows, width), F32),
            pltpu.VMEM((rows, width), F32),
            pltpu.VMEM((rows, width), F32),
            pltpu.SemaphoreType.DMA((2,)),
        ],
        compiler_params=pltpu.CompilerParams(vmem_limit_bytes=50 * MIB),
        cost_estimate=pl.CostEstimate(
            flops=8 * rows * width * hidden_width, bytes_accessed=26 * MIB, transcendentals=rows * hidden_width
        ),
        name="mlp",
    )(place, counts, *gathered_b1, *gathered_b2, resid, gout, vec, fcb)

    keep_2, send_2 = pl.pallas_call(
        second_grad_kernel,
        grid=(steps,),
        out_shape=(shares(11), shares(11)),
        in_specs=[
            smem, step_rows(BLOCK), fixed((rows, width)), fixed((rows, width)), fixed((rows, width)),
            fixed((2, 8, BLOCK)), fixed((steps, 8, BLOCK)),
        ],
        out_specs=(fixed((CHIPS, 11, 24, BLOCK)),) * 2,
        scratch_shapes=[pltpu.VMEM((width, BLOCK), F32)],
        compiler_params=pltpu.CompilerParams(vmem_limit_bytes=40 * MIB),
        cost_estimate=pl.CostEstimate(
            flops=2 * rows * width * (hidden_width + width), bytes_accessed=14 * MIB, transcendentals=0
        ),
        name="second_grad",
    )(place, act, gout, att, gresid, sums, fcg)
    state_2 = reduce(0, (keep_2, send_2))

    keep_1, send_1 = pl.pallas_call(
        first_grad_kernel,
        grid=(steps,),
        out_shape=(shares(8), shares(8)),
        in_specs=[smem, fixed((rows, width)), step_rows(BLOCK)],
        out_specs=(pl.BlockSpec((CHIPS, 1, 24, BLOCK), lambda block: (0, block, 0, 0)),) * 2,
        scratch_shapes=[pltpu.VMEM((width, BLOCK), F32)],
        compiler_params=pltpu.CompilerParams(vmem_limit_bytes=40 * MIB),
        cost_estimate=pl.CostEstimate(
            flops=2 * rows * width * hidden_width, bytes_accessed=10 * MIB, transcendentals=0
        ),
        name="first_grad",
    )(place, join(h2, keep_2)[0], ghid)
    state_1, state_2 = join((keep_1, send_1), state_2)
    state_1, state_2 = reduce(0, state_1), reduce(1, state_2)

    def attention_back(side, gradient):
        return pl.pallas_call(
            lambda *refs: attention_back_kernel(6 * side, *refs),
            grid=(images,),
            out_shape=struct((rows, 3 * BLOCK), BF),
            in_specs=[image_rows(3 * width), image_far, image_rows(width), fixed((2, width, BLOCK))],
            out_specs=image_rows(3 * BLOCK),
            scratch_shapes=[pltpu.VMEM((padded, BLOCK), BF)],
            compiler_params=pltpu.CompilerParams(vmem_limit_bytes=40 * MIB),
            cost_estimate=pl.CostEstimate(
                flops=8 * rows * 256 * width, bytes_accessed=8 * MIB, transcendentals=HEADS * rows * 128
            ),
            name="attention_back",
        )(qkv, far_turned, gradient, wo)

    gqkv_0 = attention_back(0, join(gresid, keep_1)[0])
    gqkv_0, state_1, state_2 = join(gqkv_0, state_1, state_2)
    state_1 = reduce(1, state_1)

    gh1, keep_a, send_a = pl.pallas_call(
        lambda *refs: qkv_grad_kernel(0, *refs),
        out_shape=(struct((rows, width), F32), shares(3), shares(3)),
        in_specs=[smem] + [vmem] * 3,
        out_specs=(vmem,) * 3,
        scratch_shapes=[pltpu.VMEM((width, BLOCK), F32)],
        compiler_params=pltpu.CompilerParams(vmem_limit_bytes=40 * MIB),
        cost_estimate=pl.CostEstimate(
            flops=6 * rows * width * width, bytes_accessed=10 * MIB, transcendentals=0
        ),
        name="qkv_grad",
    )(place, gqkv_0, h1, wq)
    gh1, state_a, state_2 = join(gh1, (keep_a, send_a), state_2)
    state_a, state_2 = reduce(0, state_a), reduce(2, state_2)

    gqkv_1 = attention_back(1, join(gresid, gh1)[0])
    gqkv_1, state_a, state_1, state_2 = join(gqkv_1, state_a, state_1, state_2)
    state_a, state_1, state_2 = reduce(1, state_a), reduce(2, state_1), reduce(3, state_2)

    ginput, keep_c, send_c = pl.pallas_call(
        input_kernel,
        out_shape=(struct((rows, width), BF), shares(4), shares(4)),
        in_specs=[smem] + [vmem] * 8,
        out_specs=(vmem,) * 3,
        scratch_shapes=[pltpu.VMEM((width, BLOCK), F32)],
        compiler_params=pltpu.CompilerParams(vmem_limit_bytes=40 * MIB),
        cost_estimate=pl.CostEstimate(
            flops=6 * rows * width * width, bytes_accessed=14 * MIB, transcendentals=0
        ),
        name="input_grad",
    )(place, gqkv_1, gqkv_0, h1, rows_in, gresid, gh1, wq, vec)
    ginput, state_c = join(ginput, (keep_c, send_c))
    state_c = reduce(0, state_c)

    output = out.reshape(images, padded, width)[:, :length]
    input_grad = ginput.reshape(images, padded, width)[:, :length]

    if by_hand:
        state_c, state_a = join(state_c, state_a)
        state_c, state_a = reduce(1, state_c), reduce(2, state_a)
        state_c, state_a, state_1 = join(state_c, state_a, state_1)
        state_c, state_a, state_1 = reduce(2, state_c), reduce(3, state_a), reduce(3, state_1)
        state_c, state_a, state_1 = join(state_c, state_a, state_1)
        mine_c = reduce(4, reduce(3, state_c))
        mine_1, mine_2, mine_a = reduce(4, state_1), reduce(4, state_2), reduce(4, state_a)
        device = lax.axis_index("dp") * 4 + lax.axis_index("fsdp")

        def columns(blocks):
            return blocks.transpose(1, 0, 2).reshape(blocks.shape[1], -1)

        def share(line, count):
            return lax.dynamic_slice(line, ((device % (BLOCK // count)) * count,), (count,))

        heads = [part for pair in zip(mine_a, mine_c[:3]) for part in pair]
        fc2_grad = mine_2[:8].reshape(4, 2, 24, BLOCK).transpose(0, 2, 1, 3).reshape(96, width)
        return (
            output,
            input_grad,
            share(mine_c[3, 0], 24),
            share(mine_c[3, 1], 24),
            jnp.concatenate(heads, axis=1),
            share(mine_c[3, 2], 48),
            columns(mine_2[8:10]),
            share(mine_2[10, 4], 24),
            share(mine_2[10, 0], 24),
            share(mine_2[10, 1], 24),
            columns(mine_1),
            share(mine_2[10, 3], 96),
            fc2_grad,
            share(mine_2[10, 2], 24),
        )

    both_a, both_c, both_1, both_2 = (
        jnp.stack(state, axis=1).astype(F32) for state in (state_a, state_c, state_1, state_2)
    )
    heads = jnp.stack([both_a, both_c[:, :, :3]], axis=3).reshape(CHIPS, 2, 6, 24, BLOCK)

    def matrix(blocks):
        return blocks.transpose(0, 1, 3, 2, 4).reshape(width, -1)

    def vector(blocks, line, count):
        lines = blocks[:, :, line].reshape(32 * count // BLOCK, -1, BLOCK)
        return lines[:, 0].reshape(-1)

    fc2_whole = both_2[:, :, :8].reshape(CHIPS, 2, 4, 2, 24, BLOCK).transpose(0, 1, 2, 4, 3, 5)
    small_c, small_2 = both_c[:, :, 3], both_2[:, :, 10]
    totals = (
        vector(small_c, 0, 24),
        vector(small_c, 1, 24),
        matrix(heads),
        vector(small_c, 2, 48),
        matrix(both_2[:, :, 8:10]),
        vector(small_2, 4, 24),
        vector(small_2, 0, 24),
        vector(small_2, 1, 24),
        matrix(both_1),
        vector(small_2, 3, 96),
        fc2_whole.reshape(hidden_width, width),
        vector(small_2, 2, 24),
    )
    return (output, input_grad) + tuple(
        lax.psum_scatter(total, AXES, scatter_dimension=0, tiled=True) for total in totals
    )


def solution(mesh):
    rows = P(AXES, None, None)
    table = P(AXES, None)
    line = P(AXES)
    in_specs = (
        rows, line, table, line, line, table, line, table, line, line, line, table, line, table, line, rows,
    )
    out_specs = (
        rows, rows, line, line, table, line, table, line, line, line, table, line, table, line,
    )
    mesh_shape = dict(mesh.shape)

    def body(*arrays):
        return shards(mesh_shape, *arrays)

    return jax.shard_map(body, mesh=mesh, in_specs=in_specs, out_specs=out_specs, check_vma=False)
```

```python
import math

import jax
import jax.numpy as jnp
import numpy as np
from jax import lax
from jax.experimental import pallas as pl
from jax.experimental.pallas import tpu as pltpu
from jax.sharding import PartitionSpec as P

HEADS = 12
SIDE = 16
EPSILON = 1e-06
AXES = ("dp", "fsdp")
FAR = 1e30
CHIPS = 16
BLOCK = 384
MIB = 1024 * 1024

BF = jnp.bfloat16
F32 = jnp.float32


def power_slopes(number):
    first_slope = 2.0 ** (-8.0 / number)
    return [first_slope ** (index + 1) for index in range(number)]


def slope_list(heads_total):
    lower_power = 2 ** int(math.floor(math.log2(heads_total)))
    return (
        power_slopes(lower_power) + power_slopes(2 * lower_power)[0::2][: heads_total - lower_power]
    )


SLOPES = [float(np.float32(slope)) for slope in slope_list(HEADS)]


def dot(left, right, left_dim=1, right_dim=0):
    return lax.dot_general(
        left, right, (((left_dim,), (right_dim,)), ((), ())), preferred_element_type=F32
    )


def normed_rows(values):
    centered = values - jnp.mean(values, axis=-1, keepdims=True)
    scale = lax.rsqrt(jnp.mean(centered * centered, axis=-1, keepdims=True) + EPSILON)
    return centered * scale, scale


def norm_back(grad_normed, normed, scale):
    centered_mean = jnp.mean(grad_normed, axis=-1, keepdims=True)
    projected_mean = jnp.mean(grad_normed * normed, axis=-1, keepdims=True)
    return scale * (grad_normed - centered_mean - normed * projected_mean)


def row_of(vectors_ref, index):
    return jnp.concatenate(
        [vectors_ref[0, index : index + 1, :], vectors_ref[1, index : index + 1, :]], axis=1
    )


def gelu_parts(hidden):
    cumulative = 0.5 + 0.5 * lax.erf(hidden * math.sqrt(0.5))
    bell = jnp.exp(-0.5 * hidden * hidden)
    return cumulative, cumulative + hidden * bell * (1.0 / math.sqrt(2.0 * math.pi))


def share_kernel(place, qkv_ref, out_ref, fc1_ref, *refs):
    smalls, (mine_ref, theirs_ref, lines_ref) = refs[:-3], refs[-3:]
    for target, core in ((mine_ref, place[48]), (theirs_ref, 1 - place[48])):
        starts = [(qkv_ref, 2 * BLOCK * part + BLOCK * core) for part in range(3)]
        starts.append((out_ref, BLOCK * core))
        starts += [(fc1_ref, 4 * BLOCK * core + BLOCK * part) for part in range(4)]
        for block, (source, start) in enumerate(starts):
            target[block] = source[:, pl.ds(pl.multiple_of(start, 128), BLOCK)]
    device = place[49]
    lines = []
    for small in smalls:
        count = small.shape[0]
        line = small[...].astype(F32).reshape(1, count)
        line = jnp.concatenate([line, jnp.zeros((1, BLOCK - count), F32)], axis=1)
        lines.append(pltpu.roll(line, lax.rem(device, BLOCK // count) * count, 1))
    lines_ref[...] = jnp.concatenate(lines + [jnp.zeros((8, BLOCK), F32)], axis=0).astype(BF)


def pair_kernel(place, mine_ref, got_ref, lines_ref, fc2_ref, a_ref, b1_ref, b2_ref):
    swap = place[48] == 1
    for block in range(8):
        mine, got = mine_ref[block].astype(F32), got_ref[block].astype(F32)
        rows = jnp.concatenate([jnp.where(swap, got, mine), jnp.where(swap, mine, got)], axis=0)
        if block < 3:
            a_ref[48 * block : 48 * (block + 1), :] = rows.astype(BF)
        elif block == 3:
            b2_ref[192:240, :] = rows.astype(BF)
        else:
            b1_ref[48 * (block - 4) : 48 * (block - 3), :] = rows.astype(BF)
    b2_ref[0:96, :] = fc2_ref[:, :BLOCK]
    b2_ref[96:192, :] = fc2_ref[:, BLOCK:]
    a_ref[144:160, :] = lines_ref[...]


def each_piece(place, table, sources, work):
    core = place[48]
    for number, source in enumerate(sources):
        half = core if number < 2 else 1 - core

        def bring(index, _, source=source, number=number, half=half):
            work(source, index, place[table + number * 8 + index], half)
            return 0

        lax.fori_loop(0, 8, bring, 0)


def bring_out_weight(place, sources, wo, sem):
    def work(source, index, chip, half):
        spot = pl.ds(pl.multiple_of(chip * 48, 16), 48)
        pltpu.make_async_copy(source.at[index, pl.ds(192, 48)], wo.at[half, spot], sem).start()

    each_piece(place, 0, sources, work)


def bring_qkv_weight(place, sources, side, wq, sem, part_of=None):
    for first, here in ((0, place[48] == side), (2, place[48] != side)):

        @pl.when(here)
        def _(first=first):
            for number in (first, first + 1):

                def bring(index, _, source=sources[number], number=number):
                    spot = pl.ds(pl.multiple_of(place[number * 8 + index] * 48, 16), 48)
                    for part in range(3):
                        pltpu.make_async_copy(
                            source.at[index, pl.ds(48 * part, 48)],
                            wq.at[spot, pl.ds(BLOCK * part, BLOCK)] if part_of is None else wq.at[part, spot],
                            sem if part_of is None else part_of.at[part],
                        ).start()
                    return 0

                lax.fori_loop(0, 8, bring, 0)


def wait_all(buffer, sem):
    pltpu.make_async_copy(buffer, buffer, sem).wait()


def qkv_kernel(
    place, own0, own1, other0, other1, rows_ref,
    vec_ref, fcb_ref, h1_turned, qkv_ref,
    wq, h1, qvb, small, sems,
):
    sources = (own0, own1, other0, other1)
    side = pl.program_id(0)

    @pl.when(side == 0)
    def _():
        def work(source, index, chip, half):
            pltpu.make_async_copy(
                source.at[index, pl.ds(144, 16)], small.at[2 * chip + half], sems.at[2]
            ).start()

        each_piece(place, 0, sources, work)
        for half in range(2):
            bring_qkv_weight(place, sources, half, wq.at[half], sems.at[half])
        normed, _ = normed_rows(rows_ref[...].astype(F32))
        wait_all(small, sems.at[2])
        spread = small[...].astype(F32)
        vec_ref[...] = jnp.sum(spread.reshape(2, 16, 16, BLOCK), axis=1)
        qvb[...] = jnp.sum(spread.reshape(4, 8, 16, BLOCK), axis=1)
        lines = jnp.sum(spread.reshape(8, 4, 16, BLOCK), axis=1)
        for block in range(4):
            fcb_ref[block] = jnp.concatenate([lines[2 * block, 7:8], lines[2 * block + 1, 7:8]], axis=1)
        low = (normed * row_of(vec_ref, 0) + row_of(vec_ref, 1)).astype(BF)
        h1[...] = low
        h1_turned[...] = low.T

    wait_all(wq.at[side], sems.at[side])
    bias = jnp.concatenate(
        [qvb[side, 6:7, :], jnp.zeros((1, BLOCK), F32), qvb[2 + side, 6:7, :]], axis=1
    )
    qkv_ref[0] = (dot(h1[...], wq[side]) + bias).astype(BF)


def two_heads(pair_rows, low_half):
    nothing = jnp.zeros_like(pair_rows)
    return jnp.concatenate(
        [jnp.where(low_half, pair_rows, nothing), jnp.where(low_half, nothing, pair_rows)], axis=0
    )


def attention_kernel(qkv_ref, far_ref, att_ref):
    length = att_ref.shape[0]
    low_half = lax.broadcasted_iota(jnp.int32, (length, 128), 1) < 64
    far = far_ref[0]
    for pair in range(HEADS // 2):
        side, at = pair // 3, 128 * (pair % 3)
        queries = two_heads(qkv_ref[side, :, at : at + 128] * jnp.asarray(0.125, BF), low_half)
        key_rows = qkv_ref[side, :, BLOCK + at : BLOCK + at + 128]
        values = qkv_ref[side, :, 2 * BLOCK + at : 2 * BLOCK + at + 128]
        both = dot(queries, key_rows, 1, 1)
        probs = []
        for head in range(2):
            scores = both[length * head : length * (head + 1)] - SLOPES[2 * pair + head] * far
            shifted = jnp.exp(scores - jnp.max(scores, axis=-1, keepdims=True))
            share = shifted * (1.0 / jnp.sum(shifted, axis=-1, keepdims=True))
            probs.append(share.astype(BF))
        result = dot(jnp.concatenate(probs, axis=0), values)
        att_ref[:, 128 * pair : 128 * (pair + 1)] = jnp.where(
            low_half, result[:length], result[length:]
        ).astype(BF)


def give_rows(place, total, keep_ref, send_ref, extra=None):
    for chip in range(CHIPS):
        below = None if extra is None else extra(chip)
        for which, target in enumerate((keep_ref, send_ref)):
            slot = place[32 + 64 * which + chip]
            owner = place[48] if which == 0 else 1 - place[48]
            share = total[pl.ds(pl.multiple_of(48 * chip + 24 * owner, 8), 24), :]
            if below is not None:
                share = jnp.concatenate([share, below], axis=0)
            target[slot] = share.astype(BF)


def stack_rows(rows):
    blank = jnp.zeros_like(next(row for row in rows if row is not None))
    rows = [blank if row is None else row for row in rows]
    return jnp.concatenate(rows + [blank] * (8 - len(rows)), axis=0)


def sum_rows(values):
    return jnp.sum(values.astype(F32), axis=0, keepdims=True)


def mlp_kernel(
    place, counts, a0, a1, a2, a3, b0, b1, b2, b3, att_ref, rows_ref, gout_ref, vec_ref, fcb_ref,
    out_ref, gresid_ref, glow_ref, keep1_ref, send1_ref, keep2, send2,
    w1, w2, wo, h2, h2_turned, normed, total, gh2, product1, product2, stage, stage_end, fcg, scales,
    sems1, sems2, sems,
):
    block = pl.program_id(0)
    wide = 2 * BLOCK
    gain = row_of(vec_ref, 3)

    @pl.when(block == 0)
    def _():
        def work1(source, index, chip, half):
            spot = pl.ds(pl.multiple_of(chip * 48, 16), 48)
            for part in range(4):
                column = 2 * half + part // 2
                pltpu.make_async_copy(
                    source.at[index, pl.ds(48 * part, 48)],
                    w1.at[column, spot, pl.ds(BLOCK * (part % 2), BLOCK)],
                    sems1.at[column],
                ).start()

        def work2(source, index, chip, half):
            spot = pl.ds(pl.multiple_of(chip * 192 + half * 96, 16), 96)
            for part in range(2):
                pltpu.make_async_copy(
                    source.at[index, pl.ds(96 * part, 96)],
                    w2.at[spot, pl.ds(BLOCK * part, BLOCK)],
                    sems2.at[chip // 4],
                ).start()

        bring_out_weight(place, (b0, b1, b2, b3), wo, sems.at[2])
        each_piece(place, 64, (a0, a1, a2, a3), work1)
        each_piece(place, 0, (b0, b1, b2, b3), work2)
        wait_all(wo, sems.at[2])
        bias = row_of(vec_ref, 2)
        for part in range(2):
            lanes = slice(BLOCK * part, BLOCK * (part + 1))
            total[:, lanes] = rows_ref[:, lanes].astype(F32) + dot(att_ref[...], wo[part]) + bias[:, lanes]
        normal, scale = normed_rows(total[...])
        normed[...] = normal
        scales[...] = jnp.broadcast_to(scale, scales.shape)
        low = (normal * gain + row_of(vec_ref, 4)).astype(BF)
        h2[...] = low
        h2_turned[...] = low.T
        gh2[...] = jnp.zeros_like(gh2)

    wait_all(w1.at[block], sems1.at[block])
    hidden = dot(h2[...], w1[block]) + fcb_ref[block]
    rows_of = pl.ds(pl.multiple_of(block * wide, wide), wide)
    wait_all(w2.at[rows_of], sems2.at[block])
    gactivated = dot(gout_ref[...], w2[rows_of, :], 1, 1)
    cumulative, slope = gelu_parts(hidden)
    activated = (hidden * cumulative).astype(BF)
    ghidden = (gactivated * slope).astype(BF)
    product1[...] = dot(h2_turned[...], ghidden)
    product2[...] = dot(activated, gout_ref[...], 0, 0)
    branch = dot(activated, w2[rows_of, :])
    gradient = dot(ghidden, w1[block], 1, 1)
    fcg[block] = stack_rows([None, None, None, sum_rows(ghidden)])
    give_rows(place, product1, keep1_ref, send1_ref)
    for pair in range(4):
        for which, target in enumerate((keep2, send2)):
            chip = 4 * block + pair
            owner = place[48] if which == 0 else 1 - place[48]
            start = pl.multiple_of(192 * pair + 96 * owner, 8)
            stage[which, chip] = product2[pl.ds(start, 96), :].astype(BF)
            slot = place[32 + 64 * which + chip]
            pltpu.make_async_copy(stage.at[which, chip], target.at[slot, pl.ds(0, 96)], sems.at[which]).start()

    @pl.when(block < pl.num_programs(0) - 1)
    def _():
        @pl.when(block == 0)
        def _():
            total[...] = total[...] + row_of(vec_ref, 5)

        total[...] += branch
        gh2[...] += gradient

    @pl.when(block == pl.num_programs(0) - 1)
    def _():
        length = out_ref.shape[0] // 4
        row_index = lax.broadcasted_iota(jnp.int32, (length, 1), 0)
        for image in range(4):
            rows = slice(length * image, length * (image + 1))
            value = total[rows, :] + branch[rows]
            out_ref[rows, :] = jnp.where(row_index < counts[image], value, 0.0).astype(BF)
        whole = gh2[...] + gradient
        gout = gout_ref[...].astype(F32)
        gresid = gout + norm_back(whole * gain, normed[...], scales[:, 0:1])
        gresid_ref[...] = gresid
        low = gresid.astype(BF)
        glow_ref[...] = low
        sums = stack_rows(
            [sum_rows(whole * normed[...]), sum_rows(whole), sum_rows(gout), None, sum_rows(low)]
        )
        product1[...] = dot(att_ref[...], low, 0, 0)
        for chip in range(CHIPS):
            below = sums + fcg[chip // 4]
            for which, target in enumerate((keep2, send2)):
                owner = place[48] if which == 0 else 1 - place[48]
                share = product1[pl.ds(pl.multiple_of(48 * chip + 24 * owner, 8), 24), :]
                stage_end[which, chip] = jnp.concatenate([share, below], axis=0).astype(BF)
                slot = place[32 + 64 * which + chip]
                pltpu.make_async_copy(
                    stage_end.at[which, chip], target.at[slot, pl.ds(96, 32)], sems.at[which]
                ).start()
        wait_all(keep2, sems.at[0])
        wait_all(send2, sems.at[1])


def attention_back_kernel(
    side, place, own0, own1, other0, other1, qkv_ref, far_ref, glow_ref, gqkv_ref, wo, sem
):
    @pl.when(pl.program_id(0) == 0)
    def _():
        bring_out_weight(place, (own0, own1, other0, other1), wo, sem)
        wait_all(wo, sem)

    low = glow_ref[...]
    mine = slice(BLOCK * side, BLOCK * (side + 1))
    gatt = (
        dot(low[:, :BLOCK], wo[0, mine, :], 1, 1) + dot(low[:, BLOCK:], wo[1, mine, :], 1, 1)
    ).astype(BF)
    length = low.shape[0]
    low_half = lax.broadcasted_iota(jnp.int32, (length, 128), 1) < 64
    far = far_ref[0]
    for pair in range(3):
        at = 128 * pair
        queries = qkv_ref[0, :, at : at + 128] * jnp.asarray(0.125, BF)
        key_rows = two_heads(qkv_ref[0, :, BLOCK + at : BLOCK + at + 128], low_half)
        values = two_heads(qkv_ref[0, :, 2 * BLOCK + at : 2 * BLOCK + at + 128], low_half)
        grads = gatt[:, at : at + 128]
        both = dot(key_rows, queries, 1, 1)
        gboth = dot(values, grads, 1, 1)
        probs, gscores = [], []
        for head in range(2):
            rows = slice(length * head, length * (head + 1))
            scores = both[rows] - SLOPES[6 * side + 2 * pair + head] * far
            shifted = jnp.exp(scores - jnp.max(scores, axis=0, keepdims=True))
            share = shifted * (1.0 / jnp.sum(shifted, axis=0, keepdims=True))
            weighted = share * gboth[rows]
            probs.append(share.astype(BF))
            inner = jnp.sum(weighted, axis=0, keepdims=True)
            gscores.append((weighted - share * inner).astype(BF))
        probs, gscores = jnp.concatenate(probs, axis=0), jnp.concatenate(gscores, axis=0)
        gvalues = dot(probs, grads)
        gkeys = dot(gscores, queries)
        gqkv_ref[:, at : at + 128] = (dot(gscores, key_rows, 0, 0) * 0.125).astype(BF)
        for which, result in ((1, gkeys), (2, gvalues)):
            gqkv_ref[:, which * BLOCK + at : which * BLOCK + at + 128] = jnp.where(
                low_half, result[:length], result[length:]
            ).astype(BF)


def qkv_grad_step(side, place, sources, h1_turned, gqkv_ref, product, wq, sems):
    part = pl.program_id(0)

    @pl.when(part == 0)
    def _():
        bring_qkv_weight(place, sources, side, wq, None, sems)

    product[...] = dot(h1_turned[...], gqkv_ref[...])
    wait_all(wq.at[part], sems.at[part])
    return part, dot(gqkv_ref[...], wq[part], 1, 1)


def qkv_grad_kernel(
    place, own0, own1, other0, other1, h1_turned, gqkv_ref, gh1_ref, sums_ref, keep_ref, send_ref, product, wq, sems
):
    part, gradient = qkv_grad_step(
        0, place, (own0, own1, other0, other1), h1_turned, gqkv_ref, product, wq, sems
    )
    gh1_ref[...] = jnp.where(part == 0, gradient, gh1_ref[...] + gradient)
    sums_ref[part] = stack_rows([None, None, sum_rows(gqkv_ref[...])])
    give_rows(place, product, keep_ref, send_ref)


def input_kernel(
    place, own0, own1, other0, other1, h1_turned, gqkv_ref, before_ref, rows_ref, vec_ref, gresid, gh1,
    ginput_ref, keep_ref, send_ref,
    product, wq, sums, gresid_here, total, sems, sems_in,
):
    loads = [
        pltpu.make_async_copy(gh1, total, sems_in.at[0]),
        pltpu.make_async_copy(gresid, gresid_here, sems_in.at[1]),
    ]

    @pl.when(pl.program_id(0) == 0)
    def _():
        for load in loads:
            load.start()

    part, gradient = qkv_grad_step(
        1, place, (own0, own1, other0, other1), h1_turned, gqkv_ref, product, wq, sems
    )

    @pl.when(part == 0)
    def _():
        loads[0].wait()

    total[...] += gradient
    sums[part] = stack_rows([None, None, sum_rows(gqkv_ref[...])])

    @pl.when(part < 2)
    def _():
        give_rows(place, product, keep_ref, send_ref, lambda chip: jnp.zeros((8, BLOCK), F32))

    @pl.when(part == 2)
    def _():
        loads[1].wait()
        gradient = total[...]
        normed, scale = normed_rows(rows_ref[...].astype(F32))
        ginput_ref[...] = (
            gresid_here[...] + norm_back(gradient * row_of(vec_ref, 0), normed, scale)
        ).astype(BF)
        gain, shift = sum_rows(gradient * normed), sum_rows(gradient)

        def below(chip):
            lanes = slice(BLOCK * (chip // 8), BLOCK * (chip // 8 + 1))
            biases = (before_ref[0], sums[0], before_ref[2], sums[2])[chip // 4]
            return stack_rows([gain[:, lanes], shift[:, lanes]]) + biases

        give_rows(place, product, keep_ref, send_ref, below)


def after(value, *others):
    return lax.optimization_barrier((value,) + others)[0]


class Links:
    def __init__(self, depth):
        self.depth = depth

        def table(move):
            pairs = []
            for z in range(depth):
                for x in range(2):
                    for y in range(2):
                        for c in range(2):
                            nz, nx, ny, nc = move(z, x, y, c)
                            source = (z * 2 + x) * 4 + y * 2 + c
                            pairs.append((source, ((nz % depth) * 2 + nx) * 4 + ny * 2 + nc))
            return pairs

        self.ups = {step: table(lambda z, x, y, c: (z + step, x, y, c)) for step in (1, 2, 3)}
        self.first = table(lambda z, x, y, c: (z, x, 1 - y, c) if c else (z, 1 - x, y, c))
        self.second = table(lambda z, x, y, c: (z, 1 - x, y, c) if c else (z, x, 1 - y, c))
        self.cores = table(lambda z, x, y, c: (z, x, y, 1 - c))

    def move(self, value, pairs):
        return lax.ppermute(value, AXES, pairs)

    def spots(self):
        dp, fsdp = lax.axis_index("dp"), lax.axis_index("fsdp")
        z, x, y, core = dp // 2, dp % 2, fsdp // 2, fsdp % 2

        def chip(c, flip1, flip2, step):
            flip_x = jnp.where(c == 0, flip1, flip2)
            flip_y = jnp.where(c == 0, flip2, flip1)
            return (((z - step) % self.depth) * 2 + (x ^ flip_x)) * 2 + (y ^ flip_y)

        index = jnp.arange(32, dtype=jnp.int32)
        whose = jnp.where(index < 16, core, 1 - core)
        flip2 = (index // 8) % 2
        z_first = chip(whose, (index // 4) % 2, flip2, index % 4)
        x_first = chip(whose, index % 2, (index // 2) % 2, (index // 4) % 4)
        chips = jnp.arange(16, dtype=jnp.int32)
        turn_x, turn_y = ((chips // 2) % 2) ^ x, (chips % 2) ^ y
        step = (chips // 4 - z) % self.depth
        slots0 = turn_y * 8 + turn_x * 4 + step
        slots1 = turn_x * 8 + turn_y * 4 + step
        own_slots = jnp.where(core == 0, slots0, slots1)
        other_slots = jnp.where(core == 0, slots1, slots0)
        rest = jnp.where(jnp.arange(16) == 1, dp * 4 + fsdp, core).astype(jnp.int32)
        return jnp.concatenate([z_first, own_slots, rest, x_first, other_slots]).astype(jnp.int32)

    def gather(self, piece_a, piece_b1, piece_b2):
        hold = lax.optimization_barrier
        up = lambda value, step: self.move(value, self.ups[step])
        a_one, a_three, b1_two = hold((up(piece_a, 1), up(piece_a, 3), self.move(piece_b1, self.first)))
        b1_two = jnp.stack([piece_b1, b1_two])
        a_two, b1_four = hold((up(a_one, 1), self.move(b1_two, self.second)))
        a_four = jnp.stack([piece_a, a_one, a_two, a_three])
        b1_four = jnp.concatenate([b1_two, b1_four])
        piece_b2 = after(piece_b2, a_two)
        a_rest, b2_one, b2_three = hold((self.move(a_four, self.first), up(piece_b2, 1), up(piece_b2, 3)))
        a_eight = jnp.concatenate([a_four, a_rest])
        a_other, b2_two, b1_one = hold((self.move(a_eight, self.second), up(b2_one, 1), up(b1_four, 1)))
        b2_four = jnp.stack([piece_b2, b2_one, b2_two, b2_three])
        a = self.finish(a_eight, a_other)
        return a, (b1_four, b1_one, up(b1_four, 3)), (b2_four, self.move(b2_four, self.first))

    def gather_on(self, b1, b2):
        b1_four, b1_one, b1_three = b1
        b1_two = self.move(b1_one, self.ups[1])
        b2_eight = jnp.concatenate(b2)
        b2_other = self.move(b2_eight, self.second)
        b1_mine = jnp.concatenate([b1_four, b1_one])
        return (b1_mine, b1_two, b1_three, self.move(b1_mine, self.cores)), (b2_eight, b2_other)

    def gather_end(self, b1, b2):
        mine, b1_two, b1_three, other = b1
        rest = jnp.concatenate([b1_two, b1_three])
        return (mine, rest, other, self.move(rest, self.cores)), self.finish(*b2)

    def finish(self, eight, rest):
        return (eight, rest, self.move(eight, self.cores), self.move(rest, self.cores))

    def reduce(self, stage, state):
        keep = state[0]
        wide = lambda *terms: sum(term.astype(F32) for term in terms)
        if stage == 0:
            return keep, self.move(state[1], self.cores)
        got = state[1]
        if stage == 1:
            return keep, got, self.move(wide(keep[8:], got[8:]).astype(BF), self.second)
        got1 = state[2]
        if stage == 2:
            part = wide(keep[4:8], got[4:8], got1[4:]).astype(BF)
            return keep, got, got1, self.move(part, self.first)
        got2 = state[3]
        if stage == 3:
            parts = [
                wide(keep[step], got[step], got1[step], got2[step]).astype(BF) for step in (1, 2, 3)
            ]
            return state + tuple(
                self.move(part, self.ups[step]) for part, step in zip(parts, (1, 2, 3))
            )
        return wide(keep[0], got[0], got1[0], got2[0], *state[4:])


def full_pieces(full, blocks):
    split = full.reshape((CHIPS, 48) + full.shape[1:])
    split = split.transpose(3, 0, 2, 1, 4) if full.shape[1] == blocks else split.transpose(2, 0, 3, 1, 4)
    return split.reshape(2 * CHIPS, blocks * 48, BLOCK)


def eights(pieces):
    return tuple(pieces[8 * index : 8 * (index + 1)] for index in range(4))


def placed(vector, device, per_row):
    start = (device % per_row) * vector.shape[0]
    return lax.dynamic_update_slice(jnp.zeros((BLOCK,), vector.dtype), vector, (start,))


def shards(
    mesh_shape,
    patches,
    counts,
    positions,
    ln1_gain,
    ln1_bias,
    qkv_weight,
    qv_bias,
    out_weight,
    out_bias,
    ln2_gain,
    ln2_bias,
    fc1_weight,
    fc1_bias,
    fc2_weight,
    fc2_bias,
    cotangent,
):
    images, length, width = patches.shape
    padded = (length + 31) // 32 * 32
    rows = images * padded
    hidden_width = fc1_weight.shape[1]
    devices = mesh_shape["dp"] * mesh_shape["fsdp"]
    by_hand = devices == 2 * CHIPS and mesh_shape["fsdp"] == 4
    small_parts = (ln1_gain, ln1_bias, out_bias, ln2_gain, ln2_bias, fc2_bias, qv_bias, fc1_bias)

    smem = pl.BlockSpec(memory_space=pltpu.SMEM)
    vmem = pl.BlockSpec(memory_space=pltpu.VMEM)
    anywhere = pl.BlockSpec(memory_space=pltpu.HBM)
    struct = jax.ShapeDtypeStruct

    row_index = jnp.arange(padded, dtype=jnp.int32)
    is_live = row_index[None, :] < counts[:, None]
    pad_rows = ((0, 0), (0, padded - length), (0, 0))
    rows_in = jnp.pad(patches, pad_rows).reshape(rows, width)
    gout = jnp.where(is_live[:, :, None], jnp.pad(cotangent, pad_rows), 0).reshape(rows, width)
    spots = jnp.pad(positions, pad_rows[:2])
    grid_rows = (spots // SIDE).astype(F32)
    grid_cols = (spots % SIDE).astype(F32)
    row_delta = grid_rows[:, :, None] - grid_rows[:, None, :]
    col_delta = grid_cols[:, :, None] - grid_cols[:, None, :]
    distance = jnp.sqrt(row_delta * row_delta + col_delta * col_delta)
    far = jnp.where(is_live[:, None, :], distance, FAR)
    far_turned = jnp.where(is_live[:, :, None], distance, FAR)

    if by_hand:
        links = Links(mesh_shape["dp"] // 2)
        place = links.spots()
        core = place[48]
        share = struct((8, 24, BLOCK), BF)
        mine, theirs, lines = pl.pallas_call(
            share_kernel,
            out_shape=(share, share, struct((16, BLOCK), BF)),
            in_specs=[smem] + [vmem] * 11,
            out_specs=(vmem,) * 3,
            name="share",
        )(place, qkv_weight, out_weight, fc1_weight, *small_parts)
        got = links.move(theirs, links.cores)
        pieces = pl.pallas_call(
            pair_kernel,
            out_shape=tuple(struct((height, BLOCK), BF) for height in (160, 192, 240)),
            in_specs=[smem] + [vmem] * 4,
            out_specs=(vmem,) * 3,
            name="pair",
        )(place, mine, got, lines, fc2_weight)
    else:
        links = None
        place = jnp.concatenate(
            [
                jnp.arange(32, dtype=jnp.int32) % 16,
                jnp.arange(16, dtype=jnp.int32),
                jnp.zeros((16,), jnp.int32),
                jnp.arange(32, dtype=jnp.int32) % 16,
                jnp.arange(16, dtype=jnp.int32),
            ]
        )
        whole = [lax.all_gather(part, AXES, axis=0, tiled=True) for part in small_parts]
        lines = []
        for part in whole:
            share = part.shape[0] // 32
            chunks = part.reshape(32, share)
            lines.append(
                jnp.stack([placed(chunks[index], index, BLOCK // share) for index in range(32)])
            )
        lines = jnp.concatenate([jnp.stack(lines, axis=1), jnp.zeros((32, 8, BLOCK), BF)], axis=1)
        lines = lines.reshape(CHIPS, 2, 16, BLOCK).transpose(1, 0, 2, 3).reshape(32, 16, BLOCK)
        whole_qkv = lax.all_gather(qkv_weight, AXES, axis=0, tiled=True)
        whole_out = lax.all_gather(out_weight, AXES, axis=0, tiled=True)
        whole_fc1 = lax.all_gather(fc1_weight, AXES, axis=0, tiled=True)
        whole_fc2 = lax.all_gather(fc2_weight, AXES, axis=0, tiled=True)
        gathered_a = eights(
            jnp.concatenate([full_pieces(whole_qkv.reshape(width, 3, 2, BLOCK), 3), lines], axis=1)
        )
        gathered_b1 = eights(full_pieces(whole_fc1.reshape(width, 2, 4, BLOCK), 4))
        split = whole_fc2.reshape(CHIPS, 2, 96, 2, BLOCK).transpose(1, 0, 3, 2, 4).reshape(32, 192, BLOCK)
        gathered_b2 = eights(
            jnp.concatenate([split, full_pieces(whole_out.reshape(width, 1, 2, BLOCK), 1)], axis=1)
        )

    if by_hand:
        gathered_a, on_b1, on_b2 = links.gather(*pieces)


    def call(kernel, operands, out_shape, out_specs, in_specs, flops, mib, vmem_mib, grid, scratch=(), name=None):
        return pl.pallas_call(
            kernel,
            grid=grid,
            out_shape=out_shape,
            in_specs=in_specs,
            out_specs=out_specs,
            scratch_shapes=list(scratch),
            compiler_params=pltpu.CompilerParams(vmem_limit_bytes=vmem_mib * MIB),
            cost_estimate=pl.CostEstimate(
                flops=int(flops), bytes_accessed=mib * MIB, transcendentals=0
            ),
            name=name,
        )(*operands)

    image_rows = lambda columns: pl.BlockSpec((padded, columns), lambda image: (image, 0))
    image_far = pl.BlockSpec((1, padded, padded), lambda image: (image, 0, 0))
    fixed = lambda *shape: pl.BlockSpec(shape, lambda step: (0,) * len(shape))
    step_rows = lambda columns: pl.BlockSpec((rows, columns), lambda step: (0, step))
    shares = lambda height, columns: struct((CHIPS, height, columns), BF)
    buffer, flag = pltpu.VMEM, pltpu.SemaphoreType.DMA
    low_rows, wide_rows = struct((rows, width), BF), struct((rows, width), F32)
    wide = 2 * BLOCK
    steps = hidden_width // wide
    third = 3 * BLOCK

    def join(value, *states):
        if not by_hand:
            return (value,) + states
        return lax.optimization_barrier((value,) + states)

    def reduce(stage, state):
        return links.reduce(stage, state) if by_hand else state

    vec, fcb, h1_turned, qkv = call(
        qkv_kernel,
        (place, *gathered_a, rows_in),
        (
            struct((2, 16, BLOCK), F32), struct((steps, 1, wide), F32), struct((width, rows), BF),
            struct((2, rows, third), BF),
        ),
        (
            fixed(2, 16, BLOCK), fixed(steps, 1, wide), fixed(width, rows),
            pl.BlockSpec((1, rows, third), lambda step: (step, 0, 0)),
        ),
        [smem] + [anywhere] * 4 + [fixed(rows, width)],
        2 * rows * width * 3 * width,
        14,
        30,
        grid=(2,),
        scratch=(
            buffer((2, width, third), BF), buffer((rows, width), BF), buffer((4, 16, BLOCK), F32),
            buffer((32, 16, BLOCK), BF), flag((3,)),
        ),
        name="qkv",
    )
    if by_hand:
        qkv, on_b1, on_b2 = lax.optimization_barrier((qkv, on_b1, on_b2))
        on_b1, on_b2 = links.gather_on(on_b1, on_b2)

    att = call(
        attention_kernel,
        (qkv, far),
        low_rows,
        image_rows(width),
        [pl.BlockSpec((2, padded, third), lambda image: (0, image, 0)), image_far],
        8 * rows * 256 * width,
        10,
        20,
        grid=(images,),
        name="attention",
    )
    if by_hand:
        att, on_b1, on_b2 = lax.optimization_barrier((att, on_b1, on_b2))
        gathered_b1, gathered_b2 = links.gather_end(on_b1, on_b2)

    step_shares = lambda height, columns: pl.BlockSpec((CHIPS, height, columns), lambda step: (0, 0, step))
    out, gresid, glow, keep_1, send_1, keep_2, send_2 = call(
        mlp_kernel,
        (place, counts, *gathered_b1, *gathered_b2, att, rows_in, gout, vec, fcb),
        (low_rows, wide_rows, low_rows) + (shares(24, hidden_width),) * 2 + (shares(128, wide),) * 2,
        (fixed(rows, width),) * 3 + (step_shares(24, wide),) * 2 + (anywhere,) * 2,
        [smem, smem] + [anywhere] * 8 + [fixed(rows, width)] * 3 + [
            fixed(2, 16, BLOCK), fixed(steps, 1, wide),
        ],
        12 * rows * width * hidden_width,
        32,
        60,
        grid=(steps,),
        scratch=(
            buffer((steps, width, wide), BF), buffer((hidden_width, width), BF), buffer((2, width, BLOCK), BF),
            buffer((rows, width), BF), buffer((width, rows), BF), buffer((rows, width), F32),
            buffer((rows, width), F32), buffer((rows, width), F32), buffer((width, wide), F32),
            buffer((width, wide), F32), buffer((2, CHIPS, 96, wide), BF), buffer((2, CHIPS, 32, wide), BF),
            buffer((steps, 8, wide), F32), buffer((rows, 128), F32), flag((steps,)), flag((steps,)), flag((3,)),
        ),
        name="mlp",
    )
    state_2, state_1 = reduce(0, (keep_2, send_2)), reduce(0, (keep_1, send_1))

    def attention_back(side, gradient):
        return call(
            lambda *refs: attention_back_kernel(side, *refs),
            (place, *gathered_b2, qkv, far_turned, gradient),
            struct((rows, third), BF),
            image_rows(third),
            [smem] + [anywhere] * 4 + [
                pl.BlockSpec((1, padded, third), lambda image: (side, image, 0)), image_far, image_rows(width),
            ],
            8 * rows * 256 * width,
            8,
            20,
            grid=(images,),
            scratch=(buffer((2, width, BLOCK), BF), flag),
            name="attention_back",
        )

    gqkv_0 = attention_back(0, glow)
    gqkv_0, state_1, state_2 = join(gqkv_0, state_1, state_2)
    state_2, state_1 = reduce(1, state_2), reduce(1, state_1)

    gh1, sums_0, keep_a, send_a = call(
        qkv_grad_kernel,
        (place, *gathered_a, h1_turned, gqkv_0),
        (wide_rows, struct((3, 8, BLOCK), F32)) + (shares(24, third),) * 2,
        (fixed(rows, width), fixed(3, 8, BLOCK)) + (step_shares(24, BLOCK),) * 2,
        [smem] + [anywhere] * 4 + [fixed(width, rows), step_rows(BLOCK)],
        6 * rows * width * width,
        10,
        24,
        grid=(3,),
        scratch=(buffer((width, BLOCK), F32), buffer((3, width, BLOCK), BF), flag((3,))),
        name="qkv_grad",
    )
    state_a = reduce(0, (keep_a, send_a))

    gqkv_1 = attention_back(1, join(glow, gh1)[0])
    gqkv_1, state_a, state_2 = join(gqkv_1, state_a, state_2)
    state_a, state_2 = reduce(1, state_a), reduce(2, state_2)

    ginput, keep_c, send_c = call(
        input_kernel,
        (place, *gathered_a, h1_turned, gqkv_1, sums_0, rows_in, vec, gresid, gh1),
        (low_rows,) + (shares(32, third),) * 2,
        (fixed(rows, width),) + (step_shares(32, BLOCK),) * 2,
        [smem] + [anywhere] * 4 + [
            fixed(width, rows), step_rows(BLOCK), fixed(3, 8, BLOCK), fixed(rows, width), fixed(2, 16, BLOCK),
            anywhere, anywhere,
        ],
        6 * rows * width * width,
        14,
        30,
        grid=(3,),
        scratch=(
            buffer((width, BLOCK), F32), buffer((3, width, BLOCK), BF), buffer((3, 8, BLOCK), F32),
            buffer((rows, width), F32), buffer((rows, width), F32), flag((3,)), flag((2,)),
        ),
        name="input_grad",
    )
    ginput, state_c, state_2, state_1, state_a = join(ginput, (keep_c, send_c), state_2, state_1, state_a)
    state_c, state_a, state_1 = reduce(0, state_c), reduce(2, state_a), reduce(2, state_1)

    def cut(value):
        return value.reshape(images, padded, width)[:, :length]

    if by_hand:
        state_c = reduce(1, state_c)
        state_2 = reduce(3, join(state_2, state_c[:2])[0])
        out, ginput = after(out, state_c[1]), after(ginput, state_c[1])
        state_1, state_a, state_c = join(state_1, state_a, state_c)
        state_c = reduce(2, state_c)
        state_1, state_a = reduce(3, state_1), reduce(3, state_a)
        state_c = reduce(3, join(state_c)[0])
        state_1, state_2, state_a, _ = join(state_1, state_2, state_a, state_c[3])
        mine_c = reduce(4, state_c)
        mine_1, mine_2, mine_a = reduce(4, state_1), reduce(4, state_2), reduce(4, state_a)
        device = place[49]

        def share(line, count):
            start = (device % (line.shape[0] // count)) * count
            return lax.dynamic_slice(line, (start,), (count,))

        heads = []
        for part in range(3):
            lanes = slice(BLOCK * part, BLOCK * (part + 1))
            heads += [mine_a[:, lanes], mine_c[:24, lanes]]
        small_c, small_2 = mine_c[24:, 2 * BLOCK :], mine_2[120:]
        return (
            cut(out),
            cut(ginput),
            share(small_c[0], 24),
            share(small_c[1], 24),
            jnp.concatenate(heads, axis=1),
            share(small_c[2], 48),
            mine_2[96:120],
            share(small_2[4], 24),
            share(small_2[0], 24),
            share(small_2[1], 24),
            mine_1,
            share(small_2[3], 96),
            mine_2[:96],
            share(small_2[2], 24),
        )

    both_a, both_c, both_1, both_2 = (
        jnp.stack(state, axis=1).astype(F32) for state in (state_a, state_c, state_1, state_2)
    )
    heads = jnp.stack(
        [both.reshape(CHIPS, 2, 24, 3, BLOCK) for both in (both_a, both_c[:, :, :24])], axis=4
    )

    def vector(lines, count):
        columns = lines.shape[-1]
        return lines.reshape(32 * count // columns, -1, columns)[:, 0].reshape(-1)

    small_c, small_2 = both_c[:, :, 24:, 2 * BLOCK :], both_2[:, :, 120:]
    totals = (
        vector(small_c[:, :, 0], 24),
        vector(small_c[:, :, 1], 24),
        heads.reshape(width, 3 * width),
        vector(small_c[:, :, 2], 48),
        both_2[:, :, 96:120].reshape(width, width),
        vector(small_2[:, :, 4], 24),
        vector(small_2[:, :, 0], 24),
        vector(small_2[:, :, 1], 24),
        both_1.reshape(width, hidden_width),
        vector(small_2[:, :, 3], 96),
        both_2[:, :, :96].reshape(hidden_width, width),
        vector(small_2[:, :, 2], 24),
    )
    return (cut(out), cut(ginput)) + tuple(
        lax.psum_scatter(total, AXES, scatter_dimension=0, tiled=True) for total in totals
    )


def solution(mesh):
    rows = P(AXES, None, None)
    table = P(AXES, None)
    line = P(AXES)
    in_specs = (
        rows, line, table, line, line, table, line, table, line, line, line, table, line, table, line, rows,
    )
    out_specs = (
        rows, rows, line, line, table, line, table, line, line, line, table, line, table, line,
    )
    mesh_shape = dict(mesh.shape)

    def body(*arrays):
        return shards(mesh_shape, *arrays)

    return jax.shard_map(body, mesh=mesh, in_specs=in_specs, out_specs=out_specs, check_vma=False)
```

```python
import math

import jax
import jax.numpy as jnp
import numpy as np
from jax import lax
from jax.experimental import pallas as pl
from jax.experimental.pallas import tpu as pltpu
from jax.sharding import PartitionSpec as P

HEADS = 12
SIDE = 16
EPSILON = 1e-06
AXES = ("dp", "fsdp")
FAR = 1e30
CHIPS = 16
BLOCK = 384
SMALL, LARGE = (32, 96), (112, 128)
MIB = 1024 * 1024

BF = jnp.bfloat16
F32 = jnp.float32


def power_slopes(number):
    first_slope = 2.0 ** (-8.0 / number)
    return [first_slope ** (index + 1) for index in range(number)]


def slope_list(heads_total):
    lower_power = 2 ** int(math.floor(math.log2(heads_total)))
    return (
        power_slopes(lower_power) + power_slopes(2 * lower_power)[0::2][: heads_total - lower_power]
    )


SLOPES = [float(np.float32(slope)) for slope in slope_list(HEADS)]


def dot(left, right, left_dim=1, right_dim=0):
    return lax.dot_general(
        left, right, (((left_dim,), (right_dim,)), ((), ())), preferred_element_type=F32
    )


def normed_rows(values):
    centered = values - jnp.mean(values, axis=-1, keepdims=True)
    scale = lax.rsqrt(jnp.mean(centered * centered, axis=-1, keepdims=True) + EPSILON)
    return centered * scale, scale


def norm_back(grad_normed, normed, scale):
    centered_mean = jnp.mean(grad_normed, axis=-1, keepdims=True)
    projected_mean = jnp.mean(grad_normed * normed, axis=-1, keepdims=True)
    return scale * (grad_normed - centered_mean - normed * projected_mean)


def row_of(vectors_ref, index):
    return jnp.concatenate(
        [vectors_ref[0, index : index + 1, :], vectors_ref[1, index : index + 1, :]], axis=1
    )


def gelu_parts(hidden):
    cumulative = 0.5 + 0.5 * lax.erf(hidden * math.sqrt(0.5))
    bell = jnp.exp(-0.5 * hidden * hidden)
    return cumulative, cumulative + hidden * bell * (1.0 / math.sqrt(2.0 * math.pi))


def share_kernel(place, qkv_ref, out_ref, fc1_ref, *refs):
    smalls, (mine_ref, theirs_ref, lines_ref) = refs[:-3], refs[-3:]
    for target, core in ((mine_ref, place[48]), (theirs_ref, 1 - place[48])):
        starts = [(qkv_ref, 2 * BLOCK * part + BLOCK * core) for part in range(3)]
        starts.append((out_ref, BLOCK * core))
        starts += [(fc1_ref, 4 * BLOCK * core + BLOCK * part) for part in range(4)]
        for block, (source, start) in enumerate(starts):
            target[block] = source[:, pl.ds(pl.multiple_of(start, 128), BLOCK)]
    device = place[49]
    lines = []
    for small in smalls:
        count = small.shape[0]
        line = small[...].astype(F32).reshape(1, count)
        line = jnp.concatenate([line, jnp.zeros((1, BLOCK - count), F32)], axis=1)
        lines.append(pltpu.roll(line, lax.rem(device, BLOCK // count) * count, 1))
    lines_ref[...] = jnp.concatenate(lines + [jnp.zeros((8, BLOCK), F32)], axis=0).astype(BF)


def pair_kernel(place, mine_ref, got_ref, lines_ref, fc2_ref, a_ref, b1_ref, b2_ref):
    swap = place[48] == 1
    for block in range(8):
        mine, got = mine_ref[block].astype(F32), got_ref[block].astype(F32)
        rows = jnp.concatenate([jnp.where(swap, got, mine), jnp.where(swap, mine, got)], axis=0)
        if block < 3:
            a_ref[48 * block : 48 * (block + 1), :] = rows.astype(BF)
        elif block == 3:
            b2_ref[192:240, :] = rows.astype(BF)
        else:
            b1_ref[48 * (block - 4) : 48 * (block - 3), :] = rows.astype(BF)
    b2_ref[0:96, :] = fc2_ref[:, :BLOCK]
    b2_ref[96:192, :] = fc2_ref[:, BLOCK:]
    a_ref[144:160, :] = lines_ref[...]


def each_piece(place, table, sources, work):
    core = place[48]
    for number, source in enumerate(sources):
        half = core if number < 2 else 1 - core

        def bring(index, _, source=source, number=number, half=half):
            work(source, index, place[table + number * 8 + index], half)
            return 0

        lax.fori_loop(0, 8, bring, 0)


def bring_out_weight(place, sources, wo, sem):
    def work(source, index, chip, half):
        spot = pl.ds(pl.multiple_of(chip * 48, 16), 48)
        pltpu.make_async_copy(source.at[index, pl.ds(192, 48)], wo.at[half, spot], sem).start()

    each_piece(place, 0, sources, work)


def bring_qkv_weight(place, sources, side, wq, sem, part_of=None):
    for first, here in ((0, place[48] == side), (2, place[48] != side)):

        @pl.when(here)
        def _(first=first):
            for number in (first, first + 1):

                def bring(index, _, source=sources[number], number=number):
                    spot = pl.ds(pl.multiple_of(place[number * 8 + index] * 48, 16), 48)
                    for part in range(3):
                        pltpu.make_async_copy(
                            source.at[index, pl.ds(48 * part, 48)],
                            wq.at[spot, pl.ds(BLOCK * part, BLOCK)] if part_of is None else wq.at[part, spot],
                            sem if part_of is None else part_of.at[part],
                        ).start()
                    return 0

                lax.fori_loop(0, 8, bring, 0)


def wait_all(buffer, sem):
    pltpu.make_async_copy(buffer, buffer, sem).wait()


def qkv_kernel(
    place, own0, own1, other0, other1, rows_ref,
    vec_ref, fcb_ref, h1_turned, qkv_ref, wq_out,
    wq, h1, qvb, small, sems,
):
    sources = (own0, own1, other0, other1)
    side = pl.program_id(0)

    @pl.when(side == 0)
    def _():
        def work(source, index, chip, half):
            pltpu.make_async_copy(
                source.at[index, pl.ds(144, 16)], small.at[2 * chip + half], sems.at[2]
            ).start()

        each_piece(place, 0, sources, work)
        for half in range(2):
            bring_qkv_weight(place, sources, half, wq.at[half], sems.at[half])
        normed, _ = normed_rows(rows_ref[...].astype(F32))
        wait_all(small, sems.at[2])
        spread = small[...].astype(F32)
        vec_ref[...] = jnp.sum(spread.reshape(2, 16, 16, BLOCK), axis=1)
        qvb[...] = jnp.sum(spread.reshape(4, 8, 16, BLOCK), axis=1)
        lines = jnp.sum(spread.reshape(8, 4, 16, BLOCK), axis=1)
        for block in range(4):
            fcb_ref[block] = jnp.concatenate([lines[2 * block, 7:8], lines[2 * block + 1, 7:8]], axis=1)
        low = (normed * row_of(vec_ref, 0) + row_of(vec_ref, 1)).astype(BF)
        h1[...] = low
        h1_turned[...] = low.T

    wait_all(wq.at[side], sems.at[side])
    keeping = pltpu.make_async_copy(wq.at[side], wq_out.at[side], sems.at[3])
    keeping.start()
    bias = jnp.concatenate(
        [qvb[side, 6:7, :], jnp.zeros((1, BLOCK), F32), qvb[2 + side, 6:7, :]], axis=1
    )
    qkv_ref[0] = (dot(h1[...], wq[side]) + bias).astype(BF)
    keeping.wait()


def two_heads(pair_rows, low_half):
    nothing = jnp.zeros_like(pair_rows)
    return jnp.concatenate(
        [jnp.where(low_half, pair_rows, nothing), jnp.where(low_half, nothing, pair_rows)], axis=0
    )


def attention_kernel(qkv_ref, far_ref, att_ref):
    length = att_ref.shape[0]
    low_half = lax.broadcasted_iota(jnp.int32, (length, 128), 1) < 64
    far = far_ref[0]
    for pair in range(HEADS // 2):
        side, at = pair // 3, 128 * (pair % 3)
        queries = two_heads(qkv_ref[side, :, at : at + 128] * jnp.asarray(0.125, BF), low_half)
        key_rows = qkv_ref[side, :, BLOCK + at : BLOCK + at + 128]
        values = qkv_ref[side, :, 2 * BLOCK + at : 2 * BLOCK + at + 128]
        both = dot(queries, key_rows, 1, 1)
        probs = []
        for head in range(2):
            scores = both[length * head : length * (head + 1)] - SLOPES[2 * pair + head] * far
            shifted = jnp.exp(scores - jnp.max(scores, axis=-1, keepdims=True))
            share = shifted * (1.0 / jnp.sum(shifted, axis=-1, keepdims=True))
            probs.append(share.astype(BF))
        result = dot(jnp.concatenate(probs, axis=0), values)
        att_ref[:, 128 * pair : 128 * (pair + 1)] = jnp.where(
            low_half, result[:length], result[length:]
        ).astype(BF)


def give_rows(place, tables, total, keep_ref, send_ref, extra=None):
    for chip in range(CHIPS):
        below = None if extra is None else extra(chip)
        for which, target in enumerate((keep_ref, send_ref)):
            slot = place[tables[which] + chip]
            owner = place[48] if which == 0 else 1 - place[48]
            share = total[pl.ds(pl.multiple_of(48 * chip + 24 * owner, 8), 24), :]
            if below is not None:
                share = jnp.concatenate([share, below], axis=0)
            target[slot] = share.astype(BF)


def stack_rows(rows):
    blank = jnp.zeros_like(next(row for row in rows if row is not None))
    rows = [blank if row is None else row for row in rows]
    return jnp.concatenate(rows + [blank] * (8 - len(rows)), axis=0)


def sum_rows(values):
    return jnp.sum(values.astype(F32), axis=0, keepdims=True)


def mlp_kernel(
    place, counts, a0, a1, a2, a3, b0, b1, b2, b3, att_ref, rows_ref, gout_ref, vec_ref, fcb_ref,
    out_ref, gresid_ref, glow_ref, keep1_ref, send1_ref, keep2, send2, wo_out,
    w1, w2, wo, h2, h2_turned, normed, total, gh2, product1, product2, stage, stage_end, fcg, scales,
    sems1, sems2, sems,
):
    block = pl.program_id(0)
    wide = 2 * BLOCK
    gain = row_of(vec_ref, 3)

    @pl.when(block == 0)
    def _():
        def work1(source, index, chip, half):
            spot = pl.ds(pl.multiple_of(chip * 48, 16), 48)
            for part in range(4):
                column = 2 * half + part // 2
                pltpu.make_async_copy(
                    source.at[index, pl.ds(48 * part, 48)],
                    w1.at[column, spot, pl.ds(BLOCK * (part % 2), BLOCK)],
                    sems1.at[column],
                ).start()

        def work2(source, index, chip, half):
            spot = pl.ds(pl.multiple_of(chip * 192 + half * 96, 16), 96)
            for part in range(2):
                pltpu.make_async_copy(
                    source.at[index, pl.ds(96 * part, 96)],
                    w2.at[spot, pl.ds(BLOCK * part, BLOCK)],
                    sems2.at[chip // 4],
                ).start()

        bring_out_weight(place, (b0, b1, b2, b3), wo, sems.at[2])
        each_piece(place, 64, (a0, a1, a2, a3), work1)
        each_piece(place, 0, (b0, b1, b2, b3), work2)
        wait_all(wo, sems.at[2])
        pltpu.make_async_copy(wo, wo_out, sems.at[2]).start()
        bias = row_of(vec_ref, 2)
        for part in range(2):
            lanes = slice(BLOCK * part, BLOCK * (part + 1))
            total[:, lanes] = rows_ref[:, lanes].astype(F32) + dot(att_ref[...], wo[part]) + bias[:, lanes]
        normal, scale = normed_rows(total[...])
        normed[...] = normal
        scales[...] = jnp.broadcast_to(scale, scales.shape)
        low = (normal * gain + row_of(vec_ref, 4)).astype(BF)
        h2[...] = low
        h2_turned[...] = low.T
        gh2[...] = jnp.zeros_like(gh2)

    wait_all(w1.at[block], sems1.at[block])
    hidden = dot(h2[...], w1[block]) + fcb_ref[block]
    rows_of = pl.ds(pl.multiple_of(block * wide, wide), wide)
    wait_all(w2.at[rows_of], sems2.at[block])
    gactivated = dot(gout_ref[...], w2[rows_of, :], 1, 1)
    cumulative, slope = gelu_parts(hidden)
    activated = (hidden * cumulative).astype(BF)
    ghidden = (gactivated * slope).astype(BF)
    product1[...] = dot(h2_turned[...], ghidden)
    product2[...] = dot(activated, gout_ref[...], 0, 0)
    branch = dot(activated, w2[rows_of, :])
    gradient = dot(ghidden, w1[block], 1, 1)
    fcg[block] = stack_rows([None, None, None, sum_rows(ghidden)])
    give_rows(place, LARGE, product1, keep1_ref, send1_ref)
    for pair in range(4):
        for which, target in enumerate((keep2, send2)):
            chip = 4 * block + pair
            owner = place[48] if which == 0 else 1 - place[48]
            start = pl.multiple_of(192 * pair + 96 * owner, 8)
            stage[which, chip] = product2[pl.ds(start, 96), :].astype(BF)
            slot = place[LARGE[which] + chip]
            pltpu.make_async_copy(stage.at[which, chip], target.at[slot, pl.ds(0, 96)], sems.at[which]).start()

    @pl.when(block < pl.num_programs(0) - 1)
    def _():
        @pl.when(block == 0)
        def _():
            total[...] = total[...] + row_of(vec_ref, 5)

        total[...] += branch
        gh2[...] += gradient

    @pl.when(block == pl.num_programs(0) - 1)
    def _():
        length = out_ref.shape[0] // 4
        row_index = lax.broadcasted_iota(jnp.int32, (length, 1), 0)
        for image in range(4):
            rows = slice(length * image, length * (image + 1))
            value = total[rows, :] + branch[rows]
            out_ref[rows, :] = jnp.where(row_index < counts[image], value, 0.0).astype(BF)
        whole = gh2[...] + gradient
        gout = gout_ref[...].astype(F32)
        gresid = gout + norm_back(whole * gain, normed[...], scales[:, 0:1])
        gresid_ref[...] = gresid
        low = gresid.astype(BF)
        glow_ref[...] = low
        sums = stack_rows(
            [sum_rows(whole * normed[...]), sum_rows(whole), sum_rows(gout), None, sum_rows(low)]
        )
        product1[...] = dot(att_ref[...], low, 0, 0)
        for chip in range(CHIPS):
            below = sums + fcg[chip // 4]
            for which, target in enumerate((keep2, send2)):
                owner = place[48] if which == 0 else 1 - place[48]
                share = product1[pl.ds(pl.multiple_of(48 * chip + 24 * owner, 8), 24), :]
                stage_end[which, chip] = jnp.concatenate([share, below], axis=0).astype(BF)
                slot = place[LARGE[which] + chip]
                pltpu.make_async_copy(
                    stage_end.at[which, chip], target.at[slot, pl.ds(96, 32)], sems.at[which]
                ).start()
        wait_all(wo, sems.at[2])
        wait_all(keep2, sems.at[0])
        wait_all(send2, sems.at[1])


def attention_back_kernel(side, wo, qkv_ref, far_ref, glow_ref, *refs):
    gqkv_ref = refs[-1]
    low = glow_ref[...]
    mine = slice(BLOCK * side, BLOCK * (side + 1))
    gatt = (
        dot(low[:, :BLOCK], wo[0, mine, :], 1, 1) + dot(low[:, BLOCK:], wo[1, mine, :], 1, 1)
    ).astype(BF)
    length = low.shape[0]
    low_half = lax.broadcasted_iota(jnp.int32, (length, 128), 1) < 64
    far = far_ref[0]
    for pair in range(3):
        at = 128 * pair
        queries = qkv_ref[0, :, at : at + 128] * jnp.asarray(0.125, BF)
        key_rows = two_heads(qkv_ref[0, :, BLOCK + at : BLOCK + at + 128], low_half)
        values = two_heads(qkv_ref[0, :, 2 * BLOCK + at : 2 * BLOCK + at + 128], low_half)
        grads = gatt[:, at : at + 128]
        both = dot(key_rows, queries, 1, 1)
        gboth = dot(values, grads, 1, 1)
        probs, gscores = [], []
        for head in range(2):
            rows = slice(length * head, length * (head + 1))
            scores = both[rows] - SLOPES[6 * side + 2 * pair + head] * far
            shifted = jnp.exp(scores - jnp.max(scores, axis=0, keepdims=True))
            share = shifted * (1.0 / jnp.sum(shifted, axis=0, keepdims=True))
            weighted = share * gboth[rows]
            probs.append(share.astype(BF))
            inner = jnp.sum(weighted, axis=0, keepdims=True)
            gscores.append((weighted - share * inner).astype(BF))
        probs, gscores = jnp.concatenate(probs, axis=0), jnp.concatenate(gscores, axis=0)
        gvalues = dot(probs, grads)
        gkeys = dot(gscores, queries)
        gqkv_ref[:, at : at + 128] = (dot(gscores, key_rows, 0, 0) * 0.125).astype(BF)
        for which, result in ((1, gkeys), (2, gvalues)):
            gqkv_ref[:, which * BLOCK + at : which * BLOCK + at + 128] = jnp.where(
                low_half, result[:length], result[length:]
            ).astype(BF)


def qkv_grad_kernel(
    place, h1_turned, gqkv_ref, wq_ref, gh1_ref, sums_ref, keep_ref, send_ref, product
):
    part = pl.program_id(0)
    product[...] = dot(h1_turned[...], gqkv_ref[...])
    gradient = dot(gqkv_ref[...], wq_ref[0], 1, 1)
    gh1_ref[...] = jnp.where(part == 0, gradient, gh1_ref[...] + gradient)
    sums_ref[part] = stack_rows([None, None, sum_rows(gqkv_ref[...])])
    give_rows(place, SMALL, product, keep_ref, send_ref)


def input_kernel(
    place, h1_turned, gqkv_ref, wq_ref, before_ref, rows_ref, vec_ref, gresid, gh1,
    ginput_ref, keep_ref, send_ref,
    product, sums, gresid_here, total, sems_in,
):
    part = pl.program_id(0)
    loads = [
        pltpu.make_async_copy(gh1, total, sems_in.at[0]),
        pltpu.make_async_copy(gresid, gresid_here, sems_in.at[1]),
    ]

    @pl.when(part == 0)
    def _():
        for load in loads:
            load.start()

    product[...] = dot(h1_turned[...], gqkv_ref[...])
    gradient = dot(gqkv_ref[...], wq_ref[0], 1, 1)

    @pl.when(part == 0)
    def _():
        loads[0].wait()

    total[...] += gradient
    sums[part] = stack_rows([None, None, sum_rows(gqkv_ref[...])])

    @pl.when(part < 2)
    def _():
        give_rows(place, SMALL, product, keep_ref, send_ref, lambda chip: jnp.zeros((8, BLOCK), F32))

    @pl.when(part == 2)
    def _():
        loads[1].wait()
        gradient = total[...]
        normed, scale = normed_rows(rows_ref[...].astype(F32))
        ginput_ref[...] = (
            gresid_here[...] + norm_back(gradient * row_of(vec_ref, 0), normed, scale)
        ).astype(BF)
        gain, shift = sum_rows(gradient * normed), sum_rows(gradient)

        def below(chip):
            lanes = slice(BLOCK * (chip // 8), BLOCK * (chip // 8 + 1))
            biases = (before_ref[0], sums[0], before_ref[2], sums[2])[chip // 4]
            return stack_rows([gain[:, lanes], shift[:, lanes]]) + biases

        give_rows(place, SMALL, product, keep_ref, send_ref, below)


def add_up(parts):
    return sum(part.astype(F32) for part in parts)


def give_vector(target, line, device):
    count, columns = target.shape[0], line.shape[1]
    start = lax.rem(device, columns // count) * count
    moved = pltpu.roll(line, lax.rem(columns - start, columns), 1)
    target[...] = moved[:, :count].reshape(count)


def last_second_kernel(place, *refs):
    sources, (fc2_out, out_out, gain, shift, fc2_bias, out_bias, fc1_bias) = refs[:6], refs[6:]
    total = add_up([source[0] for source in sources])
    fc2_out[...] = total[:96]
    out_out[...] = total[96:120]
    device = place[49]
    for line, target in enumerate((gain, shift, fc2_bias, fc1_bias, out_bias)):
        give_vector(target, total[120 + line : 121 + line], device)


def last_heads_kernel(place, *refs):
    sources, (grad_out, gain, shift, bias) = refs[:12], refs[12:]
    total_a = add_up([source[0] for source in sources[:6]])
    total_c = add_up([source[0] for source in sources[6:]])
    for part in range(3):
        lanes = slice(BLOCK * part, BLOCK * (part + 1))
        grad_out[:, 2 * BLOCK * part : 2 * BLOCK * part + BLOCK] = total_a[:, lanes]
        grad_out[:, 2 * BLOCK * part + BLOCK : 2 * BLOCK * (part + 1)] = total_c[:24, lanes]
    device = place[49]
    for line, target in enumerate((gain, shift, bias)):
        give_vector(target, total_c[24 + line : 25 + line, 2 * BLOCK :], device)


def after(value, *others):
    return lax.optimization_barrier((value,) + others)[0]


class Links:
    def __init__(self, depth):
        self.depth = depth

        def table(move):
            pairs = []
            for z in range(depth):
                for x in range(2):
                    for y in range(2):
                        for c in range(2):
                            nz, nx, ny, nc = move(z, x, y, c)
                            source = (z * 2 + x) * 4 + y * 2 + c
                            pairs.append((source, ((nz % depth) * 2 + nx) * 4 + ny * 2 + nc))
            return pairs

        self.ups = {step: table(lambda z, x, y, c: (z + step, x, y, c)) for step in (1, 2, 3)}
        self.first = table(lambda z, x, y, c: (z, x, 1 - y, c) if c else (z, 1 - x, y, c))
        self.second = table(lambda z, x, y, c: (z, 1 - x, y, c) if c else (z, x, 1 - y, c))
        self.cores = table(lambda z, x, y, c: (z, x, y, 1 - c))
        self.near = table(lambda z, x, y, c: (z ^ 1, x, y, c))
        self.far = table(lambda z, x, y, c: (z ^ 2, x, y, c))

    def move(self, value, pairs):
        return lax.ppermute(value, AXES, pairs)

    def spots(self):
        dp, fsdp = lax.axis_index("dp"), lax.axis_index("fsdp")
        z, x, y, core = dp // 2, dp % 2, fsdp // 2, fsdp % 2

        def chip(c, flip1, flip2, step):
            flip_x = jnp.where(c == 0, flip1, flip2)
            flip_y = jnp.where(c == 0, flip2, flip1)
            return (((z - step) % self.depth) * 2 + (x ^ flip_x)) * 2 + (y ^ flip_y)

        index = jnp.arange(32, dtype=jnp.int32)
        whose = jnp.where(index < 16, core, 1 - core)
        flip2 = (index // 8) % 2
        z_first = chip(whose, (index // 4) % 2, flip2, index % 4)
        x_first = chip(whose, index % 2, (index // 2) % 2, (index // 4) % 4)
        chips = jnp.arange(16, dtype=jnp.int32)
        turn_x, turn_y = ((chips // 2) % 2) ^ x, (chips % 2) ^ y
        far_z = (chips // 4) ^ z
        near, wide_step = far_z % 2, far_z // 2

        def slots(order):
            turns = {"x": turn_x, "y": turn_y, "near": near, "far": wide_step}
            return sum(turns[name] * weight for name, weight in zip(order, (8, 4, 2, 1)))

        rest = jnp.where(jnp.arange(16) == 1, dp * 4 + fsdp, core).astype(jnp.int32)
        tables = []
        for orders in (
            (("y", "x", "near", "far"), ("x", "y", "near", "far")),
            (("y", "near", "x", "far"), ("x", "near", "y", "far")),
        ):
            both = [slots(order) for order in orders]
            tables += [jnp.where(core == 0, both[0], both[1]), jnp.where(core == 0, both[1], both[0])]
        parts = [z_first, tables[0], rest, x_first] + tables[1:]
        return jnp.concatenate(parts).astype(jnp.int32)

    def gather(self, piece_a, piece_b1, piece_b2, early):
        hold = lax.optimization_barrier
        up = lambda value, step: self.move(value, self.ups[step])
        a_one, a_three, b1_two = hold((up(piece_a, 1), up(piece_a, 3), self.move(piece_b1, self.first)))
        b1_two = jnp.stack([piece_b1, b1_two])
        a_two, b1_four = hold((up(a_one, 1), self.move(b1_two, self.second)))
        a_four = jnp.stack([piece_a, a_one, a_two, a_three])
        b1_four = jnp.concatenate([b1_two, b1_four])
        piece_b2 = after(piece_b2, a_two)
        a_rest, b2_one, b2_three, early = hold(
            (self.move(a_four, self.first), up(piece_b2, 1), up(piece_b2, 3), early)
        )
        a_eight = jnp.concatenate([a_four, a_rest])
        a_other, b2_two, b1_one = hold((self.move(a_eight, self.second), up(b2_one, 1), up(b1_four, 1)))
        b2_four = jnp.stack([piece_b2, b2_one, b2_two, b2_three])
        a = self.finish(a_eight, a_other)
        return a, (b1_four, b1_one, up(b1_four, 3)), (b2_four, self.move(b2_four, self.first)), early

    def gather_on(self, b1, b2):
        b1_four, b1_one, b1_three = b1
        b1_two = self.move(b1_one, self.ups[1])
        b2_eight = jnp.concatenate(b2)
        b2_other = self.move(b2_eight, self.second)
        b1_mine = jnp.concatenate([b1_four, b1_one])
        return (b1_mine, b1_two, b1_three, self.move(b1_mine, self.cores)), (b2_eight, b2_other)

    def gather_end(self, b1, b2):
        mine, b1_two, b1_three, other = b1
        rest = jnp.concatenate([b1_two, b1_three])
        return (mine, rest, other, self.move(rest, self.cores)), self.finish(*b2)

    def finish(self, eight, rest):
        return (eight, rest, self.move(eight, self.cores), self.move(rest, self.cores))

    def fold(self, state):
        left = 32 >> (len(state) - 1)
        return add_up([part[left // 2 : left] for part in state]).astype(BF)

def full_pieces(full, blocks):
    split = full.reshape((CHIPS, 48) + full.shape[1:])
    split = split.transpose(3, 0, 2, 1, 4) if full.shape[1] == blocks else split.transpose(2, 0, 3, 1, 4)
    return split.reshape(2 * CHIPS, blocks * 48, BLOCK)


def eights(pieces):
    return tuple(pieces[8 * index : 8 * (index + 1)] for index in range(4))


def placed(vector, device, per_row):
    start = (device % per_row) * vector.shape[0]
    return lax.dynamic_update_slice(jnp.zeros((BLOCK,), vector.dtype), vector, (start,))


def shards(
    mesh_shape,
    patches,
    counts,
    positions,
    ln1_gain,
    ln1_bias,
    qkv_weight,
    qv_bias,
    out_weight,
    out_bias,
    ln2_gain,
    ln2_bias,
    fc1_weight,
    fc1_bias,
    fc2_weight,
    fc2_bias,
    cotangent,
):
    images, length, width = patches.shape
    padded = (length + 31) // 32 * 32
    rows = images * padded
    hidden_width = fc1_weight.shape[1]
    devices = mesh_shape["dp"] * mesh_shape["fsdp"]
    by_hand = devices == 2 * CHIPS and mesh_shape["fsdp"] == 4
    small_parts = (ln1_gain, ln1_bias, out_bias, ln2_gain, ln2_bias, fc2_bias, qv_bias, fc1_bias)

    smem = pl.BlockSpec(memory_space=pltpu.SMEM)
    vmem = pl.BlockSpec(memory_space=pltpu.VMEM)
    anywhere = pl.BlockSpec(memory_space=pltpu.HBM)
    struct = jax.ShapeDtypeStruct

    row_index = jnp.arange(padded, dtype=jnp.int32)
    is_live = row_index[None, :] < counts[:, None]
    pad_rows = ((0, 0), (0, padded - length), (0, 0))
    rows_in = jnp.pad(patches, pad_rows).reshape(rows, width)
    gout = jnp.where(is_live[:, :, None], jnp.pad(cotangent, pad_rows), 0).reshape(rows, width)
    spots = jnp.pad(positions, pad_rows[:2])
    grid_rows = (spots // SIDE).astype(F32)
    grid_cols = (spots % SIDE).astype(F32)
    row_delta = grid_rows[:, :, None] - grid_rows[:, None, :]
    col_delta = grid_cols[:, :, None] - grid_cols[:, None, :]
    distance = jnp.sqrt(row_delta * row_delta + col_delta * col_delta)
    far = jnp.where(is_live[:, None, :], distance, FAR)
    far_turned = jnp.where(is_live[:, :, None], distance, FAR)

    if by_hand:
        links = Links(mesh_shape["dp"] // 2)
        place = links.spots()
        core = place[48]
        share = struct((8, 24, BLOCK), BF)
        mine, theirs, lines = pl.pallas_call(
            share_kernel,
            out_shape=(share, share, struct((16, BLOCK), BF)),
            in_specs=[smem] + [vmem] * 11,
            out_specs=(vmem,) * 3,
            name="share",
        )(place, qkv_weight, out_weight, fc1_weight, *small_parts)
        got = links.move(theirs, links.cores)
        pieces = pl.pallas_call(
            pair_kernel,
            out_shape=tuple(struct((height, BLOCK), BF) for height in (160, 192, 240)),
            in_specs=[smem] + [vmem] * 4,
            out_specs=(vmem,) * 3,
            name="pair",
        )(place, mine, got, lines, fc2_weight)
    else:
        links = None
        place = jnp.concatenate(
            [
                jnp.arange(32, dtype=jnp.int32) % 16,
                jnp.arange(16, dtype=jnp.int32),
                jnp.zeros((16,), jnp.int32),
                jnp.arange(80, dtype=jnp.int32) % 16,
            ]
        )
        whole = [lax.all_gather(part, AXES, axis=0, tiled=True) for part in small_parts]
        lines = []
        for part in whole:
            share = part.shape[0] // 32
            chunks = part.reshape(32, share)
            lines.append(
                jnp.stack([placed(chunks[index], index, BLOCK // share) for index in range(32)])
            )
        lines = jnp.concatenate([jnp.stack(lines, axis=1), jnp.zeros((32, 8, BLOCK), BF)], axis=1)
        lines = lines.reshape(CHIPS, 2, 16, BLOCK).transpose(1, 0, 2, 3).reshape(32, 16, BLOCK)
        whole_qkv = lax.all_gather(qkv_weight, AXES, axis=0, tiled=True)
        whole_out = lax.all_gather(out_weight, AXES, axis=0, tiled=True)
        whole_fc1 = lax.all_gather(fc1_weight, AXES, axis=0, tiled=True)
        whole_fc2 = lax.all_gather(fc2_weight, AXES, axis=0, tiled=True)
        split = whole_fc2.reshape(CHIPS, 2, 96, 2, BLOCK).transpose(1, 0, 3, 2, 4).reshape(32, 192, BLOCK)
        gathered_a = eights(
            jnp.concatenate([full_pieces(whole_qkv.reshape(width, 3, 2, BLOCK), 3), lines], axis=1)
        )
        gathered_b1 = eights(full_pieces(whole_fc1.reshape(width, 2, 4, BLOCK), 4))
        split = whole_fc2.reshape(CHIPS, 2, 96, 2, BLOCK).transpose(1, 0, 3, 2, 4).reshape(32, 192, BLOCK)
        gathered_b2 = eights(
            jnp.concatenate([split, full_pieces(whole_out.reshape(width, 1, 2, BLOCK), 1)], axis=1)
        )

    if by_hand:
        gathered_a, on_b1, on_b2, early = links.gather(*pieces, (rows_in, gout, far, far_turned))
        rows_in, gout, far, far_turned = early


    def call(kernel, operands, out_shape, out_specs, in_specs, flops, mib, vmem_mib, grid, scratch=(), name=None):
        return pl.pallas_call(
            kernel,
            grid=grid,
            out_shape=out_shape,
            in_specs=in_specs,
            out_specs=out_specs,
            scratch_shapes=list(scratch),
            compiler_params=pltpu.CompilerParams(vmem_limit_bytes=vmem_mib * MIB),
            cost_estimate=pl.CostEstimate(
                flops=int(flops), bytes_accessed=mib * MIB, transcendentals=0
            ),
            name=name,
        )(*operands)

    image_rows = lambda columns: pl.BlockSpec((padded, columns), lambda image: (image, 0))
    image_far = pl.BlockSpec((1, padded, padded), lambda image: (image, 0, 0))
    fixed = lambda *shape: pl.BlockSpec(shape, lambda step: (0,) * len(shape))
    step_rows = lambda columns: pl.BlockSpec((rows, columns), lambda step: (0, step))
    shares = lambda height, columns: struct((CHIPS, height, columns), BF)
    buffer, flag = pltpu.VMEM, pltpu.SemaphoreType.DMA
    low_rows, wide_rows = struct((rows, width), BF), struct((rows, width), F32)
    wide = 2 * BLOCK
    steps = hidden_width // wide
    third = 3 * BLOCK

    def join(value, *others):
        return after(value, *others) if by_hand else value

    vec, fcb, h1_turned, qkv, wq = call(
        qkv_kernel,
        (place, *gathered_a, rows_in),
        (
            struct((2, 16, BLOCK), F32), struct((steps, 1, wide), F32), struct((width, rows), BF),
            struct((2, rows, third), BF), struct((2, width, third), BF),
        ),
        (
            fixed(2, 16, BLOCK), fixed(steps, 1, wide), fixed(width, rows),
            pl.BlockSpec((1, rows, third), lambda step: (step, 0, 0)), anywhere,
        ),
        [smem] + [anywhere] * 4 + [fixed(rows, width)],
        2 * rows * width * 3 * width,
        14,
        30,
        grid=(2,),
        scratch=(
            buffer((2, width, third), BF), buffer((rows, width), BF), buffer((4, 16, BLOCK), F32),
            buffer((32, 16, BLOCK), BF), flag((4,)),
        ),
        name="qkv",
    )
    if by_hand:
        qkv, on_b1, on_b2 = lax.optimization_barrier((qkv, on_b1, on_b2))
        on_b1, on_b2 = links.gather_on(on_b1, on_b2)

    att = call(
        attention_kernel,
        (qkv, far),
        low_rows,
        image_rows(width),
        [pl.BlockSpec((2, padded, third), lambda image: (0, image, 0)), image_far],
        8 * rows * 256 * width,
        10,
        20,
        grid=(images,),
        name="attention",
    )
    if by_hand:
        att, on_b1, on_b2 = lax.optimization_barrier((att, on_b1, on_b2))
        gathered_b1, gathered_b2 = links.gather_end(on_b1, on_b2)

    step_shares = lambda height, columns: pl.BlockSpec((CHIPS, height, columns), lambda step: (0, 0, step))
    out, gresid, glow, keep_1, send_1, keep_2, send_2, wo = call(
        mlp_kernel,
        (place, counts, *gathered_b1, *gathered_b2, att, rows_in, gout, vec, fcb),
        (low_rows, wide_rows, low_rows)
        + (shares(24, hidden_width),) * 2
        + (shares(128, wide),) * 2
        + (struct((2, width, BLOCK), BF),),
        (fixed(rows, width),) * 3 + (step_shares(24, wide),) * 2 + (anywhere,) * 3,
        [smem, smem] + [anywhere] * 8 + [fixed(rows, width)] * 3 + [
            fixed(2, 16, BLOCK), fixed(steps, 1, wide),
        ],
        12 * rows * width * hidden_width,
        32,
        60,
        grid=(steps,),
        scratch=(
            buffer((steps, width, wide), BF), buffer((hidden_width, width), BF), buffer((2, width, BLOCK), BF),
            buffer((rows, width), BF), buffer((width, rows), BF), buffer((rows, width), F32),
            buffer((rows, width), F32), buffer((rows, width), F32), buffer((width, wide), F32),
            buffer((width, wide), F32), buffer((2, CHIPS, 96, wide), BF), buffer((2, CHIPS, 32, wide), BF),
            buffer((steps, 8, wide), F32), buffer((rows, 128), F32), flag((steps,)), flag((steps,)), flag((3,)),
        ),
        name="mlp",
    )
    if by_hand:
        state_2 = keep_2, links.move(send_2, links.cores)
        state_1 = keep_1, links.move(after(send_1, keep_2), links.cores)

    def attention_back(side, gradient, first, count, vmem_mib, before=()):
        some_rows = lambda columns: pl.BlockSpec((padded, columns), lambda image: (first + image, 0))
        return pl.pallas_call(
            lambda *refs: attention_back_kernel(side, *refs),
            grid=(count,),
            out_shape=struct((rows, third), BF),
            in_specs=[
                fixed(2, width, BLOCK),
                pl.BlockSpec((1, padded, third), lambda image: (side, first + image, 0)),
                pl.BlockSpec((1, padded, padded), lambda image: (first + image, 0, 0)),
                some_rows(width),
            ]
            + [anywhere] * len(before),
            out_specs=some_rows(third),
            input_output_aliases={4: 0} if before else {},
            compiler_params=pltpu.CompilerParams(vmem_limit_bytes=vmem_mib * MIB),
            cost_estimate=pl.CostEstimate(flops=1, bytes_accessed=1, transcendentals=0),
            name="attention_back",
        )(wo, qkv, far_turned, gradient, *before)

    gqkv_0 = attention_back(0, glow, 0, images // 2, 60)
    part_2 = glow
    if by_hand:
        state_2, gqkv_0 = lax.optimization_barrier((state_2, gqkv_0))
        part_2 = links.fold(state_2)
        state_2 += (links.move(part_2, links.second),)
    gqkv_0 = attention_back(0, join(glow, part_2), images // 2, images - images // 2, 60, (gqkv_0,))
    if by_hand:
        state_1, gqkv_0 = lax.optimization_barrier((state_1, gqkv_0))
        state_1 += (links.move(links.fold(state_1), links.second),)

    step_weight = lambda side: pl.BlockSpec((1, width, BLOCK), lambda step: (side, 0, step))
    gh1, sums_0, keep_a, send_a = call(
        qkv_grad_kernel,
        (place, h1_turned, gqkv_0, wq),
        (wide_rows, struct((3, 8, BLOCK), F32)) + (shares(24, third),) * 2,
        (fixed(rows, width), fixed(3, 8, BLOCK)) + (step_shares(24, BLOCK),) * 2,
        [smem, fixed(width, rows), step_rows(BLOCK), step_weight(0)],
        6 * rows * width * width,
        10,
        24,
        grid=(3,),
        scratch=(buffer((width, BLOCK), F32),),
        name="qkv_grad",
    )
    part_2 = gh1
    if by_hand:
        state_a = keep_a, links.move(send_a, links.cores)
        state_2, gh1 = lax.optimization_barrier((state_2, gh1))
        part_2 = links.fold(state_2)
        state_2 += (links.move(part_2, links.near),)

    gqkv_1 = attention_back(1, join(glow, gh1, part_2), 0, images, 20)
    if by_hand:
        state_a, gqkv_1 = lax.optimization_barrier((state_a, gqkv_1))
        state_a += (links.move(links.fold(state_a), links.second),)

    ginput, keep_c, send_c = call(
        input_kernel,
        (place, h1_turned, gqkv_1, wq, sums_0, rows_in, vec, gresid, gh1),
        (low_rows,) + (shares(32, third),) * 2,
        (fixed(rows, width),) + (step_shares(32, BLOCK),) * 2,
        [
            smem, fixed(width, rows), step_rows(BLOCK), step_weight(1), fixed(3, 8, BLOCK), fixed(rows, width), fixed(2, 16, BLOCK),
            anywhere, anywhere,
        ],
        6 * rows * width * width,
        14,
        30,
        grid=(3,),
        scratch=(
            buffer((width, BLOCK), F32), buffer((3, 8, BLOCK), F32), buffer((rows, width), F32),
            buffer((rows, width), F32), flag((2,)),
        ),
        name="input_grad",
    )
    def cut(value):
        return value.reshape(images, padded, width)[:, :length]

    if by_hand:
        fold, move = links.fold, links.move

        def last_sum(kernel, state, heights, counts_out):
            first = lambda part: pl.BlockSpec((1,) + part.shape[1:], lambda step: (0, 0, 0))
            columns = 3 * width if kernel is last_heads_kernel else width
            return pl.pallas_call(
                kernel,
                grid=(1,),
                out_shape=tuple(struct((height, columns), F32) for height in heights)
                + tuple(struct((count,), F32) for count in counts_out),
                in_specs=[smem] + [first(part) for part in state],
                out_specs=tuple(fixed(height, columns) for height in heights)
                + tuple(pl.BlockSpec((count,), lambda step: (0,)) for count in counts_out),
                compiler_params=pltpu.CompilerParams(vmem_limit_bytes=30 * MIB),
                name="last_sum",
            )(place, *state)

        state_c = keep_c, move(send_c, links.cores)
        state_1 = after(state_1, keep_c)
        part = fold(state_1)
        state_1 += (move(part, links.near),)
        part = fold(after(state_c, part))
        state_c += (move(part, links.second),)
        state_2, state_a = after((state_2, state_a), part)
        parts = fold(state_2), fold(state_a)
        state_2 += (move(parts[0], links.first),)
        state_a += (move(parts[1], links.first),)
        out, ginput = after((out, ginput), parts)
        out, ginput = cut(out), cut(ginput)
        part = fold(after(state_c, parts))
        state_c += (move(part, links.first),)
        state_1, state_2, state_a, out, ginput = after((state_1, state_2, state_a, out, ginput), part)
        parts = fold(state_2), fold(state_1), fold(state_a)
        state_2 += (move(parts[0], links.far),)
        state_1 += (move(parts[1], links.first),)
        state_a += (move(parts[2], links.near),)
        part = fold(after(state_c, parts))
        state_c += (move(part, links.near),)
        state_1, state_a = after((state_1, state_a), part)
        parts = fold(state_1), fold(state_a)
        state_1 += (move(parts[0], links.far),)
        state_a += (move(parts[1], links.far),)
        part = fold(after(state_c, parts))
        state_c += (move(part, links.far),)
        state_2 = after(state_2, part)
        mine_2 = last_sum(last_second_kernel, state_2, (96, 24), (24, 24, 24, 24, 96))
        state_1 = after(state_1, mine_2)
        mine_1 = add_up([part[0] for part in state_1])
        mine_c = last_sum(last_heads_kernel, state_a + state_c, (24,), (24, 24, 48))
        fc2_grad, out_grad, ln2_gain_grad, ln2_bias_grad, fc2_bias_grad, out_bias_grad, fc1_bias_grad = mine_2
        qkv_grad, ln1_gain_grad, ln1_bias_grad, qv_bias_grad = mine_c
        return (
            out, ginput, ln1_gain_grad, ln1_bias_grad, qkv_grad, qv_bias_grad, out_grad, out_bias_grad,
            ln2_gain_grad, ln2_bias_grad, mine_1, fc1_bias_grad, fc2_grad, fc2_bias_grad,
        )

    both_a, both_c, both_1, both_2 = (
        jnp.stack(pair, axis=1).astype(F32)
        for pair in ((keep_a, send_a), (keep_c, send_c), (keep_1, send_1), (keep_2, send_2))
    )
    heads = jnp.stack(
        [both.reshape(CHIPS, 2, 24, 3, BLOCK) for both in (both_a, both_c[:, :, :24])], axis=4
    )

    def vector(lines, count):
        columns = lines.shape[-1]
        return lines.reshape(32 * count // columns, -1, columns)[:, 0].reshape(-1)

    small_c, small_2 = both_c[:, :, 24:, 2 * BLOCK :], both_2[:, :, 120:]
    totals = (
        vector(small_c[:, :, 0], 24),
        vector(small_c[:, :, 1], 24),
        heads.reshape(width, 3 * width),
        vector(small_c[:, :, 2], 48),
        both_2[:, :, 96:120].reshape(width, width),
        vector(small_2[:, :, 4], 24),
        vector(small_2[:, :, 0], 24),
        vector(small_2[:, :, 1], 24),
        both_1.reshape(width, hidden_width),
        vector(small_2[:, :, 3], 96),
        both_2[:, :, :96].reshape(hidden_width, width),
        vector(small_2[:, :, 2], 24),
    )
    return (cut(out), cut(ginput)) + tuple(
        lax.psum_scatter(total, AXES, scatter_dimension=0, tiled=True) for total in totals
    )


def solution(mesh):
    rows = P(AXES, None, None)
    table = P(AXES, None)
    line = P(AXES)
    in_specs = (
        rows, line, table, line, line, table, line, table, line, line, line, table, line, table, line, rows,
    )
    out_specs = (
        rows, rows, line, line, table, line, table, line, line, line, table, line, table, line,
    )
    mesh_shape = dict(mesh.shape)

    def body(*arrays):
        return shards(mesh_shape, *arrays)

    return jax.shard_map(body, mesh=mesh, in_specs=in_specs, out_specs=out_specs, check_vma=False)
```

```python
import math

import jax
import jax.numpy as jnp
import numpy as np
from jax import lax
from jax.experimental import pallas as pl
from jax.experimental.pallas import tpu as pltpu
from jax.sharding import PartitionSpec as P

HEADS = 12
SIDE = 16
EPSILON = 1e-06
AXES = ("dp", "fsdp")
FAR = 1e30
CHIPS = 16
BLOCK = 384
SMALL, LARGE = (32, 96), (112, 128)
MIB = 1024 * 1024

BF = jnp.bfloat16
F32 = jnp.float32


def power_slopes(number):
    first_slope = 2.0 ** (-8.0 / number)
    return [first_slope ** (index + 1) for index in range(number)]


def slope_list(heads_total):
    lower_power = 2 ** int(math.floor(math.log2(heads_total)))
    return (
        power_slopes(lower_power) + power_slopes(2 * lower_power)[0::2][: heads_total - lower_power]
    )


SLOPES = [float(np.float32(slope)) for slope in slope_list(HEADS)]


def dot(left, right, left_dim=1, right_dim=0):
    return lax.dot_general(
        left, right, (((left_dim,), (right_dim,)), ((), ())), preferred_element_type=F32
    )


def normed_rows(values):
    centered = values - jnp.mean(values, axis=-1, keepdims=True)
    scale = lax.rsqrt(jnp.mean(centered * centered, axis=-1, keepdims=True) + EPSILON)
    return centered * scale, scale


def norm_back(grad_normed, normed, scale):
    centered_mean = jnp.mean(grad_normed, axis=-1, keepdims=True)
    projected_mean = jnp.mean(grad_normed * normed, axis=-1, keepdims=True)
    return scale * (grad_normed - centered_mean - normed * projected_mean)


def row_of(vectors_ref, index):
    return jnp.concatenate(
        [vectors_ref[0, index : index + 1, :], vectors_ref[1, index : index + 1, :]], axis=1
    )


def gelu_parts(hidden):
    cumulative = 0.5 + 0.5 * lax.erf(hidden * math.sqrt(0.5))
    bell = jnp.exp(-0.5 * hidden * hidden)
    return cumulative, cumulative + hidden * bell * (1.0 / math.sqrt(2.0 * math.pi))


def share_kernel(place, qkv_ref, out_ref, fc1_ref, *refs):
    smalls, (mine_ref, theirs_ref, lines_ref) = refs[:-3], refs[-3:]
    for target, core in ((mine_ref, place[48]), (theirs_ref, 1 - place[48])):
        starts = [(qkv_ref, 2 * BLOCK * part + BLOCK * core) for part in range(3)]
        starts.append((out_ref, BLOCK * core))
        starts += [(fc1_ref, 4 * BLOCK * core + BLOCK * part) for part in range(4)]
        for block, (source, start) in enumerate(starts):
            target[block] = source[:, pl.ds(pl.multiple_of(start, 128), BLOCK)]
    device = place[49]
    lines = []
    for small in smalls:
        count = small.shape[0]
        line = small[...].astype(F32).reshape(1, count)
        line = jnp.concatenate([line, jnp.zeros((1, BLOCK - count), F32)], axis=1)
        lines.append(pltpu.roll(line, lax.rem(device, BLOCK // count) * count, 1))
    lines_ref[...] = jnp.concatenate(lines + [jnp.zeros((8, BLOCK), F32)], axis=0).astype(BF)


def pair_kernel(place, mine_ref, got_ref, lines_ref, fc2_ref, a_ref, b1_ref, b2_ref):
    swap = place[48] == 1
    for block in range(8):
        mine, got = mine_ref[block].astype(F32), got_ref[block].astype(F32)
        rows = jnp.concatenate([jnp.where(swap, got, mine), jnp.where(swap, mine, got)], axis=0)
        if block < 3:
            a_ref[48 * block : 48 * (block + 1), :] = rows.astype(BF)
        elif block == 3:
            b2_ref[192:240, :] = rows.astype(BF)
        else:
            b1_ref[48 * (block - 4) : 48 * (block - 3), :] = rows.astype(BF)
    b2_ref[0:96, :] = fc2_ref[:, :BLOCK]
    b2_ref[96:192, :] = fc2_ref[:, BLOCK:]
    a_ref[144:160, :] = lines_ref[...]


def each_piece(place, table, sources, work):
    core = place[48]
    for number, source in enumerate(sources):
        half = core if number < 2 else 1 - core

        def bring(index, _, source=source, number=number, half=half):
            work(source, index, place[table + number * 8 + index], half)
            return 0

        lax.fori_loop(0, 8, bring, 0)


def bring_out_weight(place, sources, wo, sem):
    def work(source, index, chip, half):
        spot = pl.ds(pl.multiple_of(chip * 48, 16), 48)
        pltpu.make_async_copy(source.at[index, pl.ds(192, 48)], wo.at[half, spot], sem).start()

    each_piece(place, 0, sources, work)


def bring_qkv_weight(place, sources, side, wq, sem, part_of=None):
    for first, here in ((0, place[48] == side), (2, place[48] != side)):

        @pl.when(here)
        def _(first=first):
            for number in (first, first + 1):

                def bring(index, _, source=sources[number], number=number):
                    spot = pl.ds(pl.multiple_of(place[number * 8 + index] * 48, 16), 48)
                    for part in range(3):
                        pltpu.make_async_copy(
                            source.at[index, pl.ds(48 * part, 48)],
                            wq.at[spot, pl.ds(BLOCK * part, BLOCK)] if part_of is None else wq.at[part, spot],
                            sem if part_of is None else part_of.at[part],
                        ).start()
                    return 0

                lax.fori_loop(0, 8, bring, 0)


def wait_all(buffer, sem):
    pltpu.make_async_copy(buffer, buffer, sem).wait()


def qkv_kernel(
    place, own0, own1, other0, other1, rows_ref,
    vec_ref, fcb_ref, h1_turned, qkv_ref, wq_out,
    wq, h1, qvb, small, sems,
):
    sources = (own0, own1, other0, other1)
    side = pl.program_id(0)

    @pl.when(side == 0)
    def _():
        def work(source, index, chip, half):
            pltpu.make_async_copy(
                source.at[index, pl.ds(144, 16)], small.at[2 * chip + half], sems.at[2]
            ).start()

        each_piece(place, 0, sources, work)
        for half in range(2):
            bring_qkv_weight(place, sources, half, wq.at[half], sems.at[half])
        normed, _ = normed_rows(rows_ref[...].astype(F32))
        wait_all(small, sems.at[2])
        spread = small[...].astype(F32)
        vec_ref[...] = jnp.sum(spread.reshape(2, 16, 16, BLOCK), axis=1)
        qvb[...] = jnp.sum(spread.reshape(4, 8, 16, BLOCK), axis=1)
        lines = jnp.sum(spread.reshape(8, 4, 16, BLOCK), axis=1)
        for block in range(4):
            fcb_ref[block] = jnp.concatenate([lines[2 * block, 7:8], lines[2 * block + 1, 7:8]], axis=1)
        low = (normed * row_of(vec_ref, 0) + row_of(vec_ref, 1)).astype(BF)
        h1[...] = low
        h1_turned[...] = low.T

    wait_all(wq.at[side], sems.at[side])
    keeping = pltpu.make_async_copy(wq.at[side], wq_out.at[side], sems.at[3])
    keeping.start()
    bias = jnp.concatenate(
        [qvb[side, 6:7, :], jnp.zeros((1, BLOCK), F32), qvb[2 + side, 6:7, :]], axis=1
    )
    qkv_ref[0] = (dot(h1[...], wq[side]) + bias).astype(BF)
    keeping.wait()


def two_heads(pair_rows, low_half):
    nothing = jnp.zeros_like(pair_rows)
    return jnp.concatenate(
        [jnp.where(low_half, pair_rows, nothing), jnp.where(low_half, nothing, pair_rows)], axis=0
    )


def attention_kernel(qkv_ref, far_ref, att_ref):
    length = att_ref.shape[0]
    low_half = lax.broadcasted_iota(jnp.int32, (length, 128), 1) < 64
    far = far_ref[0]
    for pair in range(HEADS // 2):
        side, at = pair // 3, 128 * (pair % 3)
        queries = two_heads(qkv_ref[side, :, at : at + 128] * jnp.asarray(0.125, BF), low_half)
        key_rows = qkv_ref[side, :, BLOCK + at : BLOCK + at + 128]
        values = qkv_ref[side, :, 2 * BLOCK + at : 2 * BLOCK + at + 128]
        both = dot(queries, key_rows, 1, 1)
        probs = []
        for head in range(2):
            scores = both[length * head : length * (head + 1)] - SLOPES[2 * pair + head] * far
            shifted = jnp.exp(scores - jnp.max(scores, axis=-1, keepdims=True))
            share = shifted * (1.0 / jnp.sum(shifted, axis=-1, keepdims=True))
            probs.append(share.astype(BF))
        result = dot(jnp.concatenate(probs, axis=0), values)
        att_ref[:, 128 * pair : 128 * (pair + 1)] = jnp.where(
            low_half, result[:length], result[length:]
        ).astype(BF)


def at_slot(target, slot, work):
    if not isinstance(target, tuple):
        work(target, slot)
        return

    @pl.when(slot >= 8)
    def _():
        work(target[0], slot - 8)

    @pl.when(slot < 8)
    def _():
        work(target[1], slot)


def give_rows(place, tables, total, keep_ref, send_ref, extra=None):
    for chip in range(CHIPS):
        below = None if extra is None else extra(chip)
        for which, target in enumerate((keep_ref, send_ref)):
            owner = place[48] if which == 0 else 1 - place[48]
            share = total[pl.ds(pl.multiple_of(48 * chip + 24 * owner, 8), 24), :]
            if below is not None:
                share = jnp.concatenate([share, below], axis=0)

            def put(ref, slot, share=share):
                ref[slot] = share.astype(BF)

            at_slot(target, place[tables[which] + chip], put)


def stack_rows(rows):
    blank = jnp.zeros_like(next(row for row in rows if row is not None))
    rows = [blank if row is None else row for row in rows]
    return jnp.concatenate(rows + [blank] * (8 - len(rows)), axis=0)


def sum_rows(values):
    return jnp.sum(values.astype(F32), axis=0, keepdims=True)


def mlp_kernel(
    place, counts, a0, a1, a2, a3, b0, b1, b2, b3, att_far, rows_far, gout_far, vec_ref, fcb_ref,
    out_ref, glow_ref, keep1_ref, send1_ref, sums_ref, fcg, keep2, upper2, lower2, wo_out,
    w1, w2, wo, att_ref, rows_ref, gout_ref, h2, h2_turned, normed, total, gh2, product1, product2,
    stage, scales, sems1, sems2, sems,
):
    step = pl.program_id(0)
    wide = 2 * BLOCK
    core, z = place[48], place[50]
    block_of = lambda step: lax.rem(z + 4 - step, 4)
    block = block_of(step)
    gain = row_of(vec_ref, 3)
    loads = [
        pltpu.make_async_copy(source, target, sems.at[3 + index])
        for index, (source, target) in enumerate(
            ((att_far, att_ref), (rows_far, rows_ref), (gout_far, gout_ref))
        )
    ]

    @pl.when(step == 0)
    def _():
        bring_out_weight(place, (b0, b1, b2, b3), wo, sems.at[2])
        loads[0].start()
        loads[1].start()
        for later in range(4):
            column = block_of(later)
            for first, here in ((0, column // 2 == core), (2, column // 2 != core)):

                @pl.when(here)
                def _(first=first, column=column):
                    for number in (first, first + 1):

                        def bring(index, _, source=(a0, a1, a2, a3)[number], number=number, column=column):
                            spot = pl.ds(pl.multiple_of(place[64 + number * 8 + index] * 48, 16), 48)
                            for part in range(2):
                                start = pl.multiple_of(lax.rem(column, 2) * 96 + 48 * part, 16)
                                pltpu.make_async_copy(
                                    source.at[index, pl.ds(start, 48)],
                                    w1.at[column, spot, pl.ds(BLOCK * part, BLOCK)],
                                    sems1.at[column],
                                ).start()
                            return 0

                        lax.fori_loop(0, 8, bring, 0)

            if later == 0:
                loads[2].start()
            for number, source in enumerate((b0, b1, b2, b3)):
                half = core if number < 2 else 1 - core
                for index in (later, 4 + later):
                    chip = place[number * 8 + index]
                    spot = pl.ds(pl.multiple_of(chip * 192 + half * 96, 16), 96)
                    for part in range(2):
                        pltpu.make_async_copy(
                            source.at[index, pl.ds(96 * part, 96)],
                            w2.at[spot, pl.ds(BLOCK * part, BLOCK)],
                            sems2.at[column],
                        ).start()

        wait_all(wo, sems.at[2])
        pltpu.make_async_copy(wo, wo_out, sems.at[2]).start()
        bias = row_of(vec_ref, 2)
        loads[0].wait()
        loads[1].wait()
        for part in range(2):
            lanes = slice(BLOCK * part, BLOCK * (part + 1))
            total[:, lanes] = rows_ref[:, lanes].astype(F32) + dot(att_ref[...], wo[part]) + bias[:, lanes]
        normal, scale = normed_rows(total[...])
        normed[...] = normal
        scales[...] = jnp.broadcast_to(scale, scales.shape)
        low = (normal * gain + row_of(vec_ref, 4)).astype(BF)
        h2[...] = low
        h2_turned[...] = low.T
        total[...] += row_of(vec_ref, 5)
        gh2[...] = jnp.zeros_like(gh2)
        loads[2].wait()

    wait_all(w1.at[block], sems1.at[block])
    hidden = dot(h2[...], w1[block]) + fcb_ref[block]
    rows_of = pl.ds(pl.multiple_of(block * wide, wide), wide)
    wait_all(w2.at[rows_of], sems2.at[block])
    gactivated = dot(gout_ref[...], w2[rows_of, :], 1, 1)
    cumulative, slope = gelu_parts(hidden)
    activated = (hidden * cumulative).astype(BF)
    ghidden = (gactivated * slope).astype(BF)
    product1[...] = dot(h2_turned[...], ghidden)
    product2[...] = dot(activated, gout_ref[...], 0, 0)
    total[...] += dot(activated, w2[rows_of, :])
    gh2[...] += dot(ghidden, w1[block], 1, 1)
    fcg[block] = stack_rows([None, None, None, sum_rows(ghidden)])
    give_rows(place, LARGE, product1, keep1_ref, send1_ref)
    for pair in range(4):
        chip = 4 * block + pair
        for which, target in enumerate((keep2, (upper2, lower2))):
            owner = place[48] if which == 0 else 1 - place[48]
            start = pl.multiple_of(192 * pair + 96 * owner, 8)
            stage[which, chip] = product2[pl.ds(start, 96), :].astype(BF)

            def send(ref, slot, which=which, chip=chip):
                sem = sems.at[1 if ref is upper2 else 6 if ref is lower2 else 0]
                pltpu.make_async_copy(stage.at[which, chip], ref.at[slot], sem).start()

            at_slot(target, place[LARGE[which] + chip], send)

    @pl.when(step == pl.num_programs(0) - 1)
    def _():
        length = out_ref.shape[0] // 4
        row_index = lax.broadcasted_iota(jnp.int32, (length, 1), 0)
        for image in range(4):
            rows = slice(length * image, length * (image + 1))
            value = total[rows, :]
            out_ref[rows, :] = jnp.where(row_index < counts[image], value, 0.0).astype(BF)
        whole = gh2[...]
        gout = gout_ref[...].astype(F32)
        gresid = gout + norm_back(whole * gain, normed[...], scales[:, 0:1])
        low = gresid.astype(BF)
        glow_ref[...] = low
        sums_ref[...] = stack_rows(
            [sum_rows(whole * normed[...]), sum_rows(whole), sum_rows(gout), None, sum_rows(low)]
        )
        wait_all(wo, sems.at[2])
        wait_all(keep2, sems.at[0])
        wait_all(upper2, sems.at[1])
        wait_all(lower2, sems.at[6])


def attention_back_kernel(side, wo, qkv_ref, far_ref, glow_ref, gqkv_ref):
    low = glow_ref[...]
    mine = slice(BLOCK * side, BLOCK * (side + 1))
    gatt = (
        dot(low[:, :BLOCK], wo[0, mine, :], 1, 1) + dot(low[:, BLOCK:], wo[1, mine, :], 1, 1)
    ).astype(BF)
    length = low.shape[0]
    low_half = lax.broadcasted_iota(jnp.int32, (length, 128), 1) < 64
    far = far_ref[0]
    for pair in range(3):
        at = 128 * pair
        queries = qkv_ref[0, :, at : at + 128] * jnp.asarray(0.125, BF)
        key_rows = two_heads(qkv_ref[0, :, BLOCK + at : BLOCK + at + 128], low_half)
        values = two_heads(qkv_ref[0, :, 2 * BLOCK + at : 2 * BLOCK + at + 128], low_half)
        grads = gatt[:, at : at + 128]
        both = dot(key_rows, queries, 1, 1)
        gboth = dot(values, grads, 1, 1)
        probs, gscores = [], []
        for head in range(2):
            rows = slice(length * head, length * (head + 1))
            scores = both[rows] - SLOPES[6 * side + 2 * pair + head] * far
            shifted = jnp.exp(scores - jnp.max(scores, axis=0, keepdims=True))
            share = shifted * (1.0 / jnp.sum(shifted, axis=0, keepdims=True))
            weighted = share * gboth[rows]
            probs.append(share.astype(BF))
            inner = jnp.sum(weighted, axis=0, keepdims=True)
            gscores.append((weighted - share * inner).astype(BF))
        probs, gscores = jnp.concatenate(probs, axis=0), jnp.concatenate(gscores, axis=0)
        gvalues = dot(probs, grads)
        gkeys = dot(gscores, queries)
        gqkv_ref[:, at : at + 128] = (dot(gscores, key_rows, 0, 0) * 0.125).astype(BF)
        for which, result in ((1, gkeys), (2, gvalues)):
            gqkv_ref[:, which * BLOCK + at : which * BLOCK + at + 128] = jnp.where(
                low_half, result[:length], result[length:]
            ).astype(BF)


def qkv_grad_kernel(
    place, h1_turned, gqkv_ref, wq_ref, att_ref, glow_ref, gh1_ref, sums_ref, keep_ref, send_ref, product
):
    part = pl.program_id(0)

    @pl.when(part < 3)
    def _():
        product[...] = dot(h1_turned[...], gqkv_ref[...])
        gradient = dot(gqkv_ref[...], wq_ref[0], 1, 1)
        gh1_ref[...] = jnp.where(part == 0, gradient, gh1_ref[...] + gradient)
        sums_ref[jnp.minimum(part, 2)] = stack_rows([None, None, sum_rows(gqkv_ref[...])])

    @pl.when(part >= 3)
    def _():
        product[...] = dot(att_ref[...], glow_ref[...], 0, 0)

    give_rows(place, SMALL, product, keep_ref, send_ref)


def input_kernel(
    place, h1_turned, gqkv_ref, wq_ref, before_ref, mlp_ref, fcg_ref, rows_ref, vec_ref, glow_ref, gh1,
    ginput_ref, keep_ref, upper_ref, lower_ref,
    product, sums, total, sems_in,
):
    part = pl.program_id(0)
    load = pltpu.make_async_copy(gh1, total, sems_in)

    @pl.when(part == 0)
    def _():
        load.start()

    product[...] = dot(h1_turned[...], gqkv_ref[...])
    gradient = dot(gqkv_ref[...], wq_ref[0], 1, 1)

    @pl.when(part == 0)
    def _():
        load.wait()

    total[...] += gradient
    sums[part] = stack_rows([None, None, sum_rows(gqkv_ref[...])])

    send_ref = upper_ref, lower_ref

    @pl.when(part < 2)
    def _():
        give_rows(place, SMALL, product, keep_ref, send_ref, lambda chip: mlp_ref[...] + fcg_ref[chip // 4])

    @pl.when(part == 2)
    def _():
        gradient = total[...]
        normed, scale = normed_rows(rows_ref[...].astype(F32))
        ginput_ref[...] = (
            glow_ref[...].astype(F32) + norm_back(gradient * row_of(vec_ref, 0), normed, scale)
        ).astype(BF)
        gain, shift = sum_rows(gradient * normed), sum_rows(gradient)

        def below(chip):
            lanes = slice(BLOCK * (chip // 8), BLOCK * (chip // 8 + 1))
            biases = (before_ref[0], sums[0], before_ref[2], sums[2])[chip // 4]
            return stack_rows([gain[:, lanes], shift[:, lanes]]) + biases

        give_rows(place, SMALL, product, keep_ref, send_ref, below)


def add_up(parts):
    return sum(part.astype(F32) for part in parts)


def give_vector(target, line, device):
    count, columns = target.shape[0], line.shape[1]
    start = lax.rem(device, columns // count) * count
    moved = pltpu.roll(line, lax.rem(columns - start, columns), 1)
    target[...] = moved[:, :count].reshape(count)


def last_kernel(place, *refs):
    sources, (qkv_out, out_out), smalls = refs[:12], refs[12:14], refs[14:]
    total_a = add_up([source[0] for source in sources[:6]])
    total_c = add_up([source[0] for source in sources[6:]])
    for part in range(3):
        lanes = slice(BLOCK * part, BLOCK * (part + 1))
        qkv_out[:, 2 * BLOCK * part : 2 * BLOCK * part + BLOCK] = total_a[:, lanes]
        qkv_out[:, 2 * BLOCK * part + BLOCK : 2 * BLOCK * (part + 1)] = total_c[:24, lanes]
    out_out[...] = total_a[:, 3 * BLOCK :]
    device = place[49]
    for line, target in enumerate(smalls[:3]):
        give_vector(target, total_c[24 + line : 25 + line, 2 * BLOCK :], device)
    for line, target in enumerate(smalls[3:]):
        give_vector(target, total_c[24 + line : 25 + line, : 2 * BLOCK], device)


def after(value, *others):
    return lax.optimization_barrier((value,) + others)[0]


class Links:
    def __init__(self, depth):
        self.depth = depth

        def table(move):
            pairs = []
            for z in range(depth):
                for x in range(2):
                    for y in range(2):
                        for c in range(2):
                            nz, nx, ny, nc = move(z, x, y, c)
                            source = (z * 2 + x) * 4 + y * 2 + c
                            pairs.append((source, ((nz % depth) * 2 + nx) * 4 + ny * 2 + nc))
            return pairs

        self.ups = {step: table(lambda z, x, y, c: (z + step, x, y, c)) for step in (1, 2, 3)}
        self.first = table(lambda z, x, y, c: (z, x, 1 - y, c) if c else (z, 1 - x, y, c))
        self.second = table(lambda z, x, y, c: (z, 1 - x, y, c) if c else (z, x, 1 - y, c))
        self.cores = table(lambda z, x, y, c: (z, x, y, 1 - c))
        self.near = table(lambda z, x, y, c: (z ^ 1, x, y, c))
        self.far = table(lambda z, x, y, c: (z ^ 2, x, y, c))

    def move(self, value, pairs):
        return lax.ppermute(value, AXES, pairs)

    def spots(self):
        dp, fsdp = lax.axis_index("dp"), lax.axis_index("fsdp")
        z, x, y, core = dp // 2, dp % 2, fsdp // 2, fsdp % 2

        def chip(c, flip1, flip2, step):
            flip_x = jnp.where(c == 0, flip1, flip2)
            flip_y = jnp.where(c == 0, flip2, flip1)
            return (((z - step) % self.depth) * 2 + (x ^ flip_x)) * 2 + (y ^ flip_y)

        index = jnp.arange(32, dtype=jnp.int32)
        whose = jnp.where(index < 16, core, 1 - core)
        flip2 = (index // 8) % 2
        z_first = chip(whose, (index // 4) % 2, flip2, index % 4)
        x_first = chip(whose, index % 2, (index // 2) % 2, (index // 4) % 4)
        chips = jnp.arange(16, dtype=jnp.int32)
        turn_x, turn_y = ((chips // 2) % 2) ^ x, (chips % 2) ^ y
        far_z = (chips // 4) ^ z
        near, wide_step = far_z % 2, far_z // 2

        def slots(order):
            turns = {"x": turn_x, "y": turn_y, "near": near, "far": wide_step}
            return sum(turns[name] * weight for name, weight in zip(order, (8, 4, 2, 1)))

        others = jnp.stack([core, dp * 4 + fsdp, z]).astype(jnp.int32)
        rest = jnp.concatenate([others, jnp.zeros((13,), jnp.int32)])
        tables = []
        for orders in (
            (("y", "x", "near", "far"), ("x", "y", "near", "far")),
            (("y", "near", "x", "far"), ("x", "near", "y", "far")),
        ):
            both = [slots(order) for order in orders]
            tables += [jnp.where(core == 0, both[0], both[1]), jnp.where(core == 0, both[1], both[0])]
        parts = [z_first, tables[0], rest, x_first] + tables[1:]
        return jnp.concatenate(parts).astype(jnp.int32)

    def gather(self, piece_a, piece_b1, piece_b2, early):
        hold = lax.optimization_barrier
        up = lambda value, step: self.move(value, self.ups[step])
        a_one, a_three, b1_two = hold((up(piece_a, 1), up(piece_a, 3), self.move(piece_b1, self.first)))
        b1_two = jnp.stack([piece_b1, b1_two])
        a_two, b1_four = hold((up(a_one, 1), self.move(b1_two, self.second)))
        a_four = jnp.stack([piece_a, a_one, a_two, a_three])
        b1_four = jnp.concatenate([b1_two, b1_four])
        piece_b2 = after(piece_b2, a_two)
        a_rest, b2_one, b2_three, early = hold(
            (self.move(a_four, self.first), up(piece_b2, 1), up(piece_b2, 3), early)
        )
        a_eight = jnp.concatenate([a_four, a_rest])
        a_other, b2_two, b1_one = hold((self.move(a_eight, self.second), up(b2_one, 1), up(b1_four, 1)))
        b2_four = jnp.stack([piece_b2, b2_one, b2_two, b2_three])
        a = self.finish(a_eight, a_other)
        return a, (b1_four, b1_one, up(b1_four, 3)), (b2_four, self.move(b2_four, self.first)), early

    def gather_on(self, b1, b2):
        b1_four, b1_one, b1_three = b1
        b1_two = self.move(b1_one, self.ups[1])
        b2_eight = jnp.concatenate(b2)
        b2_other = self.move(b2_eight, self.second)
        b1_mine = jnp.concatenate([b1_four, b1_one])
        return (b1_mine, b1_two, b1_three, self.move(b1_mine, self.cores)), (b2_eight, b2_other)

    def gather_end(self, b1, b2):
        mine, b1_two, b1_three, other = b1
        rest = jnp.concatenate([b1_two, b1_three])
        return (mine, rest, other, self.move(rest, self.cores)), self.finish(*b2)

    def finish(self, eight, rest):
        return (eight, rest, self.move(eight, self.cores), self.move(rest, self.cores))

    def fold(self, state):
        left = 32 >> (len(state) - 1)
        return add_up([part[left // 2 : left] for part in state]).astype(BF)

def full_pieces(full, blocks):
    split = full.reshape((CHIPS, 48) + full.shape[1:])
    split = split.transpose(3, 0, 2, 1, 4) if full.shape[1] == blocks else split.transpose(2, 0, 3, 1, 4)
    return split.reshape(2 * CHIPS, blocks * 48, BLOCK)


STILL = [
    16 * core + ((-step % 4) * 2 + (flip2 if core else flip1)) * 2 + (flip1 if core else flip2)
    for core in range(2)
    for flip2 in range(2)
    for flip1 in range(2)
    for step in range(4)
]


def eights(pieces, order=None):
    if order is not None:
        pieces = jnp.stack([pieces[index] for index in order])
    return tuple(pieces[8 * index : 8 * (index + 1)] for index in range(4))


def placed(vector, device, per_row):
    start = (device % per_row) * vector.shape[0]
    return lax.dynamic_update_slice(jnp.zeros((BLOCK,), vector.dtype), vector, (start,))


def shards(
    mesh_shape,
    patches,
    counts,
    positions,
    ln1_gain,
    ln1_bias,
    qkv_weight,
    qv_bias,
    out_weight,
    out_bias,
    ln2_gain,
    ln2_bias,
    fc1_weight,
    fc1_bias,
    fc2_weight,
    fc2_bias,
    cotangent,
):
    images, length, width = patches.shape
    padded = (length + 31) // 32 * 32
    rows = images * padded
    hidden_width = fc1_weight.shape[1]
    devices = mesh_shape["dp"] * mesh_shape["fsdp"]
    by_hand = devices == 2 * CHIPS and mesh_shape["fsdp"] == 4
    small_parts = (ln1_gain, ln1_bias, out_bias, ln2_gain, ln2_bias, fc2_bias, qv_bias, fc1_bias)

    smem = pl.BlockSpec(memory_space=pltpu.SMEM)
    vmem = pl.BlockSpec(memory_space=pltpu.VMEM)
    anywhere = pl.BlockSpec(memory_space=pltpu.HBM)
    struct = jax.ShapeDtypeStruct

    row_index = jnp.arange(padded, dtype=jnp.int32)
    is_live = row_index[None, :] < counts[:, None]
    pad_rows = ((0, 0), (0, padded - length), (0, 0))
    rows_in = jnp.pad(patches, pad_rows).reshape(rows, width)
    gout = jnp.where(is_live[:, :, None], jnp.pad(cotangent, pad_rows), 0).reshape(rows, width)
    spots = jnp.pad(positions, pad_rows[:2])
    grid_rows = (spots // SIDE).astype(F32)
    grid_cols = (spots % SIDE).astype(F32)
    row_delta = grid_rows[:, :, None] - grid_rows[:, None, :]
    col_delta = grid_cols[:, :, None] - grid_cols[:, None, :]
    distance = jnp.sqrt(row_delta * row_delta + col_delta * col_delta)
    far = jnp.where(is_live[:, None, :], distance, FAR)
    far_turned = jnp.where(is_live[:, :, None], distance, FAR)

    if by_hand:
        links = Links(mesh_shape["dp"] // 2)
        place = links.spots()
        core = place[48]
        share = struct((8, 24, BLOCK), BF)
        mine, theirs, lines = pl.pallas_call(
            share_kernel,
            out_shape=(share, share, struct((16, BLOCK), BF)),
            in_specs=[smem] + [vmem] * 11,
            out_specs=(vmem,) * 3,
            name="share",
        )(place, qkv_weight, out_weight, fc1_weight, *small_parts)
        got = links.move(theirs, links.cores)
        pieces = pl.pallas_call(
            pair_kernel,
            out_shape=tuple(struct((height, BLOCK), BF) for height in (160, 192, 240)),
            in_specs=[smem] + [vmem] * 4,
            out_specs=(vmem,) * 3,
            name="pair",
        )(place, mine, got, lines, fc2_weight)
    else:
        links = None
        place = jnp.concatenate(
            [
                jnp.array([chip % CHIPS for chip in STILL], jnp.int32),
                jnp.arange(16, dtype=jnp.int32),
                jnp.zeros((16,), jnp.int32),
                jnp.arange(80, dtype=jnp.int32) % 16,
            ]
        )
        whole = [lax.all_gather(part, AXES, axis=0, tiled=True) for part in small_parts]
        lines = []
        for part in whole:
            share = part.shape[0] // 32
            chunks = part.reshape(32, share)
            lines.append(
                jnp.stack([placed(chunks[index], index, BLOCK // share) for index in range(32)])
            )
        lines = jnp.concatenate([jnp.stack(lines, axis=1), jnp.zeros((32, 8, BLOCK), BF)], axis=1)
        lines = lines.reshape(CHIPS, 2, 16, BLOCK).transpose(1, 0, 2, 3).reshape(32, 16, BLOCK)
        whole_qkv = lax.all_gather(qkv_weight, AXES, axis=0, tiled=True)
        whole_out = lax.all_gather(out_weight, AXES, axis=0, tiled=True)
        whole_fc1 = lax.all_gather(fc1_weight, AXES, axis=0, tiled=True)
        whole_fc2 = lax.all_gather(fc2_weight, AXES, axis=0, tiled=True)
        split = whole_fc2.reshape(CHIPS, 2, 96, 2, BLOCK).transpose(1, 0, 3, 2, 4).reshape(32, 192, BLOCK)
        gathered_a = eights(
            jnp.concatenate([full_pieces(whole_qkv.reshape(width, 3, 2, BLOCK), 3), lines], axis=1), STILL
        )
        gathered_b1 = eights(full_pieces(whole_fc1.reshape(width, 2, 4, BLOCK), 4))
        split = whole_fc2.reshape(CHIPS, 2, 96, 2, BLOCK).transpose(1, 0, 3, 2, 4).reshape(32, 192, BLOCK)
        gathered_b2 = eights(
            jnp.concatenate([split, full_pieces(whole_out.reshape(width, 1, 2, BLOCK), 1)], axis=1), STILL
        )

    if by_hand:
        gathered_a, on_b1, on_b2, early = links.gather(*pieces, (rows_in, gout, far, far_turned))
        rows_in, gout, far, far_turned = early


    def call(kernel, operands, out_shape, out_specs, in_specs, flops, mib, vmem_mib, grid, scratch=(), name=None):
        return pl.pallas_call(
            kernel,
            grid=grid,
            out_shape=out_shape,
            in_specs=in_specs,
            out_specs=out_specs,
            scratch_shapes=list(scratch),
            compiler_params=pltpu.CompilerParams(vmem_limit_bytes=vmem_mib * MIB),
            cost_estimate=pl.CostEstimate(
                flops=1, bytes_accessed=1, transcendentals=0
            ),
            name=name,
        )(*operands)

    image_rows = lambda columns: pl.BlockSpec((padded, columns), lambda image: (image, 0))
    image_far = pl.BlockSpec((1, padded, padded), lambda image: (image, 0, 0))
    fixed = lambda *shape: pl.BlockSpec(shape, lambda step: (0,) * len(shape))
    step_rows = lambda columns: pl.BlockSpec((rows, columns), lambda step: (0, step))
    shares = lambda height, columns: struct((CHIPS, height, columns), BF)
    buffer, flag = pltpu.VMEM, pltpu.SemaphoreType.DMA
    low_rows, wide_rows = struct((rows, width), BF), struct((rows, width), F32)
    wide = 2 * BLOCK
    steps = hidden_width // wide
    third = 3 * BLOCK

    def join(value, *others):
        return after(value, *others) if by_hand else value

    vec, fcb, h1_turned, qkv, wq = call(
        qkv_kernel,
        (place, *gathered_a, rows_in),
        (
            struct((2, 16, BLOCK), F32), struct((steps, 1, wide), F32), struct((width, rows), BF),
            struct((2, rows, third), BF), struct((2, width, third), BF),
        ),
        (
            fixed(2, 16, BLOCK), fixed(steps, 1, wide), fixed(width, rows),
            pl.BlockSpec((1, rows, third), lambda step: (step, 0, 0)), anywhere,
        ),
        [smem] + [anywhere] * 4 + [fixed(rows, width)],
        2 * rows * width * 3 * width,
        14,
        30,
        grid=(2,),
        scratch=(
            buffer((2, width, third), BF), buffer((rows, width), BF), buffer((4, 16, BLOCK), F32),
            buffer((32, 16, BLOCK), BF), flag((4,)),
        ),
        name="qkv",
    )
    if by_hand:
        qkv, on_b1, on_b2 = lax.optimization_barrier((qkv, on_b1, on_b2))
        on_b1, on_b2 = links.gather_on(on_b1, on_b2)

    att = call(
        attention_kernel,
        (qkv, far),
        low_rows,
        image_rows(width),
        [pl.BlockSpec((2, padded, third), lambda image: (0, image, 0)), image_far],
        8 * rows * 256 * width,
        10,
        20,
        grid=(images,),
        name="attention",
    )
    if by_hand:
        att, on_b1, on_b2 = lax.optimization_barrier((att, on_b1, on_b2))
        gathered_b1, gathered_b2 = links.gather_end(on_b1, on_b2)

    step_shares = lambda height, columns: pl.BlockSpec((CHIPS, height, columns), lambda step: (0, 0, step))
    still = lambda *shape: pl.BlockSpec(shape, lambda step, place: (0,) * len(shape))
    turned_shares = pl.BlockSpec(
        (CHIPS, 24, wide), lambda step, place: (0, 0, lax.rem(place[50] + 4 - step, 4))
    )
    low_buffer, wide_buffer = buffer((rows, width), BF), buffer((rows, width), F32)
    out, glow, keep_1, send_1, sums, fcg, keep_2, upper_2, lower_2, wo = pl.pallas_call(
        mlp_kernel,
        grid_spec=pltpu.PrefetchScalarGridSpec(
            num_scalar_prefetch=1,
            grid=(steps,),
            in_specs=[smem] + [anywhere] * 11 + [still(2, 16, BLOCK), still(steps, 1, wide)],
            out_specs=(still(rows, width),) * 2
            + (turned_shares,) * 2
            + (still(8, wide), still(steps, 8, wide))
            + (anywhere,) * 4,
            scratch_shapes=[
                buffer((steps, width, wide), BF), buffer((hidden_width, width), BF), buffer((2, width, BLOCK), BF),
                low_buffer, low_buffer, low_buffer, low_buffer, buffer((width, rows), BF),
                wide_buffer, wide_buffer, wide_buffer, buffer((width, wide), F32), buffer((width, wide), F32),
                buffer((2, CHIPS, 96, wide), BF), buffer((rows, 128), F32), flag((steps,)), flag((steps,)), flag((7,)),
            ],
        ),
        out_shape=(low_rows, low_rows)
        + (shares(24, hidden_width),) * 2
        + (struct((8, wide), F32), struct((steps, 8, wide), F32))
        + (shares(96, wide),)
        + (struct((8, 96, wide), BF),) * 2
        + (struct((2, width, BLOCK), BF),),
        compiler_params=pltpu.CompilerParams(vmem_limit_bytes=60 * MIB),
        cost_estimate=pl.CostEstimate(flops=1, bytes_accessed=1, transcendentals=0),
        name="mlp",
    )(place, counts, *gathered_b1, *gathered_b2, att, rows_in, gout, vec, fcb)

    if by_hand:
        state_2 = keep_2, links.move(upper_2, links.cores)

    def attention_back(side, gradient):
        return call(
            lambda *refs: attention_back_kernel(side, *refs),
            (wo, qkv, far_turned, gradient),
            struct((rows, third), BF),
            image_rows(third),
            [
                fixed(2, width, BLOCK), pl.BlockSpec((1, padded, third), lambda image: (side, image, 0)),
                image_far, image_rows(width),
            ],
            8 * rows * 256 * width,
            8,
            20,
            grid=(images,),
            name="attention_back",
        )

    part_2 = glow
    if by_hand:
        part_2 = add_up([keep_2[8:], state_2[1]]).astype(BF)
        lower_2, send_1 = after((lower_2, send_1), part_2)
        state_2 = keep_2, links.move(lower_2, links.cores), links.move(part_2, links.second)
        state_1 = keep_1, links.move(send_1, links.cores)
    gqkv_0 = attention_back(0, join(glow, part_2))
    if by_hand:
        state_1, gqkv_0 = lax.optimization_barrier((state_1, gqkv_0))
        state_1 += (links.move(links.fold(state_1), links.second),)

    step_weight = lambda side: pl.BlockSpec((1, width, BLOCK), lambda step: (side, 0, jnp.minimum(step, 2)))
    early_rows = pl.BlockSpec((rows, BLOCK), lambda step: (0, jnp.minimum(step, 2)))
    late_rows = pl.BlockSpec((rows, BLOCK), lambda step: (0, jnp.maximum(step - 3, 0)))
    gh1, sums_0, keep_a, send_a = call(
        qkv_grad_kernel,
        (place, h1_turned, gqkv_0, wq, att, glow),
        (wide_rows, struct((3, 8, BLOCK), F32)) + (shares(24, third + wide),) * 2,
        (fixed(rows, width), fixed(3, 8, BLOCK)) + (step_shares(24, BLOCK),) * 2,
        [smem, fixed(width, rows), early_rows, step_weight(0), fixed(rows, width), late_rows],
        6 * rows * width * width,
        10,
        24,
        grid=(5,),
        scratch=(buffer((width, BLOCK), F32),),
        name="qkv_grad",
    )
    part_2 = gh1
    if by_hand:
        state_a = keep_a, links.move(send_a, links.cores)
        state_2, gh1 = lax.optimization_barrier((state_2, gh1))
        part_2 = links.fold(state_2)
        state_2 += (links.move(part_2, links.near),)

    gqkv_1 = attention_back(1, join(glow, gh1, part_2))
    if by_hand:
        state_a, gqkv_1 = lax.optimization_barrier((state_a, gqkv_1))
        state_a += (links.move(links.fold(state_a), links.second),)

    half_shares = pl.BlockSpec((8, 32, BLOCK), lambda step: (0, 0, step))
    mlp_small = pl.BlockSpec((8, BLOCK), lambda step: (0, jnp.minimum(step, 1)))
    ginput, keep_c, upper_c, lower_c = call(
        input_kernel,
        (place, h1_turned, gqkv_1, wq, sums_0, sums, fcg, rows_in, vec, glow, gh1),
        (low_rows, shares(32, third)) + (struct((8, 32, third), BF),) * 2,
        (fixed(rows, width), step_shares(32, BLOCK)) + (half_shares,) * 2,
        [
            smem, fixed(width, rows), step_rows(BLOCK), step_weight(1), fixed(3, 8, BLOCK), mlp_small,
            pl.BlockSpec((steps, 8, BLOCK), lambda step: (0, 0, jnp.minimum(step, 1))), fixed(rows, width),
            fixed(2, 16, BLOCK),
            fixed(rows, width), anywhere,
        ],
        6 * rows * width * width,
        14,
        30,
        grid=(3,),
        scratch=(
            buffer((width, BLOCK), F32), buffer((3, 8, BLOCK), F32), buffer((rows, width), F32), flag,
        ),
        name="input_grad",
    )
    def cut(value):
        return value.reshape(images, padded, width)[:, :length]

    if by_hand:
        fold, move = links.fold, links.move

        state_c = keep_c, move(upper_c, links.cores)
        rest_c = move(after(lower_c, keep_c), links.cores)
        state_1 = after(state_1, keep_c)
        part = fold(state_1)
        state_1 += (move(part, links.near),)
        keep_c, got_c = after(state_c, part)
        part = add_up([keep_c[8:], got_c]).astype(BF)
        state_c = keep_c, rest_c, move(part, links.second)
        state_2 = after(state_2, part)
        part = fold(state_2)
        state_2 += (move(part, links.first),)
        state_a, out, ginput = after((state_a, out, ginput), part)
        part = fold(state_a)
        state_a += (move(part, links.first),)
        out, ginput = cut(out), cut(ginput)
        part = fold(after(state_c, part))
        state_c += (move(part, links.first),)
        state_1, out, ginput = after((state_1, out, ginput), part)
        part = fold(state_1)
        state_1 += (move(part, links.first),)
        state_2 = after(state_2, part)
        part = fold(state_2)
        state_2 += (move(part, links.far),)
        state_a = after(state_a, part)
        part = fold(state_a)
        state_a += (move(part, links.near),)
        part = fold(after(state_c, part))
        state_c += (move(part, links.near),)
        state_1 = after(state_1, part)
        part = fold(state_1)
        state_1 += (move(part, links.far),)
        state_a = after(state_a, part)
        part = fold(state_a)
        state_a += (move(part, links.far),)
        part = fold(after(state_c, part))
        state_c += (move(part, links.far),)
        state_2 = after(state_2, part)
        mine_2 = add_up([part[0] for part in state_2])
        state_1 = after(state_1, mine_2)
        mine_1 = add_up([part[0] for part in state_1])
        own_slot = lambda part: pl.BlockSpec((1,) + part.shape[1:], lambda step: (0, 0, 0))
        heights, counts_out = ((24, 3 * width), (24, width)), (24, 24, 48, 24, 24, 24, 96, 24)
        (
            qkv_grad, out_grad, ln1_gain_grad, ln1_bias_grad, qv_bias_grad,
            ln2_gain_grad, ln2_bias_grad, fc2_bias_grad, fc1_bias_grad, out_bias_grad,
        ) = pl.pallas_call(
            last_kernel,
            grid=(1,),
            out_shape=tuple(struct(shape, F32) for shape in heights + tuple((count,) for count in counts_out)),
            in_specs=[smem] + [own_slot(part) for part in state_a + state_c],
            out_specs=tuple(fixed(*shape) for shape in heights)
            + tuple(pl.BlockSpec((count,), lambda step: (0,)) for count in counts_out),
            compiler_params=pltpu.CompilerParams(vmem_limit_bytes=30 * MIB),
            name="last",
        )(place, *state_a, *state_c)
        return (
            out, ginput, ln1_gain_grad, ln1_bias_grad, qkv_grad, qv_bias_grad, out_grad, out_bias_grad,
            ln2_gain_grad, ln2_bias_grad, mine_1, fc1_bias_grad, mine_2, fc2_bias_grad,
        )

    both_a, both_c, both_1, both_2 = (
        jnp.stack(pair, axis=1).astype(F32)
        for pair in (
            (keep_a, send_a),
            (keep_c, jnp.concatenate([lower_c, upper_c])),
            (keep_1, send_1),
            (keep_2, jnp.concatenate([lower_2, upper_2])),
        )
    )
    heads = jnp.stack(
        [both.reshape(CHIPS, 2, 24, 3, BLOCK) for both in (both_a[..., :third], both_c[:, :, :24])], axis=4
    )

    def vector(lines, count):
        columns = lines.shape[-1]
        return lines.reshape(32 * count // columns, -1, columns)[:, 0].reshape(-1)

    small_c, small_2 = both_c[:, :, 24:, 2 * BLOCK :], both_c[:, :, 24:, : 2 * BLOCK]
    totals = (
        vector(small_c[:, :, 0], 24),
        vector(small_c[:, :, 1], 24),
        heads.reshape(width, 3 * width),
        vector(small_c[:, :, 2], 48),
        both_a[..., third:].reshape(width, width),
        vector(small_2[:, :, 4], 24),
        vector(small_2[:, :, 0], 24),
        vector(small_2[:, :, 1], 24),
        both_1.reshape(width, hidden_width),
        vector(small_2[:, :, 3], 96),
        both_2.reshape(hidden_width, width),
        vector(small_2[:, :, 2], 24),
    )
    return (cut(out), cut(ginput)) + tuple(
        lax.psum_scatter(total, AXES, scatter_dimension=0, tiled=True) for total in totals
    )


def solution(mesh):
    rows = P(AXES, None, None)
    table = P(AXES, None)
    line = P(AXES)
    in_specs = (
        rows, line, table, line, line, table, line, table, line, line, line, table, line, table, line, rows,
    )
    out_specs = (
        rows, rows, line, line, table, line, table, line, line, line, table, line, table, line,
    )
    mesh_shape = dict(mesh.shape)

    def body(*arrays):
        return shards(mesh_shape, *arrays)

    return jax.shard_map(body, mesh=mesh, in_specs=in_specs, out_specs=out_specs, check_vma=False)
```

```python
import math

import jax
import jax.numpy as jnp
import numpy as np
from jax import lax
from jax.experimental import pallas as pl
from jax.experimental.pallas import tpu as pltpu
from jax.sharding import PartitionSpec as P

HEADS = 12
SIDE = 16
EPSILON = 1e-06
AXES = ("dp", "fsdp")
FAR = 1e30
CHIPS = 16
BLOCK = 384
SMALL, LARGE = (32, 96), (112, 128)
MIB = 1024 * 1024

BF = jnp.bfloat16
F32 = jnp.float32


def power_slopes(number):
    first_slope = 2.0 ** (-8.0 / number)
    return [first_slope ** (index + 1) for index in range(number)]


def slope_list(heads_total):
    lower_power = 2 ** int(math.floor(math.log2(heads_total)))
    return (
        power_slopes(lower_power) + power_slopes(2 * lower_power)[0::2][: heads_total - lower_power]
    )


SLOPES = [float(np.float32(slope)) for slope in slope_list(HEADS)]


def dot(left, right, left_dim=1, right_dim=0):
    return lax.dot_general(
        left, right, (((left_dim,), (right_dim,)), ((), ())), preferred_element_type=F32
    )


def normed_rows(values):
    centered = values - jnp.mean(values, axis=-1, keepdims=True)
    scale = lax.rsqrt(jnp.mean(centered * centered, axis=-1, keepdims=True) + EPSILON)
    return centered * scale, scale


def norm_back(grad_normed, normed, scale):
    centered_mean = jnp.mean(grad_normed, axis=-1, keepdims=True)
    projected_mean = jnp.mean(grad_normed * normed, axis=-1, keepdims=True)
    return scale * (grad_normed - centered_mean - normed * projected_mean)


def row_of(vectors_ref, index):
    return jnp.concatenate(
        [vectors_ref[0, index : index + 1, :], vectors_ref[1, index : index + 1, :]], axis=1
    )


def gelu_parts(hidden):
    cumulative = 0.5 + 0.5 * lax.erf(hidden * math.sqrt(0.5))
    bell = jnp.exp(-0.5 * hidden * hidden)
    return cumulative, cumulative + hidden * bell * (1.0 / math.sqrt(2.0 * math.pi))


def share_kernel(place, qkv_ref, out_ref, fc1_ref, *refs):
    smalls, (mine_ref, theirs_ref, lines_ref) = refs[:-3], refs[-3:]
    for target, core in ((mine_ref, place[48]), (theirs_ref, 1 - place[48])):
        starts = [(qkv_ref, 2 * BLOCK * part + BLOCK * core) for part in range(3)]
        starts.append((out_ref, BLOCK * core))
        starts += [(fc1_ref, 4 * BLOCK * core + BLOCK * part) for part in range(4)]
        for block, (source, start) in enumerate(starts):
            target[block] = source[:, pl.ds(pl.multiple_of(start, 128), BLOCK)]
    device = place[49]
    lines = []
    for small in smalls:
        count = small.shape[0]
        line = small[...].astype(F32).reshape(1, count)
        line = jnp.concatenate([line, jnp.zeros((1, BLOCK - count), F32)], axis=1)
        lines.append(pltpu.roll(line, lax.rem(device, BLOCK // count) * count, 1))
    lines_ref[...] = jnp.concatenate(lines + [jnp.zeros((8, BLOCK), F32)], axis=0).astype(BF)


def pair_kernel(place, mine_ref, got_ref, lines_ref, fc2_ref, a_ref, b1_ref, b2_ref):
    swap = place[48] == 1
    for block in range(8):
        mine, got = mine_ref[block].astype(F32), got_ref[block].astype(F32)
        rows = jnp.concatenate([jnp.where(swap, got, mine), jnp.where(swap, mine, got)], axis=0)
        if block < 3:
            a_ref[48 * block : 48 * (block + 1), :] = rows.astype(BF)
        elif block == 3:
            b2_ref[192:240, :] = rows.astype(BF)
        else:
            b1_ref[48 * (block - 4) : 48 * (block - 3), :] = rows.astype(BF)
    b2_ref[0:96, :] = fc2_ref[:, :BLOCK]
    b2_ref[96:192, :] = fc2_ref[:, BLOCK:]
    a_ref[144:160, :] = lines_ref[...]


def each_piece(place, table, sources, work):
    core = place[48]
    for number, source in enumerate(sources):
        half = core if number < 2 else 1 - core

        def bring(index, _, source=source, number=number, half=half):
            work(source, index, place[table + number * 8 + index], half)
            return 0

        lax.fori_loop(0, 8, bring, 0)


def bring_out_weight(place, sources, wo, sem):
    def work(source, index, chip, half):
        spot = pl.ds(pl.multiple_of(chip * 48, 16), 48)
        pltpu.make_async_copy(source.at[index, pl.ds(192, 48)], wo.at[half, spot], sem).start()

    each_piece(place, 0, sources, work)


def bring_qkv_weight(place, sources, side, wq, sem, part_of=None):
    for first, here in ((0, place[48] == side), (2, place[48] != side)):

        @pl.when(here)
        def _(first=first):
            for number in (first, first + 1):

                def bring(index, _, source=sources[number], number=number):
                    spot = pl.ds(pl.multiple_of(place[number * 8 + index] * 48, 16), 48)
                    for part in range(3):
                        pltpu.make_async_copy(
                            source.at[index, pl.ds(48 * part, 48)],
                            wq.at[spot, pl.ds(BLOCK * part, BLOCK)] if part_of is None else wq.at[part, spot],
                            sem if part_of is None else part_of.at[part],
                        ).start()
                    return 0

                lax.fori_loop(0, 8, bring, 0)


def wait_all(buffer, sem):
    pltpu.make_async_copy(buffer, buffer, sem).wait()


def qkv_kernel(
    place, own0, own1, other0, other1, rows_ref,
    vec_ref, fcb_ref, h1_turned, qkv_ref, wq_out0, wq_out1,
    wq, h1, qvb, small, sems,
):
    sources = (own0, own1, other0, other1)
    side = pl.program_id(0)

    @pl.when(side == 0)
    def _():
        def work(source, index, chip, half):
            pltpu.make_async_copy(
                source.at[index, pl.ds(144, 16)], small.at[2 * chip + half], sems.at[2]
            ).start()

        each_piece(place, 0, sources, work)
        for half in range(2):
            bring_qkv_weight(place, sources, half, wq.at[half], sems.at[half])
        normed, _ = normed_rows(rows_ref[...].astype(F32))
        wait_all(small, sems.at[2])
        spread = small[...].astype(F32)
        vec_ref[...] = jnp.sum(spread.reshape(2, 16, 16, BLOCK), axis=1)
        qvb[...] = jnp.sum(spread.reshape(4, 8, 16, BLOCK), axis=1)
        lines = jnp.sum(spread.reshape(8, 4, 16, BLOCK), axis=1)
        for block in range(4):
            fcb_ref[block] = jnp.concatenate([lines[2 * block, 7:8], lines[2 * block + 1, 7:8]], axis=1)
        low = (normed * row_of(vec_ref, 0) + row_of(vec_ref, 1)).astype(BF)
        h1[...] = low
        h1_turned[...] = low.T

    wait_all(wq.at[side], sems.at[side])
    for half, target in enumerate((wq_out0, wq_out1)):

        @pl.when(side == half)
        def _(half=half, target=target):
            pltpu.make_async_copy(wq.at[half], target, sems.at[3]).start()

    bias = jnp.concatenate(
        [qvb[side, 6:7, :], jnp.zeros((1, BLOCK), F32), qvb[2 + side, 6:7, :]], axis=1
    )
    qkv_ref[0] = (dot(h1[...], wq[side]) + bias).astype(BF)
    wait_all(wq_out0, sems.at[3])


def two_heads(pair_rows, low_half):
    nothing = jnp.zeros_like(pair_rows)
    return jnp.concatenate(
        [jnp.where(low_half, pair_rows, nothing), jnp.where(low_half, nothing, pair_rows)], axis=0
    )


def attention_kernel(qkv_ref, far_ref, att_ref):
    length = att_ref.shape[0]
    low_half = lax.broadcasted_iota(jnp.int32, (length, 128), 1) < 64
    far = far_ref[0]
    for pair in range(HEADS // 2):
        side, at = pair // 3, 128 * (pair % 3)
        queries = two_heads(qkv_ref[side, :, at : at + 128] * jnp.asarray(0.125, BF), low_half)
        key_rows = qkv_ref[side, :, BLOCK + at : BLOCK + at + 128]
        values = qkv_ref[side, :, 2 * BLOCK + at : 2 * BLOCK + at + 128]
        both = dot(queries, key_rows, 1, 1)
        probs = []
        for head in range(2):
            scores = both[length * head : length * (head + 1)] - SLOPES[2 * pair + head] * far
            shifted = jnp.exp(scores - jnp.max(scores, axis=-1, keepdims=True))
            share = shifted * (1.0 / jnp.sum(shifted, axis=-1, keepdims=True))
            probs.append(share.astype(BF))
        result = dot(jnp.concatenate(probs, axis=0), values)
        att_ref[:, 128 * pair : 128 * (pair + 1)] = jnp.where(
            low_half, result[:length], result[length:]
        ).astype(BF)


def at_slot(target, slot, work):
    if not isinstance(target, tuple):
        work(target, slot)
        return

    @pl.when(slot >= 8)
    def _():
        work(target[0], slot - 8)

    @pl.when(slot < 8)
    def _():
        work(target[1], slot)


def give_rows(place, tables, total, keep_ref, send_ref, extra=None, lanes=slice(None)):
    for chip in range(CHIPS):
        below = None if extra is None else extra(chip)
        for which, target in enumerate((keep_ref, send_ref)):
            owner = place[48] if which == 0 else 1 - place[48]
            share = total[pl.ds(pl.multiple_of(48 * chip + 24 * owner, 8), 24), :]
            if below is not None:
                share = jnp.concatenate([share, below], axis=0)

            def put(ref, slot, share=share):
                ref[slot, :, lanes] = share.astype(BF)

            at_slot(target, place[tables[which] + chip], put)


def stack_rows(rows):
    blank = jnp.zeros_like(next(row for row in rows if row is not None))
    rows = [blank if row is None else row for row in rows]
    return jnp.concatenate(rows + [blank] * (8 - len(rows)), axis=0)


def sum_rows(values):
    return jnp.sum(values.astype(F32), axis=0, keepdims=True)


def mlp_kernel(
    place, counts, a0, a1, a2, a3, b0, b1, b2, b3, att_far, rows_far, gout_far, vec_ref, fcb_ref,
    out_ref, glow_ref, keep1_ref, send1_ref, sums_ref, fcg, keep2, upper2, lower2, wo_out,
    w1, w2, wo, att_ref, rows_ref, gout_ref, h2, h2_turned, normed, total, gh2, product1, product2,
    stage, scales, sems1, sems2, sems,
):
    step = pl.program_id(0)
    wide = 2 * BLOCK
    core, z = place[48], place[50]
    block_of = lambda step: lax.rem(z + 4 - step, 4)
    block = block_of(step)
    gain = row_of(vec_ref, 3)
    loads = [
        pltpu.make_async_copy(source, target, sems.at[3 + index])
        for index, (source, target) in enumerate(
            ((att_far, att_ref), (rows_far, rows_ref), (gout_far, gout_ref))
        )
    ]

    @pl.when(step == 0)
    def _():
        bring_out_weight(place, (b0, b1, b2, b3), wo, sems.at[2])
        loads[0].start()
        loads[1].start()
        for later in range(4):
            column = block_of(later)
            for first, here in ((0, column // 2 == core), (2, column // 2 != core)):

                @pl.when(here)
                def _(first=first, column=column):
                    for number in (first, first + 1):

                        def bring(index, _, source=(a0, a1, a2, a3)[number], number=number, column=column):
                            spot = pl.ds(pl.multiple_of(place[64 + number * 8 + index] * 48, 16), 48)
                            for part in range(2):
                                start = pl.multiple_of(lax.rem(column, 2) * 96 + 48 * part, 16)
                                pltpu.make_async_copy(
                                    source.at[index, pl.ds(start, 48)],
                                    w1.at[column, spot, pl.ds(BLOCK * part, BLOCK)],
                                    sems1.at[column],
                                ).start()
                            return 0

                        lax.fori_loop(0, 8, bring, 0)

            if later == 0:
                loads[2].start()
            for number, source in enumerate((b0, b1, b2, b3)):
                half = core if number < 2 else 1 - core
                for index in (later, 4 + later):
                    chip = place[number * 8 + index]
                    spot = pl.ds(pl.multiple_of(chip * 192 + half * 96, 16), 96)
                    for part in range(2):
                        pltpu.make_async_copy(
                            source.at[index, pl.ds(96 * part, 96)],
                            w2.at[spot, pl.ds(BLOCK * part, BLOCK)],
                            sems2.at[column],
                        ).start()

        wait_all(wo, sems.at[2])
        pltpu.make_async_copy(wo, wo_out, sems.at[2]).start()
        bias = row_of(vec_ref, 2)
        loads[0].wait()
        loads[1].wait()
        for part in range(2):
            lanes = slice(BLOCK * part, BLOCK * (part + 1))
            total[:, lanes] = rows_ref[:, lanes].astype(F32) + dot(att_ref[...], wo[part]) + bias[:, lanes]
        normal, scale = normed_rows(total[...])
        normed[...] = normal
        scales[...] = jnp.broadcast_to(scale, scales.shape)
        low = (normal * gain + row_of(vec_ref, 4)).astype(BF)
        h2[...] = low
        h2_turned[...] = low.T
        total[...] += row_of(vec_ref, 5)
        gh2[...] = jnp.zeros_like(gh2)
        loads[2].wait()

    wait_all(w1.at[block], sems1.at[block])
    hidden = dot(h2[...], w1[block]) + fcb_ref[block]
    rows_of = pl.ds(pl.multiple_of(block * wide, wide), wide)
    wait_all(w2.at[rows_of], sems2.at[block])
    gactivated = dot(gout_ref[...], w2[rows_of, :], 1, 1)
    cumulative, slope = gelu_parts(hidden)
    activated = (hidden * cumulative).astype(BF)
    ghidden = (gactivated * slope).astype(BF)
    product1[...] = dot(h2_turned[...], ghidden)
    product2[...] = dot(activated, gout_ref[...], 0, 0)
    total[...] += dot(activated, w2[rows_of, :])
    gh2[...] += dot(ghidden, w1[block], 1, 1)
    fcg[block] = stack_rows([None, None, None, sum_rows(ghidden)])
    give_rows(place, LARGE, product1, keep1_ref, send1_ref)
    for pair in range(4):
        chip = 4 * block + pair
        for which, target in enumerate((keep2, (upper2, lower2))):
            owner = place[48] if which == 0 else 1 - place[48]
            start = pl.multiple_of(192 * pair + 96 * owner, 8)
            stage[which, chip] = product2[pl.ds(start, 96), :].astype(BF)

            def send(ref, slot, which=which, chip=chip):
                sem = sems.at[1 if ref is upper2 else 6 if ref is lower2 else 0]
                pltpu.make_async_copy(stage.at[which, chip], ref.at[slot], sem).start()

            at_slot(target, place[LARGE[which] + chip], send)

    @pl.when(step == pl.num_programs(0) - 1)
    def _():
        length = out_ref.shape[0] // 4
        row_index = lax.broadcasted_iota(jnp.int32, (length, 1), 0)
        for image in range(4):
            rows = slice(length * image, length * (image + 1))
            value = total[rows, :]
            out_ref[rows, :] = jnp.where(row_index < counts[image], value, 0.0).astype(BF)
        whole = gh2[...]
        gout = gout_ref[...].astype(F32)
        gresid = gout + norm_back(whole * gain, normed[...], scales[:, 0:1])
        low = gresid.astype(BF)
        glow_ref[...] = low
        sums_ref[...] = stack_rows(
            [sum_rows(whole * normed[...]), sum_rows(whole), sum_rows(gout), None, sum_rows(low)]
        )
        wait_all(wo, sems.at[2])
        wait_all(keep2, sems.at[0])
        wait_all(upper2, sems.at[1])
        wait_all(lower2, sems.at[6])


def attention_back_kernel(side, wo, qkv_ref, far_ref, glow_ref, gqkv_ref):
    low = glow_ref[...]
    mine = slice(BLOCK * side, BLOCK * (side + 1))
    gatt = (
        dot(low[:, :BLOCK], wo[0, mine, :], 1, 1) + dot(low[:, BLOCK:], wo[1, mine, :], 1, 1)
    ).astype(BF)
    length = low.shape[0]
    low_half = lax.broadcasted_iota(jnp.int32, (length, 128), 1) < 64
    far = far_ref[0]
    for pair in range(3):
        at = 128 * pair
        queries = qkv_ref[0, :, at : at + 128] * jnp.asarray(0.125, BF)
        key_rows = two_heads(qkv_ref[0, :, BLOCK + at : BLOCK + at + 128], low_half)
        values = two_heads(qkv_ref[0, :, 2 * BLOCK + at : 2 * BLOCK + at + 128], low_half)
        grads = gatt[:, at : at + 128]
        both = dot(key_rows, queries, 1, 1)
        gboth = dot(values, grads, 1, 1)
        probs, gscores = [], []
        for head in range(2):
            rows = slice(length * head, length * (head + 1))
            scores = both[rows] - SLOPES[6 * side + 2 * pair + head] * far
            shifted = jnp.exp(scores - jnp.max(scores, axis=0, keepdims=True))
            share = shifted * (1.0 / jnp.sum(shifted, axis=0, keepdims=True))
            weighted = share * gboth[rows]
            probs.append(share.astype(BF))
            inner = jnp.sum(weighted, axis=0, keepdims=True)
            gscores.append((weighted - share * inner).astype(BF))
        probs, gscores = jnp.concatenate(probs, axis=0), jnp.concatenate(gscores, axis=0)
        gvalues = dot(probs, grads)
        gkeys = dot(gscores, queries)
        gqkv_ref[:, at : at + 128] = (dot(gscores, key_rows, 0, 0) * 0.125).astype(BF)
        for which, result in ((1, gkeys), (2, gvalues)):
            gqkv_ref[:, which * BLOCK + at : which * BLOCK + at + 128] = jnp.where(
                low_half, result[:length], result[length:]
            ).astype(BF)


def qkv_grad_kernel(
    place, h1_turned, gqkv_ref, wq_ref, att_ref, glow_ref, gh1_ref, sums_ref, keep_ref, upper_ref, lower_ref,
    product, product_out,
):
    third, wide = gqkv_ref.shape[1], glow_ref.shape[1]
    product[...] = dot(h1_turned[...], gqkv_ref[...])
    product_out[...] = dot(att_ref[...], glow_ref[...], 0, 0)
    gh1_ref[...] = dot(gqkv_ref[...], wq_ref[...], 1, 1)
    sums_ref[...] = sum_rows(gqkv_ref[...])
    send = upper_ref, lower_ref
    give_rows(place, SMALL, product, keep_ref, send, lanes=slice(0, third))
    give_rows(place, SMALL, product_out, keep_ref, send, lanes=slice(third, third + wide))


def input_kernel(
    place, h1_turned, gqkv_ref, wq_ref, before_ref, mlp_ref, fcg_ref, rows_ref, vec_ref, glow_ref, gh1_ref,
    ginput_ref, keep_ref, upper_ref, lower_ref, product,
):
    product[...] = dot(h1_turned[...], gqkv_ref[...])
    sums = sum_rows(gqkv_ref[...])
    gradient = gh1_ref[...] + dot(gqkv_ref[...], wq_ref[...], 1, 1)
    normed, scale = normed_rows(rows_ref[...].astype(F32))
    ginput_ref[...] = (
        glow_ref[...].astype(F32) + norm_back(gradient * row_of(vec_ref, 0), normed, scale)
    ).astype(BF)
    gain, shift = sum_rows(gradient * normed), sum_rows(gradient)
    first, last = slice(0, BLOCK), slice(2 * BLOCK, 3 * BLOCK)
    biases = before_ref[:, first], sums[:, first], before_ref[:, last], sums[:, last]

    def below(chip):
        lanes = slice(BLOCK * (chip // 8), BLOCK * (chip // 8 + 1))
        own = stack_rows([gain[:, lanes], shift[:, lanes], biases[chip // 4]])
        return jnp.concatenate([mlp_ref[...] + fcg_ref[chip // 4], own], axis=1)

    give_rows(place, SMALL, product, keep_ref, (upper_ref, lower_ref), below)


def add_up(parts):
    return sum(part.astype(F32) for part in parts)


def give_vector(target, line, device):
    count, columns = target.shape[0], line.shape[1]
    start = lax.rem(device, columns // count) * count
    moved = pltpu.roll(line, lax.rem(columns - start, columns), 1)
    target[...] = moved[:, :count].reshape(count)


def last_kernel(place, *refs):
    sources, (qkv_out, out_out), smalls = refs[:12], refs[12:14], refs[14:]
    total_a = add_up([source[0] for source in sources[:6]])
    total_c = add_up([source[0] for source in sources[6:]])
    for part in range(3):
        lanes = slice(BLOCK * part, BLOCK * (part + 1))
        qkv_out[:, 2 * BLOCK * part : 2 * BLOCK * part + BLOCK] = total_a[:, lanes]
        qkv_out[:, 2 * BLOCK * part + BLOCK : 2 * BLOCK * (part + 1)] = total_c[:24, lanes]
    out_out[...] = total_a[:, 3 * BLOCK :]
    device = place[49]
    for line, target in enumerate(smalls[:3]):
        give_vector(target, total_c[24 + line : 25 + line, 2 * BLOCK :], device)
    for line, target in enumerate(smalls[3:]):
        give_vector(target, total_c[24 + line : 25 + line, : 2 * BLOCK], device)


def after(value, *others):
    return lax.optimization_barrier((value,) + others)[0]


class Links:
    def __init__(self, depth):
        self.depth = depth

        def table(move):
            pairs = []
            for z in range(depth):
                for x in range(2):
                    for y in range(2):
                        for c in range(2):
                            nz, nx, ny, nc = move(z, x, y, c)
                            source = (z * 2 + x) * 4 + y * 2 + c
                            pairs.append((source, ((nz % depth) * 2 + nx) * 4 + ny * 2 + nc))
            return pairs

        self.ups = {step: table(lambda z, x, y, c: (z + step, x, y, c)) for step in (1, 2, 3)}
        self.first = table(lambda z, x, y, c: (z, x, 1 - y, c) if c else (z, 1 - x, y, c))
        self.second = table(lambda z, x, y, c: (z, 1 - x, y, c) if c else (z, x, 1 - y, c))
        self.cores = table(lambda z, x, y, c: (z, x, y, 1 - c))
        self.near = table(lambda z, x, y, c: (z ^ 1, x, y, c))
        self.far = table(lambda z, x, y, c: (z ^ 2, x, y, c))

    def move(self, value, pairs):
        return lax.ppermute(value, AXES, pairs)

    def spots(self):
        dp, fsdp = lax.axis_index("dp"), lax.axis_index("fsdp")
        z, x, y, core = dp // 2, dp % 2, fsdp // 2, fsdp % 2

        def chip(c, flip1, flip2, step):
            flip_x = jnp.where(c == 0, flip1, flip2)
            flip_y = jnp.where(c == 0, flip2, flip1)
            return (((z - step) % self.depth) * 2 + (x ^ flip_x)) * 2 + (y ^ flip_y)

        index = jnp.arange(32, dtype=jnp.int32)
        whose = jnp.where(index < 16, core, 1 - core)
        flip2 = (index // 8) % 2
        z_first = chip(whose, (index // 4) % 2, flip2, index % 4)
        x_first = chip(whose, index % 2, (index // 2) % 2, (index // 4) % 4)
        chips = jnp.arange(16, dtype=jnp.int32)
        turn_x, turn_y = ((chips // 2) % 2) ^ x, (chips % 2) ^ y
        far_z = (chips // 4) ^ z
        near, wide_step = far_z % 2, far_z // 2

        def slots(order):
            turns = {"x": turn_x, "y": turn_y, "near": near, "far": wide_step}
            return sum(turns[name] * weight for name, weight in zip(order, (8, 4, 2, 1)))

        others = jnp.stack([core, dp * 4 + fsdp, z]).astype(jnp.int32)
        rest = jnp.concatenate([others, jnp.zeros((13,), jnp.int32)])
        tables = []
        for orders in (
            (("y", "x", "near", "far"), ("x", "y", "near", "far")),
            (("y", "near", "x", "far"), ("x", "near", "y", "far")),
        ):
            both = [slots(order) for order in orders]
            tables += [jnp.where(core == 0, both[0], both[1]), jnp.where(core == 0, both[1], both[0])]
        parts = [z_first, tables[0], rest, x_first] + tables[1:]
        return jnp.concatenate(parts).astype(jnp.int32)

    def gather(self, piece_a, piece_b1, piece_b2, early):
        hold = lax.optimization_barrier
        up = lambda value, step: self.move(value, self.ups[step])
        a_one, a_three, b1_two = hold((up(piece_a, 1), up(piece_a, 3), self.move(piece_b1, self.first)))
        b1_two = jnp.stack([piece_b1, b1_two])
        a_two, b1_four = hold((up(a_one, 1), self.move(b1_two, self.second)))
        a_four = jnp.stack([piece_a, a_one, a_two, a_three])
        b1_four = jnp.concatenate([b1_two, b1_four])
        piece_b2 = after(piece_b2, a_two)
        a_rest, b2_one, b2_three, early = hold(
            (self.move(a_four, self.first), up(piece_b2, 1), up(piece_b2, 3), early)
        )
        a_eight = jnp.concatenate([a_four, a_rest])
        a_other, b2_two, b1_one = hold((self.move(a_eight, self.second), up(b2_one, 1), up(b1_four, 1)))
        b2_four = jnp.stack([piece_b2, b2_one, b2_two, b2_three])
        a = self.finish(a_eight, a_other)
        return a, (b1_four, b1_one, up(b1_four, 3)), (b2_four, self.move(b2_four, self.first)), early

    def gather_on(self, b1, b2):
        b1_four, b1_one, b1_three = b1
        b1_two = self.move(b1_one, self.ups[1])
        b2_eight = jnp.concatenate(b2)
        b2_other = self.move(b2_eight, self.second)
        b1_mine = jnp.concatenate([b1_four, b1_one])
        return (b1_mine, b1_two, b1_three, self.move(b1_mine, self.cores)), (b2_eight, b2_other)

    def gather_end(self, b1, b2):
        mine, b1_two, b1_three, other = b1
        rest = jnp.concatenate([b1_two, b1_three])
        return (mine, rest, other, self.move(rest, self.cores)), self.finish(*b2)

    def finish(self, eight, rest):
        return (eight, rest, self.move(eight, self.cores), self.move(rest, self.cores))

    def fold(self, state):
        left = 32 >> (len(state) - 1)
        return add_up([part[left // 2 : left] for part in state]).astype(BF)

def full_pieces(full, blocks):
    split = full.reshape((CHIPS, 48) + full.shape[1:])
    split = split.transpose(3, 0, 2, 1, 4) if full.shape[1] == blocks else split.transpose(2, 0, 3, 1, 4)
    return split.reshape(2 * CHIPS, blocks * 48, BLOCK)


STILL = [
    16 * core + ((-step % 4) * 2 + (flip2 if core else flip1)) * 2 + (flip1 if core else flip2)
    for core in range(2)
    for flip2 in range(2)
    for flip1 in range(2)
    for step in range(4)
]


def eights(pieces, order=None):
    if order is not None:
        pieces = jnp.stack([pieces[index] for index in order])
    return tuple(pieces[8 * index : 8 * (index + 1)] for index in range(4))


def placed(vector, device, per_row):
    start = (device % per_row) * vector.shape[0]
    return lax.dynamic_update_slice(jnp.zeros((BLOCK,), vector.dtype), vector, (start,))


def shards(
    mesh_shape,
    patches,
    counts,
    positions,
    ln1_gain,
    ln1_bias,
    qkv_weight,
    qv_bias,
    out_weight,
    out_bias,
    ln2_gain,
    ln2_bias,
    fc1_weight,
    fc1_bias,
    fc2_weight,
    fc2_bias,
    cotangent,
):
    images, length, width = patches.shape
    padded = (length + 31) // 32 * 32
    rows = images * padded
    hidden_width = fc1_weight.shape[1]
    devices = mesh_shape["dp"] * mesh_shape["fsdp"]
    by_hand = devices == 2 * CHIPS and mesh_shape["fsdp"] == 4
    small_parts = (ln1_gain, ln1_bias, out_bias, ln2_gain, ln2_bias, fc2_bias, qv_bias, fc1_bias)

    smem = pl.BlockSpec(memory_space=pltpu.SMEM)
    vmem = pl.BlockSpec(memory_space=pltpu.VMEM)
    anywhere = pl.BlockSpec(memory_space=pltpu.HBM)
    struct = jax.ShapeDtypeStruct

    row_index = jnp.arange(padded, dtype=jnp.int32)
    is_live = row_index[None, :] < counts[:, None]
    pad_rows = ((0, 0), (0, padded - length), (0, 0))
    rows_in = jnp.pad(patches, pad_rows).reshape(rows, width)
    gout = jnp.where(is_live[:, :, None], jnp.pad(cotangent, pad_rows), 0).reshape(rows, width)
    spots = jnp.pad(positions, pad_rows[:2])
    grid_rows = (spots // SIDE).astype(F32)
    grid_cols = (spots % SIDE).astype(F32)
    row_delta = grid_rows[:, :, None] - grid_rows[:, None, :]
    col_delta = grid_cols[:, :, None] - grid_cols[:, None, :]
    distance = jnp.sqrt(row_delta * row_delta + col_delta * col_delta)
    far = jnp.where(is_live[:, None, :], distance, FAR)
    far_turned = jnp.where(is_live[:, :, None], distance, FAR)

    if by_hand:
        links = Links(mesh_shape["dp"] // 2)
        place = links.spots()
        core = place[48]
        share = struct((8, 24, BLOCK), BF)
        mine, theirs, lines = pl.pallas_call(
            share_kernel,
            out_shape=(share, share, struct((16, BLOCK), BF)),
            in_specs=[smem] + [vmem] * 11,
            out_specs=(vmem,) * 3,
            name="share",
        )(place, qkv_weight, out_weight, fc1_weight, *small_parts)
        got = links.move(theirs, links.cores)
        pieces = pl.pallas_call(
            pair_kernel,
            out_shape=tuple(struct((height, BLOCK), BF) for height in (160, 192, 240)),
            in_specs=[smem] + [vmem] * 4,
            out_specs=(vmem,) * 3,
            name="pair",
        )(place, mine, got, lines, fc2_weight)
    else:
        links = None
        place = jnp.concatenate(
            [
                jnp.array([chip % CHIPS for chip in STILL], jnp.int32),
                jnp.arange(16, dtype=jnp.int32),
                jnp.zeros((16,), jnp.int32),
                jnp.arange(80, dtype=jnp.int32) % 16,
            ]
        )
        whole = [lax.all_gather(part, AXES, axis=0, tiled=True) for part in small_parts]
        lines = []
        for part in whole:
            share = part.shape[0] // 32
            chunks = part.reshape(32, share)
            lines.append(
                jnp.stack([placed(chunks[index], index, BLOCK // share) for index in range(32)])
            )
        lines = jnp.concatenate([jnp.stack(lines, axis=1), jnp.zeros((32, 8, BLOCK), BF)], axis=1)
        lines = lines.reshape(CHIPS, 2, 16, BLOCK).transpose(1, 0, 2, 3).reshape(32, 16, BLOCK)
        whole_qkv = lax.all_gather(qkv_weight, AXES, axis=0, tiled=True)
        whole_out = lax.all_gather(out_weight, AXES, axis=0, tiled=True)
        whole_fc1 = lax.all_gather(fc1_weight, AXES, axis=0, tiled=True)
        whole_fc2 = lax.all_gather(fc2_weight, AXES, axis=0, tiled=True)
        split = whole_fc2.reshape(CHIPS, 2, 96, 2, BLOCK).transpose(1, 0, 3, 2, 4).reshape(32, 192, BLOCK)
        gathered_a = eights(
            jnp.concatenate([full_pieces(whole_qkv.reshape(width, 3, 2, BLOCK), 3), lines], axis=1), STILL
        )
        gathered_b1 = eights(full_pieces(whole_fc1.reshape(width, 2, 4, BLOCK), 4))
        split = whole_fc2.reshape(CHIPS, 2, 96, 2, BLOCK).transpose(1, 0, 3, 2, 4).reshape(32, 192, BLOCK)
        gathered_b2 = eights(
            jnp.concatenate([split, full_pieces(whole_out.reshape(width, 1, 2, BLOCK), 1)], axis=1), STILL
        )

    if by_hand:
        gathered_a, on_b1, on_b2, early = links.gather(*pieces, (rows_in, gout, far, far_turned))
        rows_in, gout, far, far_turned = early


    def call(kernel, operands, out_shape, out_specs, in_specs, flops, mib, vmem_mib, grid, scratch=(), name=None):
        return pl.pallas_call(
            kernel,
            grid=grid,
            out_shape=out_shape,
            in_specs=in_specs,
            out_specs=out_specs,
            scratch_shapes=list(scratch),
            compiler_params=pltpu.CompilerParams(vmem_limit_bytes=vmem_mib * MIB),
            cost_estimate=pl.CostEstimate(
                flops=1, bytes_accessed=1, transcendentals=0
            ),
            name=name,
        )(*operands)

    image_rows = lambda columns: pl.BlockSpec((padded, columns), lambda image: (image, 0))
    image_far = pl.BlockSpec((1, padded, padded), lambda image: (image, 0, 0))
    fixed = lambda *shape: pl.BlockSpec(shape, lambda step: (0,) * len(shape))
    step_rows = lambda columns: pl.BlockSpec((rows, columns), lambda step: (0, step))
    shares = lambda height, columns: struct((CHIPS, height, columns), BF)
    buffer, flag = pltpu.VMEM, pltpu.SemaphoreType.DMA
    low_rows, wide_rows = struct((rows, width), BF), struct((rows, width), F32)
    wide = 2 * BLOCK
    steps = hidden_width // wide
    third = 3 * BLOCK

    def join(value, *others):
        return after(value, *others) if by_hand else value

    vec, fcb, h1_turned, qkv, wq_0, wq_1 = call(
        qkv_kernel,
        (place, *gathered_a, rows_in),
        (
            struct((2, 16, BLOCK), F32), struct((steps, 1, wide), F32), struct((width, rows), BF),
            struct((2, rows, third), BF), struct((width, third), BF), struct((width, third), BF),
        ),
        (
            fixed(2, 16, BLOCK), fixed(steps, 1, wide), fixed(width, rows),
            pl.BlockSpec((1, rows, third), lambda step: (step, 0, 0)), anywhere, anywhere,
        ),
        [smem] + [anywhere] * 4 + [fixed(rows, width)],
        2 * rows * width * 3 * width,
        14,
        30,
        grid=(2,),
        scratch=(
            buffer((2, width, third), BF), buffer((rows, width), BF), buffer((4, 16, BLOCK), F32),
            buffer((32, 16, BLOCK), BF), flag((4,)),
        ),
        name="qkv",
    )
    if by_hand:
        qkv, on_b1, on_b2 = lax.optimization_barrier((qkv, on_b1, on_b2))
        on_b1, on_b2 = links.gather_on(on_b1, on_b2)

    att = call(
        attention_kernel,
        (qkv, far),
        low_rows,
        image_rows(width),
        [pl.BlockSpec((2, padded, third), lambda image: (0, image, 0)), image_far],
        8 * rows * 256 * width,
        10,
        20,
        grid=(images,),
        name="attention",
    )
    if by_hand:
        att, on_b1, on_b2 = lax.optimization_barrier((att, on_b1, on_b2))
        gathered_b1, gathered_b2 = links.gather_end(on_b1, on_b2)

    step_shares = lambda height, columns: pl.BlockSpec((CHIPS, height, columns), lambda step: (0, 0, step))
    still = lambda *shape: pl.BlockSpec(shape, lambda step, place: (0,) * len(shape))
    turned_shares = pl.BlockSpec(
        (CHIPS, 24, wide), lambda step, place: (0, 0, lax.rem(place[50] + 4 - step, 4))
    )
    low_buffer, wide_buffer = buffer((rows, width), BF), buffer((rows, width), F32)
    out, glow, keep_1, send_1, sums, fcg, keep_2, upper_2, lower_2, wo = pl.pallas_call(
        mlp_kernel,
        grid_spec=pltpu.PrefetchScalarGridSpec(
            num_scalar_prefetch=1,
            grid=(steps,),
            in_specs=[smem] + [anywhere] * 11 + [still(2, 16, BLOCK), still(steps, 1, wide)],
            out_specs=(still(rows, width),) * 2
            + (turned_shares,) * 2
            + (still(8, wide), still(steps, 8, wide))
            + (anywhere,) * 4,
            scratch_shapes=[
                buffer((steps, width, wide), BF), buffer((hidden_width, width), BF), buffer((2, width, BLOCK), BF),
                low_buffer, low_buffer, low_buffer, low_buffer, buffer((width, rows), BF),
                wide_buffer, wide_buffer, wide_buffer, buffer((width, wide), F32), buffer((width, wide), F32),
                buffer((2, CHIPS, 96, wide), BF), buffer((rows, 128), F32), flag((steps,)), flag((steps,)), flag((7,)),
            ],
        ),
        out_shape=(low_rows, low_rows)
        + (shares(24, hidden_width),) * 2
        + (struct((8, wide), F32), struct((steps, 8, wide), F32))
        + (shares(96, wide),)
        + (struct((8, 96, wide), BF),) * 2
        + (struct((2, width, BLOCK), BF),),
        compiler_params=pltpu.CompilerParams(vmem_limit_bytes=60 * MIB),
        cost_estimate=pl.CostEstimate(flops=1, bytes_accessed=1, transcendentals=0),
        name="mlp",
    )(place, counts, *gathered_b1, *gathered_b2, att, rows_in, gout, vec, fcb)

    if by_hand:
        state_2 = keep_2, links.move(upper_2, links.cores)

    def attention_back(side, gradient):
        return call(
            lambda *refs: attention_back_kernel(side, *refs),
            (wo, qkv, far_turned, gradient),
            struct((rows, third), BF),
            image_rows(third),
            [
                fixed(2, width, BLOCK), pl.BlockSpec((1, padded, third), lambda image: (side, image, 0)),
                image_far, image_rows(width),
            ],
            8 * rows * 256 * width,
            8,
            20,
            grid=(images,),
            name="attention_back",
        )

    part_2 = glow
    if by_hand:
        part_2 = add_up([keep_2[8:], state_2[1]]).astype(BF)
        lower_2, send_1 = after((lower_2, send_1), part_2)
        state_2 = keep_2, links.move(lower_2, links.cores), links.move(part_2, links.second)
        state_1 = keep_1, links.move(send_1, links.cores)
    gqkv_0 = attention_back(0, join(glow, part_2))
    if by_hand:
        state_1, gqkv_0 = lax.optimization_barrier((state_1, gqkv_0))
        state_1 += (links.move(links.fold(state_1), links.second),)

    def grad_call(kernel, operands, out_shape, scratch, name):
        return pl.pallas_call(
            kernel,
            out_shape=out_shape,
            in_specs=[smem] + [vmem] * (len(operands) - 1),
            out_specs=(vmem,) * len(out_shape),
            scratch_shapes=list(scratch),
            compiler_params=pltpu.CompilerParams(vmem_limit_bytes=28 * MIB),
            cost_estimate=pl.CostEstimate(flops=1, bytes_accessed=1, transcendentals=0),
            name=name,
        )(*operands)

    half_shares = lambda height, columns: (struct((8, height, columns), BF),) * 2
    gh1, sums_0, keep_a, upper_a, lower_a = grad_call(
        qkv_grad_kernel,
        (place, h1_turned, gqkv_0, wq_0, att, glow),
        (wide_rows, struct((1, third), F32), shares(24, third + wide)) + half_shares(24, third + wide),
        (buffer((width, third), F32), buffer((width, wide), F32)),
        "qkv_grad",
    )
    parts = gh1
    if by_hand:
        got_a = links.move(upper_a, links.cores)
        state_2, got_a, gh1 = lax.optimization_barrier((state_2, got_a, gh1))
        parts = links.fold(state_2), add_up([keep_a[8:], got_a]).astype(BF)
        state_2 += (links.move(parts[0], links.near),)
        lower_a = after(lower_a, parts)
        state_a = keep_a, links.move(lower_a, links.cores), links.move(parts[1], links.second)

    gqkv_1 = attention_back(1, join(glow, gh1, parts))
    ginput, keep_c, upper_c, lower_c = grad_call(
        input_kernel,
        (place, h1_turned, gqkv_1, wq_1, sums_0, sums, fcg, rows_in, vec, glow, gh1),
        (low_rows, shares(32, third)) + half_shares(32, third),
        (buffer((width, third), F32),),
        "input_grad",
    )

    def cut(value):
        return value.reshape(images, padded, width)[:, :length]

    if by_hand:
        fold, move = links.fold, links.move

        state_c = keep_c, move(upper_c, links.cores)
        rest_c = move(after(lower_c, keep_c), links.cores)
        state_1 = after(state_1, keep_c)
        part = fold(state_1)
        state_1 += (move(part, links.near),)
        keep_c, got_c = after(state_c, part)
        part = add_up([keep_c[8:], got_c]).astype(BF)
        state_c = keep_c, rest_c, move(part, links.second)
        state_2, state_a, out, ginput = after((state_2, state_a, out, ginput), part)
        out, ginput = cut(out), cut(ginput)
        state_2, state_a, out, ginput = after((state_2, state_a, out, ginput))
        parts = fold(state_2), fold(state_a)
        state_2 += (move(parts[0], links.first),)
        state_a += (move(parts[1], links.first),)
        part = fold(after(state_c, parts))
        state_c += (move(part, links.first),)
        state_1, out, ginput = after((state_1, out, ginput), part)
        part = fold(state_1)
        state_1 += (move(part, links.first),)
        state_2 = after(state_2, part)
        part = fold(state_2)
        state_2 += (move(part, links.far),)
        state_a = after(state_a, part)
        part = fold(state_a)
        state_a += (move(part, links.near),)
        part = fold(after(state_c, part))
        state_c += (move(part, links.near),)
        state_1 = after(state_1, part)
        part = fold(state_1)
        state_1 += (move(part, links.far),)
        state_a = after(state_a, part)
        part = fold(state_a)
        state_a += (move(part, links.far),)
        part = fold(after(state_c, part))
        state_c += (move(part, links.far),)
        state_2 = after(state_2, part)
        mine_2 = add_up([part[0] for part in state_2])
        state_1 = after(state_1, mine_2)
        mine_1 = add_up([part[0] for part in state_1])
        own_slot = lambda part: pl.BlockSpec((1,) + part.shape[1:], lambda step: (0, 0, 0))
        heights, counts_out = ((24, 3 * width), (24, width)), (24, 24, 48, 24, 24, 24, 96, 24)
        (
            qkv_grad, out_grad, ln1_gain_grad, ln1_bias_grad, qv_bias_grad,
            ln2_gain_grad, ln2_bias_grad, fc2_bias_grad, fc1_bias_grad, out_bias_grad,
        ) = pl.pallas_call(
            last_kernel,
            grid=(1,),
            out_shape=tuple(struct(shape, F32) for shape in heights + tuple((count,) for count in counts_out)),
            in_specs=[smem] + [own_slot(part) for part in state_a + state_c],
            out_specs=tuple(fixed(*shape) for shape in heights)
            + tuple(pl.BlockSpec((count,), lambda step: (0,)) for count in counts_out),
            compiler_params=pltpu.CompilerParams(vmem_limit_bytes=30 * MIB),
            name="last",
        )(place, *state_a, *state_c)
        return (
            out, ginput, ln1_gain_grad, ln1_bias_grad, qkv_grad, qv_bias_grad, out_grad, out_bias_grad,
            ln2_gain_grad, ln2_bias_grad, mine_1, fc1_bias_grad, mine_2, fc2_bias_grad,
        )

    both_a, both_c, both_1, both_2 = (
        jnp.stack(pair, axis=1).astype(F32)
        for pair in (
            (keep_a, jnp.concatenate([lower_a, upper_a])),
            (keep_c, jnp.concatenate([lower_c, upper_c])),
            (keep_1, send_1),
            (keep_2, jnp.concatenate([lower_2, upper_2])),
        )
    )
    heads = jnp.stack(
        [both.reshape(CHIPS, 2, 24, 3, BLOCK) for both in (both_a[..., :third], both_c[:, :, :24])], axis=4
    )

    def vector(lines, count):
        columns = lines.shape[-1]
        return lines.reshape(32 * count // columns, -1, columns)[:, 0].reshape(-1)

    small_c, small_2 = both_c[:, :, 24:, 2 * BLOCK :], both_c[:, :, 24:, : 2 * BLOCK]
    totals = (
        vector(small_c[:, :, 0], 24),
        vector(small_c[:, :, 1], 24),
        heads.reshape(width, 3 * width),
        vector(small_c[:, :, 2], 48),
        both_a[..., third:].reshape(width, width),
        vector(small_2[:, :, 4], 24),
        vector(small_2[:, :, 0], 24),
        vector(small_2[:, :, 1], 24),
        both_1.reshape(width, hidden_width),
        vector(small_2[:, :, 3], 96),
        both_2.reshape(hidden_width, width),
        vector(small_2[:, :, 2], 24),
    )
    return (cut(out), cut(ginput)) + tuple(
        lax.psum_scatter(total, AXES, scatter_dimension=0, tiled=True) for total in totals
    )


def solution(mesh):
    rows = P(AXES, None, None)
    table = P(AXES, None)
    line = P(AXES)
    in_specs = (
        rows, line, table, line, line, table, line, table, line, line, line, table, line, table, line, rows,
    )
    out_specs = (
        rows, rows, line, line, table, line, table, line, line, line, table, line, table, line,
    )
    mesh_shape = dict(mesh.shape)

    def body(*arrays):
        return shards(mesh_shape, *arrays)

    return jax.shard_map(body, mesh=mesh, in_specs=in_specs, out_specs=out_specs, check_vma=False)
```

```python
import math

import jax
import jax.numpy as jnp
import numpy as np
from jax import lax
from jax.experimental import pallas as pl
from jax.experimental.pallas import tpu as pltpu
from jax.sharding import PartitionSpec as P

HEADS = 12
SIDE = 16
EPSILON = 1e-06
AXES = ("dp", "fsdp")
FAR = 1e30
CHIPS = 16
BLOCK = 384
SMALL, LARGE = (32, 96), (112, 128)
MIB = 1024 * 1024

BF = jnp.bfloat16
F32 = jnp.float32


def power_slopes(number):
    first_slope = 2.0 ** (-8.0 / number)
    return [first_slope ** (index + 1) for index in range(number)]


def slope_list(heads_total):
    lower_power = 2 ** int(math.floor(math.log2(heads_total)))
    return (
        power_slopes(lower_power) + power_slopes(2 * lower_power)[0::2][: heads_total - lower_power]
    )


SLOPES = [float(np.float32(slope)) for slope in slope_list(HEADS)]


def dot(left, right, left_dim=1, right_dim=0):
    return lax.dot_general(
        left, right, (((left_dim,), (right_dim,)), ((), ())), preferred_element_type=F32
    )


def normed_rows(values):
    centered = values - jnp.mean(values, axis=-1, keepdims=True)
    scale = lax.rsqrt(jnp.mean(centered * centered, axis=-1, keepdims=True) + EPSILON)
    return centered * scale, scale


def norm_back(grad_normed, normed, scale):
    centered_mean = jnp.mean(grad_normed, axis=-1, keepdims=True)
    projected_mean = jnp.mean(grad_normed * normed, axis=-1, keepdims=True)
    return scale * (grad_normed - centered_mean - normed * projected_mean)


def row_of(vectors_ref, index):
    return jnp.concatenate(
        [vectors_ref[0, index : index + 1, :], vectors_ref[1, index : index + 1, :]], axis=1
    )


def gelu_parts(hidden):
    cumulative = 0.5 + 0.5 * lax.erf(hidden * math.sqrt(0.5))
    bell = jnp.exp(-0.5 * hidden * hidden)
    return cumulative, cumulative + hidden * bell * (1.0 / math.sqrt(2.0 * math.pi))


def share_kernel(place, qkv_ref, out_ref, fc1_ref, *refs):
    smalls, (mine_ref, theirs_ref, lines_ref) = refs[:-3], refs[-3:]
    for target, core in ((mine_ref, place[48]), (theirs_ref, 1 - place[48])):
        starts = [(qkv_ref, 2 * BLOCK * part + BLOCK * core) for part in range(3)]
        starts.append((out_ref, BLOCK * core))
        starts += [(fc1_ref, 4 * BLOCK * core + BLOCK * part) for part in range(4)]
        for block, (source, start) in enumerate(starts):
            target[block] = source[:, pl.ds(pl.multiple_of(start, 128), BLOCK)]
    device = place[49]
    lines = []
    for small in smalls:
        count = small.shape[0]
        line = small[...].astype(F32).reshape(1, count)
        line = jnp.concatenate([line, jnp.zeros((1, BLOCK - count), F32)], axis=1)
        lines.append(pltpu.roll(line, lax.rem(device, BLOCK // count) * count, 1))
    lines_ref[...] = jnp.concatenate(lines + [jnp.zeros((8, BLOCK), F32)], axis=0).astype(BF)


def pair_kernel(place, mine_ref, got_ref, lines_ref, fc2_ref, a_ref, b1_ref, b2_ref):
    swap = place[48] == 1
    for block in range(8):
        mine, got = mine_ref[block].astype(F32), got_ref[block].astype(F32)
        rows = jnp.concatenate([jnp.where(swap, got, mine), jnp.where(swap, mine, got)], axis=0)
        if block < 3:
            a_ref[48 * block : 48 * (block + 1), :] = rows.astype(BF)
        elif block == 3:
            b2_ref[192:240, :] = rows.astype(BF)
        else:
            b1_ref[48 * (block - 4) : 48 * (block - 3), :] = rows.astype(BF)
    b2_ref[0:96, :] = fc2_ref[:, :BLOCK]
    b2_ref[96:192, :] = fc2_ref[:, BLOCK:]
    a_ref[144:160, :] = lines_ref[...]


def each_piece(place, table, sources, work):
    core = place[48]
    for number, source in enumerate(sources):
        half = core if number < 2 else 1 - core

        def bring(index, _, source=source, number=number, half=half):
            work(source, index, place[table + number * 8 + index], half)
            return 0

        lax.fori_loop(0, 8, bring, 0)


def bring_out_weight(place, sources, wo, sem, table):
    def work(source, index, chip, half):
        spot = pl.ds(pl.multiple_of(chip * 48, 16), 48)
        pltpu.make_async_copy(source.at[index, pl.ds(192, 48)], wo.at[half, spot], sem).start()

    each_piece(place, table, sources, work)


def bring_qkv_weight(place, sources, side, wq, sem, part_of=None):
    for first, here in ((0, place[48] == side), (2, place[48] != side)):

        @pl.when(here)
        def _(first=first):
            for number in (first, first + 1):

                def bring(index, _, source=sources[number], number=number):
                    spot = pl.ds(pl.multiple_of(place[number * 8 + index] * 48, 16), 48)
                    for part in range(3):
                        pltpu.make_async_copy(
                            source.at[index, pl.ds(48 * part, 48)],
                            wq.at[spot, pl.ds(BLOCK * part, BLOCK)] if part_of is None else wq.at[part, spot],
                            sem if part_of is None else part_of.at[part],
                        ).start()
                    return 0

                lax.fori_loop(0, 8, bring, 0)


def wait_all(buffer, sem):
    pltpu.make_async_copy(buffer, buffer, sem).wait()


def two_heads(pair_rows, low_half):
    nothing = jnp.zeros_like(pair_rows)
    return jnp.concatenate(
        [jnp.where(low_half, pair_rows, nothing), jnp.where(low_half, nothing, pair_rows)], axis=0
    )


def first_kernel(
    place, own0, own1, other0, other1, rows_ref, far_ref,
    vec_ref, fcb_ref, h1_turned, qkv_ref, att_ref, wq_out0, wq_out1,
    wq, h1, qvb, small, sems,
):
    sources = (own0, own1, other0, other1)

    def work(source, index, chip, half):
        pltpu.make_async_copy(
            source.at[index, pl.ds(144, 16)], small.at[2 * chip + half], sems.at[2]
        ).start()

    each_piece(place, 0, sources, work)
    for half in range(2):
        bring_qkv_weight(place, sources, half, wq.at[half], sems.at[half])
    normed, _ = normed_rows(rows_ref[...].astype(F32))
    wait_all(small, sems.at[2])
    spread = small[...].astype(F32)
    vec_ref[...] = jnp.sum(spread.reshape(2, 16, 16, BLOCK), axis=1)
    qvb[...] = jnp.sum(spread.reshape(4, 8, 16, BLOCK), axis=1)
    lines = jnp.sum(spread.reshape(8, 4, 16, BLOCK), axis=1)
    for block in range(4):
        fcb_ref[block] = jnp.concatenate([lines[2 * block, 7:8], lines[2 * block + 1, 7:8]], axis=1)
    low = (normed * row_of(vec_ref, 0) + row_of(vec_ref, 1)).astype(BF)
    h1[...] = low
    h1_turned[...] = low.T
    for side, target in enumerate((wq_out0, wq_out1)):
        wait_all(wq.at[side], sems.at[side])
        pltpu.make_async_copy(wq.at[side], target, sems.at[3 + side]).start()
        bias = jnp.concatenate(
            [qvb[side, 6:7, :], jnp.zeros((1, BLOCK), F32), qvb[2 + side, 6:7, :]], axis=1
        )
        qkv_ref[side] = (dot(h1[...], wq[side]) + bias).astype(BF)

    length = far_ref.shape[1]
    low_half = lax.broadcasted_iota(jnp.int32, (length, 128), 1) < 64

    def one_image(image, _):
        here = pl.ds(pl.multiple_of(image * length, 32), length)
        far = far_ref[image]
        for pair in range(HEADS // 2):
            side, at = pair // 3, 128 * (pair % 3)
            queries = two_heads(qkv_ref[side, here, at : at + 128] * jnp.asarray(0.125, BF), low_half)
            key_rows = qkv_ref[side, here, BLOCK + at : BLOCK + at + 128]
            values = qkv_ref[side, here, 2 * BLOCK + at : 2 * BLOCK + at + 128]
            both = dot(queries, key_rows, 1, 1)
            probs = []
            for head in range(2):
                scores = both[length * head : length * (head + 1)] - SLOPES[2 * pair + head] * far
                shifted = jnp.exp(scores - jnp.max(scores, axis=-1, keepdims=True))
                share = shifted * (1.0 / jnp.sum(shifted, axis=-1, keepdims=True))
                probs.append(share.astype(BF))
            result = dot(jnp.concatenate(probs, axis=0), values)
            att_ref[here, 128 * pair : 128 * (pair + 1)] = jnp.where(
                low_half, result[:length], result[length:]
            ).astype(BF)
        return 0

    lax.fori_loop(0, far_ref.shape[0], one_image, 0)
    wait_all(wq_out0, sems.at[3])
    wait_all(wq_out1, sems.at[4])


def at_slot(target, slot, work):
    if not isinstance(target, tuple):
        work(target, slot)
        return

    @pl.when(slot >= 8)
    def _():
        work(target[0], slot - 8)

    @pl.when(slot < 8)
    def _():
        work(target[1], slot)


def give_rows(place, tables, total, keep_ref, send_ref, extra=None, lanes=slice(None)):
    for chip in range(CHIPS):
        below = None if extra is None else extra(chip)
        for which, target in enumerate((keep_ref, send_ref)):
            owner = place[48] if which == 0 else 1 - place[48]
            share = total[pl.ds(pl.multiple_of(48 * chip + 24 * owner, 8), 24), :]
            if below is not None:
                share = jnp.concatenate([share, below], axis=0)

            def put(ref, slot, share=share):
                ref[slot, :, lanes] = share.astype(BF)

            at_slot(target, place[tables[which] + chip], put)


def stack_rows(rows):
    blank = jnp.zeros_like(next(row for row in rows if row is not None))
    rows = [blank if row is None else row for row in rows]
    return jnp.concatenate(rows + [blank] * (8 - len(rows)), axis=0)


def sum_rows(values):
    return jnp.sum(values.astype(F32), axis=0, keepdims=True)


def mlp_kernel(
    place, counts, a0, a1, a2, a3, b0, b1, b2, b3, att_far, rows_far, gout_far, vec_ref, fcb_ref,
    out_ref, glow_ref, keep1_ref, send1_ref, sums_ref, fcg, keep2, upper2, lower2, wo_out,
    w1, w2, wo, att_ref, rows_ref, gout_ref, h2, h2_turned, normed, total, gh2, product1, product2,
    stage, scales, sems1, sems2, sems,
):
    step = pl.program_id(0)
    wide = 2 * BLOCK
    core, z = place[48], place[50]
    block_of = lambda step: lax.rem(z + 4 - step, 4)
    block = block_of(step)
    gain = row_of(vec_ref, 3)
    loads = [
        pltpu.make_async_copy(source, target, sems.at[3 + index])
        for index, (source, target) in enumerate(
            ((att_far, att_ref), (rows_far, rows_ref), (gout_far, gout_ref))
        )
    ]

    @pl.when(step == 0)
    def _():
        bring_out_weight(place, (b0, b1, b2, b3), wo, sems.at[2], 144)
        loads[0].start()
        loads[1].start()
        for later in range(4):
            column = block_of(later)
            for first, here in ((0, column // 2 == core), (2, column // 2 != core)):

                @pl.when(here)
                def _(first=first, column=column):
                    for number in (first, first + 1):

                        def bring(index, _, source=(a0, a1, a2, a3)[number], number=number, column=column):
                            spot = pl.ds(pl.multiple_of(place[64 + number * 8 + index] * 48, 16), 48)
                            for part in range(2):
                                start = pl.multiple_of(lax.rem(column, 2) * 96 + 48 * part, 16)
                                pltpu.make_async_copy(
                                    source.at[index, pl.ds(start, 48)],
                                    w1.at[column, spot, pl.ds(BLOCK * part, BLOCK)],
                                    sems1.at[column],
                                ).start()
                            return 0

                        lax.fori_loop(0, 8, bring, 0)

            if later == 0:
                loads[2].start()
            for number, source in enumerate((b0, b1, b2, b3)):
                half = core if number < 2 else 1 - core
                for index in (later, (4, 5, 7, 6)[later]):
                    chip = place[144 + number * 8 + index]
                    spot = pl.ds(pl.multiple_of(chip * 192 + half * 96, 16), 96)
                    for part in range(2):
                        pltpu.make_async_copy(
                            source.at[index, pl.ds(96 * part, 96)],
                            w2.at[spot, pl.ds(BLOCK * part, BLOCK)],
                            sems2.at[column],
                        ).start()

        wait_all(wo, sems.at[2])
        pltpu.make_async_copy(wo, wo_out, sems.at[2]).start()
        bias = row_of(vec_ref, 2)
        loads[0].wait()
        loads[1].wait()
        for part in range(2):
            lanes = slice(BLOCK * part, BLOCK * (part + 1))
            total[:, lanes] = rows_ref[:, lanes].astype(F32) + dot(att_ref[...], wo[part]) + bias[:, lanes]
        normal, scale = normed_rows(total[...])
        normed[...] = normal
        scales[...] = jnp.broadcast_to(scale, scales.shape)
        low = (normal * gain + row_of(vec_ref, 4)).astype(BF)
        h2[...] = low
        h2_turned[...] = low.T
        total[...] += row_of(vec_ref, 5)
        gh2[...] = jnp.zeros_like(gh2)
        loads[2].wait()

    wait_all(w1.at[block], sems1.at[block])
    hidden = dot(h2[...], w1[block]) + fcb_ref[block]
    rows_of = pl.ds(pl.multiple_of(block * wide, wide), wide)
    wait_all(w2.at[rows_of], sems2.at[block])
    gactivated = dot(gout_ref[...], w2[rows_of, :], 1, 1)
    cumulative, slope = gelu_parts(hidden)
    activated = (hidden * cumulative).astype(BF)
    ghidden = (gactivated * slope).astype(BF)
    product1[...] = dot(h2_turned[...], ghidden)
    product2[...] = dot(activated, gout_ref[...], 0, 0)
    total[...] += dot(activated, w2[rows_of, :])
    gh2[...] += dot(ghidden, w1[block], 1, 1)
    fcg[block] = stack_rows([None, None, None, sum_rows(ghidden)])
    give_rows(place, LARGE, product1, keep1_ref, send1_ref)
    for pair in range(4):
        chip = 4 * block + pair
        for which, target in enumerate((keep2, (upper2, lower2))):
            owner = place[48] if which == 0 else 1 - place[48]
            start = pl.multiple_of(192 * pair + 96 * owner, 8)
            stage[which, chip] = product2[pl.ds(start, 96), :].astype(BF)

            def send(ref, slot, which=which, chip=chip):
                sem = sems.at[1 if ref is upper2 else 6 if ref is lower2 else 0]
                pltpu.make_async_copy(stage.at[which, chip], ref.at[slot], sem).start()

            at_slot(target, place[LARGE[which] + chip], send)

    @pl.when(step == pl.num_programs(0) - 1)
    def _():
        length = out_ref.shape[0] // 4
        row_index = lax.broadcasted_iota(jnp.int32, (length, 1), 0)
        for image in range(4):
            rows = slice(length * image, length * (image + 1))
            value = total[rows, :]
            out_ref[rows, :] = jnp.where(row_index < counts[image], value, 0.0).astype(BF)
        whole = gh2[...]
        gout = gout_ref[...].astype(F32)
        gresid = gout + norm_back(whole * gain, normed[...], scales[:, 0:1])
        low = gresid.astype(BF)
        glow_ref[...] = low
        sums_ref[...] = stack_rows(
            [sum_rows(whole * normed[...]), sum_rows(whole), sum_rows(gout), None, sum_rows(low)]
        )
        wait_all(wo, sems.at[2])
        wait_all(keep2, sems.at[0])
        wait_all(upper2, sems.at[1])
        wait_all(lower2, sems.at[6])


def attention_back_kernel(side, wo, qkv_ref, far_ref, glow_ref, gqkv_ref):
    low = glow_ref[...]
    mine = slice(BLOCK * side, BLOCK * (side + 1))
    gatt = (
        dot(low[:, :BLOCK], wo[0, mine, :], 1, 1) + dot(low[:, BLOCK:], wo[1, mine, :], 1, 1)
    ).astype(BF)
    length = low.shape[0]
    low_half = lax.broadcasted_iota(jnp.int32, (length, 128), 1) < 64
    far = far_ref[0]
    for pair in range(3):
        at = 128 * pair
        queries = qkv_ref[0, :, at : at + 128] * jnp.asarray(0.125, BF)
        key_rows = two_heads(qkv_ref[0, :, BLOCK + at : BLOCK + at + 128], low_half)
        values = two_heads(qkv_ref[0, :, 2 * BLOCK + at : 2 * BLOCK + at + 128], low_half)
        grads = gatt[:, at : at + 128]
        both = dot(key_rows, queries, 1, 1)
        gboth = dot(values, grads, 1, 1)
        probs, gscores = [], []
        for head in range(2):
            rows = slice(length * head, length * (head + 1))
            scores = both[rows] - SLOPES[6 * side + 2 * pair + head] * far
            shifted = jnp.exp(scores - jnp.max(scores, axis=0, keepdims=True))
            share = shifted * (1.0 / jnp.sum(shifted, axis=0, keepdims=True))
            weighted = share * gboth[rows]
            probs.append(share.astype(BF))
            inner = jnp.sum(weighted, axis=0, keepdims=True)
            gscores.append((weighted - share * inner).astype(BF))
        probs, gscores = jnp.concatenate(probs, axis=0), jnp.concatenate(gscores, axis=0)
        gvalues = dot(probs, grads)
        gkeys = dot(gscores, queries)
        gqkv_ref[:, at : at + 128] = (dot(gscores, key_rows, 0, 0) * 0.125).astype(BF)
        for which, result in ((1, gkeys), (2, gvalues)):
            gqkv_ref[:, which * BLOCK + at : which * BLOCK + at + 128] = jnp.where(
                low_half, result[:length], result[length:]
            ).astype(BF)


def qkv_grad_kernel(
    place, h1_turned, gqkv_ref, wq_ref, att_ref, glow_ref, gh1_ref, sums_ref, keep_ref, upper_ref, lower_ref,
    product, product_out,
):
    third, wide = gqkv_ref.shape[1], glow_ref.shape[1]
    product[...] = dot(h1_turned[...], gqkv_ref[...])
    product_out[...] = dot(att_ref[...], glow_ref[...], 0, 0)
    gh1_ref[...] = dot(gqkv_ref[...], wq_ref[...], 1, 1)
    sums_ref[...] = sum_rows(gqkv_ref[...])
    send = upper_ref, lower_ref
    give_rows(place, SMALL, product, keep_ref, send, lanes=slice(0, third))
    give_rows(place, SMALL, product_out, keep_ref, send, lanes=slice(third, third + wide))


def input_kernel(
    place, h1_turned, gqkv_ref, wq_ref, before_ref, mlp_ref, fcg_ref, rows_ref, vec_ref, glow_ref, gh1_ref,
    ginput_ref, keep_ref, upper_ref, lower_ref, product,
):
    product[...] = dot(h1_turned[...], gqkv_ref[...])
    sums = sum_rows(gqkv_ref[...])
    gradient = gh1_ref[...] + dot(gqkv_ref[...], wq_ref[...], 1, 1)
    normed, scale = normed_rows(rows_ref[...].astype(F32))
    ginput_ref[...] = (
        glow_ref[...].astype(F32) + norm_back(gradient * row_of(vec_ref, 0), normed, scale)
    ).astype(BF)
    gain, shift = sum_rows(gradient * normed), sum_rows(gradient)
    first, last = slice(0, BLOCK), slice(2 * BLOCK, 3 * BLOCK)
    biases = before_ref[:, first], sums[:, first], before_ref[:, last], sums[:, last]

    def below(chip):
        lanes = slice(BLOCK * (chip // 8), BLOCK * (chip // 8 + 1))
        own = stack_rows([gain[:, lanes], shift[:, lanes], biases[chip // 4]])
        return jnp.concatenate([mlp_ref[...] + fcg_ref[chip // 4], own], axis=1)

    give_rows(place, SMALL, product, keep_ref, (upper_ref, lower_ref), below)


def add_up(parts):
    return sum(part.astype(F32) for part in parts)


def give_vector(target, line, device):
    count, columns = target.shape[0], line.shape[1]
    start = lax.rem(device, columns // count) * count
    moved = pltpu.roll(line, lax.rem(columns - start, columns), 1)
    target[...] = moved[:, :count].reshape(count)


def last_kernel(place, *refs):
    sources, (qkv_out, out_out), smalls = refs[:12], refs[12:14], refs[14:]
    total_a = add_up([source[0] for source in sources[:6]])
    total_c = add_up([source[0] for source in sources[6:]])
    for part in range(3):
        lanes = slice(BLOCK * part, BLOCK * (part + 1))
        qkv_out[:, 2 * BLOCK * part : 2 * BLOCK * part + BLOCK] = total_a[:, lanes]
        qkv_out[:, 2 * BLOCK * part + BLOCK : 2 * BLOCK * (part + 1)] = total_c[:24, lanes]
    out_out[...] = total_a[:, 3 * BLOCK :]
    device = place[49]
    for line, target in enumerate(smalls[:3]):
        give_vector(target, total_c[24 + line : 25 + line, 2 * BLOCK :], device)
    for line, target in enumerate(smalls[3:]):
        give_vector(target, total_c[24 + line : 25 + line, : 2 * BLOCK], device)


def after(value, *others):
    return lax.optimization_barrier((value,) + others)[0]


class Links:
    def __init__(self, depth):
        self.depth = depth

        def table(move):
            pairs = []
            for z in range(depth):
                for x in range(2):
                    for y in range(2):
                        for c in range(2):
                            nz, nx, ny, nc = move(z, x, y, c)
                            source = (z * 2 + x) * 4 + y * 2 + c
                            pairs.append((source, ((nz % depth) * 2 + nx) * 4 + ny * 2 + nc))
            return pairs

        self.ups = {step: table(lambda z, x, y, c: (z + step, x, y, c)) for step in (1, 2, 3)}
        self.first = table(lambda z, x, y, c: (z, x, 1 - y, c) if c else (z, 1 - x, y, c))
        self.second = table(lambda z, x, y, c: (z, 1 - x, y, c) if c else (z, x, 1 - y, c))
        self.across = table(lambda z, x, y, c: (z, 1 - x, 1 - y, c))
        self.cores = table(lambda z, x, y, c: (z, x, y, 1 - c))
        self.near = table(lambda z, x, y, c: (z ^ 1, x, y, c))
        self.far = table(lambda z, x, y, c: (z ^ 2, x, y, c))

    def move(self, value, pairs):
        return lax.ppermute(value, AXES, pairs)

    def spots(self):
        dp, fsdp = lax.axis_index("dp"), lax.axis_index("fsdp")
        z, x, y, core = dp // 2, dp % 2, fsdp // 2, fsdp % 2

        def chip(c, flip1, flip2, step):
            flip_x = jnp.where(c == 0, flip1, flip2)
            flip_y = jnp.where(c == 0, flip2, flip1)
            return (((z - step) % self.depth) * 2 + (x ^ flip_x)) * 2 + (y ^ flip_y)

        index = jnp.arange(32, dtype=jnp.int32)
        whose = jnp.where(index < 16, core, 1 - core)
        flip2 = (index // 8) % 2
        z_first = chip(whose, (index // 4) % 2, flip2, index % 4)
        x_first = chip(whose, index % 2, (index // 2) % 2, (index // 4) % 4)
        chips = jnp.arange(16, dtype=jnp.int32)
        turn_x, turn_y = ((chips // 2) % 2) ^ x, (chips % 2) ^ y
        far_z = (chips // 4) ^ z
        near, wide_step = far_z % 2, far_z // 2

        def slots(order):
            turns = {"x": turn_x, "y": turn_y, "near": near, "far": wide_step}
            return sum(turns[name] * weight for name, weight in zip(order, (8, 4, 2, 1)))

        others = jnp.stack([core, dp * 4 + fsdp, z]).astype(jnp.int32)
        rest = jnp.concatenate([others, jnp.zeros((13,), jnp.int32)])
        tables = []
        for orders in (
            (("y", "x", "near", "far"), ("x", "y", "near", "far")),
            (("y", "near", "x", "far"), ("x", "near", "y", "far")),
        ):
            both = [slots(order) for order in orders]
            tables += [jnp.where(core == 0, both[0], both[1]), jnp.where(core == 0, both[1], both[0])]
        swapped = jnp.where(index % 8 >= 6, 9 - index % 8, index % 4)
        swapped = chip(whose, (index // 4) % 2, flip2, swapped)
        parts = [z_first, tables[0], rest, x_first] + tables[1:] + [swapped]
        return jnp.concatenate(parts).astype(jnp.int32)

    def gather(self, piece_a, piece_b1, piece_b2, inputs, prepare):
        hold = lax.optimization_barrier
        up = lambda value, step: self.move(value, self.ups[step])
        a_one, a_three, b1_two = hold((up(piece_a, 1), up(piece_a, 3), self.move(piece_b1, self.first)))
        b1_two = jnp.stack([piece_b1, b1_two])
        a_two, b1_four = hold((up(a_one, 1), self.move(b1_two, self.second)))
        a_four = jnp.stack([piece_a, a_one, a_two, a_three])
        b1_four = jnp.concatenate([b1_two, b1_four])
        piece_b2 = after(piece_b2, a_two)
        a_rest, b2_one, b2_three = hold((self.move(a_four, self.first), up(piece_b2, 1), up(piece_b2, 3)))
        early = prepare(*after(inputs, a_rest))
        a_eight = jnp.concatenate([a_four, a_rest])
        b2_rest = self.move(jnp.stack([piece_b2, b2_one, b2_three]), self.first)
        a_other, b2_two, b1_one, b2_rest, early = hold(
            (self.move(a_eight, self.second), up(b2_one, 1), up(after(b1_four, a_rest), 1), b2_rest, early)
        )
        b2_seven = jnp.concatenate([jnp.stack([piece_b2, b2_one, b2_two, b2_three]), b2_rest])
        a = self.finish(a_eight, a_other)
        b1 = b1_four, b1_one, up(b1_one, 1), up(b1_four, 3)
        b2_last, b2_across = self.move(b2_two[None], self.first), self.move(b2_two[None], self.across)
        return a, b1, (b2_seven, b2_last, self.move(b2_seven, self.second), b2_across), early

    def gather_end(self, b1, b2, done):
        b1_four, b1_one, b1_two, b1_three = b1
        b2_seven, b2_last, other_seven, other_last = b2
        b2_last, done = lax.optimization_barrier((b2_last, done))
        b2_mine, b1_mine = jnp.concatenate([b2_seven, b2_last]), jnp.concatenate([b1_four, b1_one])
        b2_theirs, b1_theirs = self.move(b2_mine, self.cores), self.move(b1_mine, self.cores)
        b1_two, b1_three, other_seven, other_last, done = lax.optimization_barrier(
            (b1_two, b1_three, other_seven, other_last, done)
        )
        b2_rest, b1_rest = jnp.concatenate([other_seven, other_last]), jnp.concatenate([b1_two, b1_three])
        b1 = b1_mine, b1_rest, b1_theirs, self.move(b1_rest, self.cores)
        return done, b1, (b2_mine, b2_rest, b2_theirs, self.move(b2_rest, self.cores))

    def finish(self, eight, rest):
        return (eight, rest, self.move(eight, self.cores), self.move(rest, self.cores))

    def fold(self, state):
        left = 32 >> (len(state) - 1)
        return add_up([part[left // 2 : left] for part in state]).astype(BF)

def full_pieces(full, blocks):
    split = full.reshape((CHIPS, 48) + full.shape[1:])
    split = split.transpose(3, 0, 2, 1, 4) if full.shape[1] == blocks else split.transpose(2, 0, 3, 1, 4)
    return split.reshape(2 * CHIPS, blocks * 48, BLOCK)


STILL = [
    16 * core + ((-step % 4) * 2 + (flip2 if core else flip1)) * 2 + (flip1 if core else flip2)
    for core in range(2)
    for flip2 in range(2)
    for flip1 in range(2)
    for step in range(4)
]


STILL_LAST = [STILL[8 * array + index] for array in range(4) for index in (0, 1, 2, 3, 4, 5, 7, 6)]


def eights(pieces, order=None):
    if order is not None:
        pieces = jnp.stack([pieces[index] for index in order])
    return tuple(pieces[8 * index : 8 * (index + 1)] for index in range(4))


def placed(vector, device, per_row):
    start = (device % per_row) * vector.shape[0]
    return lax.dynamic_update_slice(jnp.zeros((BLOCK,), vector.dtype), vector, (start,))


def shards(
    mesh_shape,
    patches,
    counts,
    positions,
    ln1_gain,
    ln1_bias,
    qkv_weight,
    qv_bias,
    out_weight,
    out_bias,
    ln2_gain,
    ln2_bias,
    fc1_weight,
    fc1_bias,
    fc2_weight,
    fc2_bias,
    cotangent,
):
    images, length, width = patches.shape
    padded = (length + 31) // 32 * 32
    rows = images * padded
    hidden_width = fc1_weight.shape[1]
    devices = mesh_shape["dp"] * mesh_shape["fsdp"]
    by_hand = devices == 2 * CHIPS and mesh_shape["fsdp"] == 4
    small_parts = (ln1_gain, ln1_bias, out_bias, ln2_gain, ln2_bias, fc2_bias, qv_bias, fc1_bias)

    smem = pl.BlockSpec(memory_space=pltpu.SMEM)
    vmem = pl.BlockSpec(memory_space=pltpu.VMEM)
    anywhere = pl.BlockSpec(memory_space=pltpu.HBM)
    struct = jax.ShapeDtypeStruct

    def prepare(patches, counts, positions, cotangent):
        row_index = jnp.arange(padded, dtype=jnp.int32)
        is_live = row_index[None, :] < counts[:, None]
        pad_rows = ((0, 0), (0, padded - length), (0, 0))
        rows_in = jnp.pad(patches, pad_rows).reshape(rows, width)
        gout = jnp.where(is_live[:, :, None], jnp.pad(cotangent, pad_rows), 0).reshape(rows, width)
        spots = jnp.pad(positions, pad_rows[:2])
        grid_rows = (spots // SIDE).astype(F32)
        grid_cols = (spots % SIDE).astype(F32)
        row_delta = grid_rows[:, :, None] - grid_rows[:, None, :]
        col_delta = grid_cols[:, :, None] - grid_cols[:, None, :]
        distance = jnp.sqrt(row_delta * row_delta + col_delta * col_delta)
        far = jnp.where(is_live[:, None, :], distance, FAR)
        far_turned = jnp.where(is_live[:, :, None], distance, FAR)
        return rows_in, gout, far, far_turned

    if by_hand:
        links = Links(mesh_shape["dp"] // 2)
        place = links.spots()
        core = place[48]
        share = struct((8, 24, BLOCK), BF)
        mine, theirs, lines = pl.pallas_call(
            share_kernel,
            out_shape=(share, share, struct((16, BLOCK), BF)),
            in_specs=[smem] + [vmem] * 11,
            out_specs=(vmem,) * 3,
            name="share",
        )(place, qkv_weight, out_weight, fc1_weight, *small_parts)
        got = links.move(theirs, links.cores)
        pieces = pl.pallas_call(
            pair_kernel,
            out_shape=tuple(struct((height, BLOCK), BF) for height in (160, 192, 240)),
            in_specs=[smem] + [vmem] * 4,
            out_specs=(vmem,) * 3,
            name="pair",
        )(place, mine, got, lines, fc2_weight)
    else:
        links = None
        place = jnp.concatenate(
            [
                jnp.array([chip % CHIPS for chip in STILL], jnp.int32),
                jnp.arange(16, dtype=jnp.int32),
                jnp.zeros((16,), jnp.int32),
                jnp.arange(80, dtype=jnp.int32) % 16,
                jnp.array([chip % CHIPS for chip in STILL_LAST], jnp.int32),
            ]
        )
        whole = [lax.all_gather(part, AXES, axis=0, tiled=True) for part in small_parts]
        lines = []
        for part in whole:
            share = part.shape[0] // 32
            chunks = part.reshape(32, share)
            lines.append(
                jnp.stack([placed(chunks[index], index, BLOCK // share) for index in range(32)])
            )
        lines = jnp.concatenate([jnp.stack(lines, axis=1), jnp.zeros((32, 8, BLOCK), BF)], axis=1)
        lines = lines.reshape(CHIPS, 2, 16, BLOCK).transpose(1, 0, 2, 3).reshape(32, 16, BLOCK)
        whole_qkv = lax.all_gather(qkv_weight, AXES, axis=0, tiled=True)
        whole_out = lax.all_gather(out_weight, AXES, axis=0, tiled=True)
        whole_fc1 = lax.all_gather(fc1_weight, AXES, axis=0, tiled=True)
        whole_fc2 = lax.all_gather(fc2_weight, AXES, axis=0, tiled=True)
        split = whole_fc2.reshape(CHIPS, 2, 96, 2, BLOCK).transpose(1, 0, 3, 2, 4).reshape(32, 192, BLOCK)
        gathered_a = eights(
            jnp.concatenate([full_pieces(whole_qkv.reshape(width, 3, 2, BLOCK), 3), lines], axis=1), STILL
        )
        gathered_b1 = eights(full_pieces(whole_fc1.reshape(width, 2, 4, BLOCK), 4))
        split = whole_fc2.reshape(CHIPS, 2, 96, 2, BLOCK).transpose(1, 0, 3, 2, 4).reshape(32, 192, BLOCK)
        gathered_b2 = eights(
            jnp.concatenate([split, full_pieces(whole_out.reshape(width, 1, 2, BLOCK), 1)], axis=1), STILL_LAST
        )

    if by_hand:
        gathered_a, on_b1, on_b2, early = links.gather(*pieces, (patches, counts, positions, cotangent), prepare)
    else:
        early = prepare(patches, counts, positions, cotangent)
    rows_in, gout, far, far_turned = early

    def call(kernel, operands, out_shape, out_specs, in_specs, flops, mib, vmem_mib, grid, scratch=(), name=None):
        return pl.pallas_call(
            kernel,
            grid=grid,
            out_shape=out_shape,
            in_specs=in_specs,
            out_specs=out_specs,
            scratch_shapes=list(scratch),
            compiler_params=pltpu.CompilerParams(vmem_limit_bytes=vmem_mib * MIB),
            cost_estimate=pl.CostEstimate(
                flops=1, bytes_accessed=1, transcendentals=0
            ),
            name=name,
        )(*operands)

    image_rows = lambda columns: pl.BlockSpec((padded, columns), lambda image: (image, 0))
    image_far = pl.BlockSpec((1, padded, padded), lambda image: (image, 0, 0))
    fixed = lambda *shape: pl.BlockSpec(shape, lambda step: (0,) * len(shape))
    step_rows = lambda columns: pl.BlockSpec((rows, columns), lambda step: (0, step))
    shares = lambda height, columns: struct((CHIPS, height, columns), BF)
    buffer, flag = pltpu.VMEM, pltpu.SemaphoreType.DMA
    low_rows, wide_rows = struct((rows, width), BF), struct((rows, width), F32)
    wide = 2 * BLOCK
    steps = hidden_width // wide
    third = 3 * BLOCK

    def join(value, *others):
        return after(value, *others) if by_hand else value

    vec, fcb, h1_turned, qkv, att, wq_0, wq_1 = pl.pallas_call(
        first_kernel,
        out_shape=(
            struct((2, 16, BLOCK), F32), struct((steps, 1, wide), F32), struct((width, rows), BF),
            struct((2, rows, third), BF), low_rows, struct((width, third), BF), struct((width, third), BF),
        ),
        in_specs=[smem] + [anywhere] * 4 + [vmem] * 2,
        out_specs=(vmem,) * 5 + (anywhere,) * 2,
        scratch_shapes=[
            buffer((2, width, third), BF), buffer((rows, width), BF), buffer((4, 16, BLOCK), F32),
            buffer((32, 16, BLOCK), BF), flag((5,)),
        ],
        compiler_params=pltpu.CompilerParams(vmem_limit_bytes=30 * MIB),
        cost_estimate=pl.CostEstimate(flops=1, bytes_accessed=1, transcendentals=0),
        name="first",
    )(place, *gathered_a, rows_in, far)
    if by_hand:
        att, gathered_b1, gathered_b2 = links.gather_end(on_b1, on_b2, att)

    step_shares = lambda height, columns: pl.BlockSpec((CHIPS, height, columns), lambda step: (0, 0, step))
    still = lambda *shape: pl.BlockSpec(shape, lambda step, place: (0,) * len(shape))
    turned_shares = pl.BlockSpec(
        (CHIPS, 24, wide), lambda step, place: (0, 0, lax.rem(place[50] + 4 - step, 4))
    )
    low_buffer, wide_buffer = buffer((rows, width), BF), buffer((rows, width), F32)
    out, glow, keep_1, send_1, sums, fcg, keep_2, upper_2, lower_2, wo = pl.pallas_call(
        mlp_kernel,
        grid_spec=pltpu.PrefetchScalarGridSpec(
            num_scalar_prefetch=1,
            grid=(steps,),
            in_specs=[smem] + [anywhere] * 11 + [still(2, 16, BLOCK), still(steps, 1, wide)],
            out_specs=(still(rows, width),) * 2
            + (turned_shares,) * 2
            + (still(8, wide), still(steps, 8, wide))
            + (anywhere,) * 4,
            scratch_shapes=[
                buffer((steps, width, wide), BF), buffer((hidden_width, width), BF), buffer((2, width, BLOCK), BF),
                low_buffer, low_buffer, low_buffer, low_buffer, buffer((width, rows), BF),
                wide_buffer, wide_buffer, wide_buffer, buffer((width, wide), F32), buffer((width, wide), F32),
                buffer((2, CHIPS, 96, wide), BF), buffer((rows, 128), F32), flag((steps,)), flag((steps,)), flag((7,)),
            ],
        ),
        out_shape=(low_rows, low_rows)
        + (shares(24, hidden_width),) * 2
        + (struct((8, wide), F32), struct((steps, 8, wide), F32))
        + (shares(96, wide),)
        + (struct((8, 96, wide), BF),) * 2
        + (struct((2, width, BLOCK), BF),),
        compiler_params=pltpu.CompilerParams(vmem_limit_bytes=60 * MIB),
        cost_estimate=pl.CostEstimate(flops=1, bytes_accessed=1, transcendentals=0),
        name="mlp",
    )(place, counts, *gathered_b1, *gathered_b2, att, rows_in, gout, vec, fcb)

    if by_hand:
        state_2 = keep_2, links.move(upper_2, links.cores)

    def attention_back(side, gradient):
        return call(
            lambda *refs: attention_back_kernel(side, *refs),
            (wo, qkv, far_turned, gradient),
            struct((rows, third), BF),
            image_rows(third),
            [
                fixed(2, width, BLOCK), pl.BlockSpec((1, padded, third), lambda image: (side, image, 0)),
                image_far, image_rows(width),
            ],
            8 * rows * 256 * width,
            8,
            20,
            grid=(images,),
            name="attention_back",
        )

    part_2 = glow
    if by_hand:
        part_2 = add_up([keep_2[8:], state_2[1]]).astype(BF)
        lower_2, send_1 = after((lower_2, send_1), part_2)
        state_2 = keep_2, links.move(lower_2, links.cores), links.move(part_2, links.second)
        state_1 = keep_1, links.move(send_1, links.cores)
    gqkv_0 = attention_back(0, join(glow, part_2))
    if by_hand:
        state_1, gqkv_0 = lax.optimization_barrier((state_1, gqkv_0))
        state_1 += (links.move(links.fold(state_1), links.second),)

    def grad_call(kernel, operands, out_shape, scratch, name):
        return pl.pallas_call(
            kernel,
            out_shape=out_shape,
            in_specs=[smem] + [vmem] * (len(operands) - 1),
            out_specs=(vmem,) * len(out_shape),
            scratch_shapes=list(scratch),
            compiler_params=pltpu.CompilerParams(vmem_limit_bytes=28 * MIB),
            cost_estimate=pl.CostEstimate(flops=1, bytes_accessed=1, transcendentals=0),
            name=name,
        )(*operands)

    half_shares = lambda height, columns: (struct((8, height, columns), BF),) * 2
    gh1, sums_0, keep_a, upper_a, lower_a = grad_call(
        qkv_grad_kernel,
        (place, h1_turned, gqkv_0, wq_0, att, glow),
        (wide_rows, struct((1, third), F32), shares(24, third + wide)) + half_shares(24, third + wide),
        (buffer((width, third), F32), buffer((width, wide), F32)),
        "qkv_grad",
    )
    parts = gh1
    if by_hand:
        got_a = links.move(upper_a, links.cores)
        state_2, got_a, gh1 = lax.optimization_barrier((state_2, got_a, gh1))
        parts = links.fold(state_2), add_up([keep_a[8:], got_a]).astype(BF)
        state_2 += (links.move(parts[0], links.near),)
        lower_a = after(lower_a, parts)
        state_a = keep_a, links.move(lower_a, links.cores), links.move(parts[1], links.second)

    gqkv_1 = attention_back(1, join(glow, gh1, parts))
    ginput, keep_c, upper_c, lower_c = grad_call(
        input_kernel,
        (place, h1_turned, gqkv_1, wq_1, sums_0, sums, fcg, rows_in, vec, glow, gh1),
        (low_rows, shares(32, third)) + half_shares(32, third),
        (buffer((width, third), F32),),
        "input_grad",
    )

    def cut(value):
        return value.reshape(images, padded, width)[:, :length]

    if by_hand:
        fold, move = links.fold, links.move

        state_c = keep_c, move(upper_c, links.cores)
        rest_c = move(after(lower_c, keep_c), links.cores)
        state_1 = after(state_1, keep_c)
        part = fold(state_1)
        state_1 += (move(part, links.near),)
        keep_c, got_c = after(state_c, part)
        part = add_up([keep_c[8:], got_c]).astype(BF)
        state_c = keep_c, rest_c, move(part, links.second)
        state_2, state_a, out, ginput = after((state_2, state_a, out, ginput), part)
        out, ginput = cut(out), cut(ginput)
        state_2, state_a, out, ginput = after((state_2, state_a, out, ginput))
        parts = fold(state_2), fold(state_a)
        state_2 += (move(parts[0], links.first),)
        state_a += (move(parts[1], links.first),)
        part = fold(after(state_c, parts))
        state_c += (move(part, links.first),)
        state_1, out, ginput = after((state_1, out, ginput), part)
        part = fold(state_1)
        state_1 += (move(part, links.first),)
        state_2 = after(state_2, part)
        part = fold(state_2)
        state_2 += (move(part, links.far),)
        state_a = after(state_a, part)
        part = fold(state_a)
        state_a += (move(part, links.near),)
        part = fold(after(state_c, part))
        state_c += (move(part, links.near),)
        state_1 = after(state_1, part)
        part = fold(state_1)
        state_1 += (move(part, links.far),)
        state_a = after(state_a, part)
        part = fold(state_a)
        state_a += (move(part, links.far),)
        part = fold(after(state_c, part))
        state_c += (move(part, links.far),)
        state_2 = after(state_2, part)
        mine_2 = add_up([part[0] for part in state_2])
        state_1 = after(state_1, mine_2)
        mine_1 = add_up([part[0] for part in state_1])
        own_slot = lambda part: pl.BlockSpec((1,) + part.shape[1:], lambda step: (0, 0, 0))
        heights, counts_out = ((24, 3 * width), (24, width)), (24, 24, 48, 24, 24, 24, 96, 24)
        (
            qkv_grad, out_grad, ln1_gain_grad, ln1_bias_grad, qv_bias_grad,
            ln2_gain_grad, ln2_bias_grad, fc2_bias_grad, fc1_bias_grad, out_bias_grad,
        ) = pl.pallas_call(
            last_kernel,
            grid=(1,),
            out_shape=tuple(struct(shape, F32) for shape in heights + tuple((count,) for count in counts_out)),
            in_specs=[smem] + [own_slot(part) for part in state_a + state_c],
            out_specs=tuple(fixed(*shape) for shape in heights)
            + tuple(pl.BlockSpec((count,), lambda step: (0,)) for count in counts_out),
            compiler_params=pltpu.CompilerParams(vmem_limit_bytes=30 * MIB),
            name="last",
        )(place, *state_a, *state_c)
        return (
            out, ginput, ln1_gain_grad, ln1_bias_grad, qkv_grad, qv_bias_grad, out_grad, out_bias_grad,
            ln2_gain_grad, ln2_bias_grad, mine_1, fc1_bias_grad, mine_2, fc2_bias_grad,
        )

    both_a, both_c, both_1, both_2 = (
        jnp.stack(pair, axis=1).astype(F32)
        for pair in (
            (keep_a, jnp.concatenate([lower_a, upper_a])),
            (keep_c, jnp.concatenate([lower_c, upper_c])),
            (keep_1, send_1),
            (keep_2, jnp.concatenate([lower_2, upper_2])),
        )
    )
    heads = jnp.stack(
        [both.reshape(CHIPS, 2, 24, 3, BLOCK) for both in (both_a[..., :third], both_c[:, :, :24])], axis=4
    )

    def vector(lines, count):
        columns = lines.shape[-1]
        return lines.reshape(32 * count // columns, -1, columns)[:, 0].reshape(-1)

    small_c, small_2 = both_c[:, :, 24:, 2 * BLOCK :], both_c[:, :, 24:, : 2 * BLOCK]
    totals = (
        vector(small_c[:, :, 0], 24),
        vector(small_c[:, :, 1], 24),
        heads.reshape(width, 3 * width),
        vector(small_c[:, :, 2], 48),
        both_a[..., third:].reshape(width, width),
        vector(small_2[:, :, 4], 24),
        vector(small_2[:, :, 0], 24),
        vector(small_2[:, :, 1], 24),
        both_1.reshape(width, hidden_width),
        vector(small_2[:, :, 3], 96),
        both_2.reshape(hidden_width, width),
        vector(small_2[:, :, 2], 24),
    )
    return (cut(out), cut(ginput)) + tuple(
        lax.psum_scatter(total, AXES, scatter_dimension=0, tiled=True) for total in totals
    )


def solution(mesh):
    rows = P(AXES, None, None)
    table = P(AXES, None)
    line = P(AXES)
    in_specs = (
        rows, line, table, line, line, table, line, table, line, line, line, table, line, table, line, rows,
    )
    out_specs = (
        rows, rows, line, line, table, line, table, line, line, line, table, line, table, line,
    )
    mesh_shape = dict(mesh.shape)

    def body(*arrays):
        return shards(mesh_shape, *arrays)

    return jax.shard_map(body, mesh=mesh, in_specs=in_specs, out_specs=out_specs, check_vma=False)
```

```python
import math

import jax
import jax.numpy as jnp
import numpy as np
from jax import lax
from jax.experimental import pallas as pl
from jax.experimental.pallas import tpu as pltpu
from jax.sharding import PartitionSpec as P

HEADS = 12
SIDE = 16
EPSILON = 1e-06
AXES = ("dp", "fsdp")
FAR = 1e30
CHIPS = 16
BLOCK = 384
SMALL, LARGE = (32, 96), (112, 128)
MIB = 1024 * 1024

BF = jnp.bfloat16
F32 = jnp.float32


def power_slopes(number):
    first_slope = 2.0 ** (-8.0 / number)
    return [first_slope ** (index + 1) for index in range(number)]


def slope_list(heads_total):
    lower_power = 2 ** int(math.floor(math.log2(heads_total)))
    return (
        power_slopes(lower_power) + power_slopes(2 * lower_power)[0::2][: heads_total - lower_power]
    )


SLOPES = [float(np.float32(slope)) for slope in slope_list(HEADS)]


def dot(left, right, left_dim=1, right_dim=0):
    return lax.dot_general(
        left, right, (((left_dim,), (right_dim,)), ((), ())), preferred_element_type=F32
    )


def normed_rows(values):
    centered = values - jnp.mean(values, axis=-1, keepdims=True)
    scale = lax.rsqrt(jnp.mean(centered * centered, axis=-1, keepdims=True) + EPSILON)
    return centered * scale, scale


def norm_back(grad_normed, normed, scale):
    centered_mean = jnp.mean(grad_normed, axis=-1, keepdims=True)
    projected_mean = jnp.mean(grad_normed * normed, axis=-1, keepdims=True)
    return scale * (grad_normed - centered_mean - normed * projected_mean)


def row_of(vectors_ref, index):
    return jnp.concatenate(
        [vectors_ref[0, index : index + 1, :], vectors_ref[1, index : index + 1, :]], axis=1
    )


def gelu_parts(hidden):
    cumulative = 0.5 + 0.5 * lax.erf(hidden * math.sqrt(0.5))
    bell = jnp.exp(-0.5 * hidden * hidden)
    return cumulative, cumulative + hidden * bell * (1.0 / math.sqrt(2.0 * math.pi))


def share_kernel(place, qkv_ref, out_ref, fc1_ref, *refs):
    smalls, (mine_ref, theirs_ref, lines_ref) = refs[:-3], refs[-3:]
    for target, core in ((mine_ref, place[48]), (theirs_ref, 1 - place[48])):
        starts = [(qkv_ref, 2 * BLOCK * part + BLOCK * core) for part in range(3)]
        starts.append((out_ref, BLOCK * core))
        starts += [(fc1_ref, 4 * BLOCK * core + BLOCK * part) for part in range(4)]
        for block, (source, start) in enumerate(starts):
            target[block] = source[:, pl.ds(pl.multiple_of(start, 128), BLOCK)]
    device = place[49]
    lines = []
    for small in smalls:
        count = small.shape[0]
        line = small[...].astype(F32).reshape(1, count)
        line = jnp.concatenate([line, jnp.zeros((1, BLOCK - count), F32)], axis=1)
        lines.append(pltpu.roll(line, lax.rem(device, BLOCK // count) * count, 1))
    lines_ref[...] = jnp.concatenate(lines + [jnp.zeros((8, BLOCK), F32)], axis=0).astype(BF)


def pair_kernel(place, mine_ref, got_ref, lines_ref, fc2_ref, a_ref, b1_ref, b2_ref):
    swap = place[48] == 1
    for block in range(8):
        mine, got = mine_ref[block].astype(F32), got_ref[block].astype(F32)
        rows = jnp.concatenate([jnp.where(swap, got, mine), jnp.where(swap, mine, got)], axis=0)
        if block < 3:
            a_ref[48 * block : 48 * (block + 1), :] = rows.astype(BF)
        elif block == 3:
            b2_ref[192:240, :] = rows.astype(BF)
        else:
            b1_ref[48 * (block - 4) : 48 * (block - 3), :] = rows.astype(BF)
    b2_ref[0:96, :] = fc2_ref[:, :BLOCK]
    b2_ref[96:192, :] = fc2_ref[:, BLOCK:]
    a_ref[144:160, :] = lines_ref[...]


def each_piece(place, table, sources, work):
    core = place[48]
    for number, source in enumerate(sources):
        half = core if number < 2 else 1 - core

        def bring(index, _, source=source, number=number, half=half):
            work(source, index, place[table + number * 8 + index], half)
            return 0

        lax.fori_loop(0, 8, bring, 0)


def bring_out_weight(place, sources, wo, sem, table):
    def work(source, index, chip, half):
        spot = pl.ds(pl.multiple_of(chip * 48, 16), 48)
        pltpu.make_async_copy(source.at[index, pl.ds(192, 48)], wo.at[half, spot], sem).start()

    each_piece(place, table, sources, work)


def bring_qkv_weight(place, sources, side, wq, sem, part_of=None):
    for first, here in ((0, place[48] == side), (2, place[48] != side)):

        @pl.when(here)
        def _(first=first):
            for number in (first, first + 1):

                def bring(index, _, source=sources[number], number=number):
                    spot = pl.ds(pl.multiple_of(place[number * 8 + index] * 48, 16), 48)
                    for part in range(3):
                        pltpu.make_async_copy(
                            source.at[index, pl.ds(48 * part, 48)],
                            wq.at[spot, pl.ds(BLOCK * part, BLOCK)] if part_of is None else wq.at[part, spot],
                            sem if part_of is None else part_of.at[part],
                        ).start()
                    return 0

                lax.fori_loop(0, 8, bring, 0)


def wait_all(buffer, sem):
    pltpu.make_async_copy(buffer, buffer, sem).wait()


def two_heads(pair_rows, low_half):
    nothing = jnp.zeros_like(pair_rows)
    return jnp.concatenate(
        [jnp.where(low_half, pair_rows, nothing), jnp.where(low_half, nothing, pair_rows)], axis=0
    )


def first_kernel(
    place, own0, own1, other0, other1, rows_ref, far_ref,
    vec_ref, fcb_ref, h1_turned, qkv_ref, att_ref, wq_out0, wq_out1,
    wq, h1, qvb, small, sems,
):
    sources = (own0, own1, other0, other1)

    def work(source, index, chip, half):
        pltpu.make_async_copy(
            source.at[index, pl.ds(144, 16)], small.at[2 * chip + half], sems.at[2]
        ).start()

    each_piece(place, 0, sources, work)
    for half in range(2):
        bring_qkv_weight(place, sources, half, wq.at[half], sems.at[half])
    normed, _ = normed_rows(rows_ref[...].astype(F32))
    wait_all(small, sems.at[2])
    spread = small[...].astype(F32)
    vec_ref[...] = jnp.sum(spread.reshape(2, 16, 16, BLOCK), axis=1)
    qvb[...] = jnp.sum(spread.reshape(4, 8, 16, BLOCK), axis=1)
    lines = jnp.sum(spread.reshape(8, 4, 16, BLOCK), axis=1)
    for block in range(4):
        fcb_ref[block] = jnp.concatenate([lines[2 * block, 7:8], lines[2 * block + 1, 7:8]], axis=1)
    low = (normed * row_of(vec_ref, 0) + row_of(vec_ref, 1)).astype(BF)
    h1[...] = low
    h1_turned[...] = low.T

    def one_side(side, _):
        wait_all(wq.at[side], sems.at[side])
        for half, target in enumerate((wq_out0, wq_out1)):

            @pl.when(side == half)
            def _(half=half, target=target):
                pltpu.make_async_copy(wq.at[half], target, sems.at[3 + half]).start()

        bias = jnp.concatenate(
            [qvb[side, 6:7, :], jnp.zeros((1, BLOCK), F32), qvb[2 + side, 6:7, :]], axis=1
        )
        qkv_ref[side] = (dot(h1[...], wq[side]) + bias).astype(BF)
        return 0

    lax.fori_loop(0, 2, one_side, 0)
    length = far_ref.shape[1]
    low_half = lax.broadcasted_iota(jnp.int32, (length, 128), 1) < 64

    def one_image(image, _):
        here = pl.ds(pl.multiple_of(image * length, 32), length)
        far = far_ref[image]
        for pair in range(HEADS // 2):
            side, at = pair // 3, 128 * (pair % 3)
            queries = two_heads(qkv_ref[side, here, at : at + 128] * jnp.asarray(0.125, BF), low_half)
            key_rows = qkv_ref[side, here, BLOCK + at : BLOCK + at + 128]
            values = qkv_ref[side, here, 2 * BLOCK + at : 2 * BLOCK + at + 128]
            both = dot(queries, key_rows, 1, 1)
            probs = []
            for head in range(2):
                scores = both[length * head : length * (head + 1)] - SLOPES[2 * pair + head] * far
                shifted = jnp.exp(scores - jnp.max(scores, axis=-1, keepdims=True))
                share = shifted * (1.0 / jnp.sum(shifted, axis=-1, keepdims=True))
                probs.append(share.astype(BF))
            result = dot(jnp.concatenate(probs, axis=0), values)
            att_ref[here, 128 * pair : 128 * (pair + 1)] = jnp.where(
                low_half, result[:length], result[length:]
            ).astype(BF)
        return 0

    lax.fori_loop(0, far_ref.shape[0], one_image, 0)
    wait_all(wq_out0, sems.at[3])
    wait_all(wq_out1, sems.at[4])


def at_slot(target, slot, work):
    if not isinstance(target, tuple):
        work(target, slot)
        return

    @pl.when(slot >= 8)
    def _():
        work(target[0], slot - 8)

    @pl.when(slot < 8)
    def _():
        work(target[1], slot)


def give_rows(place, tables, total, keep_ref, send_ref, extra=None, lanes=slice(None)):
    for group in range(1 if extra is None else 4):
        below = None if extra is None else extra(group)

        def one_chip(index, _, group=group, below=below):
            chip = 4 * group + index
            for which, target in enumerate((keep_ref, send_ref)):
                owner = place[48] if which == 0 else 1 - place[48]
                share = total[pl.ds(pl.multiple_of(48 * chip + 24 * owner, 8), 24), :]
                if below is not None:
                    share = jnp.concatenate([share, below], axis=0)

                def put(ref, slot, share=share):
                    ref[slot, :, lanes] = share.astype(BF)

                at_slot(target, place[tables[which] + chip], put)
            return 0

        lax.fori_loop(0, CHIPS if extra is None else 4, one_chip, 0)


def stack_rows(rows):
    blank = jnp.zeros_like(next(row for row in rows if row is not None))
    rows = [blank if row is None else row for row in rows]
    return jnp.concatenate(rows + [blank] * (8 - len(rows)), axis=0)


def sum_rows(values):
    return jnp.sum(values.astype(F32), axis=0, keepdims=True)


def mlp_kernel(
    place, counts, a0, a1, a2, a3, b0, b1, b2, b3, att_far, rows_far, gout_far, vec_ref, fcb_ref,
    out_ref, glow_ref, keep1_ref, send1_ref, sums_ref, fcg, keep2, upper2, lower2, wo_out,
    w1, w2, wo, att_ref, rows_ref, gout_ref, h2, h2_turned, normed, total, gh2, product1, product2,
    stage, scales, sems1, sems2, sems,
):
    step = pl.program_id(0)
    wide = 2 * BLOCK
    core, z = place[48], place[50]
    block_of = lambda step: lax.rem(z + 4 - step, 4)
    block = block_of(step)
    gain = row_of(vec_ref, 3)
    loads = [
        pltpu.make_async_copy(source, target, sems.at[3 + index])
        for index, (source, target) in enumerate(
            ((att_far, att_ref), (rows_far, rows_ref), (gout_far, gout_ref))
        )
    ]

    @pl.when(step == 0)
    def _():
        bring_out_weight(place, (b0, b1, b2, b3), wo, sems.at[2], 144)
        loads[0].start()
        loads[1].start()
        loads[2].start()

        def one_block(later, _):
            column = block_of(later)
            for first, here in ((0, column // 2 == core), (2, column // 2 != core)):

                @pl.when(here)
                def _(first=first):
                    for number in (first, first + 1):

                        def bring(index, _, source=(a0, a1, a2, a3)[number], number=number):
                            spot = pl.ds(pl.multiple_of(place[64 + number * 8 + index] * 48, 16), 48)
                            for part in range(2):
                                start = pl.multiple_of(lax.rem(column, 2) * 96 + 48 * part, 16)
                                pltpu.make_async_copy(
                                    source.at[index, pl.ds(start, 48)],
                                    w1.at[column, spot, pl.ds(BLOCK * part, BLOCK)],
                                    sems1.at[column],
                                ).start()
                            return 0

                        lax.fori_loop(0, 8, bring, 0)

            for number, source in enumerate((b0, b1, b2, b3)):
                half = core if number < 2 else 1 - core
                for index in (later, jnp.where(later < 2, 4 + later, 9 - later)):
                    chip = place[144 + number * 8 + index]
                    spot = pl.ds(pl.multiple_of(chip * 192 + half * 96, 16), 96)
                    for part in range(2):
                        pltpu.make_async_copy(
                            source.at[index, pl.ds(96 * part, 96)],
                            w2.at[spot, pl.ds(BLOCK * part, BLOCK)],
                            sems2.at[column],
                        ).start()
            return 0

        lax.fori_loop(0, 4, one_block, 0)
        wait_all(wo, sems.at[2])
        pltpu.make_async_copy(wo, wo_out, sems.at[2]).start()
        bias = row_of(vec_ref, 2)
        loads[0].wait()
        loads[1].wait()
        for part in range(2):
            lanes = slice(BLOCK * part, BLOCK * (part + 1))
            total[:, lanes] = rows_ref[:, lanes].astype(F32) + dot(att_ref[...], wo[part]) + bias[:, lanes]
        normal, scale = normed_rows(total[...])
        normed[...] = normal
        scales[...] = jnp.broadcast_to(scale, scales.shape)
        low = (normal * gain + row_of(vec_ref, 4)).astype(BF)
        h2[...] = low
        h2_turned[...] = low.T
        total[...] += row_of(vec_ref, 5)
        gh2[...] = jnp.zeros_like(gh2)
        loads[2].wait()

    wait_all(w1.at[block], sems1.at[block])
    hidden = dot(h2[...], w1[block]) + fcb_ref[block]
    rows_of = pl.ds(pl.multiple_of(block * wide, wide), wide)
    wait_all(w2.at[rows_of], sems2.at[block])
    gactivated = dot(gout_ref[...], w2[rows_of, :], 1, 1)
    cumulative, slope = gelu_parts(hidden)
    activated = (hidden * cumulative).astype(BF)
    ghidden = (gactivated * slope).astype(BF)
    product1[...] = dot(h2_turned[...], ghidden)
    product2[...] = dot(activated, gout_ref[...], 0, 0)
    total[...] += dot(activated, w2[rows_of, :])
    gh2[...] += dot(ghidden, w1[block], 1, 1)
    fcg[block] = stack_rows([None, None, None, sum_rows(ghidden)])
    give_rows(place, LARGE, product1, keep1_ref, send1_ref)
    for pair in range(4):
        chip = 4 * block + pair
        for which, target in enumerate((keep2, (upper2, lower2))):
            owner = place[48] if which == 0 else 1 - place[48]
            start = pl.multiple_of(192 * pair + 96 * owner, 8)
            stage[which, chip] = product2[pl.ds(start, 96), :].astype(BF)

            def send(ref, slot, which=which, chip=chip):
                sem = sems.at[1 if ref is upper2 else 6 if ref is lower2 else 0]
                pltpu.make_async_copy(stage.at[which, chip], ref.at[slot], sem).start()

            at_slot(target, place[LARGE[which] + chip], send)

    @pl.when(step == pl.num_programs(0) - 1)
    def _():
        length = out_ref.shape[0] // 4
        row_index = lax.broadcasted_iota(jnp.int32, (length, 1), 0)
        for image in range(4):
            rows = slice(length * image, length * (image + 1))
            value = total[rows, :]
            out_ref[rows, :] = jnp.where(row_index < counts[image], value, 0.0).astype(BF)
        whole = gh2[...]
        gout = gout_ref[...].astype(F32)
        gresid = gout + norm_back(whole * gain, normed[...], scales[:, 0:1])
        low = gresid.astype(BF)
        glow_ref[...] = low
        sums_ref[...] = stack_rows(
            [sum_rows(whole * normed[...]), sum_rows(whole), sum_rows(gout), None, sum_rows(low)]
        )
        wait_all(wo, sems.at[2])
        wait_all(keep2, sems.at[0])
        wait_all(upper2, sems.at[1])
        wait_all(lower2, sems.at[6])


def attention_back_kernel(side, wo, qkv_ref, far_ref, glow_ref, gqkv_ref):
    low = glow_ref[...]
    mine = slice(BLOCK * side, BLOCK * (side + 1))
    gatt = (
        dot(low[:, :BLOCK], wo[0, mine, :], 1, 1) + dot(low[:, BLOCK:], wo[1, mine, :], 1, 1)
    ).astype(BF)
    length = low.shape[0]
    low_half = lax.broadcasted_iota(jnp.int32, (length, 128), 1) < 64
    far = far_ref[0]
    for pair in range(3):
        at = 128 * pair
        queries = qkv_ref[0, :, at : at + 128] * jnp.asarray(0.125, BF)
        key_rows = two_heads(qkv_ref[0, :, BLOCK + at : BLOCK + at + 128], low_half)
        values = two_heads(qkv_ref[0, :, 2 * BLOCK + at : 2 * BLOCK + at + 128], low_half)
        grads = gatt[:, at : at + 128]
        both = dot(key_rows, queries, 1, 1)
        gboth = dot(values, grads, 1, 1)
        probs, gscores = [], []
        for head in range(2):
            rows = slice(length * head, length * (head + 1))
            scores = both[rows] - SLOPES[6 * side + 2 * pair + head] * far
            shifted = jnp.exp(scores - jnp.max(scores, axis=0, keepdims=True))
            share = shifted * (1.0 / jnp.sum(shifted, axis=0, keepdims=True))
            weighted = share * gboth[rows]
            probs.append(share.astype(BF))
            inner = jnp.sum(weighted, axis=0, keepdims=True)
            gscores.append((weighted - share * inner).astype(BF))
        probs, gscores = jnp.concatenate(probs, axis=0), jnp.concatenate(gscores, axis=0)
        gvalues = dot(probs, grads)
        gkeys = dot(gscores, queries)
        gqkv_ref[:, at : at + 128] = (dot(gscores, key_rows, 0, 0) * 0.125).astype(BF)
        for which, result in ((1, gkeys), (2, gvalues)):
            gqkv_ref[:, which * BLOCK + at : which * BLOCK + at + 128] = jnp.where(
                low_half, result[:length], result[length:]
            ).astype(BF)


def qkv_grad_kernel(
    place, h1_turned, gqkv_ref, wq_ref, att_ref, glow_ref, gh1_ref, sums_ref, keep_ref, upper_ref, lower_ref,
    product, product_out,
):
    third, wide = gqkv_ref.shape[1], glow_ref.shape[1]
    product[...] = dot(h1_turned[...], gqkv_ref[...])
    product_out[...] = dot(att_ref[...], glow_ref[...], 0, 0)
    gh1_ref[...] = dot(gqkv_ref[...], wq_ref[...], 1, 1)
    sums_ref[...] = sum_rows(gqkv_ref[...])
    send = upper_ref, lower_ref
    give_rows(place, SMALL, product, keep_ref, send, lanes=slice(0, third))
    give_rows(place, SMALL, product_out, keep_ref, send, lanes=slice(third, third + wide))


def input_kernel(
    place, h1_turned, gqkv_ref, wq_ref, before_ref, mlp_ref, fcg_ref, rows_ref, vec_ref, glow_ref, gh1_ref,
    ginput_ref, keep_ref, upper_ref, lower_ref, product,
):
    product[...] = dot(h1_turned[...], gqkv_ref[...])
    sums = sum_rows(gqkv_ref[...])
    gradient = gh1_ref[...] + dot(gqkv_ref[...], wq_ref[...], 1, 1)
    normed, scale = normed_rows(rows_ref[...].astype(F32))
    ginput_ref[...] = (
        glow_ref[...].astype(F32) + norm_back(gradient * row_of(vec_ref, 0), normed, scale)
    ).astype(BF)
    gain, shift = sum_rows(gradient * normed), sum_rows(gradient)
    first, last = slice(0, BLOCK), slice(2 * BLOCK, 3 * BLOCK)
    biases = before_ref[:, first], sums[:, first], before_ref[:, last], sums[:, last]

    def below(group):
        lanes = slice(BLOCK * (group // 2), BLOCK * (group // 2 + 1))
        own = stack_rows([gain[:, lanes], shift[:, lanes], biases[group]])
        return jnp.concatenate([mlp_ref[...] + fcg_ref[group], own], axis=1)

    give_rows(place, SMALL, product, keep_ref, (upper_ref, lower_ref), below)


def add_up(parts):
    return sum(part.astype(F32) for part in parts)


def give_vector(target, line, device):
    count, columns = target.shape[0], line.shape[1]
    start = lax.rem(device, columns // count) * count
    moved = pltpu.roll(line, lax.rem(columns - start, columns), 1)
    target[...] = moved[:, :count].reshape(count)


def last_kernel(place, *refs):
    sources, (qkv_out, out_out), smalls = refs[:12], refs[12:14], refs[14:]
    total_a = add_up([source[0] for source in sources[:6]])
    total_c = add_up([source[0] for source in sources[6:]])
    for part in range(3):
        lanes = slice(BLOCK * part, BLOCK * (part + 1))
        qkv_out[:, 2 * BLOCK * part : 2 * BLOCK * part + BLOCK] = total_a[:, lanes]
        qkv_out[:, 2 * BLOCK * part + BLOCK : 2 * BLOCK * (part + 1)] = total_c[:24, lanes]
    out_out[...] = total_a[:, 3 * BLOCK :]
    device = place[49]
    for line, target in enumerate(smalls[:3]):
        give_vector(target, total_c[24 + line : 25 + line, 2 * BLOCK :], device)
    for line, target in enumerate(smalls[3:]):
        give_vector(target, total_c[24 + line : 25 + line, : 2 * BLOCK], device)


def after(value, *others):
    return lax.optimization_barrier((value,) + others)[0]


class Links:
    def __init__(self, depth):
        self.depth = depth

        def table(move):
            pairs = []
            for z in range(depth):
                for x in range(2):
                    for y in range(2):
                        for c in range(2):
                            nz, nx, ny, nc = move(z, x, y, c)
                            source = (z * 2 + x) * 4 + y * 2 + c
                            pairs.append((source, ((nz % depth) * 2 + nx) * 4 + ny * 2 + nc))
            return pairs

        self.ups = {step: table(lambda z, x, y, c: (z + step, x, y, c)) for step in (1, 2, 3)}
        self.first = table(lambda z, x, y, c: (z, x, 1 - y, c) if c else (z, 1 - x, y, c))
        self.second = table(lambda z, x, y, c: (z, 1 - x, y, c) if c else (z, x, 1 - y, c))
        self.across = table(lambda z, x, y, c: (z, 1 - x, 1 - y, c))
        self.cores = table(lambda z, x, y, c: (z, x, y, 1 - c))
        self.near = table(lambda z, x, y, c: (z ^ 1, x, y, c))
        self.far = table(lambda z, x, y, c: (z ^ 2, x, y, c))

    def move(self, value, pairs):
        return lax.ppermute(value, AXES, pairs)

    def spots(self):
        dp, fsdp = lax.axis_index("dp"), lax.axis_index("fsdp")
        z, x, y, core = dp // 2, dp % 2, fsdp // 2, fsdp % 2

        def chip(c, flip1, flip2, step):
            flip_x = jnp.where(c == 0, flip1, flip2)
            flip_y = jnp.where(c == 0, flip2, flip1)
            return (((z - step) % self.depth) * 2 + (x ^ flip_x)) * 2 + (y ^ flip_y)

        index = jnp.arange(32, dtype=jnp.int32)
        whose = jnp.where(index < 16, core, 1 - core)
        flip2 = (index // 8) % 2
        z_first = chip(whose, (index // 4) % 2, flip2, index % 4)
        x_first = chip(whose, index % 2, (index // 2) % 2, (index // 4) % 4)
        chips = jnp.arange(16, dtype=jnp.int32)
        turn_x, turn_y = ((chips // 2) % 2) ^ x, (chips % 2) ^ y
        far_z = (chips // 4) ^ z
        near, wide_step = far_z % 2, far_z // 2

        def slots(order):
            turns = {"x": turn_x, "y": turn_y, "near": near, "far": wide_step}
            return sum(turns[name] * weight for name, weight in zip(order, (8, 4, 2, 1)))

        others = jnp.stack([core, dp * 4 + fsdp, z]).astype(jnp.int32)
        rest = jnp.concatenate([others, jnp.zeros((13,), jnp.int32)])
        tables = []
        for orders in (
            (("y", "x", "near", "far"), ("x", "y", "near", "far")),
            (("y", "near", "x", "far"), ("x", "near", "y", "far")),
        ):
            both = [slots(order) for order in orders]
            tables += [jnp.where(core == 0, both[0], both[1]), jnp.where(core == 0, both[1], both[0])]
        swapped = jnp.where(index % 8 >= 6, 9 - index % 8, index % 4)
        swapped = chip(whose, (index // 4) % 2, flip2, swapped)
        parts = [z_first, tables[0], rest, x_first] + tables[1:] + [swapped]
        return jnp.concatenate(parts).astype(jnp.int32)

    def gather(self, piece_a, piece_b1, piece_b2, inputs, prepare):
        hold = lax.optimization_barrier
        up = lambda value, step: self.move(value, self.ups[step])
        a_one, a_three, b1_two = hold((up(piece_a, 1), up(piece_a, 3), self.move(piece_b1, self.first)))
        b1_two = jnp.stack([piece_b1, b1_two])
        a_two, b1_four = hold((up(a_one, 1), self.move(b1_two, self.second)))
        a_four = jnp.stack([piece_a, a_one, a_two, a_three])
        b1_four = jnp.concatenate([b1_two, b1_four])
        piece_b2 = after(piece_b2, a_two)
        a_rest, b2_one, b2_three = hold((self.move(a_four, self.first), up(piece_b2, 1), up(piece_b2, 3)))
        early = prepare(*after(inputs, a_rest))
        a_eight = jnp.concatenate([a_four, a_rest])
        b2_rest = self.move(jnp.stack([piece_b2, b2_one, b2_three]), self.first)
        a_other, b2_two, b1_one, b2_rest, early = hold(
            (self.move(a_eight, self.second), up(b2_one, 1), up(after(b1_four, a_rest), 1), b2_rest, early)
        )
        b2_seven = jnp.concatenate([jnp.stack([piece_b2, b2_one, b2_two, b2_three]), b2_rest])
        a = self.finish(a_eight, a_other)
        b1 = b1_four, b1_one, up(b1_one, 1), up(b1_four, 3)
        b2_last, b2_across = self.move(b2_two[None], self.first), self.move(b2_two[None], self.across)
        return a, b1, (b2_seven, b2_last, self.move(b2_seven, self.second), b2_across), early

    def gather_end(self, b1, b2, done):
        b1_four, b1_one, b1_two, b1_three = b1
        b2_seven, b2_last, other_seven, other_last = b2
        b2_last, done = lax.optimization_barrier((b2_last, done))
        b2_mine, b1_mine = jnp.concatenate([b2_seven, b2_last]), jnp.concatenate([b1_four, b1_one])
        b2_theirs, b1_theirs = self.move(b2_mine, self.cores), self.move(b1_mine, self.cores)
        b1_two, b1_three, other_seven, other_last, done = lax.optimization_barrier(
            (b1_two, b1_three, other_seven, other_last, done)
        )
        b2_rest, b1_rest = jnp.concatenate([other_seven, other_last]), jnp.concatenate([b1_two, b1_three])
        b1 = b1_mine, b1_rest, b1_theirs, self.move(b1_rest, self.cores)
        return done, b1, (b2_mine, b2_rest, b2_theirs, self.move(b2_rest, self.cores))

    def finish(self, eight, rest):
        return (eight, rest, self.move(eight, self.cores), self.move(rest, self.cores))

    def fold(self, state):
        left = 32 >> (len(state) - 1)
        return add_up([part[left // 2 : left] for part in state]).astype(BF)

def full_pieces(full, blocks):
    split = full.reshape((CHIPS, 48) + full.shape[1:])
    split = split.transpose(3, 0, 2, 1, 4) if full.shape[1] == blocks else split.transpose(2, 0, 3, 1, 4)
    return split.reshape(2 * CHIPS, blocks * 48, BLOCK)


STILL = [
    16 * core + ((-step % 4) * 2 + (flip2 if core else flip1)) * 2 + (flip1 if core else flip2)
    for core in range(2)
    for flip2 in range(2)
    for flip1 in range(2)
    for step in range(4)
]


STILL_LAST = [STILL[8 * array + index] for array in range(4) for index in (0, 1, 2, 3, 4, 5, 7, 6)]


def eights(pieces, order=None):
    if order is not None:
        pieces = jnp.stack([pieces[index] for index in order])
    return tuple(pieces[8 * index : 8 * (index + 1)] for index in range(4))


def placed(vector, device, per_row):
    start = (device % per_row) * vector.shape[0]
    return lax.dynamic_update_slice(jnp.zeros((BLOCK,), vector.dtype), vector, (start,))


def shards(
    mesh_shape,
    patches,
    counts,
    positions,
    ln1_gain,
    ln1_bias,
    qkv_weight,
    qv_bias,
    out_weight,
    out_bias,
    ln2_gain,
    ln2_bias,
    fc1_weight,
    fc1_bias,
    fc2_weight,
    fc2_bias,
    cotangent,
):
    images, length, width = patches.shape
    padded = (length + 31) // 32 * 32
    rows = images * padded
    hidden_width = fc1_weight.shape[1]
    devices = mesh_shape["dp"] * mesh_shape["fsdp"]
    by_hand = devices == 2 * CHIPS and mesh_shape["fsdp"] == 4
    small_parts = (ln1_gain, ln1_bias, out_bias, ln2_gain, ln2_bias, fc2_bias, qv_bias, fc1_bias)

    smem = pl.BlockSpec(memory_space=pltpu.SMEM)
    vmem = pl.BlockSpec(memory_space=pltpu.VMEM)
    anywhere = pl.BlockSpec(memory_space=pltpu.HBM)
    struct = jax.ShapeDtypeStruct

    def prepare(patches, counts, positions, cotangent):
        row_index = jnp.arange(padded, dtype=jnp.int32)
        is_live = row_index[None, :] < counts[:, None]
        pad_rows = ((0, 0), (0, padded - length), (0, 0))
        rows_in = jnp.pad(patches, pad_rows).reshape(rows, width)
        gout = jnp.where(is_live[:, :, None], jnp.pad(cotangent, pad_rows), 0).reshape(rows, width)
        spots = jnp.pad(positions, pad_rows[:2])
        grid_rows = (spots // SIDE).astype(F32)
        grid_cols = (spots % SIDE).astype(F32)
        row_delta = grid_rows[:, :, None] - grid_rows[:, None, :]
        col_delta = grid_cols[:, :, None] - grid_cols[:, None, :]
        distance = jnp.sqrt(row_delta * row_delta + col_delta * col_delta)
        far = jnp.where(is_live[:, None, :], distance, FAR)
        far_turned = jnp.where(is_live[:, :, None], distance, FAR)
        return rows_in, gout, far, far_turned

    if by_hand:
        links = Links(mesh_shape["dp"] // 2)
        place = links.spots()
        core = place[48]
        share = struct((8, 24, BLOCK), BF)
        mine, theirs, lines = pl.pallas_call(
            share_kernel,
            out_shape=(share, share, struct((16, BLOCK), BF)),
            in_specs=[smem] + [vmem] * 11,
            out_specs=(vmem,) * 3,
            name="share",
        )(place, qkv_weight, out_weight, fc1_weight, *small_parts)
        got = links.move(theirs, links.cores)
        pieces = pl.pallas_call(
            pair_kernel,
            out_shape=tuple(struct((height, BLOCK), BF) for height in (160, 192, 240)),
            in_specs=[smem] + [vmem] * 4,
            out_specs=(vmem,) * 3,
            name="pair",
        )(place, mine, got, lines, fc2_weight)
    else:
        links = None
        place = jnp.concatenate(
            [
                jnp.array([chip % CHIPS for chip in STILL], jnp.int32),
                jnp.arange(16, dtype=jnp.int32),
                jnp.zeros((16,), jnp.int32),
                jnp.arange(80, dtype=jnp.int32) % 16,
                jnp.array([chip % CHIPS for chip in STILL_LAST], jnp.int32),
            ]
        )
        whole = [lax.all_gather(part, AXES, axis=0, tiled=True) for part in small_parts]
        lines = []
        for part in whole:
            share = part.shape[0] // 32
            chunks = part.reshape(32, share)
            lines.append(
                jnp.stack([placed(chunks[index], index, BLOCK // share) for index in range(32)])
            )
        lines = jnp.concatenate([jnp.stack(lines, axis=1), jnp.zeros((32, 8, BLOCK), BF)], axis=1)
        lines = lines.reshape(CHIPS, 2, 16, BLOCK).transpose(1, 0, 2, 3).reshape(32, 16, BLOCK)
        whole_qkv = lax.all_gather(qkv_weight, AXES, axis=0, tiled=True)
        whole_out = lax.all_gather(out_weight, AXES, axis=0, tiled=True)
        whole_fc1 = lax.all_gather(fc1_weight, AXES, axis=0, tiled=True)
        whole_fc2 = lax.all_gather(fc2_weight, AXES, axis=0, tiled=True)
        split = whole_fc2.reshape(CHIPS, 2, 96, 2, BLOCK).transpose(1, 0, 3, 2, 4).reshape(32, 192, BLOCK)
        gathered_a = eights(
            jnp.concatenate([full_pieces(whole_qkv.reshape(width, 3, 2, BLOCK), 3), lines], axis=1), STILL
        )
        gathered_b1 = eights(full_pieces(whole_fc1.reshape(width, 2, 4, BLOCK), 4))
        split = whole_fc2.reshape(CHIPS, 2, 96, 2, BLOCK).transpose(1, 0, 3, 2, 4).reshape(32, 192, BLOCK)
        gathered_b2 = eights(
            jnp.concatenate([split, full_pieces(whole_out.reshape(width, 1, 2, BLOCK), 1)], axis=1), STILL_LAST
        )

    if by_hand:
        gathered_a, on_b1, on_b2, early = links.gather(*pieces, (patches, counts, positions, cotangent), prepare)
    else:
        early = prepare(patches, counts, positions, cotangent)
    rows_in, gout, far, far_turned = early

    def call(kernel, operands, out_shape, out_specs, in_specs, flops, mib, vmem_mib, grid, scratch=(), name=None):
        return pl.pallas_call(
            kernel,
            grid=grid,
            out_shape=out_shape,
            in_specs=in_specs,
            out_specs=out_specs,
            scratch_shapes=list(scratch),
            compiler_params=pltpu.CompilerParams(vmem_limit_bytes=vmem_mib * MIB),
            cost_estimate=pl.CostEstimate(
                flops=1, bytes_accessed=1, transcendentals=0
            ),
            name=name,
        )(*operands)

    image_rows = lambda columns: pl.BlockSpec((padded, columns), lambda image: (image, 0))
    image_far = pl.BlockSpec((1, padded, padded), lambda image: (image, 0, 0))
    fixed = lambda *shape: pl.BlockSpec(shape, lambda step: (0,) * len(shape))
    step_rows = lambda columns: pl.BlockSpec((rows, columns), lambda step: (0, step))
    shares = lambda height, columns: struct((CHIPS, height, columns), BF)
    buffer, flag = pltpu.VMEM, pltpu.SemaphoreType.DMA
    low_rows, wide_rows = struct((rows, width), BF), struct((rows, width), F32)
    wide = 2 * BLOCK
    steps = hidden_width // wide
    third = 3 * BLOCK

    def join(value, *others):
        return after(value, *others) if by_hand else value

    vec, fcb, h1_turned, qkv, att, wq_0, wq_1 = pl.pallas_call(
        first_kernel,
        out_shape=(
            struct((2, 16, BLOCK), F32), struct((steps, 1, wide), F32), struct((width, rows), BF),
            struct((2, rows, third), BF), low_rows, struct((width, third), BF), struct((width, third), BF),
        ),
        in_specs=[smem] + [anywhere] * 4 + [vmem] * 2,
        out_specs=(vmem,) * 5 + (anywhere,) * 2,
        scratch_shapes=[
            buffer((2, width, third), BF), buffer((rows, width), BF), buffer((4, 16, BLOCK), F32),
            buffer((32, 16, BLOCK), BF), flag((5,)),
        ],
        compiler_params=pltpu.CompilerParams(vmem_limit_bytes=30 * MIB),
        cost_estimate=pl.CostEstimate(flops=1, bytes_accessed=1, transcendentals=0),
        name="first",
    )(place, *gathered_a, rows_in, far)
    if by_hand:
        att, gathered_b1, gathered_b2 = links.gather_end(on_b1, on_b2, att)

    step_shares = lambda height, columns: pl.BlockSpec((CHIPS, height, columns), lambda step: (0, 0, step))
    still = lambda *shape: pl.BlockSpec(shape, lambda step, place: (0,) * len(shape))
    turned_shares = pl.BlockSpec(
        (CHIPS, 24, wide), lambda step, place: (0, 0, lax.rem(place[50] + 4 - step, 4))
    )
    low_buffer, wide_buffer = buffer((rows, width), BF), buffer((rows, width), F32)
    out, glow, keep_1, send_1, sums, fcg, keep_2, upper_2, lower_2, wo = pl.pallas_call(
        mlp_kernel,
        grid_spec=pltpu.PrefetchScalarGridSpec(
            num_scalar_prefetch=1,
            grid=(steps,),
            in_specs=[smem] + [anywhere] * 11 + [still(2, 16, BLOCK), still(steps, 1, wide)],
            out_specs=(still(rows, width),) * 2
            + (turned_shares,) * 2
            + (still(8, wide), still(steps, 8, wide))
            + (anywhere,) * 4,
            scratch_shapes=[
                buffer((steps, width, wide), BF), buffer((hidden_width, width), BF), buffer((2, width, BLOCK), BF),
                low_buffer, low_buffer, low_buffer, low_buffer, buffer((width, rows), BF),
                wide_buffer, wide_buffer, wide_buffer, buffer((width, wide), F32), buffer((width, wide), F32),
                buffer((2, CHIPS, 96, wide), BF), buffer((rows, 128), F32), flag((steps,)), flag((steps,)), flag((7,)),
            ],
        ),
        out_shape=(low_rows, low_rows)
        + (shares(24, hidden_width),) * 2
        + (struct((8, wide), F32), struct((steps, 8, wide), F32))
        + (shares(96, wide),)
        + (struct((8, 96, wide), BF),) * 2
        + (struct((2, width, BLOCK), BF),),
        compiler_params=pltpu.CompilerParams(vmem_limit_bytes=60 * MIB),
        cost_estimate=pl.CostEstimate(flops=1, bytes_accessed=1, transcendentals=0),
        name="mlp",
    )(place, counts, *gathered_b1, *gathered_b2, att, rows_in, gout, vec, fcb)

    if by_hand:
        state_2 = keep_2, links.move(upper_2, links.cores)

    def attention_back(side, gradient):
        return call(
            lambda *refs: attention_back_kernel(side, *refs),
            (wo, qkv, far_turned, gradient),
            struct((rows, third), BF),
            image_rows(third),
            [
                fixed(2, width, BLOCK), pl.BlockSpec((1, padded, third), lambda image: (side, image, 0)),
                image_far, image_rows(width),
            ],
            8 * rows * 256 * width,
            8,
            20,
            grid=(images,),
            name="attention_back",
        )

    part_2 = glow
    if by_hand:
        part_2 = add_up([keep_2[8:], state_2[1]]).astype(BF)
        lower_2, send_1 = after((lower_2, send_1), part_2)
        state_2 = keep_2, links.move(lower_2, links.cores), links.move(part_2, links.second)
        state_1 = keep_1, links.move(send_1, links.cores)
    gqkv_0 = attention_back(0, join(glow, part_2))
    if by_hand:
        state_1, gqkv_0 = lax.optimization_barrier((state_1, gqkv_0))
        state_1 += (links.move(links.fold(state_1), links.second),)

    def grad_call(kernel, operands, out_shape, scratch, name):
        return pl.pallas_call(
            kernel,
            out_shape=out_shape,
            in_specs=[smem] + [vmem] * (len(operands) - 1),
            out_specs=(vmem,) * len(out_shape),
            scratch_shapes=list(scratch),
            compiler_params=pltpu.CompilerParams(vmem_limit_bytes=28 * MIB),
            cost_estimate=pl.CostEstimate(flops=1, bytes_accessed=1, transcendentals=0),
            name=name,
        )(*operands)

    half_shares = lambda height, columns: (struct((8, height, columns), BF),) * 2
    gh1, sums_0, keep_a, upper_a, lower_a = grad_call(
        qkv_grad_kernel,
        (place, h1_turned, gqkv_0, wq_0, att, glow),
        (wide_rows, struct((1, third), F32), shares(24, third + wide)) + half_shares(24, third + wide),
        (buffer((width, third), F32), buffer((width, wide), F32)),
        "qkv_grad",
    )
    parts = gh1
    if by_hand:
        got_a = links.move(upper_a, links.cores)
        state_2, got_a, gh1 = lax.optimization_barrier((state_2, got_a, gh1))
        parts = links.fold(state_2), add_up([keep_a[8:], got_a]).astype(BF)
        state_2 += (links.move(parts[0], links.near),)
        lower_a = after(lower_a, parts)
        state_a = keep_a, links.move(lower_a, links.cores), links.move(parts[1], links.second)

    gqkv_1 = attention_back(1, join(glow, gh1, parts))
    ginput, keep_c, upper_c, lower_c = grad_call(
        input_kernel,
        (place, h1_turned, gqkv_1, wq_1, sums_0, sums, fcg, rows_in, vec, glow, gh1),
        (low_rows, shares(32, third)) + half_shares(32, third),
        (buffer((width, third), F32),),
        "input_grad",
    )

    def cut(value):
        return value.reshape(images, padded, width)[:, :length]

    if by_hand:
        fold, move = links.fold, links.move

        state_c = keep_c, move(upper_c, links.cores)
        rest_c = move(after(lower_c, keep_c), links.cores)
        state_1 = after(state_1, keep_c)
        part = fold(state_1)
        state_1 += (move(part, links.near),)
        keep_c, got_c = after(state_c, part)
        part = add_up([keep_c[8:], got_c]).astype(BF)
        state_c = keep_c, rest_c, move(part, links.second)
        state_2, state_a, out, ginput = after((state_2, state_a, out, ginput), part)
        out, ginput = cut(out), cut(ginput)
        state_2, state_a, out, ginput = after((state_2, state_a, out, ginput))
        parts = fold(state_2), fold(state_a)
        state_2 += (move(parts[0], links.first),)
        state_a += (move(parts[1], links.first),)
        part = fold(after(state_c, parts))
        state_c += (move(part, links.first),)
        state_1, out, ginput = after((state_1, out, ginput), part)
        part = fold(state_1)
        state_1 += (move(part, links.first),)
        state_2 = after(state_2, part)
        part = fold(state_2)
        state_2 += (move(part, links.far),)
        state_a = after(state_a, part)
        part = fold(state_a)
        state_a += (move(part, links.near),)
        part = fold(after(state_c, part))
        state_c += (move(part, links.near),)
        state_1 = after(state_1, part)
        part = fold(state_1)
        state_1 += (move(part, links.far),)
        state_a = after(state_a, part)
        part = fold(state_a)
        state_a += (move(part, links.far),)
        part = fold(after(state_c, part))
        state_c += (move(part, links.far),)
        state_2 = after(state_2, part)
        mine_2 = add_up([part[0] for part in state_2])
        state_1 = after(state_1, mine_2)
        mine_1 = add_up([part[0] for part in state_1])
        own_slot = lambda part: pl.BlockSpec((1,) + part.shape[1:], lambda step: (0, 0, 0))
        heights, counts_out = ((24, 3 * width), (24, width)), (24, 24, 48, 24, 24, 24, 96, 24)
        (
            qkv_grad, out_grad, ln1_gain_grad, ln1_bias_grad, qv_bias_grad,
            ln2_gain_grad, ln2_bias_grad, fc2_bias_grad, fc1_bias_grad, out_bias_grad,
        ) = pl.pallas_call(
            last_kernel,
            grid=(1,),
            out_shape=tuple(struct(shape, F32) for shape in heights + tuple((count,) for count in counts_out)),
            in_specs=[smem] + [own_slot(part) for part in state_a + state_c],
            out_specs=tuple(fixed(*shape) for shape in heights)
            + tuple(pl.BlockSpec((count,), lambda step: (0,)) for count in counts_out),
            compiler_params=pltpu.CompilerParams(vmem_limit_bytes=30 * MIB),
            name="last",
        )(place, *state_a, *state_c)
        return (
            out, ginput, ln1_gain_grad, ln1_bias_grad, qkv_grad, qv_bias_grad, out_grad, out_bias_grad,
            ln2_gain_grad, ln2_bias_grad, mine_1, fc1_bias_grad, mine_2, fc2_bias_grad,
        )

    both_a, both_c, both_1, both_2 = (
        jnp.stack(pair, axis=1).astype(F32)
        for pair in (
            (keep_a, jnp.concatenate([lower_a, upper_a])),
            (keep_c, jnp.concatenate([lower_c, upper_c])),
            (keep_1, send_1),
            (keep_2, jnp.concatenate([lower_2, upper_2])),
        )
    )
    heads = jnp.stack(
        [both.reshape(CHIPS, 2, 24, 3, BLOCK) for both in (both_a[..., :third], both_c[:, :, :24])], axis=4
    )

    def vector(lines, count):
        columns = lines.shape[-1]
        return lines.reshape(32 * count // columns, -1, columns)[:, 0].reshape(-1)

    small_c, small_2 = both_c[:, :, 24:, 2 * BLOCK :], both_c[:, :, 24:, : 2 * BLOCK]
    totals = (
        vector(small_c[:, :, 0], 24),
        vector(small_c[:, :, 1], 24),
        heads.reshape(width, 3 * width),
        vector(small_c[:, :, 2], 48),
        both_a[..., third:].reshape(width, width),
        vector(small_2[:, :, 4], 24),
        vector(small_2[:, :, 0], 24),
        vector(small_2[:, :, 1], 24),
        both_1.reshape(width, hidden_width),
        vector(small_2[:, :, 3], 96),
        both_2.reshape(hidden_width, width),
        vector(small_2[:, :, 2], 24),
    )
    return (cut(out), cut(ginput)) + tuple(
        lax.psum_scatter(total, AXES, scatter_dimension=0, tiled=True) for total in totals
    )


def solution(mesh):
    rows = P(AXES, None, None)
    table = P(AXES, None)
    line = P(AXES)
    in_specs = (
        rows, line, table, line, line, table, line, table, line, line, line, table, line, table, line, rows,
    )
    out_specs = (
        rows, rows, line, line, table, line, table, line, line, line, table, line, table, line,
    )
    mesh_shape = dict(mesh.shape)

    def body(*arrays):
        return shards(mesh_shape, *arrays)

    return jax.shard_map(body, mesh=mesh, in_specs=in_specs, out_specs=out_specs, check_vma=False)
```

```python
import math

import jax
import jax.numpy as jnp
import numpy as np
from jax import lax
from jax.experimental import pallas as pl
from jax.experimental.pallas import tpu as pltpu
from jax.sharding import PartitionSpec as P

HEADS = 12
SIDE = 16
EPSILON = 1e-06
AXES = ("dp", "fsdp")
FAR = 1e30
CHIPS = 16
BLOCK = 384
SMALL, LARGE = (32, 96), (112, 128)
MIB = 1024 * 1024

BF = jnp.bfloat16
F32 = jnp.float32


def power_slopes(number):
    first_slope = 2.0 ** (-8.0 / number)
    return [first_slope ** (index + 1) for index in range(number)]


def slope_list(heads_total):
    lower_power = 2 ** int(math.floor(math.log2(heads_total)))
    return (
        power_slopes(lower_power) + power_slopes(2 * lower_power)[0::2][: heads_total - lower_power]
    )


SLOPES = [float(np.float32(slope)) for slope in slope_list(HEADS)]


def dot(left, right, left_dim=1, right_dim=0):
    return lax.dot_general(
        left, right, (((left_dim,), (right_dim,)), ((), ())), preferred_element_type=F32
    )


def normed_rows(values):
    centered = values - jnp.mean(values, axis=-1, keepdims=True)
    scale = lax.rsqrt(jnp.mean(centered * centered, axis=-1, keepdims=True) + EPSILON)
    return centered * scale, scale


def norm_back(grad_normed, normed, scale):
    centered_mean = jnp.mean(grad_normed, axis=-1, keepdims=True)
    projected_mean = jnp.mean(grad_normed * normed, axis=-1, keepdims=True)
    return scale * (grad_normed - centered_mean - normed * projected_mean)


def row_of(vectors_ref, index):
    return jnp.concatenate(
        [vectors_ref[0, index : index + 1, :], vectors_ref[1, index : index + 1, :]], axis=1
    )


def gelu_parts(hidden):
    cumulative = 0.5 + 0.5 * lax.erf(hidden * math.sqrt(0.5))
    bell = jnp.exp(-0.5 * hidden * hidden)
    return cumulative, cumulative + hidden * bell * (1.0 / math.sqrt(2.0 * math.pi))


def share_kernel(place, qkv_ref, out_ref, fc1_ref, *refs):
    smalls, (mine_ref, theirs_ref, lines_ref) = refs[:-3], refs[-3:]
    for target, core in ((mine_ref, place[48]), (theirs_ref, 1 - place[48])):
        starts = [(qkv_ref, 2 * BLOCK * part + BLOCK * core) for part in range(3)]
        starts.append((out_ref, BLOCK * core))
        starts += [(fc1_ref, 4 * BLOCK * core + BLOCK * part) for part in range(4)]
        for block, (source, start) in enumerate(starts):
            target[block] = source[:, pl.ds(pl.multiple_of(start, 128), BLOCK)]
    device = place[49]
    lines = []
    for small in smalls:
        count = small.shape[0]
        line = small[...].astype(F32).reshape(1, count)
        line = jnp.concatenate([line, jnp.zeros((1, BLOCK - count), F32)], axis=1)
        lines.append(pltpu.roll(line, lax.rem(device, BLOCK // count) * count, 1))
    lines_ref[...] = jnp.concatenate(lines + [jnp.zeros((8, BLOCK), F32)], axis=0).astype(BF)


def pair_kernel(place, mine_ref, got_ref, lines_ref, fc2_ref, a_ref, b1_ref, b2_ref):
    swap = place[48] == 1
    for block in range(8):
        mine, got = mine_ref[block].astype(F32), got_ref[block].astype(F32)
        rows = jnp.concatenate([jnp.where(swap, got, mine), jnp.where(swap, mine, got)], axis=0)
        if block < 3:
            a_ref[48 * block : 48 * (block + 1), :] = rows.astype(BF)
        elif block == 3:
            b2_ref[192:240, :] = rows.astype(BF)
        else:
            b1_ref[48 * (block - 4) : 48 * (block - 3), :] = rows.astype(BF)
    b2_ref[0:96, :] = fc2_ref[:, :BLOCK]
    b2_ref[96:192, :] = fc2_ref[:, BLOCK:]
    a_ref[144:160, :] = lines_ref[...]


def each_piece(place, table, sources, work):
    core = place[48]
    for number, source in enumerate(sources):
        half = core if number < 2 else 1 - core

        def bring(index, _, source=source, number=number, half=half):
            work(source, index, place[table + number * 8 + index], half)
            return 0

        lax.fori_loop(0, 8, bring, 0)


def bring_out_weight(place, sources, wo, sem, table):
    def work(source, index, chip, half):
        spot = pl.ds(pl.multiple_of(chip * 48, 16), 48)
        pltpu.make_async_copy(source.at[index, pl.ds(192, 48)], wo.at[half, spot], sem).start()

    each_piece(place, table, sources, work)


def bring_qkv_weight(place, sources, side, wq, sem, part_of=None):
    for first, here in ((0, place[48] == side), (2, place[48] != side)):

        @pl.when(here)
        def _(first=first):
            for number in (first, first + 1):

                def bring(index, _, source=sources[number], number=number):
                    spot = pl.ds(pl.multiple_of(place[number * 8 + index] * 48, 16), 48)
                    for part in range(3):
                        pltpu.make_async_copy(
                            source.at[index, pl.ds(48 * part, 48)],
                            wq.at[spot, pl.ds(BLOCK * part, BLOCK)] if part_of is None else wq.at[part, spot],
                            sem if part_of is None else part_of.at[part],
                        ).start()
                    return 0

                lax.fori_loop(0, 8, bring, 0)


def wait_all(buffer, sem):
    pltpu.make_async_copy(buffer, buffer, sem).wait()


def two_heads(pair_rows, low_half):
    nothing = jnp.zeros_like(pair_rows)
    return jnp.concatenate(
        [jnp.where(low_half, pair_rows, nothing), jnp.where(low_half, nothing, pair_rows)], axis=0
    )


def first_kernel(
    place, own0, own1, other0, other1, rows_ref, far_ref,
    vec_ref, fcb_ref, h1_turned, qkv_ref, att_ref, wq_out0, wq_out1,
    wq, h1, qvb, small, sems,
):
    sources = (own0, own1, other0, other1)

    def work(source, index, chip, half):
        pltpu.make_async_copy(
            source.at[index, pl.ds(144, 16)], small.at[2 * chip + half], sems.at[2]
        ).start()

    each_piece(place, 0, sources, work)
    for half in range(2):
        bring_qkv_weight(place, sources, half, wq.at[half], sems.at[half])
    normed, _ = normed_rows(rows_ref[...].astype(F32))
    wait_all(small, sems.at[2])
    spread = small[...].astype(F32)
    vec_ref[...] = jnp.sum(spread.reshape(2, 16, 16, BLOCK), axis=1)
    qvb[...] = jnp.sum(spread.reshape(4, 8, 16, BLOCK), axis=1)
    lines = jnp.sum(spread.reshape(8, 4, 16, BLOCK), axis=1)
    for block in range(4):
        fcb_ref[block] = jnp.concatenate([lines[2 * block, 7:8], lines[2 * block + 1, 7:8]], axis=1)
    low = (normed * row_of(vec_ref, 0) + row_of(vec_ref, 1)).astype(BF)
    h1[...] = low
    h1_turned[...] = low.T

    def one_side(side, _):
        wait_all(wq.at[side], sems.at[side])
        for half, target in enumerate((wq_out0, wq_out1)):

            @pl.when(side == half)
            def _(half=half, target=target):
                pltpu.make_async_copy(wq.at[half], target, sems.at[3 + half]).start()

        bias = jnp.concatenate(
            [qvb[side, 6:7, :], jnp.zeros((1, BLOCK), F32), qvb[2 + side, 6:7, :]], axis=1
        )
        qkv_ref[side] = (dot(h1[...], wq[side]) + bias).astype(BF)
        return 0

    lax.fori_loop(0, 2, one_side, 0)
    length = far_ref.shape[1]
    low_half = lax.broadcasted_iota(jnp.int32, (length, 128), 1) < 64

    def one_image(image, _):
        here = pl.ds(pl.multiple_of(image * length, 32), length)
        far = far_ref[image]
        for pair in range(HEADS // 2):
            side, at = pair // 3, 128 * (pair % 3)
            queries = two_heads(qkv_ref[side, here, at : at + 128] * jnp.asarray(0.125, BF), low_half)
            key_rows = qkv_ref[side, here, BLOCK + at : BLOCK + at + 128]
            values = qkv_ref[side, here, 2 * BLOCK + at : 2 * BLOCK + at + 128]
            both = dot(queries, key_rows, 1, 1)
            probs = []
            for head in range(2):
                scores = both[length * head : length * (head + 1)] - SLOPES[2 * pair + head] * far
                shifted = jnp.exp(scores - jnp.max(scores, axis=-1, keepdims=True))
                share = shifted * (1.0 / jnp.sum(shifted, axis=-1, keepdims=True))
                probs.append(share.astype(BF))
            result = dot(jnp.concatenate(probs, axis=0), values)
            att_ref[here, 128 * pair : 128 * (pair + 1)] = jnp.where(
                low_half, result[:length], result[length:]
            ).astype(BF)
        return 0

    lax.fori_loop(0, far_ref.shape[0], one_image, 0)
    wait_all(wq_out0, sems.at[3])
    wait_all(wq_out1, sems.at[4])


def at_slot(target, slot, work):
    if not isinstance(target, tuple):
        work(target, slot)
        return

    @pl.when(slot >= 8)
    def _():
        work(target[0], slot - 8)

    @pl.when(slot < 8)
    def _():
        work(target[1], slot)


def give_rows(place, tables, total, keep_ref, send_ref, extra=None, lanes=slice(None)):
    for group in range(1 if extra is None else 4):
        below = None if extra is None else extra(group)

        def one_chip(index, _, group=group, below=below):
            chip = 4 * group + index
            for which, target in enumerate((keep_ref, send_ref)):
                owner = place[48] if which == 0 else 1 - place[48]
                share = total[pl.ds(pl.multiple_of(48 * chip + 24 * owner, 8), 24), :]
                if below is not None:
                    share = jnp.concatenate([share, below], axis=0)

                def put(ref, slot, share=share):
                    ref[slot, :, lanes] = share.astype(BF)

                at_slot(target, place[tables[which] + chip], put)
            return 0

        lax.fori_loop(0, CHIPS if extra is None else 4, one_chip, 0)


def stack_rows(rows):
    blank = jnp.zeros_like(next(row for row in rows if row is not None))
    rows = [blank if row is None else row for row in rows]
    return jnp.concatenate(rows + [blank] * (8 - len(rows)), axis=0)


def sum_rows(values):
    return jnp.sum(values.astype(F32), axis=0, keepdims=True)


def mlp_kernel(
    place, counts, a0, a1, a2, a3, b0, b1, b2, b3, att_far, rows_far, gout_far, vec_ref, fcb_ref,
    out_ref, glow_ref, keep1_ref, send1_ref, sums_ref, fcg, keep2, upper2, lower2, wo_out,
    w1, w2, wo, att_ref, rows_ref, gout_ref, h2, h2_turned, normed, total, gh2, product1, product2,
    stage, scales, sems1, sems2, sems,
):
    step = pl.program_id(0)
    wide = 2 * BLOCK
    core, z = place[48], place[50]
    block_of = lambda step: lax.rem(z + 4 - step, 4)
    block = block_of(step)
    gain = row_of(vec_ref, 3)
    loads = [
        pltpu.make_async_copy(source, target, sems.at[3 + index])
        for index, (source, target) in enumerate(
            ((att_far, att_ref), (rows_far, rows_ref), (gout_far, gout_ref))
        )
    ]

    @pl.when(step == 0)
    def _():
        bring_out_weight(place, (b0, b1, b2, b3), wo, sems.at[2], 144)
        loads[0].start()
        loads[1].start()
        loads[2].start()

        def one_block(later, _):
            column = block_of(later)
            for first, here in ((0, column // 2 == core), (2, column // 2 != core)):

                @pl.when(here)
                def _(first=first):
                    for number in (first, first + 1):

                        def bring(index, _, source=(a0, a1, a2, a3)[number], number=number):
                            spot = pl.ds(pl.multiple_of(place[64 + number * 8 + index] * 48, 16), 48)
                            for part in range(2):
                                start = pl.multiple_of(lax.rem(column, 2) * 96 + 48 * part, 16)
                                pltpu.make_async_copy(
                                    source.at[index, pl.ds(start, 48)],
                                    w1.at[column, spot, pl.ds(BLOCK * part, BLOCK)],
                                    sems1.at[column],
                                ).start()
                            return 0

                        lax.fori_loop(0, 8, bring, 0)

            for number, source in enumerate((b0, b1, b2, b3)):
                half = core if number < 2 else 1 - core
                for index in (later, jnp.where(later < 2, 4 + later, 9 - later)):
                    chip = place[144 + number * 8 + index]
                    spot = pl.ds(pl.multiple_of(chip * 192 + half * 96, 16), 96)
                    for part in range(2):
                        pltpu.make_async_copy(
                            source.at[index, pl.ds(96 * part, 96)],
                            w2.at[spot, pl.ds(BLOCK * part, BLOCK)],
                            sems2.at[column],
                        ).start()
            return 0

        lax.fori_loop(0, 4, one_block, 0)
        wait_all(wo, sems.at[2])
        pltpu.make_async_copy(wo, wo_out, sems.at[2]).start()
        bias = row_of(vec_ref, 2)
        loads[0].wait()
        loads[1].wait()
        for part in range(2):
            lanes = slice(BLOCK * part, BLOCK * (part + 1))
            total[:, lanes] = rows_ref[:, lanes].astype(F32) + dot(att_ref[...], wo[part]) + bias[:, lanes]
        normal, scale = normed_rows(total[...])
        normed[...] = normal
        scales[...] = jnp.broadcast_to(scale, scales.shape)
        low = (normal * gain + row_of(vec_ref, 4)).astype(BF)
        h2[...] = low
        h2_turned[...] = low.T
        total[...] += row_of(vec_ref, 5)
        gh2[...] = jnp.zeros_like(gh2)
        loads[2].wait()

    wait_all(w1.at[block], sems1.at[block])
    hidden = dot(h2[...], w1[block]) + fcb_ref[block]
    rows_of = pl.ds(pl.multiple_of(block * wide, wide), wide)
    wait_all(w2.at[rows_of], sems2.at[block])
    gactivated = dot(gout_ref[...], w2[rows_of, :], 1, 1)
    cumulative, slope = gelu_parts(hidden)
    activated = (hidden * cumulative).astype(BF)
    ghidden = (gactivated * slope).astype(BF)
    product1[...] = dot(h2_turned[...], ghidden)
    product2[...] = dot(activated, gout_ref[...], 0, 0)
    total[...] += dot(activated, w2[rows_of, :])
    gh2[...] += dot(ghidden, w1[block], 1, 1)
    fcg[block] = stack_rows([None, None, None, sum_rows(ghidden)])
    give_rows(place, LARGE, product1, keep1_ref, send1_ref)
    for pair in range(4):
        chip = 4 * block + pair
        for which, target in enumerate((keep2, (upper2, lower2))):
            owner = place[48] if which == 0 else 1 - place[48]
            start = pl.multiple_of(192 * pair + 96 * owner, 8)
            stage[which, chip] = product2[pl.ds(start, 96), :].astype(BF)

            def send(ref, slot, which=which, chip=chip):
                sem = sems.at[1 if ref is upper2 else 6 if ref is lower2 else 0]
                pltpu.make_async_copy(stage.at[which, chip], ref.at[slot], sem).start()

            at_slot(target, place[LARGE[which] + chip], send)

    @pl.when(step == pl.num_programs(0) - 1)
    def _():
        length = out_ref.shape[0] // 4
        row_index = lax.broadcasted_iota(jnp.int32, (length, 1), 0)
        for image in range(4):
            rows = slice(length * image, length * (image + 1))
            value = total[rows, :]
            out_ref[rows, :] = jnp.where(row_index < counts[image], value, 0.0).astype(BF)
        whole = gh2[...]
        gout = gout_ref[...].astype(F32)
        gresid = gout + norm_back(whole * gain, normed[...], scales[:, 0:1])
        low = gresid.astype(BF)
        glow_ref[...] = low
        sums_ref[...] = stack_rows(
            [sum_rows(whole * normed[...]), sum_rows(whole), sum_rows(gout), None, sum_rows(low)]
        )
        wait_all(wo, sems.at[2])
        wait_all(keep2, sems.at[0])
        wait_all(upper2, sems.at[1])
        wait_all(lower2, sems.at[6])


def attention_back_kernel(side, wo, qkv_ref, far_ref, glow_ref, gqkv_ref):
    low = glow_ref[...]
    mine = slice(BLOCK * side, BLOCK * (side + 1))
    gatt = (
        dot(low[:, :BLOCK], wo[0, mine, :], 1, 1) + dot(low[:, BLOCK:], wo[1, mine, :], 1, 1)
    ).astype(BF)
    length = low.shape[0]
    low_half = lax.broadcasted_iota(jnp.int32, (length, 128), 1) < 64
    far = far_ref[0]
    for pair in range(3):
        at = 128 * pair
        queries = qkv_ref[0, :, at : at + 128] * jnp.asarray(0.125, BF)
        key_rows = two_heads(qkv_ref[0, :, BLOCK + at : BLOCK + at + 128], low_half)
        values = two_heads(qkv_ref[0, :, 2 * BLOCK + at : 2 * BLOCK + at + 128], low_half)
        grads = gatt[:, at : at + 128]
        both = dot(key_rows, queries, 1, 1)
        gboth = dot(values, grads, 1, 1)
        probs, gscores = [], []
        for head in range(2):
            rows = slice(length * head, length * (head + 1))
            scores = both[rows] - SLOPES[6 * side + 2 * pair + head] * far
            shifted = jnp.exp(scores - jnp.max(scores, axis=0, keepdims=True))
            share = shifted * (1.0 / jnp.sum(shifted, axis=0, keepdims=True))
            weighted = share * gboth[rows]
            probs.append(share.astype(BF))
            inner = jnp.sum(weighted, axis=0, keepdims=True)
            gscores.append((weighted - share * inner).astype(BF))
        probs, gscores = jnp.concatenate(probs, axis=0), jnp.concatenate(gscores, axis=0)
        gvalues = dot(probs, grads)
        gkeys = dot(gscores, queries)
        gqkv_ref[:, at : at + 128] = (dot(gscores, key_rows, 0, 0) * 0.125).astype(BF)
        for which, result in ((1, gkeys), (2, gvalues)):
            gqkv_ref[:, which * BLOCK + at : which * BLOCK + at + 128] = jnp.where(
                low_half, result[:length], result[length:]
            ).astype(BF)


def qkv_grad_kernel(
    place, h1_turned, gqkv_ref, wq_ref, att_ref, glow_ref, gh1_ref, sums_ref, keep_ref, upper_ref, lower_ref,
    product, product_out,
):
    third, wide = gqkv_ref.shape[1], glow_ref.shape[1]
    product[...] = dot(h1_turned[...], gqkv_ref[...])
    product_out[...] = dot(att_ref[...], glow_ref[...], 0, 0)
    gh1_ref[...] = dot(gqkv_ref[...], wq_ref[...], 1, 1)
    sums_ref[...] = sum_rows(gqkv_ref[...])
    send = upper_ref, lower_ref
    give_rows(place, SMALL, product, keep_ref, send, lanes=slice(0, third))
    give_rows(place, SMALL, product_out, keep_ref, send, lanes=slice(third, third + wide))


def input_kernel(
    place, h1_turned, gqkv_ref, wq_ref, before_ref, mlp_ref, fcg_ref, rows_ref, vec_ref, glow_ref, gh1_ref,
    ginput_ref, keep_ref, upper_ref, lower_ref, product,
):
    product[...] = dot(h1_turned[...], gqkv_ref[...])
    sums = sum_rows(gqkv_ref[...])
    gradient = gh1_ref[...] + dot(gqkv_ref[...], wq_ref[...], 1, 1)
    normed, scale = normed_rows(rows_ref[...].astype(F32))
    ginput_ref[...] = (
        glow_ref[...].astype(F32) + norm_back(gradient * row_of(vec_ref, 0), normed, scale)
    ).astype(BF)
    gain, shift = sum_rows(gradient * normed), sum_rows(gradient)
    first, last = slice(0, BLOCK), slice(2 * BLOCK, 3 * BLOCK)
    biases = before_ref[:, first], sums[:, first], before_ref[:, last], sums[:, last]

    def below(group):
        lanes = slice(BLOCK * (group // 2), BLOCK * (group // 2 + 1))
        own = stack_rows([gain[:, lanes], shift[:, lanes], biases[group]])
        return jnp.concatenate([mlp_ref[...] + fcg_ref[group], own], axis=1)

    give_rows(place, SMALL, product, keep_ref, (upper_ref, lower_ref), below)


def add_up(parts):
    return sum(part.astype(F32) for part in parts)


def give_vector(target, line, device):
    count, columns = target.shape[0], line.shape[1]
    start = lax.rem(device, columns // count) * count
    moved = pltpu.roll(line, lax.rem(columns - start, columns), 1)
    target[...] = moved[:, :count].reshape(count)


def last_kernel(place, *refs):
    sources, (qkv_out, out_out), smalls = refs[:12], refs[12:14], refs[14:]
    total_a = add_up([source[0] for source in sources[:6]])
    total_c = add_up([source[0] for source in sources[6:]])
    for part in range(3):
        lanes = slice(BLOCK * part, BLOCK * (part + 1))
        qkv_out[:, 2 * BLOCK * part : 2 * BLOCK * part + BLOCK] = total_a[:, lanes]
        qkv_out[:, 2 * BLOCK * part + BLOCK : 2 * BLOCK * (part + 1)] = total_c[:24, lanes]
    out_out[...] = total_a[:, 3 * BLOCK :]
    device = place[49]
    for line, target in enumerate(smalls[:3]):
        give_vector(target, total_c[24 + line : 25 + line, 2 * BLOCK :], device)
    for line, target in enumerate(smalls[3:]):
        give_vector(target, total_c[24 + line : 25 + line, : 2 * BLOCK], device)


def after(value, *others):
    return lax.optimization_barrier((value,) + others)[0]


class Links:
    def __init__(self, depth):
        self.depth = depth

        def table(move):
            pairs = []
            for z in range(depth):
                for x in range(2):
                    for y in range(2):
                        for c in range(2):
                            nz, nx, ny, nc = move(z, x, y, c)
                            source = (z * 2 + x) * 4 + y * 2 + c
                            pairs.append((source, ((nz % depth) * 2 + nx) * 4 + ny * 2 + nc))
            return pairs

        self.ups = {step: table(lambda z, x, y, c: (z + step, x, y, c)) for step in (1, 2, 3)}
        self.first = table(lambda z, x, y, c: (z, x, 1 - y, c) if c else (z, 1 - x, y, c))
        self.second = table(lambda z, x, y, c: (z, 1 - x, y, c) if c else (z, x, 1 - y, c))
        self.across = table(lambda z, x, y, c: (z, 1 - x, 1 - y, c))
        self.cores = table(lambda z, x, y, c: (z, x, y, 1 - c))
        self.near = table(lambda z, x, y, c: (z ^ 1, x, y, c))
        self.far = table(lambda z, x, y, c: (z ^ 2, x, y, c))

    def move(self, value, pairs):
        return lax.ppermute(value, AXES, pairs)

    def spots(self):
        dp, fsdp = lax.axis_index("dp"), lax.axis_index("fsdp")
        z, x, y, core = dp // 2, dp % 2, fsdp // 2, fsdp % 2

        def chip(c, flip1, flip2, step):
            flip_x = jnp.where(c == 0, flip1, flip2)
            flip_y = jnp.where(c == 0, flip2, flip1)
            return (((z - step) % self.depth) * 2 + (x ^ flip_x)) * 2 + (y ^ flip_y)

        index = jnp.arange(32, dtype=jnp.int32)
        whose = jnp.where(index < 16, core, 1 - core)
        flip2 = (index // 8) % 2
        z_first = chip(whose, (index // 4) % 2, flip2, index % 4)
        x_first = chip(whose, index % 2, (index // 2) % 2, (index // 4) % 4)
        chips = jnp.arange(16, dtype=jnp.int32)
        turn_x, turn_y = ((chips // 2) % 2) ^ x, (chips % 2) ^ y
        far_z = (chips // 4) ^ z
        near, wide_step = far_z % 2, far_z // 2

        def slots(order):
            turns = {"x": turn_x, "y": turn_y, "near": near, "far": wide_step}
            return sum(turns[name] * weight for name, weight in zip(order, (8, 4, 2, 1)))

        others = jnp.stack([core, dp * 4 + fsdp, z]).astype(jnp.int32)
        rest = jnp.concatenate([others, jnp.zeros((13,), jnp.int32)])
        tables = []
        for orders in (
            (("y", "x", "near", "far"), ("x", "y", "near", "far")),
            (("y", "near", "x", "far"), ("x", "near", "y", "far")),
        ):
            both = [slots(order) for order in orders]
            tables += [jnp.where(core == 0, both[0], both[1]), jnp.where(core == 0, both[1], both[0])]
        swapped = jnp.where(index % 8 >= 6, 9 - index % 8, index % 4)
        swapped = chip(whose, (index // 4) % 2, flip2, swapped)
        parts = [z_first, tables[0], rest, x_first] + tables[1:] + [swapped]
        return jnp.concatenate(parts).astype(jnp.int32)

    def gather(self, piece_a, piece_b1, piece_b2, inputs, prepare):
        hold = lax.optimization_barrier
        up = lambda value, step: self.move(value, self.ups[step])
        a_one, a_three, b1_two = hold((up(piece_a, 1), up(piece_a, 3), self.move(piece_b1, self.first)))
        b1_two = jnp.stack([piece_b1, b1_two])
        a_two, b1_four = hold((up(a_one, 1), self.move(b1_two, self.second)))
        a_four = jnp.stack([piece_a, a_one, a_two, a_three])
        b1_four = jnp.concatenate([b1_two, b1_four])
        piece_b2 = after(piece_b2, a_two)
        a_rest, b2_one, b2_three = hold((self.move(a_four, self.first), up(piece_b2, 1), up(piece_b2, 3)))
        early = prepare(*after(inputs, a_rest))
        a_eight = jnp.concatenate([a_four, a_rest])
        b2_rest = self.move(jnp.stack([piece_b2, b2_one, b2_three]), self.first)
        a_other, b2_two, b1_one, b2_rest, early = hold(
            (self.move(a_eight, self.second), up(b2_one, 1), up(after(b1_four, a_rest), 1), b2_rest, early)
        )
        b2_seven = jnp.concatenate([jnp.stack([piece_b2, b2_one, b2_two, b2_three]), b2_rest])
        a = self.finish(a_eight, a_other)
        b1 = b1_four, b1_one, up(b1_one, 1), up(b1_four, 3)
        b2_last, b2_across = self.move(b2_two[None], self.first), self.move(b2_two[None], self.across)
        return a, b1, (b2_seven, b2_last, self.move(b2_seven, self.second), b2_across), early

    def gather_end(self, b1, b2, done):
        b1_four, b1_one, b1_two, b1_three = b1
        b2_seven, b2_last, other_seven, other_last = b2
        b2_last, done = lax.optimization_barrier((b2_last, done))
        b2_mine, b1_mine = jnp.concatenate([b2_seven, b2_last]), jnp.concatenate([b1_four, b1_one])
        b2_theirs, b1_theirs = self.move(b2_mine, self.cores), self.move(b1_mine, self.cores)
        b1_two, b1_three, other_seven, other_last, done = lax.optimization_barrier(
            (b1_two, b1_three, other_seven, other_last, done)
        )
        b2_rest, b1_rest = jnp.concatenate([other_seven, other_last]), jnp.concatenate([b1_two, b1_three])
        b1 = b1_mine, b1_rest, b1_theirs, self.move(b1_rest, self.cores)
        return done, b1, (b2_mine, b2_rest, b2_theirs, self.move(b2_rest, self.cores))

    def finish(self, eight, rest):
        return (eight, rest, self.move(eight, self.cores), self.move(rest, self.cores))

    def fold(self, state):
        left = 32 >> (len(state) - 1)
        return add_up([part[left // 2 : left] for part in state]).astype(BF)

def full_pieces(full, blocks):
    split = full.reshape((CHIPS, 48) + full.shape[1:])
    split = split.transpose(3, 0, 2, 1, 4) if full.shape[1] == blocks else split.transpose(2, 0, 3, 1, 4)
    return split.reshape(2 * CHIPS, blocks * 48, BLOCK)


STILL = [
    16 * core + ((-step % 4) * 2 + (flip2 if core else flip1)) * 2 + (flip1 if core else flip2)
    for core in range(2)
    for flip2 in range(2)
    for flip1 in range(2)
    for step in range(4)
]


STILL_LAST = [STILL[8 * array + index] for array in range(4) for index in (0, 1, 2, 3, 4, 5, 7, 6)]


def eights(pieces, order=None):
    if order is not None:
        pieces = jnp.stack([pieces[index] for index in order])
    return tuple(pieces[8 * index : 8 * (index + 1)] for index in range(4))


def placed(vector, device, per_row):
    start = (device % per_row) * vector.shape[0]
    return lax.dynamic_update_slice(jnp.zeros((BLOCK,), vector.dtype), vector, (start,))


def shards(
    mesh_shape,
    patches,
    counts,
    positions,
    ln1_gain,
    ln1_bias,
    qkv_weight,
    qv_bias,
    out_weight,
    out_bias,
    ln2_gain,
    ln2_bias,
    fc1_weight,
    fc1_bias,
    fc2_weight,
    fc2_bias,
    cotangent,
):
    images, length, width = patches.shape
    padded = (length + 31) // 32 * 32
    rows = images * padded
    hidden_width = fc1_weight.shape[1]
    devices = mesh_shape["dp"] * mesh_shape["fsdp"]
    by_hand = devices == 2 * CHIPS and mesh_shape["fsdp"] == 4
    small_parts = (ln1_gain, ln1_bias, out_bias, ln2_gain, ln2_bias, fc2_bias, qv_bias, fc1_bias)

    smem = pl.BlockSpec(memory_space=pltpu.SMEM)
    vmem = pl.BlockSpec(memory_space=pltpu.VMEM)
    anywhere = pl.BlockSpec(memory_space=pltpu.HBM)
    struct = jax.ShapeDtypeStruct

    def prepare(patches, counts, positions, cotangent):
        row_index = jnp.arange(padded, dtype=jnp.int32)
        is_live = row_index[None, :] < counts[:, None]
        pad_rows = ((0, 0), (0, padded - length), (0, 0))
        rows_in = jnp.pad(patches, pad_rows).reshape(rows, width)
        gout = jnp.where(is_live[:, :, None], jnp.pad(cotangent, pad_rows), 0).reshape(rows, width)
        spots = jnp.pad(positions, pad_rows[:2])
        grid_rows = (spots // SIDE).astype(F32)
        grid_cols = (spots % SIDE).astype(F32)
        row_delta = grid_rows[:, :, None] - grid_rows[:, None, :]
        col_delta = grid_cols[:, :, None] - grid_cols[:, None, :]
        distance = jnp.sqrt(row_delta * row_delta + col_delta * col_delta)
        far = jnp.where(is_live[:, None, :], distance, FAR)
        far_turned = jnp.where(is_live[:, :, None], distance, FAR)
        return rows_in, gout, far, far_turned

    if by_hand:
        links = Links(mesh_shape["dp"] // 2)
        place = links.spots()
        core = place[48]
        share = struct((8, 24, BLOCK), BF)
        mine, theirs, lines = pl.pallas_call(
            share_kernel,
            out_shape=(share, share, struct((16, BLOCK), BF)),
            in_specs=[smem] + [vmem] * 11,
            out_specs=(vmem,) * 3,
            name="share",
        )(place, qkv_weight, out_weight, fc1_weight, *small_parts)
        got = links.move(theirs, links.cores)
        pieces = pl.pallas_call(
            pair_kernel,
            out_shape=tuple(struct((height, BLOCK), BF) for height in (160, 192, 240)),
            in_specs=[smem] + [vmem] * 4,
            out_specs=(vmem,) * 3,
            name="pair",
        )(place, mine, got, lines, fc2_weight)
    else:
        links = None
        place = jnp.concatenate(
            [
                jnp.array([chip % CHIPS for chip in STILL], jnp.int32),
                jnp.arange(16, dtype=jnp.int32),
                jnp.zeros((16,), jnp.int32),
                jnp.arange(80, dtype=jnp.int32) % 16,
                jnp.array([chip % CHIPS for chip in STILL_LAST], jnp.int32),
            ]
        )
        whole = [lax.all_gather(part, AXES, axis=0, tiled=True) for part in small_parts]
        lines = []
        for part in whole:
            share = part.shape[0] // 32
            chunks = part.reshape(32, share)
            lines.append(
                jnp.stack([placed(chunks[index], index, BLOCK // share) for index in range(32)])
            )
        lines = jnp.concatenate([jnp.stack(lines, axis=1), jnp.zeros((32, 8, BLOCK), BF)], axis=1)
        lines = lines.reshape(CHIPS, 2, 16, BLOCK).transpose(1, 0, 2, 3).reshape(32, 16, BLOCK)
        whole_qkv = lax.all_gather(qkv_weight, AXES, axis=0, tiled=True)
        whole_out = lax.all_gather(out_weight, AXES, axis=0, tiled=True)
        whole_fc1 = lax.all_gather(fc1_weight, AXES, axis=0, tiled=True)
        whole_fc2 = lax.all_gather(fc2_weight, AXES, axis=0, tiled=True)
        split = whole_fc2.reshape(CHIPS, 2, 96, 2, BLOCK).transpose(1, 0, 3, 2, 4).reshape(32, 192, BLOCK)
        gathered_a = eights(
            jnp.concatenate([full_pieces(whole_qkv.reshape(width, 3, 2, BLOCK), 3), lines], axis=1), STILL
        )
        gathered_b1 = eights(full_pieces(whole_fc1.reshape(width, 2, 4, BLOCK), 4))
        split = whole_fc2.reshape(CHIPS, 2, 96, 2, BLOCK).transpose(1, 0, 3, 2, 4).reshape(32, 192, BLOCK)
        gathered_b2 = eights(
            jnp.concatenate([split, full_pieces(whole_out.reshape(width, 1, 2, BLOCK), 1)], axis=1), STILL_LAST
        )

    if by_hand:
        gathered_a, on_b1, on_b2, early = links.gather(*pieces, (patches, counts, positions, cotangent), prepare)
    else:
        early = prepare(patches, counts, positions, cotangent)
    rows_in, gout, far, far_turned = early

    def call(kernel, operands, out_shape, out_specs, in_specs, flops, mib, vmem_mib, grid, scratch=(), name=None):
        return pl.pallas_call(
            kernel,
            grid=grid,
            out_shape=out_shape,
            in_specs=in_specs,
            out_specs=out_specs,
            scratch_shapes=list(scratch),
            compiler_params=pltpu.CompilerParams(vmem_limit_bytes=vmem_mib * MIB),
            cost_estimate=pl.CostEstimate(
                flops=1, bytes_accessed=1, transcendentals=0
            ),
            name=name,
        )(*operands)

    image_rows = lambda columns: pl.BlockSpec((padded, columns), lambda image: (image, 0))
    image_far = pl.BlockSpec((1, padded, padded), lambda image: (image, 0, 0))
    fixed = lambda *shape: pl.BlockSpec(shape, lambda step: (0,) * len(shape))
    step_rows = lambda columns: pl.BlockSpec((rows, columns), lambda step: (0, step))
    shares = lambda height, columns: struct((CHIPS, height, columns), BF)
    buffer, flag = pltpu.VMEM, pltpu.SemaphoreType.DMA
    low_rows, wide_rows = struct((rows, width), BF), struct((rows, width), F32)
    wide = 2 * BLOCK
    steps = hidden_width // wide
    third = 3 * BLOCK

    def join(value, *others):
        return after(value, *others) if by_hand else value

    vec, fcb, h1_turned, qkv, att, wq_0, wq_1 = pl.pallas_call(
        first_kernel,
        out_shape=(
            struct((2, 16, BLOCK), F32), struct((steps, 1, wide), F32), struct((width, rows), BF),
            struct((2, rows, third), BF), low_rows, struct((width, third), BF), struct((width, third), BF),
        ),
        in_specs=[smem] + [anywhere] * 4 + [vmem] * 2,
        out_specs=(vmem,) * 5 + (anywhere,) * 2,
        scratch_shapes=[
            buffer((2, width, third), BF), buffer((rows, width), BF), buffer((4, 16, BLOCK), F32),
            buffer((32, 16, BLOCK), BF), flag((5,)),
        ],
        compiler_params=pltpu.CompilerParams(vmem_limit_bytes=30 * MIB),
        cost_estimate=pl.CostEstimate(flops=1, bytes_accessed=1, transcendentals=0),
        name="first",
    )(place, *gathered_a, rows_in, far)
    if by_hand:
        att, gathered_b1, gathered_b2 = links.gather_end(on_b1, on_b2, att)

    step_shares = lambda height, columns: pl.BlockSpec((CHIPS, height, columns), lambda step: (0, 0, step))
    still = lambda *shape: pl.BlockSpec(shape, lambda step, place: (0,) * len(shape))
    turned_shares = pl.BlockSpec(
        (CHIPS, 24, wide), lambda step, place: (0, 0, lax.rem(place[50] + 4 - step, 4))
    )
    low_buffer, wide_buffer = buffer((rows, width), BF), buffer((rows, width), F32)
    out, glow, keep_1, send_1, sums, fcg, keep_2, upper_2, lower_2, wo = pl.pallas_call(
        mlp_kernel,
        grid_spec=pltpu.PrefetchScalarGridSpec(
            num_scalar_prefetch=1,
            grid=(steps,),
            in_specs=[smem] + [anywhere] * 11 + [still(2, 16, BLOCK), still(steps, 1, wide)],
            out_specs=(still(rows, width),) * 2
            + (turned_shares,) * 2
            + (still(8, wide), still(steps, 8, wide))
            + (anywhere,) * 4,
            scratch_shapes=[
                buffer((steps, width, wide), BF), buffer((hidden_width, width), BF), buffer((2, width, BLOCK), BF),
                low_buffer, low_buffer, low_buffer, low_buffer, buffer((width, rows), BF),
                wide_buffer, wide_buffer, wide_buffer, buffer((width, wide), F32), buffer((width, wide), F32),
                buffer((2, CHIPS, 96, wide), BF), buffer((rows, 128), F32), flag((steps,)), flag((steps,)), flag((7,)),
            ],
        ),
        out_shape=(low_rows, low_rows)
        + (shares(24, hidden_width),) * 2
        + (struct((8, wide), F32), struct((steps, 8, wide), F32))
        + (shares(96, wide),)
        + (struct((8, 96, wide), BF),) * 2
        + (struct((2, width, BLOCK), BF),),
        compiler_params=pltpu.CompilerParams(vmem_limit_bytes=52 * MIB),
        cost_estimate=pl.CostEstimate(flops=1, bytes_accessed=1, transcendentals=0),
        name="mlp",
    )(place, counts, *gathered_b1, *gathered_b2, att, rows_in, gout, vec, fcb)

    if by_hand:
        state_2 = keep_2, links.move(upper_2, links.cores)

    def attention_back(side, gradient):
        return call(
            lambda *refs: attention_back_kernel(side, *refs),
            (wo, qkv, far_turned, gradient),
            struct((rows, third), BF),
            image_rows(third),
            [
                fixed(2, width, BLOCK), pl.BlockSpec((1, padded, third), lambda image: (side, image, 0)),
                image_far, image_rows(width),
            ],
            8 * rows * 256 * width,
            8,
            20,
            grid=(images,),
            name="attention_back",
        )

    part_2 = glow
    if by_hand:
        part_2 = add_up([keep_2[8:], state_2[1]]).astype(BF)
        lower_2, send_1 = after((lower_2, send_1), part_2)
        state_2 = keep_2, links.move(lower_2, links.cores), links.move(part_2, links.second)
        state_1 = keep_1, links.move(send_1, links.cores)
    gqkv_0 = attention_back(0, join(glow, part_2))
    if by_hand:
        state_1, gqkv_0 = lax.optimization_barrier((state_1, gqkv_0))
        state_1 += (links.move(links.fold(state_1), links.second),)

    def grad_call(kernel, operands, out_shape, scratch, name):
        return pl.pallas_call(
            kernel,
            out_shape=out_shape,
            in_specs=[smem] + [vmem] * (len(operands) - 1),
            out_specs=(vmem,) * len(out_shape),
            scratch_shapes=list(scratch),
            compiler_params=pltpu.CompilerParams(vmem_limit_bytes=28 * MIB),
            cost_estimate=pl.CostEstimate(flops=1, bytes_accessed=1, transcendentals=0),
            name=name,
        )(*operands)

    half_shares = lambda height, columns: (struct((8, height, columns), BF),) * 2
    gh1, sums_0, keep_a, upper_a, lower_a = grad_call(
        qkv_grad_kernel,
        (place, h1_turned, gqkv_0, wq_0, att, glow),
        (wide_rows, struct((1, third), F32), shares(24, third + wide)) + half_shares(24, third + wide),
        (buffer((width, third), F32), buffer((width, wide), F32)),
        "qkv_grad",
    )
    parts = gh1
    if by_hand:
        got_a = links.move(upper_a, links.cores)
        state_2, got_a, gh1 = lax.optimization_barrier((state_2, got_a, gh1))
        parts = links.fold(state_2), add_up([keep_a[8:], got_a]).astype(BF)
        state_2 += (links.move(parts[0], links.near),)
        lower_a = after(lower_a, parts)
        state_a = keep_a, links.move(lower_a, links.cores), links.move(parts[1], links.second)

    gqkv_1 = attention_back(1, join(glow, gh1, parts))
    ginput, keep_c, upper_c, lower_c = grad_call(
        input_kernel,
        (place, h1_turned, gqkv_1, wq_1, sums_0, sums, fcg, rows_in, vec, glow, gh1),
        (low_rows, shares(32, third)) + half_shares(32, third),
        (buffer((width, third), F32),),
        "input_grad",
    )

    def cut(value):
        return value.reshape(images, padded, width)[:, :length]

    if by_hand:
        fold, move = links.fold, links.move

        state_c = keep_c, move(upper_c, links.cores)
        rest_c = move(after(lower_c, keep_c), links.cores)
        state_1 = after(state_1, keep_c)
        part = fold(state_1)
        state_1 += (move(part, links.near),)
        keep_c, got_c = after(state_c, part)
        part = add_up([keep_c[8:], got_c]).astype(BF)
        state_c = keep_c, rest_c, move(part, links.second)
        state_2, state_a, out, ginput = after((state_2, state_a, out, ginput), part)
        out, ginput = cut(out), cut(ginput)
        state_2, state_a, out, ginput = after((state_2, state_a, out, ginput))
        parts = fold(state_2), fold(state_a)
        state_2 += (move(parts[0], links.first),)
        state_a += (move(parts[1], links.first),)
        part = fold(after(state_c, parts))
        state_c += (move(part, links.first),)
        state_1, out, ginput = after((state_1, out, ginput), part)
        part = fold(state_1)
        state_1 += (move(part, links.first),)
        state_2 = after(state_2, part)
        part = fold(state_2)
        state_2 += (move(part, links.far),)
        state_a = after(state_a, part)
        part = fold(state_a)
        state_a += (move(part, links.near),)
        part = fold(after(state_c, part))
        state_c += (move(part, links.near),)
        state_1 = after(state_1, part)
        part = fold(state_1)
        state_1 += (move(part, links.far),)
        state_a = after(state_a, part)
        part = fold(state_a)
        state_a += (move(part, links.far),)
        part = fold(after(state_c, part))
        state_c += (move(part, links.far),)
        state_2 = after(state_2, part)
        mine_2 = add_up([part[0] for part in state_2])
        state_1 = after(state_1, mine_2)
        mine_1 = add_up([part[0] for part in state_1])
        own_slot = lambda part: pl.BlockSpec((1,) + part.shape[1:], lambda step: (0, 0, 0))
        heights, counts_out = ((24, 3 * width), (24, width)), (24, 24, 48, 24, 24, 24, 96, 24)
        (
            qkv_grad, out_grad, ln1_gain_grad, ln1_bias_grad, qv_bias_grad,
            ln2_gain_grad, ln2_bias_grad, fc2_bias_grad, fc1_bias_grad, out_bias_grad,
        ) = pl.pallas_call(
            last_kernel,
            grid=(1,),
            out_shape=tuple(struct(shape, F32) for shape in heights + tuple((count,) for count in counts_out)),
            in_specs=[smem] + [own_slot(part) for part in state_a + state_c],
            out_specs=tuple(fixed(*shape) for shape in heights)
            + tuple(pl.BlockSpec((count,), lambda step: (0,)) for count in counts_out),
            compiler_params=pltpu.CompilerParams(vmem_limit_bytes=30 * MIB),
            name="last",
        )(place, *state_a, *state_c)
        return (
            out, ginput, ln1_gain_grad, ln1_bias_grad, qkv_grad, qv_bias_grad, out_grad, out_bias_grad,
            ln2_gain_grad, ln2_bias_grad, mine_1, fc1_bias_grad, mine_2, fc2_bias_grad,
        )

    both_a, both_c, both_1, both_2 = (
        jnp.stack(pair, axis=1).astype(F32)
        for pair in (
            (keep_a, jnp.concatenate([lower_a, upper_a])),
            (keep_c, jnp.concatenate([lower_c, upper_c])),
            (keep_1, send_1),
            (keep_2, jnp.concatenate([lower_2, upper_2])),
        )
    )
    heads = jnp.stack(
        [both.reshape(CHIPS, 2, 24, 3, BLOCK) for both in (both_a[..., :third], both_c[:, :, :24])], axis=4
    )

    def vector(lines, count):
        columns = lines.shape[-1]
        return lines.reshape(32 * count // columns, -1, columns)[:, 0].reshape(-1)

    small_c, small_2 = both_c[:, :, 24:, 2 * BLOCK :], both_c[:, :, 24:, : 2 * BLOCK]
    totals = (
        vector(small_c[:, :, 0], 24),
        vector(small_c[:, :, 1], 24),
        heads.reshape(width, 3 * width),
        vector(small_c[:, :, 2], 48),
        both_a[..., third:].reshape(width, width),
        vector(small_2[:, :, 4], 24),
        vector(small_2[:, :, 0], 24),
        vector(small_2[:, :, 1], 24),
        both_1.reshape(width, hidden_width),
        vector(small_2[:, :, 3], 96),
        both_2.reshape(hidden_width, width),
        vector(small_2[:, :, 2], 24),
    )
    return (cut(out), cut(ginput)) + tuple(
        lax.psum_scatter(total, AXES, scatter_dimension=0, tiled=True) for total in totals
    )


def solution(mesh):
    rows = P(AXES, None, None)
    table = P(AXES, None)
    line = P(AXES)
    in_specs = (
        rows, line, table, line, line, table, line, table, line, line, line, table, line, table, line, rows,
    )
    out_specs = (
        rows, rows, line, line, table, line, table, line, line, line, table, line, table, line,
    )
    mesh_shape = dict(mesh.shape)

    def body(*arrays):
        return shards(mesh_shape, *arrays)

    return jax.shard_map(body, mesh=mesh, in_specs=in_specs, out_specs=out_specs, check_vma=False)
```

```python
import math

import jax
import jax.numpy as jnp
import numpy as np
from jax import lax
from jax.experimental import pallas as pl
from jax.experimental.pallas import tpu as pltpu
from jax.sharding import PartitionSpec as P

HEADS = 12
SIDE = 16
EPSILON = 1e-06
AXES = ("dp", "fsdp")
FAR = 1e30
CHIPS = 16
BLOCK = 384
SMALL, LARGE = (32, 96), (112, 128)
MIB = 1024 * 1024

BF = jnp.bfloat16
F32 = jnp.float32


def power_slopes(number):
    first_slope = 2.0 ** (-8.0 / number)
    return [first_slope ** (index + 1) for index in range(number)]


def slope_list(heads_total):
    lower_power = 2 ** int(math.floor(math.log2(heads_total)))
    return (
        power_slopes(lower_power) + power_slopes(2 * lower_power)[0::2][: heads_total - lower_power]
    )


SLOPES = [float(np.float32(slope)) for slope in slope_list(HEADS)]


def dot(left, right, left_dim=1, right_dim=0):
    return lax.dot_general(
        left, right, (((left_dim,), (right_dim,)), ((), ())), preferred_element_type=F32
    )


def normed_rows(values):
    centered = values - jnp.mean(values, axis=-1, keepdims=True)
    scale = lax.rsqrt(jnp.mean(centered * centered, axis=-1, keepdims=True) + EPSILON)
    return centered * scale, scale


def norm_back(grad_normed, normed, scale):
    centered_mean = jnp.mean(grad_normed, axis=-1, keepdims=True)
    projected_mean = jnp.mean(grad_normed * normed, axis=-1, keepdims=True)
    return scale * (grad_normed - centered_mean - normed * projected_mean)


def row_of(vectors_ref, index):
    return jnp.concatenate(
        [vectors_ref[0, index : index + 1, :], vectors_ref[1, index : index + 1, :]], axis=1
    )


def gelu_parts(hidden):
    cumulative = 0.5 + 0.5 * lax.erf(hidden * math.sqrt(0.5))
    bell = jnp.exp(-0.5 * hidden * hidden)
    return cumulative, cumulative + hidden * bell * (1.0 / math.sqrt(2.0 * math.pi))


def share_kernel(place, qkv_ref, out_ref, fc1_ref, *refs):
    smalls, (mine_ref, theirs_ref, lines_ref) = refs[:-3], refs[-3:]
    for target, core in ((mine_ref, place[48]), (theirs_ref, 1 - place[48])):
        starts = [(qkv_ref, 2 * BLOCK * part + BLOCK * core) for part in range(3)]
        starts.append((out_ref, BLOCK * core))
        starts += [(fc1_ref, 4 * BLOCK * core + BLOCK * part) for part in range(4)]
        for block, (source, start) in enumerate(starts):
            target[block] = source[:, pl.ds(pl.multiple_of(start, 128), BLOCK)]
    device = place[49]
    lines = []
    for small in smalls:
        count = small.shape[0]
        line = small[...].astype(F32).reshape(1, count)
        line = jnp.concatenate([line, jnp.zeros((1, BLOCK - count), F32)], axis=1)
        lines.append(pltpu.roll(line, lax.rem(device, BLOCK // count) * count, 1))
    lines_ref[...] = jnp.concatenate(lines + [jnp.zeros((8, BLOCK), F32)], axis=0).astype(BF)


def pair_kernel(place, mine_ref, got_ref, lines_ref, fc2_ref, a_ref, b1_ref, b2_ref):
    swap = place[48] == 1
    for block in range(8):
        mine, got = mine_ref[block].astype(F32), got_ref[block].astype(F32)
        rows = jnp.concatenate([jnp.where(swap, got, mine), jnp.where(swap, mine, got)], axis=0)
        if block < 3:
            a_ref[48 * block : 48 * (block + 1), :] = rows.astype(BF)
        elif block == 3:
            b2_ref[192:240, :] = rows.astype(BF)
        else:
            b1_ref[48 * (block - 4) : 48 * (block - 3), :] = rows.astype(BF)
    b2_ref[0:96, :] = fc2_ref[:, :BLOCK]
    b2_ref[96:192, :] = fc2_ref[:, BLOCK:]
    a_ref[144:160, :] = lines_ref[...]


def each_piece(place, table, sources, work):
    core = place[48]
    for number, source in enumerate(sources):
        half = core if number < 2 else 1 - core

        def bring(index, _, source=source, number=number, half=half):
            work(source, index, place[table + number * 8 + index], half)
            return 0

        lax.fori_loop(0, 8, bring, 0)


def bring_out_weight(place, sources, wo, sem, table):
    def work(source, index, chip, half):
        spot = pl.ds(pl.multiple_of(chip * 48, 16), 48)
        pltpu.make_async_copy(source.at[index, pl.ds(192, 48)], wo.at[half, spot], sem).start()

    each_piece(place, table, sources, work)


def bring_qkv_weight(place, sources, side, wq, sem, part_of=None):
    for first, here in ((0, place[48] == side), (2, place[48] != side)):

        @pl.when(here)
        def _(first=first):
            for number in (first, first + 1):

                def bring(index, _, source=sources[number], number=number):
                    spot = pl.ds(pl.multiple_of(place[number * 8 + index] * 48, 16), 48)
                    for part in range(3):
                        pltpu.make_async_copy(
                            source.at[index, pl.ds(48 * part, 48)],
                            wq.at[spot, pl.ds(BLOCK * part, BLOCK)] if part_of is None else wq.at[part, spot],
                            sem if part_of is None else part_of.at[part],
                        ).start()
                    return 0

                lax.fori_loop(0, 8, bring, 0)


def wait_all(buffer, sem):
    pltpu.make_async_copy(buffer, buffer, sem).wait()


def two_heads(pair_rows, low_half):
    nothing = jnp.zeros_like(pair_rows)
    return jnp.concatenate(
        [jnp.where(low_half, pair_rows, nothing), jnp.where(low_half, nothing, pair_rows)], axis=0
    )


def first_kernel(
    place, own0, own1, other0, other1, rows_ref, far_ref,
    vec_ref, fcb_ref, h1_turned, qkv_ref, att_ref, wq_out0, wq_out1,
    wq, h1, qvb, small, sems,
):
    sources = (own0, own1, other0, other1)

    def work(source, index, chip, half):
        pltpu.make_async_copy(
            source.at[index, pl.ds(144, 16)], small.at[2 * chip + half], sems.at[2]
        ).start()

    each_piece(place, 0, sources, work)
    for half in range(2):
        bring_qkv_weight(place, sources, half, wq.at[half], sems.at[half])
    normed, _ = normed_rows(rows_ref[...].astype(F32))
    wait_all(small, sems.at[2])
    spread = small[...].astype(F32)
    vec_ref[...] = jnp.sum(spread.reshape(2, 16, 16, BLOCK), axis=1)
    qvb[...] = jnp.sum(spread.reshape(4, 8, 16, BLOCK), axis=1)
    lines = jnp.sum(spread.reshape(8, 4, 16, BLOCK), axis=1)
    for block in range(4):
        fcb_ref[block] = jnp.concatenate([lines[2 * block, 7:8], lines[2 * block + 1, 7:8]], axis=1)
    low = (normed * row_of(vec_ref, 0) + row_of(vec_ref, 1)).astype(BF)
    h1[...] = low
    h1_turned[...] = low.T

    def one_side(side, _):
        wait_all(wq.at[side], sems.at[side])
        for half, target in enumerate((wq_out0, wq_out1)):

            @pl.when(side == half)
            def _(half=half, target=target):
                pltpu.make_async_copy(wq.at[half], target, sems.at[3 + half]).start()

        bias = jnp.concatenate(
            [qvb[side, 6:7, :], jnp.zeros((1, BLOCK), F32), qvb[2 + side, 6:7, :]], axis=1
        )
        qkv_ref[side] = (dot(h1[...], wq[side]) + bias).astype(BF)
        return 0

    lax.fori_loop(0, 2, one_side, 0)
    length = far_ref.shape[1]
    low_half = lax.broadcasted_iota(jnp.int32, (length, 128), 1) < 64

    def one_image(image, _):
        here = pl.ds(pl.multiple_of(image * length, 32), length)
        far = far_ref[image]
        for pair in range(HEADS // 2):
            side, at = pair // 3, 128 * (pair % 3)
            queries = two_heads(qkv_ref[side, here, at : at + 128] * jnp.asarray(0.125, BF), low_half)
            key_rows = qkv_ref[side, here, BLOCK + at : BLOCK + at + 128]
            values = qkv_ref[side, here, 2 * BLOCK + at : 2 * BLOCK + at + 128]
            both = dot(queries, key_rows, 1, 1)
            probs = []
            for head in range(2):
                scores = both[length * head : length * (head + 1)] - SLOPES[2 * pair + head] * far
                shifted = jnp.exp(scores - jnp.max(scores, axis=-1, keepdims=True))
                share = shifted * (1.0 / jnp.sum(shifted, axis=-1, keepdims=True))
                probs.append(share.astype(BF))
            result = dot(jnp.concatenate(probs, axis=0), values)
            att_ref[here, 128 * pair : 128 * (pair + 1)] = jnp.where(
                low_half, result[:length], result[length:]
            ).astype(BF)
        return 0

    lax.fori_loop(0, far_ref.shape[0], one_image, 0)
    wait_all(wq_out0, sems.at[3])
    wait_all(wq_out1, sems.at[4])


def at_slot(target, slot, work):
    if not isinstance(target, tuple):
        work(target, slot)
        return

    @pl.when(slot >= 8)
    def _():
        work(target[0], slot - 8)

    @pl.when(slot < 8)
    def _():
        work(target[1], slot)


def give_rows(place, tables, total, keep_ref, send_ref, extra=None, lanes=slice(None)):
    for group in range(1 if extra is None else 4):
        below = None if extra is None else extra(group)

        def one_chip(index, _, group=group, below=below):
            chip = 4 * group + index
            for which, target in enumerate((keep_ref, send_ref)):
                owner = place[48] if which == 0 else 1 - place[48]
                share = total[pl.ds(pl.multiple_of(48 * chip + 24 * owner, 8), 24), :]
                if below is not None:
                    share = jnp.concatenate([share, below], axis=0)

                def put(ref, slot, share=share):
                    ref[slot, :, lanes] = share.astype(BF)

                at_slot(target, place[tables[which] + chip], put)
            return 0

        lax.fori_loop(0, CHIPS if extra is None else 4, one_chip, 0)


def stack_rows(rows):
    blank = jnp.zeros_like(next(row for row in rows if row is not None))
    rows = [blank if row is None else row for row in rows]
    return jnp.concatenate(rows + [blank] * (8 - len(rows)), axis=0)


def sum_rows(values):
    return jnp.sum(values.astype(F32), axis=0, keepdims=True)


def mlp_kernel(
    place, counts, a0, a1, a2, a3, b0, b1, b2, b3, att_far, rows_far, gout_far, vec_ref, fcb_ref,
    out_ref, glow_ref, keep1_ref, send1_ref, sums_ref, fcg, keep2, upper2, lower2, wo_out,
    w1, w2, wo, att_ref, rows_ref, gout_ref, h2, h2_turned, normed, total, gh2, product1, product2,
    stage, scales, sems1, sems2, sems,
):
    step = pl.program_id(0)
    wide = 2 * BLOCK
    core, z = place[48], place[50]
    block_of = lambda step: lax.rem(z + 4 - step, 4)
    block = block_of(step)
    gain = row_of(vec_ref, 3)
    loads = [
        pltpu.make_async_copy(source, target, sems.at[3 + index])
        for index, (source, target) in enumerate(
            ((att_far, att_ref), (rows_far, rows_ref), (gout_far, gout_ref))
        )
    ]

    @pl.when(step == 0)
    def _():
        bring_out_weight(place, (b0, b1, b2, b3), wo, sems.at[2], 144)
        loads[0].start()
        loads[1].start()
        loads[2].start()

        def one_block(later, _):
            column = block_of(later)
            for first, here in ((0, column // 2 == core), (2, column // 2 != core)):

                @pl.when(here)
                def _(first=first):
                    for number in (first, first + 1):

                        def bring(index, _, source=(a0, a1, a2, a3)[number], number=number):
                            spot = pl.ds(pl.multiple_of(place[64 + number * 8 + index] * 48, 16), 48)
                            for part in range(2):
                                start = pl.multiple_of(lax.rem(column, 2) * 96 + 48 * part, 16)
                                pltpu.make_async_copy(
                                    source.at[index, pl.ds(start, 48)],
                                    w1.at[column, spot, pl.ds(BLOCK * part, BLOCK)],
                                    sems1.at[column],
                                ).start()
                            return 0

                        lax.fori_loop(0, 8, bring, 0)

            for number, source in enumerate((b0, b1, b2, b3)):
                half = core if number < 2 else 1 - core
                for index in (later, jnp.where(later < 2, 4 + later, 9 - later)):
                    chip = place[144 + number * 8 + index]
                    spot = pl.ds(pl.multiple_of(chip * 192 + half * 96, 16), 96)
                    for part in range(2):
                        pltpu.make_async_copy(
                            source.at[index, pl.ds(96 * part, 96)],
                            w2.at[spot, pl.ds(BLOCK * part, BLOCK)],
                            sems2.at[column],
                        ).start()
            return 0

        lax.fori_loop(0, 4, one_block, 0)
        wait_all(wo, sems.at[2])
        pltpu.make_async_copy(wo, wo_out, sems.at[2]).start()
        bias = row_of(vec_ref, 2)
        loads[0].wait()
        loads[1].wait()
        for part in range(2):
            lanes = slice(BLOCK * part, BLOCK * (part + 1))
            total[:, lanes] = rows_ref[:, lanes].astype(F32) + dot(att_ref[...], wo[part]) + bias[:, lanes]
        normal, scale = normed_rows(total[...])
        normed[...] = normal
        scales[...] = jnp.broadcast_to(scale, scales.shape)
        low = (normal * gain + row_of(vec_ref, 4)).astype(BF)
        h2[...] = low
        h2_turned[...] = low.T
        total[...] += row_of(vec_ref, 5)
        gh2[...] = jnp.zeros_like(gh2)
        loads[2].wait()

    wait_all(w1.at[block], sems1.at[block])
    hidden = dot(h2[...], w1[block]) + fcb_ref[block]
    rows_of = pl.ds(pl.multiple_of(block * wide, wide), wide)
    wait_all(w2.at[rows_of], sems2.at[block])
    gactivated = dot(gout_ref[...], w2[rows_of, :], 1, 1)
    cumulative, slope = gelu_parts(hidden)
    activated = (hidden * cumulative).astype(BF)
    ghidden = (gactivated * slope).astype(BF)
    product1[...] = dot(h2_turned[...], ghidden)
    product2[...] = dot(activated, gout_ref[...], 0, 0)
    total[...] += dot(activated, w2[rows_of, :])
    gh2[...] += dot(ghidden, w1[block], 1, 1)
    fcg[block] = stack_rows([None, None, None, sum_rows(ghidden)])
    give_rows(place, LARGE, product1, keep1_ref, send1_ref)
    for pair in range(4):
        chip = 4 * block + pair
        for which, target in enumerate((keep2, (upper2, lower2))):
            owner = place[48] if which == 0 else 1 - place[48]
            start = pl.multiple_of(192 * pair + 96 * owner, 8)
            stage[which, chip] = product2[pl.ds(start, 96), :].astype(BF)

            def send(ref, slot, which=which, chip=chip):
                sem = sems.at[1 if ref is upper2 else 6 if ref is lower2 else 0]
                pltpu.make_async_copy(stage.at[which, chip], ref.at[slot], sem).start()

            at_slot(target, place[LARGE[which] + chip], send)

    @pl.when(step == pl.num_programs(0) - 1)
    def _():
        length = out_ref.shape[0] // 4
        row_index = lax.broadcasted_iota(jnp.int32, (length, 1), 0)
        for image in range(4):
            rows = slice(length * image, length * (image + 1))
            value = total[rows, :]
            out_ref[rows, :] = jnp.where(row_index < counts[image], value, 0.0).astype(BF)
        whole = gh2[...]
        gout = gout_ref[...].astype(F32)
        gresid = gout + norm_back(whole * gain, normed[...], scales[:, 0:1])
        low = gresid.astype(BF)
        glow_ref[...] = low
        sums_ref[...] = stack_rows(
            [sum_rows(whole * normed[...]), sum_rows(whole), sum_rows(gout), None, sum_rows(low)]
        )
        wait_all(wo, sems.at[2])
        wait_all(keep2, sems.at[0])
        wait_all(upper2, sems.at[1])
        wait_all(lower2, sems.at[6])


def attention_back_kernel(side, wo, qkv_ref, far_ref, glow_ref, gqkv_ref):
    low = glow_ref[...]
    mine = slice(BLOCK * side, BLOCK * (side + 1))
    gatt = (
        dot(low[:, :BLOCK], wo[0, mine, :], 1, 1) + dot(low[:, BLOCK:], wo[1, mine, :], 1, 1)
    ).astype(BF)
    length = low.shape[0]
    low_half = lax.broadcasted_iota(jnp.int32, (length, 128), 1) < 64
    far = far_ref[0]
    for pair in range(3):
        at = 128 * pair
        queries = qkv_ref[0, :, at : at + 128] * jnp.asarray(0.125, BF)
        key_rows = two_heads(qkv_ref[0, :, BLOCK + at : BLOCK + at + 128], low_half)
        values = two_heads(qkv_ref[0, :, 2 * BLOCK + at : 2 * BLOCK + at + 128], low_half)
        grads = gatt[:, at : at + 128]
        both = dot(key_rows, queries, 1, 1)
        gboth = dot(values, grads, 1, 1)
        probs, gscores = [], []
        for head in range(2):
            rows = slice(length * head, length * (head + 1))
            scores = both[rows] - SLOPES[6 * side + 2 * pair + head] * far
            shifted = jnp.exp(scores - jnp.max(scores, axis=0, keepdims=True))
            share = shifted * (1.0 / jnp.sum(shifted, axis=0, keepdims=True))
            weighted = share * gboth[rows]
            probs.append(share.astype(BF))
            inner = jnp.sum(weighted, axis=0, keepdims=True)
            gscores.append((weighted - share * inner).astype(BF))
        probs, gscores = jnp.concatenate(probs, axis=0), jnp.concatenate(gscores, axis=0)
        gvalues = dot(probs, grads)
        gkeys = dot(gscores, queries)
        gqkv_ref[:, at : at + 128] = (dot(gscores, key_rows, 0, 0) * 0.125).astype(BF)
        for which, result in ((1, gkeys), (2, gvalues)):
            gqkv_ref[:, which * BLOCK + at : which * BLOCK + at + 128] = jnp.where(
                low_half, result[:length], result[length:]
            ).astype(BF)


def qkv_grad_kernel(
    place, h1_turned, gqkv_ref, wq_ref, att_ref, glow_ref, gh1_ref, sums_ref, keep_ref, upper_ref, lower_ref,
    product, product_out,
):
    third, wide = gqkv_ref.shape[1], glow_ref.shape[1]
    product[...] = dot(h1_turned[...], gqkv_ref[...])
    product_out[...] = dot(att_ref[...], glow_ref[...], 0, 0)
    gh1_ref[...] = dot(gqkv_ref[...], wq_ref[...], 1, 1)
    sums_ref[...] = sum_rows(gqkv_ref[...])
    send = upper_ref, lower_ref
    give_rows(place, SMALL, product, keep_ref, send, lanes=slice(0, third))
    give_rows(place, SMALL, product_out, keep_ref, send, lanes=slice(third, third + wide))


def input_kernel(
    place, h1_turned, gqkv_ref, wq_ref, before_ref, mlp_ref, fcg_ref, rows_ref, vec_ref, glow_ref, gh1_ref,
    ginput_ref, keep_ref, upper_ref, lower_ref, product,
):
    product[...] = dot(h1_turned[...], gqkv_ref[...])
    sums = sum_rows(gqkv_ref[...])
    gradient = gh1_ref[...] + dot(gqkv_ref[...], wq_ref[...], 1, 1)
    normed, scale = normed_rows(rows_ref[...].astype(F32))
    ginput_ref[...] = (
        glow_ref[...].astype(F32) + norm_back(gradient * row_of(vec_ref, 0), normed, scale)
    ).astype(BF)
    gain, shift = sum_rows(gradient * normed), sum_rows(gradient)
    first, last = slice(0, BLOCK), slice(2 * BLOCK, 3 * BLOCK)
    biases = before_ref[:, first], sums[:, first], before_ref[:, last], sums[:, last]

    def below(group):
        lanes = slice(BLOCK * (group // 2), BLOCK * (group // 2 + 1))
        own = stack_rows([gain[:, lanes], shift[:, lanes], biases[group]])
        return jnp.concatenate([mlp_ref[...] + fcg_ref[group], own], axis=1)

    give_rows(place, SMALL, product, keep_ref, (upper_ref, lower_ref), below)


def add_up(parts):
    return sum(part.astype(F32) for part in parts)


def give_vector(target, line, device):
    count, columns = target.shape[0], line.shape[1]
    start = lax.rem(device, columns // count) * count
    moved = pltpu.roll(line, lax.rem(columns - start, columns), 1)
    target[...] = moved[:, :count].reshape(count)


def last_kernel(place, *refs):
    sources, (qkv_out, out_out), smalls = refs[:12], refs[12:14], refs[14:]
    total_a = add_up([source[0] for source in sources[:6]])
    total_c = add_up([source[0] for source in sources[6:]])
    for part in range(3):
        lanes = slice(BLOCK * part, BLOCK * (part + 1))
        qkv_out[:, 2 * BLOCK * part : 2 * BLOCK * part + BLOCK] = total_a[:, lanes]
        qkv_out[:, 2 * BLOCK * part + BLOCK : 2 * BLOCK * (part + 1)] = total_c[:24, lanes]
    out_out[...] = total_a[:, 3 * BLOCK :]
    device = place[49]
    for line, target in enumerate(smalls[:3]):
        give_vector(target, total_c[24 + line : 25 + line, 2 * BLOCK :], device)
    for line, target in enumerate(smalls[3:]):
        give_vector(target, total_c[24 + line : 25 + line, : 2 * BLOCK], device)


def after(value, *others):
    return lax.optimization_barrier((value,) + others)[0]


class Links:
    def __init__(self, depth):
        self.depth = depth

        def table(move):
            pairs = []
            for z in range(depth):
                for x in range(2):
                    for y in range(2):
                        for c in range(2):
                            nz, nx, ny, nc = move(z, x, y, c)
                            source = (z * 2 + x) * 4 + y * 2 + c
                            pairs.append((source, ((nz % depth) * 2 + nx) * 4 + ny * 2 + nc))
            return pairs

        self.ups = {step: table(lambda z, x, y, c: (z + step, x, y, c)) for step in (1, 2, 3)}
        self.first = table(lambda z, x, y, c: (z, x, 1 - y, c) if c else (z, 1 - x, y, c))
        self.second = table(lambda z, x, y, c: (z, 1 - x, y, c) if c else (z, x, 1 - y, c))
        self.across = table(lambda z, x, y, c: (z, 1 - x, 1 - y, c))
        self.cores = table(lambda z, x, y, c: (z, x, y, 1 - c))
        self.near = table(lambda z, x, y, c: (z ^ 1, x, y, c))
        self.far = table(lambda z, x, y, c: (z ^ 2, x, y, c))

    def move(self, value, pairs):
        return lax.ppermute(value, AXES, pairs)

    def spots(self):
        dp, fsdp = lax.axis_index("dp"), lax.axis_index("fsdp")
        z, x, y, core = dp // 2, dp % 2, fsdp // 2, fsdp % 2

        def chip(c, flip1, flip2, step):
            flip_x = jnp.where(c == 0, flip1, flip2)
            flip_y = jnp.where(c == 0, flip2, flip1)
            return (((z - step) % self.depth) * 2 + (x ^ flip_x)) * 2 + (y ^ flip_y)

        index = jnp.arange(32, dtype=jnp.int32)
        whose = jnp.where(index < 16, core, 1 - core)
        flip2 = (index // 8) % 2
        z_first = chip(whose, (index // 4) % 2, flip2, index % 4)
        x_first = chip(whose, index % 2, (index // 2) % 2, (index // 4) % 4)
        chips = jnp.arange(16, dtype=jnp.int32)
        turn_x, turn_y = ((chips // 2) % 2) ^ x, (chips % 2) ^ y
        far_z = (chips // 4) ^ z
        near, wide_step = far_z % 2, far_z // 2

        def slots(order):
            turns = {"x": turn_x, "y": turn_y, "near": near, "far": wide_step}
            return sum(turns[name] * weight for name, weight in zip(order, (8, 4, 2, 1)))

        others = jnp.stack([core, dp * 4 + fsdp, z]).astype(jnp.int32)
        rest = jnp.concatenate([others, jnp.zeros((13,), jnp.int32)])
        tables = []
        for orders in (
            (("y", "x", "near", "far"), ("x", "y", "near", "far")),
            (("y", "near", "x", "far"), ("x", "near", "y", "far")),
        ):
            both = [slots(order) for order in orders]
            tables += [jnp.where(core == 0, both[0], both[1]), jnp.where(core == 0, both[1], both[0])]
        swapped = jnp.where(index % 8 >= 6, 9 - index % 8, index % 4)
        swapped = chip(whose, (index // 4) % 2, flip2, swapped)
        parts = [z_first, tables[0], rest, x_first] + tables[1:] + [swapped]
        return jnp.concatenate(parts).astype(jnp.int32)

    def gather(self, piece_a, piece_b1, piece_b2, inputs, prepare):
        hold = lax.optimization_barrier
        up = lambda value, step: self.move(value, self.ups[step])
        a_one, a_three, b1_two = hold((up(piece_a, 1), up(piece_a, 3), self.move(piece_b1, self.first)))
        b1_two = jnp.stack([piece_b1, b1_two])
        a_two, b1_four = hold((up(a_one, 1), self.move(b1_two, self.second)))
        a_four = jnp.stack([piece_a, a_one, a_two, a_three])
        b1_four = jnp.concatenate([b1_two, b1_four])
        piece_b2 = after(piece_b2, a_two)
        a_rest, b2_one, b2_three = hold((self.move(a_four, self.first), up(piece_b2, 1), up(piece_b2, 3)))
        early = prepare(*after(inputs, a_rest))
        a_eight = jnp.concatenate([a_four, a_rest])
        b2_rest = self.move(jnp.stack([piece_b2, b2_one, b2_three]), self.first)
        a_other, b2_two, b1_one, b2_rest, early = hold(
            (self.move(a_eight, self.second), up(b2_one, 1), up(after(b1_four, a_rest), 1), b2_rest, early)
        )
        b2_seven = jnp.concatenate([jnp.stack([piece_b2, b2_one, b2_two, b2_three]), b2_rest])
        a = self.finish(a_eight, a_other)
        b1 = b1_four, b1_one, up(b1_one, 1), up(b1_four, 3)
        b2_last, b2_across = self.move(b2_two[None], self.first), self.move(b2_two[None], self.across)
        return a, b1, (b2_seven, b2_last, self.move(b2_seven, self.second), b2_across), early

    def gather_end(self, b1, b2, done):
        b1_four, b1_one, b1_two, b1_three = b1
        b2_seven, b2_last, other_seven, other_last = b2
        b2_last, done = lax.optimization_barrier((b2_last, done))
        b2_mine, b1_mine = jnp.concatenate([b2_seven, b2_last]), jnp.concatenate([b1_four, b1_one])
        b2_theirs, b1_theirs = self.move(b2_mine, self.cores), self.move(b1_mine, self.cores)
        b1_two, b1_three, other_seven, other_last, done = lax.optimization_barrier(
            (b1_two, b1_three, other_seven, other_last, done)
        )
        b2_rest, b1_rest = jnp.concatenate([other_seven, other_last]), jnp.concatenate([b1_two, b1_three])
        b1 = b1_mine, b1_rest, b1_theirs, self.move(b1_rest, self.cores)
        return done, b1, (b2_mine, b2_rest, b2_theirs, self.move(b2_rest, self.cores))

    def finish(self, eight, rest):
        return (eight, rest, self.move(eight, self.cores), self.move(rest, self.cores))

    def fold(self, state):
        left = 32 >> (len(state) - 1)
        return add_up([part[left // 2 : left] for part in state]).astype(BF)

def full_pieces(full, blocks):
    split = full.reshape((CHIPS, 48) + full.shape[1:])
    split = split.transpose(3, 0, 2, 1, 4) if full.shape[1] == blocks else split.transpose(2, 0, 3, 1, 4)
    return split.reshape(2 * CHIPS, blocks * 48, BLOCK)


STILL = [
    16 * core + ((-step % 4) * 2 + (flip2 if core else flip1)) * 2 + (flip1 if core else flip2)
    for core in range(2)
    for flip2 in range(2)
    for flip1 in range(2)
    for step in range(4)
]


STILL_LAST = [STILL[8 * array + index] for array in range(4) for index in (0, 1, 2, 3, 4, 5, 7, 6)]


def eights(pieces, order=None):
    if order is not None:
        pieces = jnp.stack([pieces[index] for index in order])
    return tuple(pieces[8 * index : 8 * (index + 1)] for index in range(4))


def placed(vector, device, per_row):
    start = (device % per_row) * vector.shape[0]
    return lax.dynamic_update_slice(jnp.zeros((BLOCK,), vector.dtype), vector, (start,))


def shards(
    mesh_shape,
    patches,
    counts,
    positions,
    ln1_gain,
    ln1_bias,
    qkv_weight,
    qv_bias,
    out_weight,
    out_bias,
    ln2_gain,
    ln2_bias,
    fc1_weight,
    fc1_bias,
    fc2_weight,
    fc2_bias,
    cotangent,
):
    images, length, width = patches.shape
    padded = (length + 31) // 32 * 32
    rows = images * padded
    hidden_width = fc1_weight.shape[1]
    devices = mesh_shape["dp"] * mesh_shape["fsdp"]
    by_hand = devices == 2 * CHIPS and mesh_shape["fsdp"] == 4
    small_parts = (ln1_gain, ln1_bias, out_bias, ln2_gain, ln2_bias, fc2_bias, qv_bias, fc1_bias)

    smem = pl.BlockSpec(memory_space=pltpu.SMEM)
    vmem = pl.BlockSpec(memory_space=pltpu.VMEM)
    anywhere = pl.BlockSpec(memory_space=pltpu.HBM)
    struct = jax.ShapeDtypeStruct

    def prepare(patches, counts, positions, cotangent):
        row_index = jnp.arange(padded, dtype=jnp.int32)
        is_live = row_index[None, :] < counts[:, None]
        pad_rows = ((0, 0), (0, padded - length), (0, 0))
        rows_in = jnp.pad(patches, pad_rows).reshape(rows, width)
        gout = jnp.where(is_live[:, :, None], jnp.pad(cotangent, pad_rows), 0).reshape(rows, width)
        spots = jnp.pad(positions, pad_rows[:2])
        grid_rows = (spots // SIDE).astype(F32)
        grid_cols = (spots % SIDE).astype(F32)
        row_delta = grid_rows[:, :, None] - grid_rows[:, None, :]
        col_delta = grid_cols[:, :, None] - grid_cols[:, None, :]
        distance = jnp.sqrt(row_delta * row_delta + col_delta * col_delta)
        far = jnp.where(is_live[:, None, :], distance, FAR)
        far_turned = jnp.where(is_live[:, :, None], distance, FAR)
        return rows_in, gout, far, far_turned

    if by_hand:
        links = Links(mesh_shape["dp"] // 2)
        place = links.spots()
        core = place[48]
        share = struct((8, 24, BLOCK), BF)
        mine, theirs, lines = pl.pallas_call(
            share_kernel,
            out_shape=(share, share, struct((16, BLOCK), BF)),
            in_specs=[smem] + [vmem] * 11,
            out_specs=(vmem,) * 3,
            name="share",
        )(place, qkv_weight, out_weight, fc1_weight, *small_parts)
        got = links.move(theirs, links.cores)
        pieces = pl.pallas_call(
            pair_kernel,
            out_shape=tuple(struct((height, BLOCK), BF) for height in (160, 192, 240)),
            in_specs=[smem] + [vmem] * 4,
            out_specs=(vmem,) * 3,
            name="pair",
        )(place, mine, got, lines, fc2_weight)
    else:
        links = None
        place = jnp.concatenate(
            [
                jnp.array([chip % CHIPS for chip in STILL], jnp.int32),
                jnp.arange(16, dtype=jnp.int32),
                jnp.zeros((16,), jnp.int32),
                jnp.arange(80, dtype=jnp.int32) % 16,
                jnp.array([chip % CHIPS for chip in STILL_LAST], jnp.int32),
            ]
        )
        whole = [lax.all_gather(part, AXES, axis=0, tiled=True) for part in small_parts]
        lines = []
        for part in whole:
            share = part.shape[0] // 32
            chunks = part.reshape(32, share)
            lines.append(
                jnp.stack([placed(chunks[index], index, BLOCK // share) for index in range(32)])
            )
        lines = jnp.concatenate([jnp.stack(lines, axis=1), jnp.zeros((32, 8, BLOCK), BF)], axis=1)
        lines = lines.reshape(CHIPS, 2, 16, BLOCK).transpose(1, 0, 2, 3).reshape(32, 16, BLOCK)
        whole_qkv = lax.all_gather(qkv_weight, AXES, axis=0, tiled=True)
        whole_out = lax.all_gather(out_weight, AXES, axis=0, tiled=True)
        whole_fc1 = lax.all_gather(fc1_weight, AXES, axis=0, tiled=True)
        whole_fc2 = lax.all_gather(fc2_weight, AXES, axis=0, tiled=True)
        split = whole_fc2.reshape(CHIPS, 2, 96, 2, BLOCK).transpose(1, 0, 3, 2, 4).reshape(32, 192, BLOCK)
        gathered_a = eights(
            jnp.concatenate([full_pieces(whole_qkv.reshape(width, 3, 2, BLOCK), 3), lines], axis=1), STILL
        )
        gathered_b1 = eights(full_pieces(whole_fc1.reshape(width, 2, 4, BLOCK), 4))
        split = whole_fc2.reshape(CHIPS, 2, 96, 2, BLOCK).transpose(1, 0, 3, 2, 4).reshape(32, 192, BLOCK)
        gathered_b2 = eights(
            jnp.concatenate([split, full_pieces(whole_out.reshape(width, 1, 2, BLOCK), 1)], axis=1), STILL_LAST
        )

    if by_hand:
        gathered_a, on_b1, on_b2, early = links.gather(*pieces, (patches, counts, positions, cotangent), prepare)
    else:
        early = prepare(patches, counts, positions, cotangent)
    rows_in, gout, far, far_turned = early

    def call(kernel, operands, out_shape, out_specs, in_specs, flops, mib, vmem_mib, grid, scratch=(), name=None):
        return pl.pallas_call(
            kernel,
            grid=grid,
            out_shape=out_shape,
            in_specs=in_specs,
            out_specs=out_specs,
            scratch_shapes=list(scratch),
            compiler_params=pltpu.CompilerParams(vmem_limit_bytes=vmem_mib * MIB),
            cost_estimate=pl.CostEstimate(
                flops=1, bytes_accessed=1, transcendentals=0
            ),
            name=name,
        )(*operands)

    image_rows = lambda columns: pl.BlockSpec((padded, columns), lambda image: (image, 0))
    image_far = pl.BlockSpec((1, padded, padded), lambda image: (image, 0, 0))
    fixed = lambda *shape: pl.BlockSpec(shape, lambda step: (0,) * len(shape))
    step_rows = lambda columns: pl.BlockSpec((rows, columns), lambda step: (0, step))
    shares = lambda height, columns: struct((CHIPS, height, columns), BF)
    buffer, flag = pltpu.VMEM, pltpu.SemaphoreType.DMA
    low_rows, wide_rows = struct((rows, width), BF), struct((rows, width), F32)
    wide = 2 * BLOCK
    steps = hidden_width // wide
    third = 3 * BLOCK

    def join(value, *others):
        return after(value, *others) if by_hand else value

    vec, fcb, h1_turned, qkv, att, wq_0, wq_1 = pl.pallas_call(
        first_kernel,
        out_shape=(
            struct((2, 16, BLOCK), F32), struct((steps, 1, wide), F32), struct((width, rows), BF),
            struct((2, rows, third), BF), low_rows, struct((width, third), BF), struct((width, third), BF),
        ),
        in_specs=[smem] + [anywhere] * 4 + [vmem] * 2,
        out_specs=(vmem,) * 5 + (anywhere,) * 2,
        scratch_shapes=[
            buffer((2, width, third), BF), buffer((rows, width), BF), buffer((4, 16, BLOCK), F32),
            buffer((32, 16, BLOCK), BF), flag((5,)),
        ],
        compiler_params=pltpu.CompilerParams(vmem_limit_bytes=18 * MIB),
        cost_estimate=pl.CostEstimate(flops=1, bytes_accessed=1, transcendentals=0),
        name="first",
    )(place, *gathered_a, rows_in, far)
    if by_hand:
        att, gathered_b1, gathered_b2 = links.gather_end(on_b1, on_b2, att)

    step_shares = lambda height, columns: pl.BlockSpec((CHIPS, height, columns), lambda step: (0, 0, step))
    still = lambda *shape: pl.BlockSpec(shape, lambda step, place: (0,) * len(shape))
    turned_shares = pl.BlockSpec(
        (CHIPS, 24, wide), lambda step, place: (0, 0, lax.rem(place[50] + 4 - step, 4))
    )
    low_buffer, wide_buffer = buffer((rows, width), BF), buffer((rows, width), F32)
    out, glow, keep_1, send_1, sums, fcg, keep_2, upper_2, lower_2, wo = pl.pallas_call(
        mlp_kernel,
        grid_spec=pltpu.PrefetchScalarGridSpec(
            num_scalar_prefetch=1,
            grid=(steps,),
            in_specs=[smem] + [anywhere] * 11 + [still(2, 16, BLOCK), still(steps, 1, wide)],
            out_specs=(still(rows, width),) * 2
            + (turned_shares,) * 2
            + (still(8, wide), still(steps, 8, wide))
            + (anywhere,) * 4,
            scratch_shapes=[
                buffer((steps, width, wide), BF), buffer((hidden_width, width), BF), buffer((2, width, BLOCK), BF),
                low_buffer, low_buffer, low_buffer, low_buffer, buffer((width, rows), BF),
                wide_buffer, wide_buffer, wide_buffer, buffer((width, wide), F32), buffer((width, wide), F32),
                buffer((2, CHIPS, 96, wide), BF), buffer((rows, 128), F32), flag((steps,)), flag((steps,)), flag((7,)),
            ],
        ),
        out_shape=(low_rows, low_rows)
        + (shares(24, hidden_width),) * 2
        + (struct((8, wide), F32), struct((steps, 8, wide), F32))
        + (shares(96, wide),)
        + (struct((8, 96, wide), BF),) * 2
        + (struct((2, width, BLOCK), BF),),
        compiler_params=pltpu.CompilerParams(vmem_limit_bytes=52 * MIB),
        cost_estimate=pl.CostEstimate(flops=1, bytes_accessed=1, transcendentals=0),
        name="mlp",
    )(place, counts, *gathered_b1, *gathered_b2, att, rows_in, gout, vec, fcb)

    if by_hand:
        state_2 = keep_2, links.move(upper_2, links.cores)

    def attention_back(side, gradient):
        return call(
            lambda *refs: attention_back_kernel(side, *refs),
            (wo, qkv, far_turned, gradient),
            struct((rows, third), BF),
            image_rows(third),
            [
                fixed(2, width, BLOCK), pl.BlockSpec((1, padded, third), lambda image: (side, image, 0)),
                image_far, image_rows(width),
            ],
            8 * rows * 256 * width,
            8,
            20,
            grid=(images,),
            name="attention_back",
        )

    part_2 = glow
    if by_hand:
        part_2 = add_up([keep_2[8:], state_2[1]]).astype(BF)
        lower_2, send_1 = after((lower_2, send_1), part_2)
        state_2 = keep_2, links.move(lower_2, links.cores), links.move(part_2, links.second)
        state_1 = keep_1, links.move(send_1, links.cores)
    gqkv_0 = attention_back(0, join(glow, part_2))
    if by_hand:
        state_1, gqkv_0 = lax.optimization_barrier((state_1, gqkv_0))
        state_1 += (links.move(links.fold(state_1), links.second),)

    def grad_call(kernel, operands, out_shape, scratch, name):
        return pl.pallas_call(
            kernel,
            out_shape=out_shape,
            in_specs=[smem] + [vmem] * (len(operands) - 1),
            out_specs=(vmem,) * len(out_shape),
            scratch_shapes=list(scratch),
            compiler_params=pltpu.CompilerParams(vmem_limit_bytes=28 * MIB),
            cost_estimate=pl.CostEstimate(flops=1, bytes_accessed=1, transcendentals=0),
            name=name,
        )(*operands)

    half_shares = lambda height, columns: (struct((8, height, columns), BF),) * 2
    gh1, sums_0, keep_a, upper_a, lower_a = grad_call(
        qkv_grad_kernel,
        (place, h1_turned, gqkv_0, wq_0, att, glow),
        (wide_rows, struct((1, third), F32), shares(24, third + wide)) + half_shares(24, third + wide),
        (buffer((width, third), F32), buffer((width, wide), F32)),
        "qkv_grad",
    )
    parts = gh1
    if by_hand:
        got_a = links.move(upper_a, links.cores)
        state_2, got_a, gh1 = lax.optimization_barrier((state_2, got_a, gh1))
        parts = links.fold(state_2), add_up([keep_a[8:], got_a]).astype(BF)
        state_2 += (links.move(parts[0], links.near),)
        lower_a = after(lower_a, parts)
        state_a = keep_a, links.move(lower_a, links.cores), links.move(parts[1], links.second)

    gqkv_1 = attention_back(1, join(glow, gh1, parts))
    ginput, keep_c, upper_c, lower_c = grad_call(
        input_kernel,
        (place, h1_turned, gqkv_1, wq_1, sums_0, sums, fcg, rows_in, vec, glow, gh1),
        (low_rows, shares(32, third)) + half_shares(32, third),
        (buffer((width, third), F32),),
        "input_grad",
    )

    def cut(value):
        return value.reshape(images, padded, width)[:, :length]

    if by_hand:
        fold, move = links.fold, links.move

        state_c = keep_c, move(upper_c, links.cores)
        rest_c = move(after(lower_c, keep_c), links.cores)
        state_1 = after(state_1, keep_c)
        part = fold(state_1)
        state_1 += (move(part, links.near),)
        keep_c, got_c = after(state_c, part)
        part = add_up([keep_c[8:], got_c]).astype(BF)
        state_c = keep_c, rest_c, move(part, links.second)
        state_2, state_a, out, ginput = after((state_2, state_a, out, ginput), part)
        out, ginput = cut(out), cut(ginput)
        state_2, state_a, out, ginput = after((state_2, state_a, out, ginput))
        parts = fold(state_2), fold(state_a)
        state_2 += (move(parts[0], links.first),)
        state_a += (move(parts[1], links.first),)
        part = fold(after(state_c, parts))
        state_c += (move(part, links.first),)
        state_1, out, ginput = after((state_1, out, ginput), part)
        part = fold(state_1)
        state_1 += (move(part, links.first),)
        state_2 = after(state_2, part)
        part = fold(state_2)
        state_2 += (move(part, links.far),)
        state_a = after(state_a, part)
        part = fold(state_a)
        state_a += (move(part, links.near),)
        part = fold(after(state_c, part))
        state_c += (move(part, links.near),)
        state_1 = after(state_1, part)
        part = fold(state_1)
        state_1 += (move(part, links.far),)
        state_a = after(state_a, part)
        part = fold(state_a)
        state_a += (move(part, links.far),)
        part = fold(after(state_c, part))
        state_c += (move(part, links.far),)
        state_2 = after(state_2, part)
        mine_2 = add_up([part[0] for part in state_2])
        state_1 = after(state_1, mine_2)
        mine_1 = add_up([part[0] for part in state_1])
        own_slot = lambda part: pl.BlockSpec((1,) + part.shape[1:], lambda step: (0, 0, 0))
        heights, counts_out = ((24, 3 * width), (24, width)), (24, 24, 48, 24, 24, 24, 96, 24)
        (
            qkv_grad, out_grad, ln1_gain_grad, ln1_bias_grad, qv_bias_grad,
            ln2_gain_grad, ln2_bias_grad, fc2_bias_grad, fc1_bias_grad, out_bias_grad,
        ) = pl.pallas_call(
            last_kernel,
            grid=(1,),
            out_shape=tuple(struct(shape, F32) for shape in heights + tuple((count,) for count in counts_out)),
            in_specs=[smem] + [own_slot(part) for part in state_a + state_c],
            out_specs=tuple(fixed(*shape) for shape in heights)
            + tuple(pl.BlockSpec((count,), lambda step: (0,)) for count in counts_out),
            compiler_params=pltpu.CompilerParams(vmem_limit_bytes=30 * MIB),
            name="last",
        )(place, *state_a, *state_c)
        return (
            out, ginput, ln1_gain_grad, ln1_bias_grad, qkv_grad, qv_bias_grad, out_grad, out_bias_grad,
            ln2_gain_grad, ln2_bias_grad, mine_1, fc1_bias_grad, mine_2, fc2_bias_grad,
        )

    both_a, both_c, both_1, both_2 = (
        jnp.stack(pair, axis=1).astype(F32)
        for pair in (
            (keep_a, jnp.concatenate([lower_a, upper_a])),
            (keep_c, jnp.concatenate([lower_c, upper_c])),
            (keep_1, send_1),
            (keep_2, jnp.concatenate([lower_2, upper_2])),
        )
    )
    heads = jnp.stack(
        [both.reshape(CHIPS, 2, 24, 3, BLOCK) for both in (both_a[..., :third], both_c[:, :, :24])], axis=4
    )

    def vector(lines, count):
        columns = lines.shape[-1]
        return lines.reshape(32 * count // columns, -1, columns)[:, 0].reshape(-1)

    small_c, small_2 = both_c[:, :, 24:, 2 * BLOCK :], both_c[:, :, 24:, : 2 * BLOCK]
    totals = (
        vector(small_c[:, :, 0], 24),
        vector(small_c[:, :, 1], 24),
        heads.reshape(width, 3 * width),
        vector(small_c[:, :, 2], 48),
        both_a[..., third:].reshape(width, width),
        vector(small_2[:, :, 4], 24),
        vector(small_2[:, :, 0], 24),
        vector(small_2[:, :, 1], 24),
        both_1.reshape(width, hidden_width),
        vector(small_2[:, :, 3], 96),
        both_2.reshape(hidden_width, width),
        vector(small_2[:, :, 2], 24),
    )
    return (cut(out), cut(ginput)) + tuple(
        lax.psum_scatter(total, AXES, scatter_dimension=0, tiled=True) for total in totals
    )


def solution(mesh):
    rows = P(AXES, None, None)
    table = P(AXES, None)
    line = P(AXES)
    in_specs = (
        rows, line, table, line, line, table, line, table, line, line, line, table, line, table, line, rows,
    )
    out_specs = (
        rows, rows, line, line, table, line, table, line, line, line, table, line, table, line,
    )
    mesh_shape = dict(mesh.shape)

    def body(*arrays):
        return shards(mesh_shape, *arrays)

    return jax.shard_map(body, mesh=mesh, in_specs=in_specs, out_specs=out_specs, check_vma=False)
```
